32 devices in a mesh: rep: 2 (over y), fsdp: 16 (over z, x, core).
Axes of the slice: x: 2, y: 2, z: 4, core: 2. Of those that a mesh axis runs over, the one named last changes fastest.
Arguments:
- tokens: bfloat16 [32, 256, 1536], P(('rep', 'fsdp')), may hold values from -6 to 6
- doc_lengths: int32 [32, 8], P(('rep', 'fsdp')), may hold values from 1 to 128, 256 in all within a row
- pad_counts: int32 [32], P(('rep', 'fsdp')), may hold values from 0 to 63
- norm_in: bfloat16 [1536], P('fsdp'), may hold values from 0.25 to 1.75
- w_qkv: bfloat16 [1536, 4608], P('fsdp'), may hold values from -0.15625 to 0.15625
- kernel: float32 [16, 6, 11], replicated, may hold values from -1.2 to 1.2
- mixing: float32 [16, 2], replicated, may hold values from -4.2 to 4.2
- norm_heads: bfloat16 [1536], P('fsdp'), may hold values from 0.25 to 1.75
- w_out: bfloat16 [1536, 1536], P('fsdp'), may hold values from -0.15625 to 0.15625
- norm_mid: bfloat16 [1536], P('fsdp'), may hold values from 0.25 to 1.75
- w_gate: bfloat16 [1536, 4096], P('fsdp'), may hold values from -0.15625 to 0.15625
- w_up: bfloat16 [1536, 4096], P('fsdp'), may hold values from -0.15625 to 0.15625
- w_down: bfloat16 [4096, 1536], P('fsdp'), may hold values from -0.09375 to 0.09375
- cotangent: bfloat16 [32, 256, 1536], P(('rep', 'fsdp')), may hold values from -6 to 6
Outputs:
- layer_out: float32 [32, 256, 1536], P(('rep', 'fsdp'))
- grad_tokens: float32 [32, 256, 1536], P(('rep', 'fsdp'))
- grad_norm_in: float32 [1536], P('fsdp')
- grad_w_qkv: float32 [1536, 4608], P('fsdp')
- grad_kernel: float32 [16, 6, 11], replicated
- grad_mixing: float32 [16, 2], replicated
- grad_norm_heads: float32 [1536], P('fsdp')
- grad_w_out: float32 [1536, 1536], P('fsdp')
- grad_norm_mid: float32 [1536], P('fsdp')
- grad_w_gate: float32 [1536, 4096], P('fsdp')
- grad_w_up: float32 [1536, 4096], P('fsdp')
- grad_w_down: float32 [4096, 1536], P('fsdp')
The draws below stay inside these ranges and needn't reach their ends.
Inputs may be any that keep to these rules, and one draw needn't show every extreme that they name: `doc_lengths`: in each row the 8 lengths sum to 256; the longest is 128.
All inputs are finite; a program needn't handle non-finite values.
Results may differ from the reference program's by a relative error of at most 0.019.
The reference program's roundings to bfloat16 on the way count: a program that leaves them out, or rounds other values in their place, can miss the bound.
Values may be sent and summed in bfloat16 or wider, within the bound.
A program may use at most 320 MiB of HBM per device.

```python
import math
import jax
import jax.numpy as jnp
import numpy as np
from jax import lax

D = 1536
H = 16
FF = 4096
KQ = 6
KK = 11
DOCS = 8
ROW = 256
ROWS = 32


def with_ends(drawn, own_key, low, top_value):
    spot = [jax.random.randint(jax.random.fold_in(own_key, axis), (), 0, length) for axis, length in enumerate(drawn.shape)]
    main_axis = drawn.shape.index(max(drawn.shape))
    beside = spot[:main_axis] + [(spot[main_axis] + 1) % drawn.shape[main_axis]] + spot[main_axis + 1:]
    return drawn.at[tuple(spot)].set(low).at[tuple(beside)].set(top_value)


def shard_levels(stream_key, extent, shards, smallest, high):
    def one(axis_at, blocks):
        draws = jax.random.uniform(jax.random.fold_in(jax.random.fold_in(stream_key, 6), axis_at), (blocks,), jnp.float32, smallest / len(shards), high / len(shards))
        return jnp.repeat(jnp.exp(draws), extent[axis_at] // blocks).reshape((-1,) + (1,) * (len(extent) - axis_at - 1))

    factor_of = one(*shards[0])
    for cut in shards[1:]:
        factor_of = factor_of * one(*cut)
    return factor_of


def split_up(amount, total, limit, slope):
    weights = [(1 << 20) // math.isqrt(standing ** slope) + 1 for standing in range(2, amount + 1)]
    spare, counts = total - limit - (amount - 1), [1] * (amount - 1)
    while spare > 0:
        candidates = [i for i in range(amount - 1) if counts[i] < limit]
        pool, remaining = sum([weights[i] for i in candidates]), spare
        for i in candidates:
            extra = min(limit - counts[i], max(1, remaining * weights[i] // pool), spare)
            counts[i] = counts[i] + extra
            spare = spare - extra
    return np.array([limit] + counts)


def uneven(rng, number_of, total, bound, slope):
    if number_of == 2:
        one = jax.random.randint(rng, (), max(1, total - bound), min(bound, total - 1) + 1)
        return jnp.stack([one, total - one])
    lengths = jnp.asarray(split_up(number_of, total, bound, slope), jnp.int32)
    couples = (number_of - 1) // 2
    giver, receiver = lengths[1:1 + 2 * couples:2], lengths[2:2 + 2 * couples:2]
    room = jnp.minimum(giver - 1, bound - receiver)
    passed = jax.random.randint(jax.random.fold_in(rng, 1), (couples,), 0, 1 << 20) % (room + 1)
    lengths = lengths.at[1:1 + 2 * couples:2].set(giver - passed).at[2:2 + 2 * couples:2].set(receiver + passed)
    return lengths[jax.random.permutation(jax.random.fold_in(rng, 2), number_of)]


def noise(own_key, extent, scale, bound, cuts=(), kind=jnp.bfloat16):
    result = jax.random.normal(own_key, extent, jnp.float32) * scale
    if len(cuts) > 0:
        result = shard_levels(own_key, extent, cuts, -0.22, 0.18) * result
    return jnp.clip(result, min=-bound, max=bound).astype(kind)


def setup_inputs(seed: int = 0) -> dict:
    key_list = jax.random.split(jax.random.key(seed), 15)
    tokens = noise(key_list[0], (ROWS, ROW, D), 1.0, 6.0, ((0, 32),))
    doc_lengths = jax.vmap(lambda own: uneven(own, DOCS, ROW, ROW // 2, 2))(jax.random.split(key_list[1], ROWS)).reshape((ROWS, DOCS)).astype(jnp.int32)
    pad_counts = with_ends(jax.random.randint(key_list[2], (ROWS,), 0, ROW // 4), jax.random.fold_in(key_list[2], 1), 0, (ROW // 4) - 1).astype(jnp.int32)
    norm_in = jnp.clip(1.0 + 0.15 * jax.random.normal(key_list[3], (D,), jnp.float32), 0.25, 1.75).astype(jnp.bfloat16)
    w_qkv = noise(key_list[4], (D, 3 * D), D ** -0.5, 0.15625, ((0, 16),))
    kernel = noise(key_list[5], (H, KQ, KK), 0.2, 1.2, (), jnp.float32)
    mixing = noise(key_list[6], (H, 2), 0.7, 4.2, (), jnp.float32)
    norm_heads = jnp.clip(1.0 + 0.15 * jax.random.normal(key_list[7], (D,), jnp.float32), 0.25, 1.75).astype(jnp.bfloat16)
    w_out = noise(key_list[8], (D, D), D ** -0.5, 0.15625, ((0, 16),))
    norm_mid = jnp.clip(1.0 + 0.15 * jax.random.normal(key_list[9], (D,), jnp.float32), 0.25, 1.75).astype(jnp.bfloat16)
    w_gate = noise(key_list[10], (D, FF), D ** -0.5, 0.15625, ((0, 16),))
    w_up = noise(key_list[11], (D, FF), D ** -0.5, 0.15625, ((0, 16),))
    w_down = noise(key_list[12], (FF, D), FF ** -0.5, 0.09375, ((0, 16),))
    cotangent = noise(key_list[13], (ROWS, ROW, D), 1.0, 6.0, ((0, 32),))
    return dict(tokens=tokens, doc_lengths=doc_lengths, pad_counts=pad_counts, norm_in=norm_in, w_qkv=w_qkv, kernel=kernel, mixing=mixing, norm_heads=norm_heads, w_out=w_out, norm_mid=norm_mid, w_gate=w_gate, w_up=w_up, w_down=w_down, cotangent=cotangent)


@jax.custom_vjp
def low(v):
    return lax.optimization_barrier(v.astype(jnp.bfloat16)).astype(jnp.float32)

@jax.custom_vjp
def low_back(v):
    return v

def low_keep(v):
    return (low(v), None)

def low_pass(kept, grad):
    return (grad,)

def back_keep(v):
    return (v, None)

def back_low(kept, grad):
    return (low(grad),)
low.defvjp(low_keep, low_pass)
low_back.defvjp(back_keep, back_low)
HIGH = lax.Precision.HIGHEST
NEG_FILL = -1e+30

def rms_norm(values_in, scaling):
    return values_in * lax.rsqrt(lax.optimization_barrier(jnp.mean(values_in * values_in, axis=-1, keepdims=True)) + 1e-06) * scaling

def group_norm(values_in, scaling):
    centred = values_in - lax.optimization_barrier(jnp.mean(values_in, axis=-1, keepdims=True))
    scaled = centred * lax.rsqrt(lax.optimization_barrier(jnp.mean(centred * centred, axis=-1, keepdims=True)) + 1e-05)
    return scaled.reshape(values_in.shape[0], -1) * scaling

def convolve(scores, kernel):
    length = scores.shape[1]
    taps_query = kernel.shape[1]
    taps_key = kernel.shape[2]
    half_width = taps_key // 2
    padded = jnp.pad(scores, ((0, 0), (taps_query - 1, 0), (half_width, half_width)))
    summed = jnp.zeros_like(scores)
    for shift_q in range(taps_query):
        for shift_k in range(taps_key):
            start_q = taps_query - 1 - shift_q
            window = padded[:, start_q:start_q + length, shift_k:shift_k + length]
            summed = summed + kernel[:, shift_q, shift_k][:, None, None] * window
    return summed

def build_mask(doc_lengths, pad_count, length):
    places = jnp.arange(length, dtype=jnp.int32)
    doc_ends = jnp.cumsum(doc_lengths).astype(jnp.int32)
    segment = lax.optimization_barrier(jnp.sum((places[:, None] >= doc_ends[None, :]).astype(jnp.int32), axis=1))
    live_end = length - pad_count
    same_doc = segment[:, None] == segment[None, :]
    causal = places[None, :] <= places[:, None]
    usable = (places[None, :] < live_end) | (places[None, :] == places[:, None])
    return same_doc & causal & usable

def attend(queries, key_rows, value_rows, kernel, mixing, allowed):
    length = queries.shape[0]
    head_count = queries.shape[1]
    score_scale = queries.shape[-1] ** (-0.5)
    raw_scores = jnp.einsum('ihe,jhe->hij', queries, key_rows, precision=HIGH) * score_scale
    masked = jnp.where(allowed[None], raw_scores, 0.0)
    logits = jnp.where(allowed[None], convolve(masked, kernel), NEG_FILL)
    row_peak = lax.optimization_barrier(jnp.max(logits, axis=-1, keepdims=True))
    log_total = row_peak + jnp.log(lax.optimization_barrier(jnp.sum(jnp.exp(logits - row_peak), axis=-1, keepdims=True)))
    attn_probs = jnp.exp(logits - log_total)
    pair_probs = attn_probs.reshape(head_count // 2, 2, length, length)
    mix_pairs = mixing.reshape(head_count // 2, 2, 2)
    mixed_probs = jnp.einsum('pog,pgij->poij', mix_pairs, pair_probs, precision=HIGH)
    mixed_probs = mixed_probs.reshape(head_count, length, length)
    return low_back(jnp.einsum('hij,jhe->ihe', mixed_probs, value_rows, precision=HIGH))

def layer_row(weight_set, row_inputs):
    norm_in, w_qkv, kernel, mixing, norm_heads, w_out, norm_mid, w_gate, w_up, w_down = weight_set
    tokens, doc_lengths, pad_count = row_inputs
    length = tokens.shape[0]
    model_width = tokens.shape[1]
    head_count = kernel.shape[0]
    allowed = build_mask(doc_lengths, pad_count, length)
    normed = low(rms_norm(tokens, norm_in))
    projected = low(low_back(jnp.dot(normed, w_qkv, precision=HIGH)))
    split_qkv = projected.reshape(length, 3, head_count, model_width // head_count)
    attended = attend(split_qkv[:, 0], split_qkv[:, 1], split_qkv[:, 2], kernel, mixing, allowed)
    gated_out = low(group_norm(attended, norm_heads))
    branch = low_back(jnp.dot(gated_out, w_out, precision=HIGH))
    residual = tokens + branch
    normed_mid = low(rms_norm(residual, norm_mid))
    gate_pre = low_back(jnp.dot(normed_mid, w_gate, precision=HIGH))
    up_pre = low_back(jnp.dot(normed_mid, w_up, precision=HIGH))
    hidden = low(jax.nn.silu(gate_pre) * up_pre)
    ffn_out = low_back(jnp.dot(hidden, w_down, precision=HIGH))
    return residual + ffn_out

def reference(tokens, doc_lengths, pad_counts, norm_in, w_qkv, kernel, mixing, norm_heads, w_out, norm_mid, w_gate, w_up, w_down, cotangent):
    params = tuple((argument.astype(jnp.float32) for argument in (norm_in, w_qkv, kernel, mixing, norm_heads, w_out, norm_mid, w_gate, w_up, w_down)))

    def forward(inputs_all, weight_set):

        def one_row(row_inputs):
            return layer_row(weight_set, row_inputs)
        return lax.map(jax.checkpoint(one_row), (inputs_all, doc_lengths, pad_counts))
    outputs, pullback = jax.vjp(forward, tokens.astype(jnp.float32), params)
    grad_inputs, grad_params = pullback(cotangent.astype(jnp.float32))
    return (outputs, grad_inputs, grad_params[0], grad_params[1], grad_params[2], grad_params[3], grad_params[4], grad_params[5], grad_params[6], grad_params[7], grad_params[8], grad_params[9])
```

```python
import functools

import jax
import jax.numpy as jnp
from jax import lax
from jax.experimental import pallas as pl
from jax.experimental.pallas import tpu as pltpu
from jax.sharding import PartitionSpec as P

F32 = jnp.float32
BF16 = jnp.bfloat16
NEG_FILL = -1e30
MESH = pl.DeviceIdType.MESH
PLANE = 4
GROUP = 8
SIDE = 256
SLOTS = 4
QKV = 640


class Place:
    def __init__(self, planes):
        self.planes = planes
        self.y = lax.axis_index("rep")
        self.f = lax.axis_index("fsdp")
        self.g = lax.div(self.f, PLANE)
        self.s = lax.rem(self.f, PLANE)
        self.x = lax.div(self.s, 2)
        self.c = lax.rem(self.s, 2)
        self.slot = self.y * PLANE + self.s
        self.pair = self.y * 4 + self.c * 2 + self.x

    def dev(self, y, x, c):
        return (y, self.g * PLANE + x * 2 + c)

    def sib(self):
        return self.dev(self.y, self.x, 1 - self.c)

    def xn(self):
        return self.dev(self.y, 1 - self.x, self.c)

    def yn(self):
        return self.dev(1 - self.y, self.x, self.c)

    def plane_dev(self, g):
        return (self.y, g * PLANE + self.s)

    def row(self, dy, dx, dc):
        y = self.y + dy - 2 * dy * self.y
        x = self.x + dx - 2 * dx * self.x
        c = self.c + dc - 2 * dc * self.c
        return y * 4 + x * 2 + c

    def greet(self):
        sem = pltpu.get_barrier_semaphore()
        n = self.planes * PLANE
        for d in range(1, n):
            pl.semaphore_signal(sem, inc=1, device_id=(self.y, lax.rem(self.f + d, n)), device_id_type=MESH)
        for s in range(PLANE):
            pl.semaphore_signal(sem, inc=1, device_id=(1 - self.y, self.g * PLANE + s), device_id_type=MESH)
        pl.semaphore_wait(sem, n - 1 + PLANE)


def remote(src, dst, send, recv, dev):
    return pltpu.make_async_remote_copy(
        src_ref=src, dst_ref=dst, send_sem=send, recv_sem=recv, device_id=dev, device_id_type=MESH
    )


class Gather:
    SENDS = 14
    RECVS = 14

    def __init__(self, me, own, buf, send, recv, local):
        self.me, self.own, self.buf = me, own, buf
        self.send, self.recv, self.local = send, recv, local
        self.half = own.shape[0] // 2
        self.sent = []

    def _own(self, h):
        return self.own.at[pl.ds(h * self.half, self.half)]

    def _blk(self, row, h):
        return self.buf.at[row, pl.ds(h * self.half, self.half)]

    def _go(self, src, row, h, kind, dev):
        cp = remote(src, self._blk(row, h), self.send.at[len(self.sent)], self.recv.at[kind * 2 + h], dev)
        cp.start()
        self.sent.append(cp)

    def _await(self, row, h, kind):
        b = self._blk(row, h)
        remote(b, b, self.send.at[0], self.recv.at[kind * 2 + h], self.me.sib()).wait_recv()

    def start(self):
        me = self.me
        self.rows = [me.row(0, 0, 1), me.row(0, 1, 0), me.row(1, 0, 0), me.row(1, 1, 0), me.row(0, 1, 1), me.row(1, 0, 1), me.row(1, 1, 1)]
        self.here = pltpu.make_async_copy(self.own, self.buf.at[me.slot], self.local)
        self.here.start()
        self._go(self._own(0), me.slot, 0, 1, me.xn())
        self._go(self._own(1), me.slot, 1, 2, me.yn())
        self._go(self._own(0), me.slot, 0, 0, me.sib())
        self._go(self._own(1), me.slot, 1, 0, me.sib())
        self._go(self._own(1), me.slot, 1, 1, me.xn())
        self._go(self._own(0), me.slot, 0, 2, me.yn())

    def relay(self):
        me, rows = self.me, self.rows
        self._await(rows[1], 0, 1)
        self._go(self._blk(rows[1], 0), rows[1], 0, 3, me.yn())
        self._go(self._blk(rows[1], 0), rows[1], 0, 4, me.sib())
        self._await(rows[2], 1, 2)
        self._go(self._blk(rows[2], 1), rows[2], 1, 3, me.xn())
        self._go(self._blk(rows[2], 1), rows[2], 1, 5, me.sib())

    def share(self):
        me, rows = self.me, self.rows
        self._await(rows[1], 1, 1)
        self._go(self._blk(rows[1], 1), rows[1], 1, 4, me.sib())
        self._await(rows[2], 0, 2)
        self._go(self._blk(rows[2], 0), rows[2], 0, 5, me.sib())

    def last(self):
        me, rows = self.me, self.rows
        for h in (0, 1):
            self._await(rows[3], h, 3)
            self._go(self._blk(rows[3], h), rows[3], h, 6, me.sib())

    def finish(self):
        for kind in (0, 4, 5, 6):
            for h in (0, 1):
                self._await(self.rows[kind], h, kind)
        for cp in self.sent:
            cp.wait_send()
        self.here.wait()


class Scatter:
    SENDS = 10
    RECVS = 10

    @staticmethod
    def scratch(rows, width):
        return [
            pltpu.VMEM((2, rows, width), BF16),
            pltpu.VMEM((4, rows, width), BF16),
            pltpu.VMEM((2, rows // 2, width), BF16),
            pltpu.VMEM((2, rows, width), BF16),
            pltpu.SemaphoreType.DMA((Scatter.SENDS,)),
            pltpu.SemaphoreType.DMA((Scatter.RECVS,)),
        ]

    def __init__(self, me, out, red, diag, near, send, recv):
        self.me, self.out, self.red, self.diag, self.near = me, out, red, diag, near
        self.send, self.recv = send, recv
        self.half = diag.shape[1]

    def _sib(self, k):
        return remote(self.out.at[lax.rem(k, 2)], self.red.at[k], self.send.at[k], self.recv.at[k], self.me.sib())

    def put_sib(self, k, value):
        @pl.when(k >= 2)
        def _():
            self._sib(k - 2).wait_send()

        self.out[lax.rem(k, 2)] = value.astype(BF16)
        self._sib(k).start()

    def put_self(self, k, value):
        self._sib(k).wait_recv()
        self.red[k] = (value + self.red[k].astype(F32)).astype(BF16)

    def _copy(self, name):
        h, me = self.half, self.me
        lo, hi = pl.ds(0, h), pl.ds(h, h)
        src, dst, i, dev = {
            "da": (self.red.at[0, lo], self.diag.at[0], 4, me.xn()),
            "db": (self.red.at[0, hi], self.diag.at[1], 5, me.yn()),
            "xa": (self.red.at[1, lo], self.near.at[0, lo], 6, me.xn()),
            "xb": (self.red.at[1, hi], self.near.at[0, hi], 7, me.xn()),
            "ya": (self.red.at[2, lo], self.near.at[1, lo], 8, me.yn()),
            "yb": (self.red.at[2, hi], self.near.at[1, hi], 9, me.yn()),
        }[name]
        return remote(src, dst, self.send.at[i], self.recv.at[i], dev)

    def push(self, i):
        @pl.when(i == 1)
        def _():
            self._copy("da").start()
            self._copy("db").start()

        @pl.when(i == 3)
        def _():
            self._copy("xa").start()

        @pl.when(i == 5)
        def _():
            self._copy("yb").start()

    def turn(self):
        h = self.half
        self._copy("db").wait_recv()
        self.red[1, h:] = (self.red[1, h:].astype(F32) + self.diag[1].astype(F32)).astype(BF16)
        self._copy("xb").start()
        self._copy("da").wait_recv()
        self.red[2, :h] = (self.red[2, :h].astype(F32) + self.diag[0].astype(F32)).astype(BF16)
        self._copy("ya").start()

    def arrive(self):
        for name in ("xa", "xb", "ya", "yb"):
            self._copy(name).wait_recv()

    def total(self, at):
        return self.red[3, at].astype(F32) + self.near[0, at].astype(F32) + self.near[1, at].astype(F32)

    def finish(self):
        for k in (2, 3):
            self._sib(k).wait_send()
        for name in ("da", "db", "xa", "xb", "ya", "yb"):
            self._copy(name).wait_send()


class Chain:
    def __init__(self, me, blocks, send, recv):
        self.me, self.blocks, self.send, self.recv = me, blocks, send, recv

    def _copy(self, b, way, hop):
        to = self.me.g + 1 if way == 0 else self.me.g - 1
        return remote(self.blocks(b), self.blocks(b), self.send.at[way, hop], self.recv.at[b], self.me.plane_dev(to))

    def _each(self, hop, act):
        g, z = self.me.g, self.me.planes
        for way, b, have, more in ((0, g - hop, g - hop >= 0, g + 1 < z), (1, g + hop, g + hop < z, g >= 1)):
            act(way, b, have, more)

    def hop(self, hop):
        def act(way, b, have, more):
            @pl.when(have)
            def _():
                if hop > 0:
                    self._copy(b, way, hop).wait_recv()

                @pl.when(more)
                def _():
                    self._copy(b, way, hop).start()

        self._each(hop, act)

    def finish(self):
        for hop in range(self.me.planes):

            def act(way, b, have, more):
                @pl.when(jnp.logical_and(have, more))
                def _():
                    self._copy(b, way, hop).wait_send()

            self._each(hop, act)


def order(me, i):
    k = lax.div(i, 2)
    dx = 1 - lax.div(k, 2)
    dy = 1 - lax.rem(k, 2)
    dc = 1 - lax.rem(i, 2)
    return me.row(dy, dx, dc), k


def strips(length, body, strip=64):
    def one(i, carry):
        body(pl.ds(pl.multiple_of(i * strip, strip), strip))
        return carry

    lax.fori_loop(0, length // strip, one, 0)


def lanes(rows, width):
    return lax.broadcasted_iota(jnp.int32, (rows, width), 1)


def nt(a, b):
    return lax.dot_general(a, b, (((1,), (1,)), ((), ())), preferred_element_type=F32)


def tn(a, b):
    return lax.dot_general(a, b, (((0,), (0,)), ((), ())), preferred_element_type=F32)


def nn(a, b):
    return jnp.dot(a, b, preferred_element_type=F32)


def head_lanes(rows, dh):
    at = lanes(rows, SIDE)
    return at < dh, (at >= dh) & (at < 2 * dh)


def allowed_mask(length, ends):
    i = lax.broadcasted_iota(jnp.int32, (length, length), 0)
    j = lax.broadcasted_iota(jnp.int32, (length, length), 1)
    return (i >= j) & (i.astype(F32) < ends)


def mix_lanes(mix_ref, pair, g, dh):
    at = lanes(1, SIDE)
    m0, m1 = mix_ref[2 * pair, g], mix_ref[2 * pair + 1, g]
    return jnp.where(at < dh, m0, jnp.where(at < 2 * dh, m1, 0.0))


def head_stats(value, dh, h0, h1):
    m0 = jnp.sum(jnp.where(h0, value, 0.0), axis=-1, keepdims=True) / dh
    m1 = jnp.sum(jnp.where(h1, value, 0.0), axis=-1, keepdims=True) / dh
    return jnp.where(h0, m0, jnp.where(h1, m1, 0.0))


def band(kern_ref, head, a, taps_q, taps_k, length, flip):
    r = lax.broadcasted_iota(jnp.int32, (length, length), 0)
    c = lax.broadcasted_iota(jnp.int32, (length, length), 1)
    diff = (c - r) if flip else (r - c)
    acc = jnp.zeros((length, length), F32)
    for b in range(taps_k):
        acc = jnp.where(diff == b - taps_k // 2, kern_ref[(head * taps_q + a) * taps_k + b], acc)
    return acc


def rms_norm(values_in, scaling):
    return (
        values_in
        * lax.rsqrt(jnp.mean(values_in * values_in, axis=-1, keepdims=True) + 1e-06)
        * scaling
    )


def group_norm(values_in, scaling):
    centred = values_in - jnp.mean(values_in, axis=-1, keepdims=True)
    scaled = centred * lax.rsqrt(jnp.mean(centred * centred, axis=-1, keepdims=True) + 1e-05)
    return scaled.reshape(values_in.shape[0], -1) * scaling


def convolve(scores, kernel):
    length = scores.shape[1]
    taps_query = kernel.shape[1]
    taps_key = kernel.shape[2]
    half_width = taps_key // 2
    padded = jnp.pad(scores, ((0, 0), (taps_query - 1, 0), (half_width, half_width)))
    summed = jnp.zeros_like(scores)
    for shift_q in range(taps_query):
        for shift_k in range(taps_key):
            start_q = taps_query - 1 - shift_q
            window = padded[:, start_q : start_q + length, shift_k : shift_k + length]
            summed = summed + kernel[:, shift_q, shift_k][:, None, None] * window
    return summed


def convolve_back(grad_conv, masked, kernel):
    length = masked.shape[1]
    taps_query = kernel.shape[1]
    taps_key = kernel.shape[2]
    half_width = taps_key // 2
    padded = jnp.pad(masked, ((0, 0), (taps_query - 1, 0), (half_width, half_width)))
    grad_padded = jnp.pad(grad_conv, ((0, 0), (0, taps_query - 1), (half_width, half_width)))
    grad_masked = jnp.zeros_like(masked)
    grad_taps = []
    for shift_q in range(taps_query):
        for shift_k in range(taps_key):
            start_q = taps_query - 1 - shift_q
            window = padded[:, start_q : start_q + length, shift_k : shift_k + length]
            grad_taps.append(jnp.sum(grad_conv * window, axis=(1, 2)))
            start_k = taps_key - 1 - shift_k
            back_window = grad_padded[:, shift_q : shift_q + length, start_k : start_k + length]
            grad_masked = grad_masked + kernel[:, shift_q, shift_k][:, None, None] * back_window
    grad_kern = jnp.stack(grad_taps, axis=1).reshape(kernel.shape)
    return (grad_masked, grad_kern)


def build_mask(doc_lengths, pad_count, length):
    places = jnp.arange(length, dtype=jnp.int32)
    doc_ends = jnp.cumsum(doc_lengths)
    segment = jnp.sum((places[:, None] >= doc_ends[None, :]).astype(jnp.int32), axis=1)
    live_end = length - pad_count
    same_doc = segment[:, None] == segment[None, :]
    causal = places[None, :] <= places[:, None]
    usable = (places[None, :] < live_end) | (places[None, :] == places[:, None])
    return same_doc & causal & usable


def outer_sum(left_rows, right_rows):
    return lax.dot_general(
        left_rows, right_rows, (((0,), (0,)), ((), ())), preferred_element_type=jnp.float32
    )


def back_product(grad_rows, weight_full):
    return lax.dot_general(
        grad_rows, weight_full, (((1,), (1,)), ((), ())), preferred_element_type=jnp.float32
    )


def attention_weights(norm_in, w_qkv, norm_heads, w_out):
    return (
        lax.all_gather(norm_in, "fsdp", axis=0, tiled=True),
        lax.all_gather(w_qkv, "fsdp", axis=0, tiled=True),
        lax.all_gather(norm_heads, "fsdp", axis=0, tiled=True),
        lax.all_gather(w_out, "fsdp", axis=0, tiled=True),
    )


def feed_weights(norm_mid, w_gate, w_up, w_down):
    return (
        lax.all_gather(norm_mid, "fsdp", axis=0, tiled=True),
        lax.all_gather(w_gate, "fsdp", axis=0, tiled=True),
        lax.all_gather(w_up, "fsdp", axis=0, tiled=True),
        lax.all_gather(w_down, "fsdp", axis=0, tiled=True),
    )


def per_device(
    tokens,
    doc_lengths,
    pad_counts,
    norm_in,
    w_qkv,
    kernel,
    mixing,
    norm_heads,
    w_out,
    norm_mid,
    w_gate,
    w_up,
    w_down,
    cotangent,
):
    inputs = tokens[0].astype(jnp.float32)
    length = inputs.shape[0]
    model_width = inputs.shape[1]
    head_count = kernel.shape[0]
    head_size = model_width // head_count
    pair_count = head_count // 2
    score_scale = head_size ** (-0.5)
    allowed = build_mask(doc_lengths[0], pad_counts[0], length)[None]
    kern_pairs = kernel.reshape(pair_count, 2, kernel.shape[1], kernel.shape[2])
    mix_pairs = mixing.reshape(pair_count, 2, 2)
    attn_set = attention_weights(norm_in, w_qkv, norm_heads, w_out)
    normed = rms_norm(inputs, attn_set[0].astype(jnp.float32)).astype(jnp.bfloat16)
    projected = jnp.dot(normed, attn_set[1], preferred_element_type=jnp.float32).astype(
        jnp.bfloat16
    )
    split_qkv = projected.reshape(length, 3, pair_count, 2, head_size).transpose(1, 2, 3, 0, 4)

    def pair_scores(queries, key_rows, kern_pair):
        raw_scores = (
            jnp.einsum("gie,gje->gij", queries, key_rows, preferred_element_type=jnp.float32)
            * score_scale
        )
        masked = jnp.where(allowed, raw_scores, 0.0)
        logits = jnp.where(allowed, convolve(masked, kern_pair), NEG_FILL)
        return (masked, logits)

    def pair_forward(pieces):
        queries, key_rows, value_rows, kern_pair, mix_pair = pieces
        masked, logits = pair_scores(queries, key_rows, kern_pair)
        row_peak = jnp.max(logits, axis=-1, keepdims=True)
        log_total = row_peak + jnp.log(jnp.sum(jnp.exp(logits - row_peak), axis=-1, keepdims=True))
        attn_probs = jnp.exp(logits - log_total)
        mixed_probs = jnp.einsum("og,gij->oij", mix_pair, attn_probs, precision=lax.Precision.HIGHEST)
        output = jnp.einsum(
            "oij,oje->oie", mixed_probs, value_rows.astype(jnp.float32), precision=lax.Precision.HIGHEST
        )
        return (output, log_total)

    attended_pairs, log_totals = lax.map(
        pair_forward, (split_qkv[0], split_qkv[1], split_qkv[2], kern_pairs, mix_pairs)
    )
    attended = attended_pairs.transpose(2, 0, 1, 3).reshape(length, head_count, head_size)
    gated_out = group_norm(attended, attn_set[2].astype(jnp.float32)).astype(jnp.bfloat16)
    residual = inputs + jnp.dot(gated_out, attn_set[3], preferred_element_type=jnp.float32)
    ffn_set = feed_weights(norm_mid, w_gate, w_up, w_down)
    normed_mid = rms_norm(residual, ffn_set[0].astype(jnp.float32)).astype(jnp.bfloat16)
    gate_pre = jnp.dot(normed_mid, ffn_set[1], preferred_element_type=jnp.float32)
    up_pre = jnp.dot(normed_mid, ffn_set[2], preferred_element_type=jnp.float32)
    sigmoid_gate = jax.nn.sigmoid(gate_pre)
    silu_gate = gate_pre * sigmoid_gate
    hidden = (silu_gate * up_pre).astype(jnp.bfloat16)
    layer_out = (residual + jnp.dot(hidden, ffn_set[3], preferred_element_type=jnp.float32))[None]
    ffn_again = feed_weights(norm_mid, w_gate, w_up, w_down)
    grad_y = cotangent[0]
    grad_w_down = outer_sum(hidden, grad_y)
    grad_hidden = back_product(grad_y, ffn_again[3])
    grad_gate = (
        grad_hidden * up_pre * sigmoid_gate * (1.0 + gate_pre * (1.0 - sigmoid_gate))
    ).astype(jnp.bfloat16)
    grad_up = (grad_hidden * silu_gate).astype(jnp.bfloat16)
    grad_w_gate = outer_sum(normed_mid, grad_gate)
    grad_w_up = outer_sum(normed_mid, grad_up)
    grad_mid = back_product(grad_gate, ffn_again[1]) + back_product(grad_up, ffn_again[2])
    mid_pull = jax.vjp(rms_norm, residual, ffn_again[0].astype(jnp.float32))[1]
    grad_residual_norm, grad_norm_mid = mid_pull(grad_mid)
    grad_residual = grad_y.astype(jnp.float32) + grad_residual_norm
    ffn_shards = (
        lax.psum_scatter(grad_norm_mid, "fsdp", scatter_dimension=0, tiled=True),
        lax.psum_scatter(grad_w_gate, "fsdp", scatter_dimension=0, tiled=True),
        lax.psum_scatter(grad_w_up, "fsdp", scatter_dimension=0, tiled=True),
        lax.psum_scatter(grad_w_down, "fsdp", scatter_dimension=0, tiled=True),
    )
    attn_again = attention_weights(norm_in, w_qkv, norm_heads, w_out)
    grad_branch = grad_residual.astype(jnp.bfloat16)
    grad_w_out = outer_sum(gated_out, grad_branch)
    grad_gated = back_product(grad_branch, attn_again[3])
    head_pull = jax.vjp(group_norm, attended, attn_again[2].astype(jnp.float32))[1]
    grad_attended, grad_norm_heads = head_pull(grad_gated)
    grad_att_pairs = (
        grad_attended.astype(jnp.bfloat16)
        .reshape(length, pair_count, 2, head_size)
        .transpose(1, 2, 0, 3)
    )

    def pair_backward(pieces):
        queries, key_rows, value_rows, kern_pair, mix_pair, log_total, grad_output = pieces
        masked, logits = pair_scores(queries, key_rows, kern_pair)
        attn_probs = jnp.exp(logits - log_total)
        mixed_probs = jnp.einsum("og,gij->oij", mix_pair, attn_probs, precision=lax.Precision.HIGHEST)
        grad_wide = grad_output.astype(jnp.float32)
        grad_mixed = jnp.einsum(
            "oie,oje->oij", grad_wide, value_rows.astype(jnp.float32), precision=lax.Precision.HIGHEST
        )
        grad_values = jnp.einsum("oij,oie->oje", mixed_probs, grad_wide, precision=lax.Precision.HIGHEST)
        grad_mix = jnp.einsum("oij,gij->og", grad_mixed, attn_probs, precision=lax.Precision.HIGHEST)
        grad_probs = jnp.einsum("og,oij->gij", mix_pair, grad_mixed, precision=lax.Precision.HIGHEST)
        grad_logits = attn_probs * (
            grad_probs - jnp.sum(attn_probs * grad_probs, axis=-1, keepdims=True)
        )
        grad_conv = jnp.where(allowed, grad_logits, 0.0)
        grad_masked, grad_kern = convolve_back(grad_conv, masked, kern_pair)
        grad_raw = jnp.where(allowed, grad_masked, 0.0)
        grad_query = (
            jnp.einsum("gij,gje->gie", grad_raw, key_rows.astype(jnp.float32), precision=lax.Precision.HIGHEST)
            * score_scale
        )
        grad_key = (
            jnp.einsum("gij,gie->gje", grad_raw, queries.astype(jnp.float32), precision=lax.Precision.HIGHEST)
            * score_scale
        )
        return (
            grad_query.astype(jnp.bfloat16),
            grad_key.astype(jnp.bfloat16),
            grad_values.astype(jnp.bfloat16),
            grad_kern,
            grad_mix,
        )

    grads_query, grads_key, grads_value, grad_kern_pairs, grad_mix_pairs = lax.map(
        pair_backward,
        (
            split_qkv[0],
            split_qkv[1],
            split_qkv[2],
            kern_pairs,
            mix_pairs,
            log_totals,
            grad_att_pairs,
        ),
    )
    grad_qkv = (
        jnp.stack([grads_query, grads_key, grads_value])
        .transpose(3, 0, 1, 2, 4)
        .reshape(length, 3 * model_width)
    )
    grad_w_qkv = outer_sum(normed, grad_qkv)
    grad_normed = back_product(grad_qkv, attn_again[1])
    in_pull = jax.vjp(rms_norm, inputs, attn_again[0].astype(jnp.float32))[1]
    grad_inputs_norm, grad_norm_in = in_pull(grad_normed)
    grad_tokens = (grad_residual + grad_inputs_norm)[None]
    small_sums = lax.psum(
        (grad_kern_pairs.reshape(kernel.shape), grad_mix_pairs.reshape(mixing.shape)),
        ("rep", "fsdp"),
    )
    attn_shards = (
        lax.psum_scatter(grad_norm_in, "fsdp", scatter_dimension=0, tiled=True),
        lax.psum_scatter(grad_w_qkv, "fsdp", scatter_dimension=0, tiled=True),
        lax.psum_scatter(grad_norm_heads, "fsdp", scatter_dimension=0, tiled=True),
        lax.psum_scatter(grad_w_out, "fsdp", scatter_dimension=0, tiled=True),
    )
    summed = (
        lax.psum(ffn_shards[0].astype(jnp.bfloat16), "rep").astype(jnp.float32),
        lax.psum(ffn_shards[1].astype(jnp.bfloat16), "rep").astype(jnp.float32),
        lax.psum(ffn_shards[2].astype(jnp.bfloat16), "rep").astype(jnp.float32),
        lax.psum(ffn_shards[3].astype(jnp.bfloat16), "rep").astype(jnp.float32),
        lax.psum(attn_shards[0].astype(jnp.bfloat16), "rep").astype(jnp.float32),
        lax.psum(attn_shards[1].astype(jnp.bfloat16), "rep").astype(jnp.float32),
        lax.psum(attn_shards[2].astype(jnp.bfloat16), "rep").astype(jnp.float32),
        lax.psum(attn_shards[3].astype(jnp.bfloat16), "rep").astype(jnp.float32),
    )
    return (
        layer_out,
        grad_tokens,
        summed[4],
        summed[5],
        small_sums[0],
        small_sums[1],
        summed[6],
        summed[7],
        summed[0],
        summed[1],
        summed[2],
        summed[3],
    )


def forward_kernel(cfg, *refs):
    (tok, ct, w_a, w_b, w_d, w_o, meta, kern, mix,
     tok_all, ct_all, a_all, b_all, d_all, o_all, nrm_all, qkv_all, p_all, m_all, gated_all, mid_all, resid, gains, ends,
     x_v, wa_v, wo_v, t_v, cat_v, shift_v, qkv_v, p_v, m_v, gated_v, meta_v, mid_v, tok_v,
     out_v, red, diag, near, rs_send, rs_recv,
     g_send, g_recv, g_loc, a_send, a_recv, ch_send, ch_recv, o_send, o_recv, meta_send, meta_recv, loc, row_in, row_out) = refs
    planes, dh, taps_q, taps_k = cfg["planes"], cfg["dh"], cfg["kq"], cfg["kk"]
    length, width = tok.shape
    per_pair = o_all.shape[0]
    scale = dh ** (-0.5)
    me = Place(planes)
    me.greet()

    def first(src, dst_all, base):
        cps = []
        for d in range(1, PLANE):
            s = lax.rem(me.s + d, PLANE)
            cp = remote(src.at[s], dst_all.at[me.f], a_send.at[base + d], a_recv.at[base + d], (me.y, me.g * PLANE + s))
            cp.start()
            cps.append(cp)
        own = pltpu.make_async_copy(src.at[me.s], dst_all.at[me.f], a_send.at[base])
        own.start()
        return cps, own

    def first_wait(src, dst_all, base, own):
        for d in range(1, PLANE):
            s = lax.rem(me.s - d + PLANE, PLANE)
            blk = dst_all.at[me.g * PLANE + s]
            remote(blk, blk, a_send.at[base + d], a_recv.at[base + d], me.sib()).wait_recv()
        own.wait()

    meta_sent = []
    for d in range(1, GROUP):
        to = lax.rem(me.slot + d, GROUP)
        cp = remote(
            meta, meta_v.at[me.slot], meta_send.at[d], meta_recv.at[d],
            (lax.div(to, PLANE), me.g * PLANE + lax.rem(to, PLANE)),
        )
        cp.start()
        meta_sent.append(cp)
    meta_here = pltpu.make_async_copy(meta, meta_v.at[me.slot], meta_send.at[0])
    meta_here.start()
    sent_a, own_a = first(w_a, a_all, 0)
    tokens = Gather(me, tok, tok_all, g_send.at[0], g_recv.at[0], g_loc.at[0])
    tokens.start()
    tok_in = pltpu.make_async_copy(tok, tok_v, loc.at[0])
    tok_in.start()

    blocks4 = lambda ref: (lambda b: ref.at[pl.ds(b * PLANE, PLANE)])
    chain_a = Chain(me, blocks4(a_all), ch_send.at[0], ch_recv.at[0])
    chain_b = Chain(me, blocks4(b_all), ch_send.at[1], ch_recv.at[1])
    chain_d = Chain(me, lambda b: d_all.at[b], ch_send.at[2], ch_recv.at[2])

    for g in range(2):
        for a in range(taps_q):
            t = band(kern, 2 * me.pair + g, a, taps_q, taps_k, length, False)
            hi = t.astype(BF16)
            t_v[g, 0, a * length : (a + 1) * length] = hi
            t_v[g, 1, a * length : (a + 1) * length] = (t - hi.astype(F32)).astype(BF16)
    shift_v[0:8] = jnp.zeros((8, length), F32)
    wo_v[...] = jnp.zeros(wo_v.shape, BF16)

    first_wait(w_a, a_all, 0, own_a)
    chain_a.hop(0)

    src_pair = lax.div(me.f, per_pair)
    src_y, src_s = lax.div(src_pair, 4), lax.rem(src_pair, 2) * 2 + lax.rem(lax.div(src_pair, 2), 2)
    src_j = lax.rem(me.f, per_pair)

    def o_copy(g):
        return remote(w_o, o_all.at[src_j], o_send.at[g], o_recv.at[src_j], (me.y, g * PLANE + src_s))

    o_here = pltpu.make_async_copy(w_o, o_all.at[src_j], o_send.at[planes])

    def o_each(act, act_here):
        for g in range(planes):
            mine = g * PLANE + src_s == me.f

            if act is not None:

                @pl.when((src_y == me.y) & jnp.logical_not(mine))
                def _():
                    act(o_copy(g))

        if act_here is not None:

            @pl.when((src_y == me.y) & (src_s == me.s))
            def _():
                act_here(o_here)

    o_each(lambda cp: cp.start(), lambda cp: cp.start())

    tokens.relay()
    for hop in range(1, planes - 1):
        chain_a.hop(hop)
    tokens.share()
    tokens.last()
    sent_b, own_b = first(w_b, b_all, PLANE)
    tokens.finish()
    cots = Gather(me, ct, ct_all, g_send.at[1], g_recv.at[1], g_loc.at[1])
    cots.start()
    for r in range(GROUP):
        pltpu.make_async_copy(tok_all.at[r], x_v.at[r], row_in.at[r]).start()
    chain_a.hop(planes - 1)

    wa_in = pltpu.make_async_copy(a_all, wa_v, loc.at[1])
    wa_in.start()
    for j in range(per_pair):
        from_f = me.pair * per_pair + j

        @pl.when(from_f != me.f)
        def _():
            remote(w_o, o_all.at[j], o_send.at[0], o_recv.at[j], me.sib()).wait_recv()

    o_each(None, lambda cp: cp.wait())
    wo_in = pltpu.make_async_copy(o_all, wo_v.at[pl.ds(0, per_pair)], loc.at[2])
    wo_in.start()
    pltpu.make_async_copy(w_d, d_all.at[me.g], loc.at[3]).start()
    pltpu.make_async_copy(w_d, d_all.at[me.g], loc.at[3]).wait()
    first_wait(w_b, b_all, PLANE, own_b)
    wa_in.wait()
    chain_d.hop(0)
    chain_b.hop(0)
    wo_in.wait()
    for d in range(1, GROUP):
        fr = lax.rem(me.slot - d + GROUP, GROUP)
        remote(meta, meta_v.at[fr], meta_send.at[d], meta_recv.at[d], me.sib()).wait_recv()
    meta_here.wait()
    ends[...] = meta_v[...]

    rows_o = per_pair * w_o.shape[0]
    weights_a = wa_v[...].reshape(width, QKV)
    gain_rows = jnp.transpose(weights_a[:, 384:512].astype(F32))
    gains[...] = jnp.zeros(gains.shape, F32)
    gains[0:1] = gain_rows[64:65]
    gains[1:2] = gain_rows[65:66]
    heads_col = wo_v[:, :, width:].reshape(wo_v.shape[0] * wo_v.shape[1], 128).astype(F32)
    gains[2:3] = jnp.concatenate(
        [jnp.transpose(heads_col[0:SIDE])[0:1], jnp.zeros((1, width - SIDE), F32)], axis=1
    )

    h0, h1 = head_lanes(length, dh)
    scatter = Scatter(me, out_v, red, diag, near, rs_send, rs_recv)

    def one(i, carry):
        row, k = order(me, i)
        pltpu.make_async_copy(tok_all.at[row], x_v.at[row], row_in.at[row]).wait()

        def norm(at):
            x = x_v[row, at].astype(F32)
            s = lax.rsqrt(jnp.mean(x * x, axis=-1, keepdims=True) + 1e-6)
            x_v[row, at] = (x * s * gains[0:1]).astype(BF16)

        strips(length, norm)
        pltpu.make_async_copy(x_v.at[row], nrm_all.at[row], row_out.at[0, row]).start()
        acc = nn(x_v[row], wa_v[...].reshape(width, QKV))
        at = lanes(length, 128)
        q = jnp.where(h0 | h1, acc[:, 0:SIDE], 0.0)
        kk = jnp.where(h0 | h1, acc[:, SIDE : 2 * SIDE], 0.0)
        tail = jnp.where(at < 64, pltpu.roll(acc[:, 128:256], 64, 1), 0.0)
        v = jnp.concatenate([acc[:, 2 * SIDE : QKV], tail], axis=1)
        q, kk, v = q.astype(BF16), kk.astype(BF16), v.astype(BF16)
        qkv_v[row, :, 0:SIDE] = q
        qkv_v[row, :, SIDE : 2 * SIDE] = kk
        qkv_v[row, :, 2 * SIDE : 3 * SIDE] = v
        pltpu.make_async_copy(qkv_v.at[row], qkv_all.at[row], row_out.at[1, row]).start()
        ok = allowed_mask(length, meta_v[row, 0:1, :])
        attended = jnp.zeros((length, SIDE), F32)
        for g in range(2):
            kg = jnp.where(h0 if g == 0 else h1, kk.astype(F32), 0.0).astype(BF16)
            raw = nt(q, kg) * scale
            masked = jnp.where(ok, raw, 0.0)
            m_v[row, g] = masked.astype(BF16)
            shift_v[8 : 8 + length] = masked
            for a in range(taps_q):
                sh = shift_v[8 - a : 8 - a + length]
                hi = sh.astype(BF16)
                cat_v[0, :, a * length : (a + 1) * length] = hi
                cat_v[1, :, a * length : (a + 1) * length] = (sh - hi.astype(F32)).astype(BF16)
            conv = nn(cat_v[0], t_v[g, 0]) + nn(cat_v[1], t_v[g, 0]) + nn(cat_v[0], t_v[g, 1])
            logits = jnp.where(ok, conv, NEG_FILL)
            e = jnp.exp(logits - jnp.max(logits, axis=-1, keepdims=True))
            probs = e / jnp.sum(e, axis=-1, keepdims=True)
            high = probs.astype(BF16)
            low = (probs - high.astype(F32)).astype(BF16)
            p_v[row, g, 0] = high
            p_v[row, g, 1] = low
            attended = attended + (nn(high, v) + nn(low, v)) * mix_lanes(mix, me.pair, g, dh)
        pltpu.make_async_copy(m_v.at[row], m_all.at[row], row_out.at[2, row]).start()
        pltpu.make_async_copy(p_v.at[row], p_all.at[row], row_out.at[3, row]).start()
        centred = attended - head_stats(attended, dh, h0, h1)
        centred = jnp.where(h0 | h1, centred, 0.0)
        scaled = centred * lax.rsqrt(head_stats(centred * centred, dh, h0, h1) + 1e-5)
        gated = (scaled * gains[2:3, 0:SIDE]).astype(BF16)
        gated_v[row] = gated
        pltpu.make_async_copy(gated_v.at[row], gated_all.at[row], row_out.at[4, row]).start()
        wo = wo_v[:, :, 0:width].reshape(wo_v.shape[0] * wo_v.shape[1], width)
        part = nn(gated, wo[0:SIDE])

        @pl.when(lax.rem(i, 2) == 0)
        def _():
            scatter.put_sib(k, part)

        @pl.when(lax.rem(i, 2) == 1)
        def _():
            scatter.put_self(k, part)

        scatter.push(i)
        return carry

    lax.fori_loop(0, GROUP, one, 0)
    cots.relay()
    scatter.turn()
    cots.share()
    cots.last()
    cots.finish()
    tok_in.wait()
    scatter.arrive()

    def middle(at):
        res = tok_v[at].astype(F32) + scatter.total(at)
        resid[at] = res
        s = lax.rsqrt(jnp.mean(res * res, axis=-1, keepdims=True) + 1e-6)
        mid_v[at] = (res * s * gains[1:2]).astype(BF16)

    strips(length, middle)
    mids = Gather(me, mid_v, mid_all, g_send.at[2], g_recv.at[2], g_loc.at[2])
    mids.start()
    chain_d.hop(1)
    chain_b.hop(1)
    mids.relay()
    mids.share()
    mids.last()
    for hop in range(2, planes):
        chain_d.hop(hop)
        chain_b.hop(hop)
    mids.finish()
    scatter.finish()
    for ch in (chain_a, chain_b, chain_d):
        ch.finish()
    o_each(lambda cp: cp.wait_send(), None)
    for cp in meta_sent + sent_a + sent_b:
        cp.wait_send()
    for r in range(GROUP):
        pltpu.make_async_copy(x_v.at[r], nrm_all.at[r], row_out.at[0, r]).wait()
        pltpu.make_async_copy(qkv_v.at[r], qkv_all.at[r], row_out.at[1, r]).wait()
        pltpu.make_async_copy(m_v.at[r], m_all.at[r], row_out.at[2, r]).wait()
        pltpu.make_async_copy(p_v.at[r], p_all.at[r], row_out.at[3, r]).wait()
        pltpu.make_async_copy(gated_v.at[r], gated_all.at[r], row_out.at[4, r]).wait()


def forward_call(cfg, tok, ct, w_a, w_b, w_d, w_o, meta, kern, mix):
    length, width = tok.shape
    planes, ff, r = cfg["planes"], cfg["ff"], w_a.shape[1]
    n = planes * PLANE
    chunk = w_d.shape[0]
    per_pair = n // GROUP
    taps = cfg["kq"] * length
    pad_rows = -(-SIDE // w_o.shape[0])
    hbm, vmem, smem = pl.BlockSpec(memory_space=pl.ANY), pl.BlockSpec(memory_space=pltpu.VMEM), pl.BlockSpec(memory_space=pltpu.SMEM)
    sds = jax.ShapeDtypeStruct
    rows = (GROUP, length)
    dma = pltpu.SemaphoreType.DMA
    return pl.pallas_call(
        functools.partial(forward_kernel, cfg),
        out_shape=(
            sds(rows + (width,), BF16), sds(rows + (width,), BF16),
            sds((n, r, QKV), BF16), sds((n, r, 2 * ff), BF16), sds((planes, chunk, width), BF16),
            sds((per_pair,) + w_o.shape, BF16), sds(rows + (width,), BF16), sds(rows + (3 * SIDE,), BF16),
            sds((GROUP, 2, 2, length, length), BF16), sds((GROUP, 2, length, length), BF16), sds(rows + (SIDE,), BF16),
            sds(rows + (width,), BF16), sds((length, width), F32), sds((8, width), F32), sds((GROUP, 8, length), F32),
        ),
        in_specs=[hbm] * 7 + [smem] * 2,
        out_specs=(hbm,) * 12 + (vmem,) * 3,
        scratch_shapes=[
            pltpu.VMEM(rows + (width,), BF16), pltpu.VMEM((n, r, QKV), BF16), pltpu.VMEM((pad_rows,) + w_o.shape, BF16),
            pltpu.VMEM((2, 2, taps, length), BF16), pltpu.VMEM((2, length, taps), BF16), pltpu.VMEM((length + 8, length), F32),
            pltpu.VMEM(rows + (3 * SIDE,), BF16), pltpu.VMEM((GROUP, 2, 2, length, length), BF16),
            pltpu.VMEM((GROUP, 2, length, length), BF16), pltpu.VMEM(rows + (SIDE,), BF16),
            pltpu.VMEM((GROUP, 8, length), F32), pltpu.VMEM((length, width), BF16), pltpu.VMEM((length, width), BF16),
            *Scatter.scratch(length, width),
            dma((3, Gather.SENDS)), dma((3, Gather.RECVS)), dma((3,)), dma((2 * PLANE,)), dma((2 * PLANE,)),
            dma((3, 2, planes)), dma((3, planes)), dma((planes + 1,)), dma((per_pair,)), dma((GROUP,)), dma((GROUP,)),
            dma((4,)), dma((GROUP,)), dma((5, GROUP)),
        ],
        compiler_params=pltpu.CompilerParams(collective_id=1, has_side_effects=True, vmem_limit_bytes=50 * 2**20),
        name="attention_forward",
    )(tok, ct, w_a, w_b, w_d, w_o, meta, kern, mix)


def feed_kernel(cfg, *refs):
    (mid_all, ct_all, w_b, w_d, resid, gains,
     layer_out, g_res, branch_all, dw_b, dw_d, g_mid_gain,
     mid_v, ct_v, wb_v, wd_v, hid_v, gu_v, tile_v,
     o_out, o_red, o_diag, o_near, o_send, o_recv,
     m_out, m_red, m_diag, m_near, m_send, m_recv,
     g_send, g_recv, g_loc, loc, row_in, out_sem) = refs
    length, width = resid.shape
    ff = cfg["ff"]
    me = Place(cfg["planes"])
    wb_in = pltpu.make_async_copy(w_b, wb_v, loc.at[0])
    wb_in.start()
    wd_in = pltpu.make_async_copy(w_d, wd_v, loc.at[1])
    wd_in.start()

    def row_copies(row):
        return (
            pltpu.make_async_copy(mid_all.at[row], mid_v.at[row], row_in.at[0, row]),
            pltpu.make_async_copy(ct_all.at[row], ct_v.at[row], row_in.at[1, row]),
        )

    for i in range(GROUP):
        for cp in row_copies(order(me, i)[0]):
            cp.start()
    me.greet()
    sum_out = Scatter(me, o_out, o_red, o_diag, o_near, o_send, o_recv)
    sum_mid = Scatter(me, m_out, m_red, m_diag, m_near, m_send, m_recv)
    wb_in.wait()
    wd_in.wait()

    def one(i, carry):
        row, k = order(me, i)
        for cp in row_copies(row):
            cp.wait()
        wb = wb_v[...].reshape(width, 2 * ff)
        wd = wd_v[...].reshape(ff, width)
        pre = nn(mid_v[row], wb)
        gate, up = pre[:, :ff], pre[:, ff:]
        g_hidden = nt(ct_v[row], wd)
        sig = jax.nn.sigmoid(gate)
        silu = gate * sig
        hidden = (silu * up).astype(BF16)
        hid_v[row] = hidden
        g_gate = (g_hidden * up * sig * (1.0 + gate * (1.0 - sig))).astype(BF16)
        g_up = (g_hidden * silu).astype(BF16)
        gu_v[row, :, :ff] = g_gate
        gu_v[row, :, ff:] = g_up
        mid_part = nt(gu_v[row], wb)
        out_part = nn(hidden, wd)

        @pl.when(lax.rem(i, 2) == 0)
        def _():
            sum_mid.put_sib(k, mid_part)
            sum_out.put_sib(k, out_part)

        @pl.when(lax.rem(i, 2) == 1)
        def _():
            sum_mid.put_self(k, mid_part)
            sum_out.put_self(k, out_part)

        sum_mid.push(i)
        return carry

    lax.fori_loop(0, GROUP, one, 0)
    sum_mid.turn()

    tokens = GROUP * length
    tile = SIDE

    steps_down, steps_up = ff // tile, width // tile

    def tile_out(i, down):
        slot = lax.rem(i, 2)
        if down:
            src, dst = tile_v.at[slot], dw_d.at[pl.ds(pl.multiple_of(i * tile, tile), tile)]
        else:
            at = pl.ds(pl.multiple_of((i - steps_down) * tile, tile), tile)
            src, dst = tile_v.at[slot, :, pl.ds(0, 2 * ff)], dw_b.at[at]
        return pltpu.make_async_copy(src, dst, out_sem.at[slot])

    def down(i, carry):
        at = pl.ds(pl.multiple_of(i * tile, tile), tile)
        tile_v[lax.rem(i, 2)] = tn(hid_v[:, :, at].reshape(tokens, tile), ct_v[...].reshape(tokens, width)).astype(BF16)
        tile_out(i, True).start()
        return carry

    lax.fori_loop(0, steps_down, down, 0)
    for i in range(steps_down):
        tile_out(i, True).wait()

    g_mid_gain[...] = jnp.zeros(g_mid_gain.shape, F32)
    sum_mid.arrive()

    def middle(at):
        g_mid = sum_mid.total(at)
        res = resid[at]
        s = lax.rsqrt(jnp.mean(res * res, axis=-1, keepdims=True) + 1e-6)
        g_mid_gain[0:1] = g_mid_gain[0:1] + jnp.sum(g_mid * res * s, axis=0, keepdims=True)
        pulled = g_mid * gains[1:2]
        back = ct_v[me.slot, at].astype(F32) + s * pulled
        back = back - res * (s * s * s * jnp.mean(pulled * res, axis=-1, keepdims=True))
        g_res[at] = back
        ct_v[me.slot, at] = back.astype(BF16)

    strips(length, middle)
    branch = Gather(me, ct_v.at[me.slot], branch_all, g_send, g_recv, g_loc.at[0])
    branch.start()
    for i in (1, 3, 5):
        sum_out.push(i)

    def gate_up(i, carry):
        @pl.when(i >= steps_down + 2)
        def _():
            tile_out(i - 2, False).wait()

        at = pl.ds(pl.multiple_of((i - steps_down) * tile, tile), tile)
        value = tn(mid_v[:, :, at].reshape(tokens, tile), gu_v[...].reshape(tokens, 2 * ff))
        tile_v[lax.rem(i, 2), :, 0 : 2 * ff] = value.astype(BF16)
        tile_out(i, False).start()
        return carry

    end = steps_down + steps_up
    lax.fori_loop(steps_down, steps_down + steps_up // 2, gate_up, 0)
    branch.relay()
    lax.fori_loop(steps_down + steps_up // 2, end, gate_up, 0)
    branch.share()
    sum_out.turn()
    branch.last()
    sum_out.arrive()

    def result(at):
        layer_out[at] = resid[at] + sum_out.total(at)

    strips(length, result)
    branch.finish()
    sum_mid.finish()
    sum_out.finish()
    tile_out(end - 2, False).wait()
    tile_out(end - 1, False).wait()


def feed_call(cfg, mid_all, ct_all, w_b, w_d, resid, gains):
    length, width = resid.shape
    ff = cfg["ff"]
    hbm, vmem = pl.BlockSpec(memory_space=pl.ANY), pl.BlockSpec(memory_space=pltpu.VMEM)
    sds = jax.ShapeDtypeStruct
    dma = pltpu.SemaphoreType.DMA
    rows = (GROUP, length)
    return pl.pallas_call(
        functools.partial(feed_kernel, cfg),
        out_shape=(
            sds((length, width), F32), sds((length, width), F32), sds(rows + (width,), BF16),
            sds((width, 2 * ff), BF16), sds((ff, width), BF16), sds((8, width), F32),
        ),
        in_specs=[hbm] * 4 + [vmem] * 2,
        out_specs=(vmem, vmem, hbm, hbm, hbm, vmem),
        scratch_shapes=[
            pltpu.VMEM(rows + (width,), BF16), pltpu.VMEM(rows + (width,), BF16),
            pltpu.VMEM(w_b.shape, BF16), pltpu.VMEM(w_d.shape, BF16),
            pltpu.VMEM(rows + (ff,), BF16), pltpu.VMEM(rows + (2 * ff,), BF16),
            pltpu.VMEM((2, SIDE, width), BF16),
            *Scatter.scratch(length, width), *Scatter.scratch(length, width),
            dma((Gather.SENDS,)), dma((Gather.RECVS,)), dma((1,)), dma((2,)), dma((2, GROUP)), dma((2,)),
        ],
        compiler_params=pltpu.CompilerParams(collective_id=2, has_side_effects=True, vmem_limit_bytes=50 * 2**20),
        name="feed_forward",
    )(mid_all, ct_all, w_b, w_d, resid, gains)


def backward_kernel(cfg, *refs):
    (branch_all, o_all, a_all, nrm_all, qkv_all, p_all, m_all, gated_all, dw_b, dw_d, tok, g_res, gains, ends, g_mid_gain, kern, mix,
     g_tokens, out_a, out_b, out_d, out_o, out_small,
     gb_v, wo_v, wa_v, nrm_v, qkv_v, p_v, m_v, gated_v, t_v, cat_v, shift_v, corr_v, gq_v, da_v, do_v, tok_v, rows_v, line_v,
     zb_v, zd_v, za_v, zo_v, sb_v, sd_v, sa_v, so_v, own_b, own_d, small_v, small_in,
     s_out, s_red, s_diag, s_near, rs_send, rs_recv,
     z_send, z_recv, t_send, t_recv, loc, row_in) = refs
    planes, dh, taps_q, taps_k = cfg["planes"], cfg["dh"], cfg["kq"], cfg["kk"]
    length, width = tok.shape
    scale = dh ** (-0.5)
    me = Place(planes)
    per_pair = o_all.shape[0]
    r = a_all.shape[1]
    loads = [
        pltpu.make_async_copy(src, dst, loc.at[i])
        for i, (src, dst) in enumerate(
            [(a_all, wa_v), (o_all, wo_v.at[pl.ds(0, per_pair)]), (tok, tok_v), (gated_all, gated_v)]
            + [(dw_b.at[pl.ds(me.g * PLANE, PLANE)], own_b), (dw_d.at[me.g], own_d)]
        )
    ]

    span = PLANE * r

    def nrm_copy(j):
        at = pl.ds(j * span, span)
        return pltpu.make_async_copy(nrm_all.at[:, :, at], nrm_v.at[j % 2], loc.at[6 + j % 2])

    def row_copies(i):
        row = order(me, i)[0]
        at = lax.rem(i, SLOTS)
        cps = [pltpu.make_async_copy(branch_all.at[row], gb_v.at[row], row_in.at[0, i])]
        for j, (src, dst) in enumerate(((qkv_all, qkv_v), (p_all, p_v), (m_all, m_v))):
            cps.append(pltpu.make_async_copy(src.at[row], dst.at[at], row_in.at[j + 1, i]))
        return cps

    wo_v[...] = jnp.zeros(wo_v.shape, BF16)
    loads[1].start()
    loads[0].start()
    for i in range(SLOTS):
        for cp in row_copies(i):
            cp.start()
    for cp in loads[2:]:
        cp.start()
    for j in range(2):
        nrm_copy(j).start()
    me.greet()

    def z_copies(kind, src_of, landing):
        cps = []
        for d in range(1, planes):
            to = lax.rem(me.g + d, planes)
            cps.append(remote(src_of(to), landing.at[d - 1], z_send.at[kind, d - 1], z_recv.at[kind, d - 1], me.plane_dev(to)))
        return cps

    blocks4 = lambda ref: (lambda b: ref.at[pl.ds(b * PLANE, PLANE)])
    send_d = z_copies(0, lambda b: dw_d.at[b], zd_v)
    send_b = z_copies(1, blocks4(dw_b), zb_v)
    send_a = z_copies(2, blocks4(da_v), za_v)
    send_o = z_copies(3, lambda b: do_v.at[b], zo_v)
    send_s = z_copies(4, lambda b: small_v, small_in)
    for cp in send_d + send_b:
        cp.start()

    for g in range(2):
        for a in range(taps_q):
            t_v[g, a * length : (a + 1) * length] = band(kern, 2 * me.pair + g, a, taps_q, taps_k, length, True).astype(BF16)
    shift_v[length:] = jnp.zeros((8, length), F32)
    corr_v[...] = jnp.zeros(corr_v.shape, F32)
    rows_v[...] = jnp.zeros(rows_v.shape, F32)
    small_v[...] = jnp.zeros(small_v.shape, F32)
    h0, h1 = head_lanes(length, dh)
    scatter = Scatter(me, s_out, s_red, s_diag, s_near, rs_send, rs_recv)
    loads[0].wait()
    loads[1].wait()

    def one(i, carry):
        row, k = order(me, i)
        at = lax.rem(i, SLOTS)
        for cp in row_copies(i):
            cp.wait()
        wo = wo_v[:, :, 0:width].reshape(wo_v.shape[0] * wo_v.shape[1], width)[0:SIDE]
        q, kk, v = qkv_v[at, :, 0:SIDE], qkv_v[at, :, SIDE : 2 * SIDE], qkv_v[at, :, 2 * SIDE : 3 * SIDE]
        parts = [nn(p_v[at, g, 0], v) + nn(p_v[at, g, 1], v) for g in range(2)]
        probs = [p_v[at, g, 0].astype(F32) + p_v[at, g, 1].astype(F32) for g in range(2)]
        lane_mix = [mix_lanes(mix, me.pair, g, dh) for g in range(2)]
        attended = parts[0] * lane_mix[0] + parts[1] * lane_mix[1]
        centred = jnp.where(h0 | h1, attended - head_stats(attended, dh, h0, h1), 0.0)
        inv = lax.rsqrt(head_stats(centred * centred, dh, h0, h1) + 1e-5)
        normal = centred * inv
        g_gated = nt(gb_v[row], wo)
        rows_v[0:1] = rows_v[0:1] + jnp.sum(g_gated * normal, axis=0, keepdims=True)
        u = g_gated * gains[2:3, 0:SIDE]
        g_att = inv * (u - head_stats(u, dh, h0, h1) - normal * head_stats(u * normal, dh, h0, h1))
        g_exact = jnp.where(h0 | h1, g_att, 0.0)
        g_att = g_exact.astype(BF16).astype(F32)
        ok = allowed_mask(length, ends[row, 0:1, :])
        g_q = jnp.zeros((length, SIDE), F32)
        g_k = jnp.zeros((length, SIDE), F32)
        g_v = jnp.zeros((length, SIDE), F32)
        for o in range(2):
            mixed = mix[2 * me.pair + o, 0] * probs[0] + mix[2 * me.pair + o, 1] * probs[1]
            g_v = g_v + tn(mixed.astype(BF16), jnp.where(h0 if o == 0 else h1, g_att, 0.0).astype(BF16))
        for g in range(2):
            mine = h0 if g == 0 else h1
            rows_v[1 + g : 2 + g] = rows_v[1 + g : 2 + g] + jnp.sum(g_exact * parts[g], axis=0, keepdims=True)
            g_out = (g_att * lane_mix[g]).astype(BF16)
            g_probs = nt(g_out, v)
            g_conv = probs[g] * (g_probs - jnp.sum(probs[g] * g_probs, axis=-1, keepdims=True))
            shift_v[0:length] = g_conv
            for a in range(taps_q):
                cat_v[:, a * length : (a + 1) * length] = shift_v[a : a + length].astype(BF16)
            corr_v[g] = corr_v[g] + tn(m_v[at, g], cat_v[...])
            g_raw = jnp.where(ok, nn(cat_v[...], t_v[g]), 0.0).astype(BF16)
            g_q = g_q + nn(g_raw, jnp.where(mine, kk.astype(F32), 0.0).astype(BF16))
            g_k = g_k + tn(g_raw, jnp.where(mine, q.astype(F32), 0.0).astype(BF16))
        g_q, g_k = g_q * scale, g_k * scale
        mid_tile = g_q[:, 128:256] + pltpu.roll(g_v[:, 128:256], 64, 1)
        packed = jnp.concatenate([g_q[:, 0:128], mid_tile, g_k, g_v[:, 0:128]], axis=1).astype(BF16)
        gq_v[row] = packed
        part = nt(packed, wa_v[...].reshape(width, QKV))

        @pl.when(lax.rem(i, 2) == 0)
        def _():
            scatter.put_sib(k, part)

        @pl.when(lax.rem(i, 2) == 1)
        def _():
            scatter.put_self(k, part)

        scatter.push(i)

        @pl.when(i + SLOTS < GROUP)
        def _():
            for cp in row_copies(i + SLOTS):
                cp.start()

        return carry

    lax.fori_loop(0, GROUP, one, 0)
    scatter.turn()

    for cp in loads[2:]:
        cp.wait()
    tokens = GROUP * length
    for j in range(planes):
        nrm_copy(j).wait()
        value = tn(nrm_v[j % 2].reshape(tokens, span), gq_v[...].reshape(tokens, QKV))
        da_v[j * PLANE : (j + 1) * PLANE] = value.astype(BF16).reshape(PLANE, r, QKV)
        if j + 2 < planes:
            nrm_copy(j + 2).start()
    for cp in send_a:
        cp.start()
    value = tn(gated_v[...].reshape(tokens, SIDE), gb_v[...].reshape(tokens, width))
    do_v[...] = value[0 : 2 * dh].astype(BF16).reshape(do_v.shape)
    for cp in send_o:
        cp.start()

    def taps(at, carry):
        g, a = lax.div(at, taps_q), lax.rem(at, taps_q)
        lanes_at = pl.ds(pl.multiple_of(a * length, length), length)
        e = corr_v[g, :, lanes_at]
        diff = lax.broadcasted_iota(jnp.int32, (length, length), 0) - lax.broadcasted_iota(jnp.int32, (length, length), 1)
        for b in range(taps_k):
            line = jnp.sum(jnp.where(diff == b - taps_k // 2, e, 0.0), axis=0, keepdims=True)
            small_v[at, b : b + 1] = line[:, 0:128] + line[:, 128:256]
        return carry

    lax.fori_loop(0, 2 * taps_q, taps, 0)
    base = 2 * taps_q
    at = lanes(1, SIDE)
    for o in range(2):
        for g in range(2):
            line = jnp.where((at >= o * dh) & (at < (o + 1) * dh), rows_v[1 + g : 2 + g], 0.0)
            small_v[base, 2 * o + g : 2 * o + g + 1] = line[:, 0:128] + line[:, 128:256]
    for j in range(2):
        small_v[base, 4 + j : 5 + j] = rows_v[0:1, j * 128 : (j + 1) * 128]

    scatter.arrive()

    def middle(at):
        g_normed = scatter.total(at)
        tok32 = tok_v[at].astype(F32)
        s = lax.rsqrt(jnp.mean(tok32 * tok32, axis=-1, keepdims=True) + 1e-6)
        line_v[0:1] = line_v[0:1] + jnp.sum(g_normed * tok32 * s, axis=0, keepdims=True)
        pulled = g_normed * gains[0:1]
        back = g_res[at] + s * pulled
        g_tokens[at] = back - tok32 * (s * s * s * jnp.mean(pulled * tok32, axis=-1, keepdims=True))

    line_v[...] = jnp.zeros(line_v.shape, F32)
    strips(length, middle)
    line = line_v[0:1]
    for j in range(width // 128):
        small_v[base + 1, j : j + 1] = line[:, j * 128 : (j + 1) * 128]
        small_v[base + 2, j : j + 1] = g_mid_gain[0:1, j * 128 : (j + 1) * 128]
    for cp in send_s:
        cp.start()

    def to_slot(d):
        to = lax.rem(me.slot + d, GROUP)
        return lax.div(to, PLANE), lax.rem(to, PLANE)

    def group_copies(kind, src_of, landing):
        cps = []
        for d in range(1, GROUP):
            y, sl = to_slot(d)
            cps.append(remote(src_of(sl), landing.at[me.slot], t_send.at[kind, d], t_recv.at[kind, d], (y, me.g * PLANE + sl)))
        cps.append(pltpu.make_async_copy(src_of(me.s), landing.at[me.slot], t_send.at[kind, 0]))
        return cps

    def group_wait(kind, cps, landing):
        for d in range(1, GROUP):
            fr = lax.rem(me.slot - d + GROUP, GROUP)
            remote(landing.at[fr], landing.at[fr], t_send.at[kind, d], t_recv.at[kind, d], me.sib()).wait_recv()
        for cp in cps[:-1]:
            cp.wait_send()
        cps[-1].wait()

    for cp in send_s:
        cp.wait_recv()
    for cp in send_s:
        cp.wait_send()
    small_v[...] = small_v[...] + sum(small_in[d] for d in range(planes - 1))
    small_cps = group_copies(2, lambda sl: small_v, out_small)
    for cp in small_cps:
        cp.start()

    def sums(landing, own):
        total = own.astype(F32)
        for d in range(planes - 1):
            total = total + landing[d].astype(F32)
        return total.astype(BF16)

    for cp in send_d:
        cp.wait_recv()
    sd_v[...] = sums(zd_v, own_d[...])
    d_cp = remote(sd_v, out_d.at[me.y], t_send.at[3, 0], t_recv.at[3, 0], me.yn())
    d_cp.start()
    d_here = pltpu.make_async_copy(sd_v, out_d.at[me.y], t_send.at[3, 1])
    d_here.start()
    for cp in send_b:
        cp.wait_recv()
    sb_v[...] = sums(zb_v, own_b[...])
    b_cps = group_copies(0, lambda sl: sb_v.at[sl], out_b)
    for cp in b_cps:
        cp.start()
    for cp in send_o:
        cp.wait_recv()
    so_v[...] = sums(zo_v, do_v[me.g])
    o_to = me.pair * per_pair + lax.div(me.g, 2)
    o_half = lax.rem(me.g, 2)

    def o_copy(y):
        return remote(so_v, out_o.at[o_half], t_send.at[4, y], t_recv.at[4, o_half], (y, o_to))

    o_here = pltpu.make_async_copy(so_v, out_o.at[o_half], t_send.at[4, 2])

    def o_each(act, act_here):
        for y in range(2):
            mine = (y == me.y) & (o_to == me.f)

            @pl.when(jnp.logical_not(mine))
            def _():
                act(o_copy(y))

            @pl.when(mine)
            def _():
                act_here(o_here)

    o_each(lambda cp: cp.start(), lambda cp: cp.start())
    for cp in send_a:
        cp.wait_recv()
    sa_v[...] = sums(za_v, da_v[pl.ds(me.g * PLANE, PLANE)])
    a_cps = group_copies(1, lambda sl: sa_v.at[sl], out_a)
    for cp in a_cps:
        cp.start()

    group_wait(2, small_cps, out_small)
    d_cp.wait_send()
    remote(out_d.at[1 - me.y], out_d.at[1 - me.y], t_send.at[3, 0], t_recv.at[3, 0], me.yn()).wait_recv()
    d_here.wait()
    group_wait(0, b_cps, out_b)
    src_pair = lax.div(me.f, per_pair)
    src_y, src_s = lax.div(src_pair, 4), lax.rem(src_pair, 2) * 2 + lax.rem(lax.div(src_pair, 2), 2)
    for h in range(2):
        src_f = (2 * lax.rem(me.f, per_pair) + h) * PLANE + src_s

        @pl.when(jnp.logical_not((src_y == me.y) & (src_f == me.f)))
        def _():
            remote(out_o.at[h], out_o.at[h], t_send.at[4, 0], t_recv.at[4, h], me.sib()).wait_recv()

    o_each(lambda cp: cp.wait_send(), lambda cp: cp.wait())
    group_wait(1, a_cps, out_a)
    for cp in send_d + send_b + send_a + send_o:
        cp.wait_send()
    scatter.finish()


def backward_call(cfg, branch_all, o_all, a_all, nrm_all, qkv_all, p_all, m_all, gated_all, dw_b, dw_d, tok, g_res, gains, ends, g_mid_gain, kern, mix):
    length, width = tok.shape
    planes, ff = cfg["planes"], cfg["ff"]
    n, r = a_all.shape[:2]
    chunk = ff // planes
    taps = cfg["kq"] * length
    pad_rows = -(-SIDE // o_all.shape[1])
    piece = 2 * cfg["dh"] // planes
    small = (2 * cfg["kq"] + 3, 16, 128)
    hbm, vmem, smem = pl.BlockSpec(memory_space=pl.ANY), pl.BlockSpec(memory_space=pltpu.VMEM), pl.BlockSpec(memory_space=pltpu.SMEM)
    sds = jax.ShapeDtypeStruct
    dma = pltpu.SemaphoreType.DMA
    rows = (GROUP, length)
    v16 = lambda *shape: pltpu.VMEM(shape, BF16)
    v32 = lambda *shape: pltpu.VMEM(shape, F32)
    return pl.pallas_call(
        functools.partial(backward_kernel, cfg),
        out_shape=(
            sds((length, width), F32), sds((GROUP, r, QKV), BF16), sds((GROUP, r, 2 * ff), BF16),
            sds((2, chunk, width), BF16), sds((2, piece, width), BF16), sds((GROUP,) + small, F32),
        ),
        in_specs=[hbm] * 11 + [vmem] * 4 + [smem] * 2,
        out_specs=(vmem,) + (hbm,) * 5,
        scratch_shapes=[
            v16(*rows, width), v16(pad_rows, *o_all.shape[1:]), v16(n, r, QKV), v16(2, *rows, PLANE * r), v16(SLOTS, length, 3 * SIDE),
            v16(SLOTS, 2, 2, length, length), v16(SLOTS, 2, length, length), v16(*rows, SIDE),
            v16(2, taps, length), v16(length, taps), v32(length + 8, length), v32(2, length, taps), v16(*rows, QKV),
            v16(n, r, QKV), v16(planes, piece, width), v16(length, width), v32(8, SIDE), v32(8, width),
            v16(planes - 1, PLANE, r, 2 * ff), v16(planes - 1, chunk, width), v16(planes - 1, PLANE, r, QKV), v16(planes - 1, piece, width),
            v16(PLANE, r, 2 * ff), v16(chunk, width), v16(PLANE, r, QKV), v16(piece, width), v16(PLANE, r, 2 * ff), v16(chunk, width),
            v32(*small), v32(planes - 1, *small),
            *Scatter.scratch(length, width),
            dma((5, planes - 1)), dma((5, planes - 1)), dma((5, GROUP)), dma((5, GROUP)), dma((8,)), dma((4, GROUP)),
        ],
        compiler_params=pltpu.CompilerParams(collective_id=3, has_side_effects=True, vmem_limit_bytes=54 * 2**20),
        name="attention_backward",
    )(branch_all, o_all, a_all, nrm_all, qkv_all, p_all, m_all, gated_all, dw_b, dw_d, tok, g_res, gains, ends, g_mid_gain, kern, mix)


def pair_order(blocks):
    rest = blocks.shape[1:]
    return jnp.swapaxes(blocks.reshape((2, 2, 2) + rest), 1, 2).reshape((GROUP,) + rest)


def fits(mesh, tokens, kernel, w_gate):
    n = mesh.shape["fsdp"]
    width, length, heads, ff = tokens.shape[2], tokens.shape[1], kernel.shape[0], w_gate.shape[1]
    return (
        mesh.shape["rep"] == 2
        and n % GROUP == 0
        and heads == 2 * GROUP
        and width == heads * 96
        and (width // n) % 32 == 0
        and ff % (2 * n * 128) == 0
        and length == SIDE
    )


def per_device_group(
    planes,
    tokens,
    doc_lengths,
    pad_counts,
    norm_in,
    w_qkv,
    kernel,
    mixing,
    norm_heads,
    w_out,
    norm_mid,
    w_gate,
    w_up,
    w_down,
    cotangent,
):
    length, width = tokens.shape[1:]
    heads, kq, kk = kernel.shape
    dh = width // heads
    n = planes * PLANE
    r = width // n
    chunk = w_down.shape[0] // 2
    ff = planes * chunk
    cfg = dict(planes=planes, dh=dh, kq=kq, kk=kk, ff=ff)
    y = lax.axis_index("rep")
    f = lax.axis_index("fsdp")

    with jax.named_scope("slices_to_send"):
        by_pair = lax.dynamic_index_in_dim(w_qkv.reshape(r, 3, 2, 2, 2, 2 * dh), y, 2, keepdims=False)
        by_pair = by_pair.transpose(3, 2, 0, 1, 4).reshape(PLANE, r, 3, 2 * dh)
        gains_at = jnp.stack([norm_in, norm_mid], axis=1)
        gains_at = jnp.broadcast_to(jnp.pad(gains_at, ((0, 0), (0, 62)))[None], (PLANE, r, 64))
        w_a = jnp.concatenate(
            [by_pair[:, :, 0], by_pair[:, :, 2, 128:], by_pair[:, :, 1], gains_at, by_pair[:, :, 2, :128]], axis=-1
        )

        def columns(w):
            w = lax.dynamic_index_in_dim(w.reshape(r, planes, PLANE, 2, chunk), y, 3, keepdims=False)
            return w.transpose(2, 0, 1, 3).reshape(PLANE, r, ff)

        w_b = jnp.concatenate([columns(w_gate), columns(w_up)], axis=-1)
        w_d = lax.dynamic_index_in_dim(w_down.reshape(2, chunk, width), y, 0, keepdims=False)
        w_o = jnp.concatenate([w_out, jnp.pad(norm_heads[:, None], ((0, 0), (0, 127)))], axis=1)
        places = jnp.arange(length, dtype=jnp.int32)
        doc_ends = jnp.cumsum(doc_lengths[0])
        own_end = jnp.min(jnp.where(doc_ends[None, :] > places[:, None], doc_ends[None, :], length), axis=1)
        ends = jnp.where(places < length - pad_counts[0], own_end, places + 1).astype(F32)
        meta = jnp.broadcast_to(ends[None], (8, length))
    tok, ct = tokens[0], cotangent[0]
    kern_flat = kernel.reshape(-1)

    (_, ct_all, a_all, b_all, d_all, o_all, nrm_all, qkv_all, p_all, m_all, gated_all, mid_all, resid, gains, ends_all) = (
        forward_call(cfg, tok, ct, w_a, w_b, w_d, w_o, meta, kern_flat, mixing)
    )
    layer_out, g_res, branch_all, dw_b, dw_d, g_mid_gain = feed_call(
        cfg, mid_all, ct_all, b_all, d_all, resid, gains
    )
    g_tokens, out_a, out_b, out_d, out_o, small = backward_call(
        cfg, branch_all, o_all, a_all, nrm_all, qkv_all, p_all, m_all, gated_all, dw_b.reshape(n, r, 2 * ff),
        dw_d.reshape(planes, chunk, width), tok, g_res, gains, ends_all, g_mid_gain, kern_flat, mixing,
    )

    with jax.named_scope("results"):
        q = out_a[:, :, 0 : 2 * dh]
        k = out_a[:, :, SIDE : SIDE + 2 * dh]
        v = jnp.concatenate([out_a[:, :, 2 * SIDE :], out_a[:, :, 2 * dh : SIDE]], axis=-1)
        g_qkv = jnp.stack([pair_order(part) for part in (q, k, v)]).transpose(2, 0, 1, 3)
        g_qkv = g_qkv.reshape(r, 3 * width).astype(F32)

        def whole(part):
            part = part.reshape(2, PLANE, r, planes, chunk).transpose(2, 3, 1, 0, 4)
            return part.reshape(r, n * 2 * chunk).astype(F32)

        g_gate, g_up = whole(out_b[:, :, :ff]), whole(out_b[:, :, ff:])
        g_down = out_d.reshape(2 * chunk, width).astype(F32)
        g_out = out_o.reshape(r, width).astype(F32)
        g_kernel = pair_order(small[:, : 2 * kq, :kk].sum(-1)).reshape(heads, kq, kk)
        base = 2 * kq
        g_mixing = pair_order(small[:, base, 0:4].sum(-1)).reshape(heads, 2)

        def own(line):
            return lax.dynamic_slice_in_dim(line, f * r, r)

        g_heads = own(pair_order(small[:, base, 4:6].reshape(GROUP, 256)[:, : 2 * dh]).reshape(width))
        lines = small[:, base + 1 :, : width // 128].sum(0).reshape(2, width)
        g_in, g_mid = own(lines[0]), own(lines[1])
    return (layer_out[None], g_tokens[None], g_in, g_qkv, g_kernel, g_mixing, g_heads, g_out, g_mid, g_gate, g_up, g_down)


def solution(mesh):
    in_specs = (
        P(("rep", "fsdp"), None, None),
        P(("rep", "fsdp"), None),
        P(("rep", "fsdp")),
        P("fsdp"),
        P("fsdp", None),
        P(),
        P(),
        P("fsdp"),
        P("fsdp", None),
        P("fsdp"),
        P("fsdp", None),
        P("fsdp", None),
        P("fsdp", None),
        P(("rep", "fsdp"), None, None),
    )
    out_specs = (
        P(("rep", "fsdp"), None, None),
        P(("rep", "fsdp"), None, None),
        P("fsdp"),
        P("fsdp", None),
        P(),
        P(),
        P("fsdp"),
        P("fsdp", None),
        P("fsdp"),
        P("fsdp", None),
        P("fsdp", None),
        P("fsdp", None),
    )

    def layer(*args):
        body = per_device
        if fits(mesh, args[0], args[5], args[10]):
            body = functools.partial(per_device_group, mesh.shape["fsdp"] // PLANE)
        return jax.shard_map(body, mesh=mesh, in_specs=in_specs, out_specs=out_specs, check_vma=False)(*args)

    return layer
```

```python
import functools

import jax
import jax.numpy as jnp
from jax import lax
from jax.experimental import pallas as pl
from jax.experimental.pallas import tpu as pltpu
from jax.sharding import PartitionSpec as P

F32 = jnp.float32
BF16 = jnp.bfloat16
NEG_FILL = -1e30
MESH = pl.DeviceIdType.MESH
PLANE = 4
GROUP = 8
SIDE = 256
LAG = 3
SLOTS = 2
QKV = 640


class Place:
    def __init__(self, planes):
        self.planes = planes
        self.y = lax.axis_index("rep")
        self.f = lax.axis_index("fsdp")
        self.g = lax.div(self.f, PLANE)
        self.s = lax.rem(self.f, PLANE)
        self.x = lax.div(self.s, 2)
        self.c = lax.rem(self.s, 2)
        self.slot = self.y * PLANE + self.s
        self.home = self.y + self.c * (planes - 1 - 2 * self.y)
        self.pair = 2 * self.home + self.x
        self.sib = self.dev(self.y, self.x, 1 - self.c)
        self.xn = self.dev(self.y, 1 - self.x, self.c)
        self.yn = self.dev(1 - self.y, self.x, self.c)

    def dev(self, y, x, c):
        return (y, self.g * PLANE + x * 2 + c)

    def plane_dev(self, g):
        return (self.y, g * PLANE + self.s)

    def row(self, dy, dx, dc):
        y = self.y + dy - 2 * dy * self.y
        x = self.x + dx - 2 * dx * self.x
        c = self.c + dc - 2 * dc * self.c
        return y * 4 + x * 2 + c

    def greet(self):
        sem = pltpu.get_barrier_semaphore()
        n = self.planes * PLANE
        for d in range(1, n):
            pl.semaphore_signal(sem, inc=1, device_id=(self.y, lax.rem(self.f + d, n)), device_id_type=MESH)
        for s in range(PLANE):
            pl.semaphore_signal(sem, inc=1, device_id=(1 - self.y, self.g * PLANE + s), device_id_type=MESH)
        pl.semaphore_wait(sem, n - 1 + PLANE)


def meet(me, sem):
    pl.semaphore_signal(sem, inc=1, device_id=me.sib, device_id_type=MESH)
    pl.semaphore_wait(sem, 1)


def remote(src, dst, send, recv, dev):
    return pltpu.make_async_remote_copy(
        src_ref=src, dst_ref=dst, send_sem=send, recv_sem=recv, device_id=dev, device_id_type=MESH
    )


class Gather:
    SENDS = 14
    RECVS = 14

    def __init__(self, me, own, buf, send, recv, local):
        self.me, self.own, self.buf = me, own, buf
        self.send, self.recv, self.local = send, recv, local
        self.half = own.shape[0] // 2
        self.sent = []

    def _own(self, h):
        return self.own.at[pl.ds(h * self.half, self.half)]

    def _blk(self, row, h):
        return self.buf.at[row, pl.ds(h * self.half, self.half)]

    def _copy(self, i):
        own, row, h, kind, dev = self.sent[i]
        src = self._own(h) if own else self._blk(row, h)
        return remote(src, self._blk(row, h), self.send.at[i], self.recv.at[kind * 2 + h], dev)

    def _go(self, own, row, h, kind, dev):
        self.sent.append((own, row, h, kind, dev))
        self._copy(len(self.sent) - 1).start()

    def _await(self, row, h, kind):
        b = self._blk(row, h)
        remote(b, b, self.send.at[0], self.recv.at[kind * 2 + h], self.me.sib).wait_recv()

    def start(self):
        me = self.me
        self.rows = [me.row(0, 0, 1), me.row(0, 1, 0), me.row(1, 0, 0), me.row(1, 1, 0), me.row(0, 1, 1), me.row(1, 0, 1), me.row(1, 1, 1)]
        self.here = pltpu.make_async_copy(self.own, self.buf.at[me.slot], self.local)
        self.here.start()
        self._go(True, me.slot, 0, 1, me.xn)
        self._go(True, me.slot, 1, 2, me.yn)
        self._go(True, me.slot, 0, 0, me.sib)
        self._go(True, me.slot, 1, 0, me.sib)
        self._go(True, me.slot, 1, 1, me.xn)
        self._go(True, me.slot, 0, 2, me.yn)

    def relay(self):
        me, rows = self.me, self.rows
        self._await(rows[1], 0, 1)
        self._go(False, rows[1], 0, 3, me.yn)
        self._go(False, rows[1], 0, 4, me.sib)
        self._await(rows[2], 1, 2)
        self._go(False, rows[2], 1, 3, me.xn)
        self._go(False, rows[2], 1, 5, me.sib)

    def share(self):
        me, rows = self.me, self.rows
        self._await(rows[1], 1, 1)
        self._go(False, rows[1], 1, 4, me.sib)
        self._await(rows[2], 0, 2)
        self._go(False, rows[2], 0, 5, me.sib)

    def last(self):
        me, rows = self.me, self.rows
        for h in (0, 1):
            self._await(rows[3], h, 3)
            self._go(False, rows[3], h, 6, me.sib)

    def finish(self):
        for kind in (0, 4, 5, 6):
            for h in (0, 1):
                self._await(self.rows[kind], h, kind)
        for i in range(len(self.sent)):
            self._copy(i).wait_send()
        self.here.wait()


class Scatter:
    SENDS = 10
    RECVS = 10

    @staticmethod
    def scratch(rows, width, cores=True, chips=True):
        bufs = []
        if cores:
            bufs.append(pltpu.VMEM((2, rows, width), BF16))
        bufs.append(pltpu.VMEM((4, rows, width), BF16))
        if chips:
            bufs += [pltpu.VMEM((2, rows // 2, width), BF16), pltpu.VMEM((2, rows, width), BF16)]
        return bufs + [pltpu.SemaphoreType.DMA((Scatter.SENDS,)), pltpu.SemaphoreType.DMA((Scatter.RECVS,))]

    def __init__(self, me, out, red, diag, near, send, recv):
        self.me, self.out, self.red, self.diag, self.near = me, out, red, diag, near
        self.send, self.recv = send, recv
        self.half = red.shape[1] // 2

    def _sib(self, k):
        return remote(self.out.at[lax.rem(k, 2)], self.red.at[k], self.send.at[k], self.recv.at[k], self.me.sib)

    def put_sib(self, k, value):
        @pl.when(k >= 2)
        def _():
            self._sib(k - 2).wait_send()

        self.out[lax.rem(k, 2)] = value.astype(BF16)
        self._sib(k).start()

    def put_self(self, k, value):
        self._sib(k).wait_recv()
        self.red[k] = (value + self.red[k].astype(F32)).astype(BF16)

    def _copy(self, name):
        h, me = self.half, self.me
        lo, hi = pl.ds(0, h), pl.ds(h, h)
        src, dst, i, dev = {
            "da": (self.red.at[0, lo], self.diag.at[0], 4, me.xn),
            "db": (self.red.at[0, hi], self.diag.at[1], 5, me.yn),
            "xa": (self.red.at[1, lo], self.near.at[0, lo], 6, me.xn),
            "xb": (self.red.at[1, hi], self.near.at[0, hi], 7, me.xn),
            "ya": (self.red.at[2, lo], self.near.at[1, lo], 8, me.yn),
            "yb": (self.red.at[2, hi], self.near.at[1, hi], 9, me.yn),
        }[name]
        return remote(src, dst, self.send.at[i], self.recv.at[i], dev)

    def push(self, i):
        @pl.when(i == 1)
        def _():
            self._copy("da").start()
            self._copy("db").start()

        @pl.when(i == 3)
        def _():
            self._copy("xa").start()

        @pl.when(i == 5)
        def _():
            self._copy("yb").start()
            self.turn()

    def ahead(self):
        self._copy("yb").start()

    def turn(self):
        h = self.half
        self._copy("db").wait_recv()
        self.red[1, h:] = (self.red[1, h:].astype(F32) + self.diag[1].astype(F32)).astype(BF16)
        self._copy("xb").start()
        self._copy("da").wait_recv()
        self.red[2, :h] = (self.red[2, :h].astype(F32) + self.diag[0].astype(F32)).astype(BF16)
        self._copy("ya").start()

    def arrive(self):
        for name in ("xa", "xb", "ya", "yb"):
            self._copy(name).wait_recv()

    def total(self, at):
        return self.red[3, at].astype(F32) + self.near[0, at].astype(F32) + self.near[1, at].astype(F32)

    def finish_cores(self):
        for k in (2, 3):
            self._sib(k).wait_send()

    def finish_chips(self):
        for name in ("da", "db", "xa", "xb", "ya", "yb"):
            self._copy(name).wait_send()


class Spread:
    def __init__(self, me, blocks, send, recv):
        self.me, self.blocks, self.send, self.recv = me, blocks, send, recv

    def _copy(self, b, t, i):
        return remote(self.blocks(b), self.blocks(b), self.send.at[i], self.recv.at[b], self.me.plane_dev(t))

    def _sends(self, b):
        last = self.me.planes - 1
        if b in (0, last):
            return [(b, 1 if b == 0 else last - 1, 0)] + [(b, t, 1) for t in sorted(range(last + 1), key=lambda t: abs(t - b))[2:]]
        other, end = (2, 0) if b == 1 else (1, 3)
        return [(b, b - 1, 0), (b, b + 1, 0), (other, end, 1)]

    def _each(self, act, steps):
        for g in range(self.me.planes):

            @pl.when(self.me.g == g)
            def _():
                for i, (b, t, step) in enumerate(self._sends(g)):
                    if step in steps:
                        act(self._copy(b, t, i))

    def near(self):
        self._each(lambda cp: cp.start(), (0,))

    def settle(self):
        inner = (self.me.g == 0) | (self.me.g == 2)

        @pl.when(inner)
        def _():
            self._copy(1, 0, 0).wait_recv()

        @pl.when(jnp.logical_not(inner))
        def _():
            self._copy(2, 0, 0).wait_recv()

    def rest(self):
        self._each(lambda cp: cp.start(), (1,))

    def arrive(self):
        for g in range(self.me.planes):

            @pl.when(self.me.g == g)
            def _():
                for b in range(self.me.planes):
                    if b not in (g, 1 if g in (0, 2) else 2):
                        self._copy(b, b, 0).wait_recv()

    def finish(self):
        self._each(lambda cp: cp.wait_send(), (0, 1))


class Collect:
    def __init__(self, me, blocks, landing, via, send, recv):
        self.me, self.blocks, self.landing, self.via, self.send, self.recv = me, blocks, landing, via, send, recv
        self.by = {(0, 3): 1, (3, 0): 2} if me.planes == 4 else {}

    def _copy(self, b, t, src, i):
        at = (b - t) % self.me.planes - 1
        return remote(src, self.landing.at[at], self.send.at[i], self.recv.at[at], self.me.plane_dev(t))

    def _plan(self, b):
        combined = [t for (s, t), by in self.by.items() if by == b]
        direct = [t for t in range(self.me.planes) if t != b and t not in combined]
        direct.sort(key=lambda t: -abs(t - b))
        return [(t, (b, t) in self.by, i) for i, t in enumerate(direct)]

    def _each(self, b, act):
        @pl.when(self.me.g == b)
        def _():
            for t, through, i in self._plan(b):
                if through:
                    z = self.me.planes
                    by = self.by[(b, t)]
                    act(remote(self.blocks(t), self.via, self.send.at[i], self.recv.at[z - 1], self.me.plane_dev(by)))
                else:
                    act(self._copy(b, t, self.blocks(t), i))

    def start(self):
        for b in range(self.me.planes):
            self._each(b, lambda cp: cp.start())

    def _combined(self, b, t):
        return self._copy(b, t, self.via, self.me.planes - 2)

    def combine(self, own):
        for (s, t), by in self.by.items():

            @pl.when(self.me.g == by)
            def _():
                z = self.me.planes
                remote(self.via, self.via, self.send.at[0], self.recv.at[z - 1], self.me.plane_dev(by)).wait_recv()
                for q in range(self.via.shape[0]):
                    self.via[q] = (self.via[q].astype(F32) + own(t)[q].astype(F32)).astype(BF16)
                self._combined(by, t).start()

    def clear(self):
        for s, t in self.by:

            @pl.when(self.me.g == t)
            def _():
                at = (s - t) % self.me.planes - 1
                self.landing[at] = jnp.zeros(self.landing.shape[1:], BF16)

    def total(self, out, own):
        z = self.me.planes
        for t in range(z):

            @pl.when(self.me.g == t)
            def _():
                for b in range(z):
                    if b != t and (b, t) not in self.by:
                        at = (b - t) % z - 1
                        self._copy(b, t, self.landing.at[at], 0).wait_recv()

        for q in range(out.shape[0]):
            value = own[q].astype(F32)
            for at in range(z - 1):
                value = value + self.landing[at, q].astype(F32)
            out[q] = value.astype(BF16)

    def finish(self):
        for b in range(self.me.planes):
            self._each(b, lambda cp: cp.wait_send())
        for (s, t), by in self.by.items():

            @pl.when(self.me.g == by)
            def _():
                self._combined(by, t).wait_send()


def order(me, i):
    k = lax.div(i, 2)
    dx = 1 - lax.div(k, 2)
    dy = 1 - lax.rem(k, 2)
    dc = 1 - lax.rem(i, 2)
    return me.row(dy, dx, dc), k


def strips(length, body, strip=64):
    def one(i, carry):
        body(pl.ds(pl.multiple_of(i * strip, strip), strip))
        return carry

    lax.fori_loop(0, length // strip, one, 0)


def lanes(rows, width):
    return lax.broadcasted_iota(jnp.int32, (rows, width), 1)


def nt(a, b):
    return lax.dot_general(a, b, (((1,), (1,)), ((), ())), preferred_element_type=F32)


def tn(a, b):
    return lax.dot_general(a, b, (((0,), (0,)), ((), ())), preferred_element_type=F32)


def nn(a, b):
    return jnp.dot(a, b, preferred_element_type=F32)


def head_lanes(rows, dh):
    at = lanes(rows, SIDE)
    return at < dh, (at >= dh) & (at < 2 * dh)


def allowed_mask(length, ends):
    i = lax.broadcasted_iota(jnp.int32, (length, length), 0)
    j = lax.broadcasted_iota(jnp.int32, (length, length), 1)
    return (i >= j) & (i.astype(F32) < ends)


def mix_lanes(mix_ref, pair, g, dh):
    at = lanes(1, SIDE)
    m0, m1 = mix_ref[2 * pair, g], mix_ref[2 * pair + 1, g]
    return jnp.where(at < dh, m0, jnp.where(at < 2 * dh, m1, 0.0))


def head_stats(value, dh, h0, h1):
    m0 = jnp.sum(jnp.where(h0, value, 0.0), axis=-1, keepdims=True) / dh
    m1 = jnp.sum(jnp.where(h1, value, 0.0), axis=-1, keepdims=True) / dh
    return jnp.where(h0, m0, jnp.where(h1, m1, 0.0))


def band(kern_ref, head, a, taps_q, taps_k, length, flip):
    r = lax.broadcasted_iota(jnp.int32, (length, length), 0)
    c = lax.broadcasted_iota(jnp.int32, (length, length), 1)
    diff = (c - r) if flip else (r - c)
    acc = jnp.zeros((length, length), F32)
    for b in range(taps_k):
        acc = jnp.where(diff == b - taps_k // 2, kern_ref[(head * taps_q + a) * taps_k + b], acc)
    return acc


def rms_norm(values_in, scaling):
    return (
        values_in
        * lax.rsqrt(jnp.mean(values_in * values_in, axis=-1, keepdims=True) + 1e-06)
        * scaling
    )


def group_norm(values_in, scaling):
    centred = values_in - jnp.mean(values_in, axis=-1, keepdims=True)
    scaled = centred * lax.rsqrt(jnp.mean(centred * centred, axis=-1, keepdims=True) + 1e-05)
    return scaled.reshape(values_in.shape[0], -1) * scaling


def convolve(scores, kernel):
    length = scores.shape[1]
    taps_query = kernel.shape[1]
    taps_key = kernel.shape[2]
    half_width = taps_key // 2
    padded = jnp.pad(scores, ((0, 0), (taps_query - 1, 0), (half_width, half_width)))
    summed = jnp.zeros_like(scores)
    for shift_q in range(taps_query):
        for shift_k in range(taps_key):
            start_q = taps_query - 1 - shift_q
            window = padded[:, start_q : start_q + length, shift_k : shift_k + length]
            summed = summed + kernel[:, shift_q, shift_k][:, None, None] * window
    return summed


def convolve_back(grad_conv, masked, kernel):
    length = masked.shape[1]
    taps_query = kernel.shape[1]
    taps_key = kernel.shape[2]
    half_width = taps_key // 2
    padded = jnp.pad(masked, ((0, 0), (taps_query - 1, 0), (half_width, half_width)))
    grad_padded = jnp.pad(grad_conv, ((0, 0), (0, taps_query - 1), (half_width, half_width)))
    grad_masked = jnp.zeros_like(masked)
    grad_taps = []
    for shift_q in range(taps_query):
        for shift_k in range(taps_key):
            start_q = taps_query - 1 - shift_q
            window = padded[:, start_q : start_q + length, shift_k : shift_k + length]
            grad_taps.append(jnp.sum(grad_conv * window, axis=(1, 2)))
            start_k = taps_key - 1 - shift_k
            back_window = grad_padded[:, shift_q : shift_q + length, start_k : start_k + length]
            grad_masked = grad_masked + kernel[:, shift_q, shift_k][:, None, None] * back_window
    grad_kern = jnp.stack(grad_taps, axis=1).reshape(kernel.shape)
    return (grad_masked, grad_kern)


def build_mask(doc_lengths, pad_count, length):
    places = jnp.arange(length, dtype=jnp.int32)
    doc_ends = jnp.cumsum(doc_lengths)
    segment = jnp.sum((places[:, None] >= doc_ends[None, :]).astype(jnp.int32), axis=1)
    live_end = length - pad_count
    same_doc = segment[:, None] == segment[None, :]
    causal = places[None, :] <= places[:, None]
    usable = (places[None, :] < live_end) | (places[None, :] == places[:, None])
    return same_doc & causal & usable


def outer_sum(left_rows, right_rows):
    return lax.dot_general(
        left_rows, right_rows, (((0,), (0,)), ((), ())), preferred_element_type=jnp.float32
    )


def back_product(grad_rows, weight_full):
    return lax.dot_general(
        grad_rows, weight_full, (((1,), (1,)), ((), ())), preferred_element_type=jnp.float32
    )


def attention_weights(norm_in, w_qkv, norm_heads, w_out):
    return (
        lax.all_gather(norm_in, "fsdp", axis=0, tiled=True),
        lax.all_gather(w_qkv, "fsdp", axis=0, tiled=True),
        lax.all_gather(norm_heads, "fsdp", axis=0, tiled=True),
        lax.all_gather(w_out, "fsdp", axis=0, tiled=True),
    )


def feed_weights(norm_mid, w_gate, w_up, w_down):
    return (
        lax.all_gather(norm_mid, "fsdp", axis=0, tiled=True),
        lax.all_gather(w_gate, "fsdp", axis=0, tiled=True),
        lax.all_gather(w_up, "fsdp", axis=0, tiled=True),
        lax.all_gather(w_down, "fsdp", axis=0, tiled=True),
    )


def per_device(
    tokens,
    doc_lengths,
    pad_counts,
    norm_in,
    w_qkv,
    kernel,
    mixing,
    norm_heads,
    w_out,
    norm_mid,
    w_gate,
    w_up,
    w_down,
    cotangent,
):
    inputs = tokens[0].astype(jnp.float32)
    length = inputs.shape[0]
    model_width = inputs.shape[1]
    head_count = kernel.shape[0]
    head_size = model_width // head_count
    pair_count = head_count // 2
    score_scale = head_size ** (-0.5)
    allowed = build_mask(doc_lengths[0], pad_counts[0], length)[None]
    kern_pairs = kernel.reshape(pair_count, 2, kernel.shape[1], kernel.shape[2])
    mix_pairs = mixing.reshape(pair_count, 2, 2)
    attn_set = attention_weights(norm_in, w_qkv, norm_heads, w_out)
    normed = rms_norm(inputs, attn_set[0].astype(jnp.float32)).astype(jnp.bfloat16)
    projected = jnp.dot(normed, attn_set[1], preferred_element_type=jnp.float32).astype(
        jnp.bfloat16
    )
    split_qkv = projected.reshape(length, 3, pair_count, 2, head_size).transpose(1, 2, 3, 0, 4)

    def pair_scores(queries, key_rows, kern_pair):
        raw_scores = (
            jnp.einsum("gie,gje->gij", queries, key_rows, preferred_element_type=jnp.float32)
            * score_scale
        )
        masked = jnp.where(allowed, raw_scores, 0.0)
        logits = jnp.where(allowed, convolve(masked, kern_pair), NEG_FILL)
        return (masked, logits)

    def pair_forward(pieces):
        queries, key_rows, value_rows, kern_pair, mix_pair = pieces
        masked, logits = pair_scores(queries, key_rows, kern_pair)
        row_peak = jnp.max(logits, axis=-1, keepdims=True)
        log_total = row_peak + jnp.log(jnp.sum(jnp.exp(logits - row_peak), axis=-1, keepdims=True))
        attn_probs = jnp.exp(logits - log_total)
        mixed_probs = jnp.einsum("og,gij->oij", mix_pair, attn_probs, precision=lax.Precision.HIGHEST)
        output = jnp.einsum(
            "oij,oje->oie", mixed_probs, value_rows.astype(jnp.float32), precision=lax.Precision.HIGHEST
        )
        return (output, log_total)

    attended_pairs, log_totals = lax.map(
        pair_forward, (split_qkv[0], split_qkv[1], split_qkv[2], kern_pairs, mix_pairs)
    )
    attended = attended_pairs.transpose(2, 0, 1, 3).reshape(length, head_count, head_size)
    gated_out = group_norm(attended, attn_set[2].astype(jnp.float32)).astype(jnp.bfloat16)
    residual = inputs + jnp.dot(gated_out, attn_set[3], preferred_element_type=jnp.float32)
    ffn_set = feed_weights(norm_mid, w_gate, w_up, w_down)
    normed_mid = rms_norm(residual, ffn_set[0].astype(jnp.float32)).astype(jnp.bfloat16)
    gate_pre = jnp.dot(normed_mid, ffn_set[1], preferred_element_type=jnp.float32)
    up_pre = jnp.dot(normed_mid, ffn_set[2], preferred_element_type=jnp.float32)
    sigmoid_gate = jax.nn.sigmoid(gate_pre)
    silu_gate = gate_pre * sigmoid_gate
    hidden = (silu_gate * up_pre).astype(jnp.bfloat16)
    layer_out = (residual + jnp.dot(hidden, ffn_set[3], preferred_element_type=jnp.float32))[None]
    ffn_again = feed_weights(norm_mid, w_gate, w_up, w_down)
    grad_y = cotangent[0]
    grad_w_down = outer_sum(hidden, grad_y)
    grad_hidden = back_product(grad_y, ffn_again[3])
    grad_gate = (
        grad_hidden * up_pre * sigmoid_gate * (1.0 + gate_pre * (1.0 - sigmoid_gate))
    ).astype(jnp.bfloat16)
    grad_up = (grad_hidden * silu_gate).astype(jnp.bfloat16)
    grad_w_gate = outer_sum(normed_mid, grad_gate)
    grad_w_up = outer_sum(normed_mid, grad_up)
    grad_mid = back_product(grad_gate, ffn_again[1]) + back_product(grad_up, ffn_again[2])
    mid_pull = jax.vjp(rms_norm, residual, ffn_again[0].astype(jnp.float32))[1]
    grad_residual_norm, grad_norm_mid = mid_pull(grad_mid)
    grad_residual = grad_y.astype(jnp.float32) + grad_residual_norm
    ffn_shards = (
        lax.psum_scatter(grad_norm_mid, "fsdp", scatter_dimension=0, tiled=True),
        lax.psum_scatter(grad_w_gate, "fsdp", scatter_dimension=0, tiled=True),
        lax.psum_scatter(grad_w_up, "fsdp", scatter_dimension=0, tiled=True),
        lax.psum_scatter(grad_w_down, "fsdp", scatter_dimension=0, tiled=True),
    )
    attn_again = attention_weights(norm_in, w_qkv, norm_heads, w_out)
    grad_branch = grad_residual.astype(jnp.bfloat16)
    grad_w_out = outer_sum(gated_out, grad_branch)
    grad_gated = back_product(grad_branch, attn_again[3])
    head_pull = jax.vjp(group_norm, attended, attn_again[2].astype(jnp.float32))[1]
    grad_attended, grad_norm_heads = head_pull(grad_gated)
    grad_att_pairs = (
        grad_attended.astype(jnp.bfloat16)
        .reshape(length, pair_count, 2, head_size)
        .transpose(1, 2, 0, 3)
    )

    def pair_backward(pieces):
        queries, key_rows, value_rows, kern_pair, mix_pair, log_total, grad_output = pieces
        masked, logits = pair_scores(queries, key_rows, kern_pair)
        attn_probs = jnp.exp(logits - log_total)
        mixed_probs = jnp.einsum("og,gij->oij", mix_pair, attn_probs, precision=lax.Precision.HIGHEST)
        grad_wide = grad_output.astype(jnp.float32)
        grad_mixed = jnp.einsum(
            "oie,oje->oij", grad_wide, value_rows.astype(jnp.float32), precision=lax.Precision.HIGHEST
        )
        grad_values = jnp.einsum("oij,oie->oje", mixed_probs, grad_wide, precision=lax.Precision.HIGHEST)
        grad_mix = jnp.einsum("oij,gij->og", grad_mixed, attn_probs, precision=lax.Precision.HIGHEST)
        grad_probs = jnp.einsum("og,oij->gij", mix_pair, grad_mixed, precision=lax.Precision.HIGHEST)
        grad_logits = attn_probs * (
            grad_probs - jnp.sum(attn_probs * grad_probs, axis=-1, keepdims=True)
        )
        grad_conv = jnp.where(allowed, grad_logits, 0.0)
        grad_masked, grad_kern = convolve_back(grad_conv, masked, kern_pair)
        grad_raw = jnp.where(allowed, grad_masked, 0.0)
        grad_query = (
            jnp.einsum("gij,gje->gie", grad_raw, key_rows.astype(jnp.float32), precision=lax.Precision.HIGHEST)
            * score_scale
        )
        grad_key = (
            jnp.einsum("gij,gie->gje", grad_raw, queries.astype(jnp.float32), precision=lax.Precision.HIGHEST)
            * score_scale
        )
        return (
            grad_query.astype(jnp.bfloat16),
            grad_key.astype(jnp.bfloat16),
            grad_values.astype(jnp.bfloat16),
            grad_kern,
            grad_mix,
        )

    grads_query, grads_key, grads_value, grad_kern_pairs, grad_mix_pairs = lax.map(
        pair_backward,
        (
            split_qkv[0],
            split_qkv[1],
            split_qkv[2],
            kern_pairs,
            mix_pairs,
            log_totals,
            grad_att_pairs,
        ),
    )
    grad_qkv = (
        jnp.stack([grads_query, grads_key, grads_value])
        .transpose(3, 0, 1, 2, 4)
        .reshape(length, 3 * model_width)
    )
    grad_w_qkv = outer_sum(normed, grad_qkv)
    grad_normed = back_product(grad_qkv, attn_again[1])
    in_pull = jax.vjp(rms_norm, inputs, attn_again[0].astype(jnp.float32))[1]
    grad_inputs_norm, grad_norm_in = in_pull(grad_normed)
    grad_tokens = (grad_residual + grad_inputs_norm)[None]
    small_sums = lax.psum(
        (grad_kern_pairs.reshape(kernel.shape), grad_mix_pairs.reshape(mixing.shape)),
        ("rep", "fsdp"),
    )
    attn_shards = (
        lax.psum_scatter(grad_norm_in, "fsdp", scatter_dimension=0, tiled=True),
        lax.psum_scatter(grad_w_qkv, "fsdp", scatter_dimension=0, tiled=True),
        lax.psum_scatter(grad_norm_heads, "fsdp", scatter_dimension=0, tiled=True),
        lax.psum_scatter(grad_w_out, "fsdp", scatter_dimension=0, tiled=True),
    )
    summed = (
        lax.psum(ffn_shards[0].astype(jnp.bfloat16), "rep").astype(jnp.float32),
        lax.psum(ffn_shards[1].astype(jnp.bfloat16), "rep").astype(jnp.float32),
        lax.psum(ffn_shards[2].astype(jnp.bfloat16), "rep").astype(jnp.float32),
        lax.psum(ffn_shards[3].astype(jnp.bfloat16), "rep").astype(jnp.float32),
        lax.psum(attn_shards[0].astype(jnp.bfloat16), "rep").astype(jnp.float32),
        lax.psum(attn_shards[1].astype(jnp.bfloat16), "rep").astype(jnp.float32),
        lax.psum(attn_shards[2].astype(jnp.bfloat16), "rep").astype(jnp.float32),
        lax.psum(attn_shards[3].astype(jnp.bfloat16), "rep").astype(jnp.float32),
    )
    return (
        layer_out,
        grad_tokens,
        summed[4],
        summed[5],
        small_sums[0],
        small_sums[1],
        summed[6],
        summed[7],
        summed[0],
        summed[1],
        summed[2],
        summed[3],
    )


def forward_kernel(cfg, *refs):
    (tok, ct, w_qkv, w_gate, w_up, w_down, w_o, gain_cols, docs, pads, kern, mix,
     tok_all, ct_all, a_all, b_all, d_all, o_all, nrm_all, qkv_all, p_all, m_all, gated_all, mid_all, resid, gains, ends,
     wq_v, w_a, w_b, meta,
     x_v, wa_v, wo_v, t_v, cat_v, shift_v, qkv_v, p_v, m_v, gated_v, meta_v, mid_v, tok_v,
     out_v, red, diag, near, rs_send, rs_recv,
     g_send, g_recv, g_loc, a_send, a_recv, ch_send, ch_recv, o_send, o_recv, meta_send, meta_recv, meet_sems, loc, pack, row_in, row_out) = refs
    planes, dh, taps_q, taps_k = cfg["planes"], cfg["dh"], cfg["kq"], cfg["kk"]
    length, width = tok.shape
    per_pair = o_all.shape[0]
    scale = dh ** (-0.5)
    ff, chunk = cfg["ff"], cfg["ff"] // planes
    me = Place(planes)

    wq_in = pltpu.make_async_copy(w_qkv, wq_v, loc.at[1])
    wq_in.start()
    tok_in = pltpu.make_async_copy(tok, tok_v, loc.at[0])
    tok_in.start()
    down_in = pltpu.make_async_copy(w_down.at[pl.ds(me.y * chunk, chunk)], d_all.at[me.g], loc.at[3])
    down_in.start()

    def columns(j, s, z):
        at = pl.multiple_of(z * (2 * PLANE * chunk) + s * (2 * chunk) + me.y * chunk, 128)
        src = (w_gate, w_up)[j].at[:, pl.ds(at, chunk)]
        return pltpu.make_async_copy(src, w_b.at[s, :, pl.ds(j * ff + z * chunk, chunk)], pack.at[j, s, z])

    for j in range(2):
        for s in range(PLANE):
            for z in range(planes):
                columns(j, s, z).start()

    places = lanes(8, length).astype(F32)
    last = length * 1.0
    reach = [docs[0, 0]]
    for k in range(1, docs.shape[1]):
        reach.append(reach[-1] + docs[0, k])
    own_end = jnp.full((8, length), last, F32)
    for end in reversed(reach):
        own_end = jnp.where(places < end.astype(F32), end.astype(F32), own_end)
    meta[...] = jnp.where(places < last - pads[0].astype(F32), own_end, places + 1.0)

    wq_in.wait()
    low = lanes(w_qkv.shape[0], 128) < 64
    for s in range(PLANE):
        base = (me.y if s % 2 == 0 else planes - 1 - me.y) * (4 * dh)

        def part(j):
            blk = wq_v[:, pl.ds(pl.multiple_of(j * width + base, 128), 4 * dh)].astype(F32)
            t0, t1, t2 = blk[:, 0:128], blk[:, 128:256], blk[:, 256:384]
            if s // 2 == 0:
                return t0, t1
            t1, t2 = pltpu.roll(t1, 64, 1), pltpu.roll(t2, 64, 1)
            return jnp.where(low, t1, t2), t2

        (q0, q1), (k0, k1), (v0, v1) = part(0), part(1), part(2)
        tiles = (
            q0,
            jnp.where(low, q1, pltpu.roll(v1, 64, 1)),
            k0,
            jnp.where(low, k1, pltpu.roll(gain_cols[...], 64, 1)),
            v0,
        )
        for i, t in enumerate(tiles):
            w_a[s, :, i * 128 : (i + 1) * 128] = t.astype(BF16)

    me.greet()

    def first(src, dst_all, base):
        cps = []
        for d in range(1, PLANE):
            s = lax.rem(me.s + d, PLANE)
            cp = remote(src.at[s], dst_all.at[me.f], a_send.at[base + d], a_recv.at[base + d], (me.y, me.g * PLANE + s))
            cp.start()
            cps.append(cp)
        own = pltpu.make_async_copy(src.at[me.s], dst_all.at[me.f], a_send.at[base])
        own.start()
        return cps, own

    def first_wait(src, dst_all, base, own):
        for d in range(1, PLANE):
            s = lax.rem(me.s - d + PLANE, PLANE)
            blk = dst_all.at[me.g * PLANE + s]
            remote(blk, blk, a_send.at[base + d], a_recv.at[base + d], me.sib).wait_recv()
        own.wait()

    meta_sent = []
    for d in range(1, GROUP):
        to = lax.rem(me.slot + d, GROUP)
        cp = remote(
            meta, meta_v.at[me.slot], meta_send.at[d], meta_recv.at[d],
            (lax.div(to, PLANE), me.g * PLANE + lax.rem(to, PLANE)),
        )
        cp.start()
        meta_sent.append(cp)
    meta_here = pltpu.make_async_copy(meta, meta_v.at[me.slot], meta_send.at[0])
    meta_here.start()
    sent_a, own_a = first(w_a, a_all, 0)
    tokens = Gather(me, tok, tok_all, g_send.at[0], g_recv.at[0], g_loc.at[0])
    tokens.start()

    o_y = jnp.where((me.g == 1) | (me.g == 2), 1, 0)
    o_c = jnp.where(me.g >= 2, 1, 0)
    o_here = pltpu.make_async_copy(w_o, o_all.at[me.c], o_send.at[0])
    o_sib = remote(w_o, o_all.at[me.c], o_send.at[0], o_recv.at[0], me.sib)

    @pl.when((o_y == me.y) & (o_c == me.c))
    def _():
        o_here.start()

    @pl.when((o_y == me.y) & (o_c != me.c))
    def _():
        o_sib.start()

    def o_next(way):
        return remote(o_all, o_all, o_send.at[1 + way], o_recv.at[1], me.plane_dev(me.g + 1 - 2 * way))

    def o_each(act):
        @pl.when((me.g >= me.home) & (me.g + 1 < planes))
        def _():
            act(o_next(0))

        @pl.when((me.g <= me.home) & (me.g >= 1))
        def _():
            act(o_next(1))

    apart = jnp.where(me.g > me.home, me.g - me.home, me.home - me.g)
    inner = (me.g == 1) | (me.g == 2)

    def o_from_home():
        o_here.wait()
        remote(o_all.at[1 - me.c], o_all.at[1 - me.c], o_send.at[0], o_recv.at[0], me.sib).wait_recv()
        o_each(lambda cp: cp.start())

    def o_pass_on():
        o_next(0).wait_recv()
        o_each(lambda cp: cp.start())

    blocks4 = lambda ref: (lambda b: ref.at[pl.ds(b * PLANE, PLANE)])
    spread_a = Spread(me, blocks4(a_all), ch_send.at[0], ch_recv.at[0])
    spread_b = Spread(me, blocks4(b_all), ch_send.at[1], ch_recv.at[1])
    spread_d = Spread(me, lambda b: d_all.at[b], ch_send.at[2], ch_recv.at[2])

    for g in range(2):
        for a in range(taps_q):
            t = band(kern, 2 * me.pair + g, a, taps_q, taps_k, length, False)
            high = t.astype(BF16)
            at = slice(a * length, (a + 1) * length)
            t_v[g, 0:length, at] = high
            t_v[g, length : 2 * length, at] = high
            t_v[g, 2 * length :, at] = (t - high.astype(F32)).astype(BF16)
    shift_v[0:8] = jnp.zeros((8, taps_q * length), F32)
    wo_v[...] = jnp.zeros(wo_v.shape, BF16)

    pl.when((apart == 0) & jnp.logical_not(inner))(o_from_home)
    first_wait(w_a, a_all, 0, own_a)
    spread_a.near()
    pl.when((apart == 0) & inner)(o_from_home)
    pl.when((apart == 1) & inner & (me.y == 0))(o_pass_on)

    tokens.relay()
    for j in range(2):
        for s in range(PLANE):
            for z in range(planes):
                columns(j, s, z).wait()
    sent_b, own_b = first(w_b, b_all, PLANE)
    cots = Gather(me, ct, ct_all, g_send.at[1], g_recv.at[1], g_loc.at[1])
    cots.start()
    spread_a.settle()
    meet(me, meet_sems.at[0])
    spread_a.rest()

    down_in.wait()

    tokens.share()
    tokens.last()
    tokens.finish()
    for row in range(GROUP):
        pltpu.make_async_copy(tok_all.at[row], x_v.at[row], row_in.at[row]).start()
    first_wait(w_b, b_all, PLANE, own_b)

    spread_a.arrive()
    wa_in = pltpu.make_async_copy(a_all, wa_v, loc.at[1])
    wa_in.start()
    pl.when((apart > 0) & inner & ((apart == 2) | (me.y == 1)))(o_pass_on)
    spread_d.near()
    spread_b.near()
    wa_in.wait()
    for d in range(1, GROUP):
        fr = lax.rem(me.slot - d + GROUP, GROUP)
        remote(meta, meta_v.at[fr], meta_send.at[d], meta_recv.at[d], me.sib).wait_recv()
    meta_here.wait()
    ends[...] = meta_v[...]

    gain_rows = jnp.transpose(wa_v[:, :, 384:512].reshape(width, 128).astype(F32))
    gains[...] = jnp.zeros(gains.shape, F32)
    gains[0:1] = gain_rows[64:65]
    gains[1:2] = gain_rows[65:66]
    heads_at = wa_v[pl.ds(me.pair * per_pair, per_pair), :, 384:512].reshape(2 * dh, 128).astype(F32)
    heads_at = jnp.concatenate([heads_at, jnp.zeros((SIDE - 2 * dh, 128), F32)], axis=0)
    gains[2:3, 0:SIDE] = jnp.transpose(heads_at)[66:67]

    h0, h1 = head_lanes(length, dh)
    scatter = Scatter(me, out_v, red, diag, near, rs_send, rs_recv)

    def attention(i):
        row, k = order(me, i)
        pltpu.make_async_copy(tok_all.at[row], x_v.at[row], row_in.at[row]).wait()

        def norm(at):
            x = x_v[row, at].astype(F32)
            s = lax.rsqrt(jnp.mean(x * x, axis=-1, keepdims=True) + 1e-6)
            x_v[row, at] = (x * s * gains[0:1]).astype(BF16)

        strips(length, norm)
        pltpu.make_async_copy(x_v.at[row], nrm_all.at[row], row_out.at[0, row]).start()
        acc = nn(x_v[row], wa_v[...].reshape(width, QKV))
        at = lanes(length, 128)
        q = jnp.where(h0 | h1, acc[:, 0:SIDE], 0.0)
        kk = jnp.where(h0 | h1, acc[:, SIDE : 2 * SIDE], 0.0)
        tail = jnp.where(at < 64, pltpu.roll(acc[:, 128:256], 64, 1), 0.0)
        v = jnp.concatenate([acc[:, 2 * SIDE : QKV], tail], axis=1)
        q, kk, v = q.astype(BF16), kk.astype(BF16), v.astype(BF16)
        qkv_v[row, :, 0:SIDE] = q
        qkv_v[row, :, SIDE : 2 * SIDE] = kk
        qkv_v[row, :, 2 * SIDE : 3 * SIDE] = v
        pltpu.make_async_copy(qkv_v.at[row], qkv_all.at[row], row_out.at[1, row]).start()
        ok = allowed_mask(length, meta_v[row, 0:1, :])
        attended = jnp.zeros((length, SIDE), F32)
        for g in range(2):
            kg = jnp.where(h0 if g == 0 else h1, kk.astype(F32), 0.0).astype(BF16)
            raw = nt(q, kg) * scale
            masked = jnp.where(ok, raw, 0.0)
            m_v[row, g] = masked.astype(BF16)
            high = masked.astype(BF16)
            cat_v[:, 0:length] = high
            cat_v[:, length : 2 * length] = (masked - high.astype(F32)).astype(BF16)
            cat_v[:, 2 * length :] = high
            shift_v[8 : 8 + length] = nn(cat_v[...], t_v[g])
            conv = shift_v[8 : 8 + length, 0:length]
            for a in range(1, taps_q):
                conv = conv + shift_v[8 - a : 8 - a + length, a * length : (a + 1) * length]
            logits = jnp.where(ok, conv, NEG_FILL)
            e = jnp.exp(logits - jnp.max(logits, axis=-1, keepdims=True))
            probs = e / jnp.sum(e, axis=-1, keepdims=True)
            high = probs.astype(BF16)
            low = (probs - high.astype(F32)).astype(BF16)
            p_v[row, g, 0] = high
            p_v[row, g, 1] = low
            attended = attended + (nn(high, v) + nn(low, v)) * mix_lanes(mix, me.pair, g, dh)
        pltpu.make_async_copy(m_v.at[row], m_all.at[row], row_out.at[2, row]).start()
        pltpu.make_async_copy(p_v.at[row], p_all.at[row], row_out.at[3, row]).start()
        centred = attended - head_stats(attended, dh, h0, h1)
        centred = jnp.where(h0 | h1, centred, 0.0)
        scaled = centred * lax.rsqrt(head_stats(centred * centred, dh, h0, h1) + 1e-5)
        gated = (scaled * gains[2:3, 0:SIDE]).astype(BF16)
        gated_v[row] = gated
        pltpu.make_async_copy(gated_v.at[row], gated_all.at[row], row_out.at[4, row]).start()
        wo = wo_v[...].reshape(wo_v.shape[0] * wo_v.shape[1], width)

    wo_in = pltpu.make_async_copy(o_all, wo_v.at[pl.ds(0, per_pair)], loc.at[2])

    def project(i):
        row, k = order(me, i)
        wo = wo_v[...].reshape(wo_v.shape[0] * wo_v.shape[1], width)
        part = nn(gated_v[row], wo[0:SIDE])

        @pl.when(lax.rem(i, 2) == 0)
        def _():
            scatter.put_sib(k, part)

        @pl.when(lax.rem(i, 2) == 1)
        def _():
            scatter.put_self(k, part)

        scatter.push(i)

    def one(i, carry):
        attention(i)

        @pl.when(i == LAG)
        def _():
            wo_in.wait()

            def late(j, carry):
                project(j)
                return carry

            lax.fori_loop(0, LAG, late, 0)

        @pl.when(i >= LAG)
        def _():
            project(i)

        @pl.when(i == 1)
        def _():
            cots.relay()

            @pl.when((apart > 0) & jnp.logical_not(inner))
            def _():
                o_next(0).wait_recv()

            wo_in.start()

        @pl.when(i == 4)
        def _():
            spread_d.settle()
            spread_b.settle()
            meet(me, meet_sems.at[1])
            spread_d.rest()
            spread_b.rest()

        @pl.when(i == 5)
        def _():
            cots.share()
            cots.last()

        return carry

    lax.fori_loop(0, GROUP, one, 0)
    tok_in.wait()
    scatter.arrive()

    def middle(at):
        res = tok_v[at].astype(F32) + scatter.total(at)
        resid[at] = res
        s = lax.rsqrt(jnp.mean(res * res, axis=-1, keepdims=True) + 1e-6)
        mid_v[at] = (res * s * gains[1:2]).astype(BF16)

    strips(length, middle)
    mids = Gather(me, mid_v, mid_all, g_send.at[2], g_recv.at[2], g_loc.at[2])
    mids.start()
    mids.relay()
    mids.share()
    mids.last()
    mids.finish()
    cots.finish()
    spread_d.arrive()
    spread_b.arrive()
    scatter.finish_cores()
    scatter.finish_chips()
    for sp in (spread_a, spread_b, spread_d):
        sp.finish()
    o_each(lambda cp: cp.wait_send())

    @pl.when((o_y == me.y) & (o_c != me.c))
    def _():
        o_sib.wait_send()

    for cp in meta_sent + sent_a + sent_b:
        cp.wait_send()
    for r in range(GROUP):
        pltpu.make_async_copy(x_v.at[r], nrm_all.at[r], row_out.at[0, r]).wait()
        pltpu.make_async_copy(qkv_v.at[r], qkv_all.at[r], row_out.at[1, r]).wait()
        pltpu.make_async_copy(m_v.at[r], m_all.at[r], row_out.at[2, r]).wait()
        pltpu.make_async_copy(p_v.at[r], p_all.at[r], row_out.at[3, r]).wait()
        pltpu.make_async_copy(gated_v.at[r], gated_all.at[r], row_out.at[4, r]).wait()


def forward_call(cfg, tok, ct, w_qkv, w_gate, w_up, w_down, w_o, gain_cols, docs, pads, kern, mix):
    length, width = tok.shape
    planes, ff, r = cfg["planes"], cfg["ff"], w_qkv.shape[0]
    n = planes * PLANE
    chunk = ff // planes
    per_pair = n // GROUP
    taps = cfg["kq"] * length
    pad_rows = -(-SIDE // w_o.shape[0])
    hbm, vmem, smem = pl.BlockSpec(memory_space=pl.ANY), pl.BlockSpec(memory_space=pltpu.VMEM), pl.BlockSpec(memory_space=pltpu.SMEM)
    sds = jax.ShapeDtypeStruct
    rows = (GROUP, length)
    dma = pltpu.SemaphoreType.DMA
    v16 = lambda *shape: pltpu.VMEM(shape, BF16)
    v32 = lambda *shape: pltpu.VMEM(shape, F32)
    return pl.pallas_call(
        functools.partial(forward_kernel, cfg),
        out_shape=(
            sds(rows + (width,), BF16), sds(rows + (width,), BF16),
            sds((n, r, QKV), BF16), sds((n, r, 2 * ff), BF16), sds((planes, chunk, width), BF16),
            sds((per_pair,) + w_o.shape, BF16), sds(rows + (width,), BF16), sds(rows + (3 * SIDE,), BF16),
            sds((GROUP, 2, 2, length, length), BF16), sds((GROUP, 2, length, length), BF16), sds(rows + (SIDE,), BF16),
            sds(rows + (width,), BF16), sds((length, width), F32), sds((8, width), F32), sds((GROUP, 8, length), F32),
        ),
        in_specs=[hbm] * 7 + [vmem] + [smem] * 4,
        out_specs=(hbm,) * 12 + (vmem,) * 3,
        scratch_shapes=[
            v16(*w_qkv.shape), v16(PLANE, r, QKV), v16(PLANE, r, 2 * ff), v32(8, length),
            v16(*rows, width), v16(n, r, QKV), v16(pad_rows, *w_o.shape),
            v16(2, 3 * length, taps), v16(length, 3 * length), v32(length + 8, taps),
            v16(*rows, 3 * SIDE), v16(GROUP, 2, 2, length, length), v16(GROUP, 2, length, length), v16(*rows, SIDE),
            v32(GROUP, 8, length), v16(length, width), v16(length, width),
            *Scatter.scratch(length, width),
            dma((3, Gather.SENDS)), dma((3, Gather.RECVS)), dma((3,)), dma((2 * PLANE,)), dma((2 * PLANE,)),
            dma((3, planes)), dma((3, planes)), dma((3,)), dma((2,)), dma((GROUP,)), dma((GROUP,)), pltpu.SemaphoreType.REGULAR((2,)),
            dma((4,)), dma((2, PLANE, planes)), dma((GROUP,)), dma((5, GROUP)),
        ],
        compiler_params=pltpu.CompilerParams(collective_id=1, has_side_effects=True, vmem_limit_bytes=52 * 2**20),
        name="attention_forward",
    )(tok, ct, w_qkv, w_gate, w_up, w_down, w_o, gain_cols, docs, pads, kern, mix)


def feed_kernel(cfg, *refs):
    (mid_all, ct_all, w_b, w_d, resid, gains,
     g_res, branch_all, dw_b, sum_d, sum_first, out_red, g_mid_gain,
     mid_v, ct_v, wb_v, wd_v, hid_v, gu_v, tile_v, dd_v, zd_v, via_v, sd_v, first_v, zf_v, via_f, sf_v,
     o_out, o_red, o_send, o_recv,
     m_out, m_red, m_diag, m_near, m_send, m_recv,
     g_send, g_recv, g_loc, z_send, z_recv, loc, row_in, out_sem) = refs
    length, width = resid.shape
    ff = cfg["ff"]
    me = Place(cfg["planes"])
    wb_in = pltpu.make_async_copy(w_b, wb_v, loc.at[0])
    wb_in.start()
    wd_in = pltpu.make_async_copy(w_d, wd_v, loc.at[1])
    wd_in.start()

    def row_copies(row):
        return (
            pltpu.make_async_copy(mid_all.at[row], mid_v.at[row], row_in.at[0, row]),
            pltpu.make_async_copy(ct_all.at[row], ct_v.at[row], row_in.at[1, row]),
        )

    for i in range(GROUP):
        for cp in row_copies(order(me, i)[0]):
            cp.start()
    me.greet()
    sum_out = Scatter(me, o_out, o_red, None, None, o_send, o_recv)
    down_sum = Collect(me, lambda b: dd_v.at[pl.ds(b, 1)], zd_v, via_v, z_send.at[0], z_recv.at[0])
    down_sum.clear()
    first_sum = Collect(me, lambda b: first_v.at[pl.ds(b, 1)], zf_v, via_f, z_send.at[1], z_recv.at[1])
    first_sum.clear()
    sum_mid = Scatter(me, m_out, m_red, m_diag, m_near, m_send, m_recv)
    wb_in.wait()
    wd_in.wait()

    def one(i, carry):
        row, k = order(me, i)
        for cp in row_copies(row):
            cp.wait()
        wb = wb_v[...].reshape(width, 2 * ff)
        wd = wd_v[...].reshape(ff, width)
        pre = nn(mid_v[row], wb)
        gate, up = pre[:, :ff], pre[:, ff:]
        g_hidden = nt(ct_v[row], wd)
        sig = jax.nn.sigmoid(gate)
        silu = gate * sig
        hidden = (silu * up).astype(BF16)
        hid_v[row] = hidden
        g_gate = (g_hidden * up * sig * (1.0 + gate * (1.0 - sig))).astype(BF16)
        g_up = (g_hidden * silu).astype(BF16)
        gu_v[row, :, :ff] = g_gate
        gu_v[row, :, ff:] = g_up
        mid_part = nt(gu_v[row], wb)
        out_part = nn(hidden, wd)

        @pl.when(lax.rem(i, 2) == 0)
        def _():
            sum_mid.put_sib(k, mid_part)
            sum_out.put_sib(k, out_part)

        @pl.when(lax.rem(i, 2) == 1)
        def _():
            sum_mid.put_self(k, mid_part)
            sum_out.put_self(k, out_part)

        sum_mid.push(i)
        return carry

    lax.fori_loop(0, GROUP, one, 0)

    tokens = GROUP * length
    tile = SIDE

    def down(i, carry):
        at = pl.ds(pl.multiple_of(i * tile, tile), tile)
        value = tn(hid_v[:, :, at].reshape(tokens, tile), ct_v[...].reshape(tokens, width)).astype(BF16)
        per = tile // dd_v.shape[1]
        dd_v[pl.ds(i * per, per)] = value.reshape((per,) + dd_v.shape[1:])
        return carry

    lax.fori_loop(0, ff // tile, down, 0)
    down_sum.start()

    g_mid_gain[...] = jnp.zeros(g_mid_gain.shape, F32)
    sum_mid.arrive()

    def middle(at):
        g_mid = sum_mid.total(at)
        res = resid[at]
        s = lax.rsqrt(jnp.mean(res * res, axis=-1, keepdims=True) + 1e-6)
        g_mid_gain[0:1] = g_mid_gain[0:1] + jnp.sum(g_mid * res * s, axis=0, keepdims=True)
        pulled = g_mid * gains[1:2]
        back = ct_v[me.slot, at].astype(F32) + s * pulled
        back = back - res * (s * s * s * jnp.mean(pulled * res, axis=-1, keepdims=True))
        g_res[at] = back
        ct_v[me.slot, at] = back.astype(BF16)

    strips(length, middle)
    branch = Gather(me, ct_v.at[me.slot], branch_all, g_send, g_recv, g_loc.at[0])
    branch.start()
    red_out = pltpu.make_async_copy(o_red, out_red, out_sem.at[2])
    red_out.start()

    steps = width // tile

    def tile_out(i):
        slot = lax.rem(i, 2)
        at = pl.ds(pl.multiple_of(i * tile, tile), tile)
        return pltpu.make_async_copy(tile_v.at[slot], dw_b.at[at], out_sem.at[slot])

    def gate_up(i, carry):
        @pl.when(i >= 2)
        def _():
            tile_out(i - 2).wait()

        at = pl.ds(pl.multiple_of(i * tile, tile), tile)
        value = tn(mid_v[:, :, at].reshape(tokens, tile), gu_v[...].reshape(tokens, 2 * ff)).astype(BF16)
        tile_v[lax.rem(i, 2)] = value
        tile_out(i).start()
        for z in range(first_v.shape[0]):
            lo = z * PLANE * first_v.shape[1]

            @pl.when(i == lo // tile)
            def _():
                first_v[z] = value[lo % tile : lo % tile + first_v.shape[1]]

        return carry

    lax.fori_loop(0, steps, gate_up, 0)
    first_sum.start()
    down_sum.combine(lambda t: dd_v.at[pl.ds(t, 1)])
    branch.relay()
    branch.share()
    first_sum.combine(lambda t: first_v.at[pl.ds(t, 1)])
    branch.last()
    down_sum.total(sd_v, dd_v.at[pl.ds(me.g, 1)])
    sd_out = pltpu.make_async_copy(sd_v.at[0], sum_d, out_sem.at[3])
    sd_out.start()
    first_sum.total(sf_v, first_v.at[pl.ds(me.g, 1)])
    sf_out = pltpu.make_async_copy(sf_v.at[0], sum_first, out_sem.at[4])
    sf_out.start()
    branch.finish()
    sum_mid.finish_cores()
    sum_mid.finish_chips()
    sum_out.finish_cores()
    down_sum.finish()
    first_sum.finish()
    tile_out(steps - 2).wait()
    tile_out(steps - 1).wait()
    red_out.wait()
    sd_out.wait()
    sf_out.wait()


def feed_call(cfg, mid_all, ct_all, w_b, w_d, resid, gains):
    length, width = resid.shape
    ff = cfg["ff"]
    hbm, vmem = pl.BlockSpec(memory_space=pl.ANY), pl.BlockSpec(memory_space=pltpu.VMEM)
    sds = jax.ShapeDtypeStruct
    dma = pltpu.SemaphoreType.DMA
    rows = (GROUP, length)
    chunk = ff // cfg["planes"]
    others = cfg["planes"] - 1
    r = w_b.shape[1]
    v16 = lambda *shape: pltpu.VMEM(shape, BF16)
    return pl.pallas_call(
        functools.partial(feed_kernel, cfg),
        out_shape=(
            sds((length, width), F32), sds(rows + (width,), BF16),
            sds((width, 2 * ff), BF16), sds((chunk, width), BF16), sds((r, 2 * ff), BF16), sds((4, length, width), BF16), sds((8, width), F32),
        ),
        in_specs=[hbm] * 4 + [vmem] * 2,
        out_specs=(vmem, hbm, hbm, hbm, hbm, hbm, vmem),
        scratch_shapes=[
            v16(*rows, width), v16(*rows, width), v16(*w_b.shape), v16(*w_d.shape), v16(*rows, ff), v16(*rows, 2 * ff),
            v16(2, SIDE, 2 * ff), v16(others + 1, chunk, width), v16(others, 1, chunk, width), v16(1, chunk, width), v16(1, chunk, width),
            v16(others + 1, r, 2 * ff), v16(others, 1, r, 2 * ff), v16(1, r, 2 * ff), v16(1, r, 2 * ff),
            *Scatter.scratch(length, width, chips=False), *Scatter.scratch(length, width),
            dma((Gather.SENDS,)), dma((Gather.RECVS,)), dma((1,)), dma((2, others + 1)), dma((2, others + 1)),
            dma((2,)), dma((2, GROUP)), dma((5,)),
        ],
        compiler_params=pltpu.CompilerParams(collective_id=2, has_side_effects=True, vmem_limit_bytes=52 * 2**20),
        name="feed_forward",
    )(mid_all, ct_all, w_b, w_d, resid, gains)


def backward_kernel(cfg, *refs):
    (branch_all, o_all, a_all, nrm_all, qkv_all, p_all, m_all, gated_all, dw_b, sum_d, sum_first, out_red, tok,
     resid, g_res, gains, ends, g_mid_gain, kern, mix,
     g_tokens, layer_out, out_a, out_b, out_d, out_o, out_small,
     gb_v, wo_v, wa_v, nrm_v, qkv_v, p_v, m_v, t_v, cat_v, shift_v, corr_v, gq_v, da_v, do_v, tok_v, rows_v, line_v, taps_v,
     zb_v, za_v, zo_v, via_b, via_a, via_o, sb_v, sa_v, so_v, far_b, strip_v, small_v, small_in,
     s_out, s_red, s_diag, s_near, rs_send, rs_recv,
     l_red, l_diag, l_near, l_send, l_recv,
     z_send, z_recv, small_send, small_recv, t_send, t_recv, loc, row_in) = refs
    planes, dh, taps_q, taps_k = cfg["planes"], cfg["dh"], cfg["kq"], cfg["kk"]
    length, width = tok.shape
    scale = dh ** (-0.5)
    me = Place(planes)
    per_pair = o_all.shape[0]
    r = a_all.shape[1]
    far = jnp.where(me.g == 1, planes - 1, 0)
    loads = [
        pltpu.make_async_copy(src, dst, loc.at[i])
        for i, (src, dst) in enumerate(
            [(a_all, wa_v), (o_all, wo_v.at[pl.ds(0, per_pair)]), (tok, tok_v)]
            + [(dw_b.at[pl.ds(me.g * PLANE + 1, PLANE - 1)], sb_v.at[pl.ds(1, PLANE - 1)]), (sum_first, sb_v.at[0])]
            + [(dw_b.at[pl.ds(far * PLANE + 1, PLANE - 1)], far_b), (out_red, l_red)]
        )
    ]

    span = PLANE * r

    def nrm_copy(j):
        at = pl.ds(j * span, span)
        return pltpu.make_async_copy(nrm_all.at[:, :, at], nrm_v.at[j % 2], loc.at[7 + j % 2])

    def row_copies(i):
        row = order(me, i)[0]
        at = lax.rem(i, SLOTS)
        cps = [pltpu.make_async_copy(branch_all.at[row], gb_v.at[row], row_in.at[0, i])]
        for j, (src, dst) in enumerate(((qkv_all, qkv_v), (p_all, p_v), (m_all, m_v))):
            cps.append(pltpu.make_async_copy(src.at[row], dst.at[at], row_in.at[j + 1, i]))
        return cps

    wo_v[...] = jnp.zeros(wo_v.shape, BF16)
    loads[1].start()
    loads[0].start()
    for i in range(SLOTS):
        for cp in row_copies(i):
            cp.start()
    for cp in loads[2:]:
        cp.start()
    for j in range(2):
        nrm_copy(j).start()
    me.greet()

    blocks4 = lambda ref: (lambda b: ref.at[pl.ds(b * PLANE, PLANE)])
    sum_b = Collect(me, lambda b: dw_b.at[pl.ds(b * PLANE + 1, PLANE - 1)], zb_v, via_b, z_send.at[0], z_recv.at[0])
    sum_a = Collect(me, blocks4(da_v), za_v, via_a, z_send.at[1], z_recv.at[1])
    sum_o = Collect(me, lambda b: do_v.at[pl.ds(b, 1)], zo_v, via_o, z_send.at[2], z_recv.at[2])
    send_s = []
    for d in range(1, planes):
        to = lax.rem(me.g + d, planes)
        send_s.append(remote(small_v, small_in.at[d - 1], small_send.at[d - 1], small_recv.at[d - 1], me.plane_dev(to)))
    sum_b.start()
    for group in (sum_b, sum_a, sum_o):
        group.clear()
    d_cp = remote(sum_d, out_d.at[me.y], t_send.at[3, 0], t_recv.at[3, 0], me.yn)
    d_cp.start()
    d_here = pltpu.make_async_copy(sum_d, out_d.at[me.y], t_send.at[3, 1])
    d_here.start()

    for g in range(2):
        for a in range(taps_q):
            t_v[g, a * length : (a + 1) * length] = band(kern, 2 * me.pair + g, a, taps_q, taps_k, length, True).astype(BF16)
    shift_v[length:] = jnp.zeros((8, length), F32)
    corr_v[...] = jnp.zeros(corr_v.shape, F32)
    rows_v[...] = jnp.zeros(rows_v.shape, F32)
    small_v[...] = jnp.zeros(small_v.shape, F32)
    h0, h1 = head_lanes(length, dh)
    scatter = Scatter(me, s_out, s_red, s_diag, s_near, rs_send, rs_recv)
    layer = Scatter(me, None, l_red, l_diag, l_near, l_send, l_recv)
    loads[0].wait()
    loads[1].wait()
    loads[5].wait()

    def one(i, carry):
        row, k = order(me, i)
        at = lax.rem(i, SLOTS)
        for cp in row_copies(i):
            cp.wait()
        wo = wo_v[...].reshape(wo_v.shape[0] * wo_v.shape[1], width)[0:SIDE]
        q, kk, v = qkv_v[at, :, 0:SIDE], qkv_v[at, :, SIDE : 2 * SIDE], qkv_v[at, :, 2 * SIDE : 3 * SIDE]
        parts = [nn(p_v[at, g, 0], v) + nn(p_v[at, g, 1], v) for g in range(2)]
        probs = [p_v[at, g, 0].astype(F32) + p_v[at, g, 1].astype(F32) for g in range(2)]
        lane_mix = [mix_lanes(mix, me.pair, g, dh) for g in range(2)]
        attended = parts[0] * lane_mix[0] + parts[1] * lane_mix[1]
        centred = jnp.where(h0 | h1, attended - head_stats(attended, dh, h0, h1), 0.0)
        inv = lax.rsqrt(head_stats(centred * centred, dh, h0, h1) + 1e-5)
        normal = centred * inv
        g_gated = nt(gb_v[row], wo)
        rows_v[0:1] = rows_v[0:1] + jnp.sum(g_gated * normal, axis=0, keepdims=True)
        u = g_gated * gains[2:3, 0:SIDE]
        g_att = inv * (u - head_stats(u, dh, h0, h1) - normal * head_stats(u * normal, dh, h0, h1))
        g_exact = jnp.where(h0 | h1, g_att, 0.0)
        g_att = g_exact.astype(BF16).astype(F32)
        ok = allowed_mask(length, ends[row, 0:1, :])
        g_q = jnp.zeros((length, SIDE), F32)
        g_k = jnp.zeros((length, SIDE), F32)
        g_v = jnp.zeros((length, SIDE), F32)
        for o in range(2):
            mixed = mix[2 * me.pair + o, 0] * probs[0] + mix[2 * me.pair + o, 1] * probs[1]
            g_v = g_v + tn(mixed.astype(BF16), jnp.where(h0 if o == 0 else h1, g_att, 0.0).astype(BF16))
        for g in range(2):
            mine = h0 if g == 0 else h1
            rows_v[1 + g : 2 + g] = rows_v[1 + g : 2 + g] + jnp.sum(g_exact * parts[g], axis=0, keepdims=True)
            g_out = (g_att * lane_mix[g]).astype(BF16)
            g_probs = nt(g_out, v)
            g_conv = probs[g] * (g_probs - jnp.sum(probs[g] * g_probs, axis=-1, keepdims=True))
            shift_v[0:length] = g_conv
            for a in range(taps_q):
                cat_v[:, a * length : (a + 1) * length] = shift_v[a : a + length].astype(BF16)
            corr_v[g] = corr_v[g] + tn(m_v[at, g], cat_v[...])
            g_raw = jnp.where(ok, nn(cat_v[...], t_v[g]), 0.0).astype(BF16)
            g_q = g_q + nn(g_raw, jnp.where(mine, kk.astype(F32), 0.0).astype(BF16))
            g_k = g_k + tn(g_raw, jnp.where(mine, q.astype(F32), 0.0).astype(BF16))
        g_q, g_k = g_q * scale, g_k * scale
        mid_tile = g_q[:, 128:256] + pltpu.roll(g_v[:, 128:256], 64, 1)
        packed = jnp.concatenate([g_q[:, 0:128], mid_tile, g_k, g_v[:, 0:128]], axis=1).astype(BF16)
        gq_v[row] = packed
        part = nt(packed, wa_v[...].reshape(width, QKV))

        @pl.when(lax.rem(i, 2) == 0)
        def _():
            scatter.put_sib(k, part)

        @pl.when(lax.rem(i, 2) == 1)
        def _():
            scatter.put_self(k, part)

        scatter.push(i)

        @pl.when(i + SLOTS < GROUP)
        def _():
            for cp in row_copies(i + SLOTS):
                cp.start()

        @pl.when(i == 5)
        def _():
            sum_b.combine(lambda t: far_b)

        return carry

    lax.fori_loop(0, GROUP, one, 0)
    for i in (2, 3, 4, 6):
        loads[i].wait()
    for i in (1, 3):
        layer.push(i)
    layer.ahead()
    gated_in = [
        pltpu.make_async_copy(gated_all.at[i], p_v.at[i // 4, i // 2 % 2, i % 2], row_in.at[0, i]) for i in range(GROUP)
    ]
    for cp in gated_in:
        cp.start()

    tokens = GROUP * length
    for j in range(planes):
        nrm_copy(j).wait()
        value = tn(nrm_v[j % 2].reshape(tokens, span), gq_v[...].reshape(tokens, QKV))
        da_v[j * PLANE : (j + 1) * PLANE] = value.astype(BF16).reshape(PLANE, r, QKV)
        if j + 2 < planes:
            nrm_copy(j + 2).start()
    sum_a.start()
    for cp in gated_in:
        cp.wait()
    value = tn(p_v[...].reshape(tokens, SIDE), gb_v[...].reshape(tokens, width))
    do_v[...] = value[0 : 2 * dh].astype(BF16).reshape(do_v.shape)

    sum_o.start()
    def taps(at, carry):
        g, a = lax.div(at, taps_q), lax.rem(at, taps_q)
        lanes_at = pl.ds(pl.multiple_of(a * length, length), length)
        e = corr_v[g, :, lanes_at]
        diff = lax.broadcasted_iota(jnp.int32, (length, length), 0) - lax.broadcasted_iota(jnp.int32, (length, length), 1)
        for b in range(taps_k):
            line = jnp.sum(jnp.where(diff == b - taps_k // 2, e, 0.0), axis=0, keepdims=True)
            taps_v[b : b + 1] = line[:, 0:128] + line[:, 128:256]
        each = jnp.sum(taps_v[...], axis=-1, keepdims=True)
        small_v[0] = jnp.where(lanes(16, 128) == at, each, small_v[0])
        return carry

    taps_v[...] = jnp.zeros(taps_v.shape, F32)
    lax.fori_loop(0, 2 * taps_q, taps, 0)
    base = 1
    at = lanes(1, SIDE)
    for o in range(2):
        for g in range(2):
            line = jnp.where((at >= o * dh) & (at < (o + 1) * dh), rows_v[1 + g : 2 + g], 0.0)
            small_v[base, 2 * o + g : 2 * o + g + 1] = line[:, 0:128] + line[:, 128:256]
    for j in range(2):
        small_v[base, 4 + j : 5 + j] = rows_v[0:1, j * 128 : (j + 1) * 128]

    scatter.arrive()

    def middle(at):
        g_normed = scatter.total(at)
        tok32 = tok_v[at].astype(F32)
        s = lax.rsqrt(jnp.mean(tok32 * tok32, axis=-1, keepdims=True) + 1e-6)
        line_v[0:1] = line_v[0:1] + jnp.sum(g_normed * tok32 * s, axis=0, keepdims=True)
        pulled = g_normed * gains[0:1]
        back = g_res[at] + s * pulled
        g_tokens[at] = back - tok32 * (s * s * s * jnp.mean(pulled * tok32, axis=-1, keepdims=True))

    line_v[...] = jnp.zeros(line_v.shape, F32)
    strips(length, middle)
    line = line_v[0:1]
    for j in range(width // 128):
        small_v[base + 1, j : j + 1] = line[:, j * 128 : (j + 1) * 128]
        small_v[base + 2, j : j + 1] = g_mid_gain[0:1, j * 128 : (j + 1) * 128]
    for cp in send_s:
        cp.start()

    def to_slot(d):
        to = lax.rem(me.slot + d, GROUP)
        return lax.div(to, PLANE), lax.rem(to, PLANE)

    def group_copies(kind, src_of, landing):
        cps = []
        for d in range(1, GROUP):
            y, sl = to_slot(d)
            cps.append(remote(src_of(sl), landing.at[me.slot], t_send.at[kind, d], t_recv.at[kind, d], (y, me.g * PLANE + sl)))
        cps.append(pltpu.make_async_copy(src_of(me.s), landing.at[me.slot], t_send.at[kind, 0]))
        for cp in cps:
            cp.start()
        return cps

    def group_wait(kind, cps, landing):
        for d in range(1, GROUP):
            fr = lax.rem(me.slot - d + GROUP, GROUP)
            remote(landing.at[fr], landing.at[fr], t_send.at[kind, d], t_recv.at[kind, d], me.sib).wait_recv()
        for cp in cps[:-1]:
            cp.wait_send()
        cps[-1].wait()

    layer.turn()
    sum_b.total(sb_v.at[pl.ds(1, PLANE - 1)], sb_v.at[pl.ds(1, PLANE - 1)])
    b_cps = group_copies(0, lambda sl: sb_v.at[sl], out_b)

    sum_a.combine(lambda t: da_v.at[pl.ds(t * PLANE, PLANE)])

    sum_o.combine(lambda t: do_v.at[pl.ds(t, 1)])
    sum_a.total(sa_v, da_v.at[pl.ds(me.g * PLANE, PLANE)])
    a_cps = group_copies(1, lambda sl: sa_v.at[sl], out_a)

    sum_o.total(so_v, do_v.at[pl.ds(me.g, 1)])
    o_to = me.pair * per_pair + lax.div(me.g, 2)
    o_half = lax.rem(me.g, 2)

    def o_copy(y):
        return remote(so_v.at[0], out_o.at[o_half], t_send.at[4, y], t_recv.at[4, o_half], (y, o_to))

    o_here = pltpu.make_async_copy(so_v.at[0], out_o.at[o_half], t_send.at[4, 2])

    def o_each(act, act_here):
        for y in range(2):
            mine = (y == me.y) & (o_to == me.f)

            @pl.when(jnp.logical_not(mine))
            def _():
                act(o_copy(y))

            @pl.when(mine)
            def _():
                act_here(o_here)

    o_each(lambda cp: cp.start(), lambda cp: cp.start())
    for cp in send_s:
        cp.wait_recv()
    for cp in send_s:
        cp.wait_send()
    small_v[...] = small_v[...] + sum(small_in[d] for d in range(planes - 1))
    small_cps = group_copies(2, lambda sl: small_v, out_small)

    layer.arrive()

    def result(at):
        cp = pltpu.make_async_copy(resid.at[at], strip_v, loc.at[0])
        cp.start()
        cp.wait()
        strip_v[...] = strip_v[...] + layer.total(at)
        cp = pltpu.make_async_copy(strip_v, layer_out.at[at], loc.at[0])
        cp.start()
        cp.wait()

    strips(length, result)

    group_wait(2, small_cps, out_small)
    d_cp.wait_send()
    remote(out_d.at[1 - me.y], out_d.at[1 - me.y], t_send.at[3, 0], t_recv.at[3, 0], me.yn).wait_recv()
    d_here.wait()
    group_wait(0, b_cps, out_b)
    src_y = jnp.where((me.g == 1) | (me.g == 2), 1, 0)
    src_s = me.x * 2 + jnp.where(me.g >= 2, 1, 0)
    for h in range(2):
        src_f = (2 * lax.rem(me.f, per_pair) + h) * PLANE + src_s

        @pl.when(jnp.logical_not((src_y == me.y) & (src_f == me.f)))
        def _():
            remote(out_o.at[h], out_o.at[h], t_send.at[4, 0], t_recv.at[4, h], me.sib).wait_recv()

    o_each(lambda cp: cp.wait_send(), lambda cp: cp.wait())
    group_wait(1, a_cps, out_a)
    for group in (sum_b, sum_a, sum_o):
        group.finish()
    scatter.finish_cores()
    scatter.finish_chips()
    layer.finish_chips()


def backward_call(cfg, *args):
    branch_all, o_all, a_all, tok = args[0], args[1], args[2], args[12]
    length, width = tok.shape
    planes, ff = cfg["planes"], cfg["ff"]
    n, r = a_all.shape[:2]
    chunk = ff // planes
    taps = cfg["kq"] * length
    pad_rows = -(-SIDE // o_all.shape[1])
    piece = 2 * cfg["dh"] // planes
    small = (4, 16, 128)
    hbm, vmem, smem = pl.BlockSpec(memory_space=pl.ANY), pl.BlockSpec(memory_space=pltpu.VMEM), pl.BlockSpec(memory_space=pltpu.SMEM)
    sds = jax.ShapeDtypeStruct
    dma = pltpu.SemaphoreType.DMA
    rows = (GROUP, length)
    others = planes - 1
    v16 = lambda *shape: pltpu.VMEM(shape, BF16)
    v32 = lambda *shape: pltpu.VMEM(shape, F32)
    b_block, a_block, o_block = (PLANE - 1, r, 2 * ff), (PLANE, r, QKV), (1, piece, width)
    return pl.pallas_call(
        functools.partial(backward_kernel, cfg),
        out_shape=(
            sds((length, width), F32), sds((length, width), F32), sds((GROUP, r, QKV), BF16), sds((GROUP, r, 2 * ff), BF16),
            sds((2, chunk, width), BF16), sds((2, piece, width), BF16), sds((GROUP,) + small, F32),
        ),
        in_specs=[hbm] * 14 + [vmem] * 4 + [smem] * 2,
        out_specs=(vmem,) + (hbm,) * 6,
        scratch_shapes=[
            v16(*rows, width), v16(pad_rows, *o_all.shape[1:]), v16(n, r, QKV), v16(2, *rows, PLANE * r), v16(SLOTS, length, 3 * SIDE),
            v16(SLOTS, 2, 2, length, length), v16(SLOTS, 2, length, length),
            v16(2, taps, length), v16(length, taps), v32(length + 8, length), v32(2, length, taps), v16(*rows, QKV),
            v16(n, r, QKV), v16(planes, piece, width), v16(length, width), v32(8, SIDE), v32(8, width), v32(16, 128),
            v16(others, *b_block), v16(others, *a_block), v16(others, *o_block), v16(*b_block), v16(*a_block), v16(*o_block),
            v16(PLANE, r, 2 * ff), v16(*a_block), v16(*o_block), v16(*b_block), v32(64, width),
            v32(*small), v32(others, *small),
            *Scatter.scratch(length, width), *Scatter.scratch(length, width, cores=False),
            dma((3, planes)), dma((3, planes)), dma((others,)), dma((others,)), dma((5, GROUP)), dma((5, GROUP)),
            dma((9,)), dma((4, GROUP)),
        ],
        compiler_params=pltpu.CompilerParams(collective_id=3, has_side_effects=True, vmem_limit_bytes=54 * 2**20),
        name="attention_backward",
    )(*args)


def results_kernel(cfg, a_ref, b_ref, d_ref, o_ref, small_ref, qkv_ref, gate_ref, up_ref, down_ref, out_ref, taps_ref, vec_ref):
    planes, ff = cfg["planes"], cfg["ff"]
    rows, width = out_ref.shape
    chunk = ff // planes
    low = lanes(rows, 128) < 64

    def slot(pair):
        home, x = pair // 2, pair % 2
        y, c = (0, 1, 1, 0)[home], (0, 0, 1, 1)[home]
        return y * PLANE + x * 2 + c

    def joined(even, odd, low):
        o0, o1 = pltpu.roll(odd[0], 64, 1), pltpu.roll(odd[1], 64, 1)
        return even[0], jnp.where(low, even[1], o0), jnp.where(low, o0, o1)

    def tiles(pair, j):
        t = lambda i: a_ref[slot(pair), :, i * 128 : (i + 1) * 128].astype(F32)
        if j == 2:
            return t(4), pltpu.roll(t(1), 64, 1)
        return t(2 * j), t(2 * j + 1)

    for j in range(3):
        for two in range(GROUP // 2):
            for i, t in enumerate(joined(tiles(2 * two, j), tiles(2 * two + 1, j), low)):
                at = j * width + two * 384 + i * 128
                qkv_ref[:, at : at + 128] = t
    for z in range(planes):
        for s in range(PLANE):
            for y in range(2):
                at = ((z * PLANE + s) * 2 + y) * chunk
                src = b_ref.at[y * PLANE + s]
                gate_ref[:, at : at + chunk] = src[:, z * chunk : (z + 1) * chunk].astype(F32)
                up_ref[:, at : at + chunk] = src[:, ff + z * chunk : ff + (z + 1) * chunk].astype(F32)
    down_ref[...] = d_ref[0].astype(F32)
    out_ref[...] = o_ref[0].astype(F32)

    @pl.when(pl.program_id(0) == 0)
    def _():
        base = 1
        for pair in range(GROUP):
            mixed = jnp.sum(small_ref[slot(pair), base], axis=-1, keepdims=True)
            taps_ref[pair] = jnp.where(lanes(16, 128) == 127, mixed, small_ref[slot(pair), 0])
        vec_ref[...] = jnp.zeros(vec_ref.shape, F32)
        for k in range(2):
            total = small_ref[0, base + 1 + k]
            for s in range(1, GROUP):
                total = total + small_ref[s, base + 1 + k]
            for j in range(width // 128):
                vec_ref[k : k + 1, j * 128 : (j + 1) * 128] = total[j : j + 1]
        line = lambda pair: tuple(small_ref[slot(pair), base, 4 + j : 5 + j] for j in range(2))
        for two in range(GROUP // 2):
            for i, t in enumerate(joined(line(2 * two), line(2 * two + 1), lanes(1, 128) < 64)):
                vec_ref[2:3, two * 384 + i * 128 : two * 384 + (i + 1) * 128] = t


def results_call(cfg, out_a, out_b, out_d, out_o, small):
    r = out_a.shape[1]
    _, chunk, width = out_d.shape
    half = r // 2
    sds = jax.ShapeDtypeStruct
    whole = lambda shape: pl.BlockSpec(shape, lambda i: (0,) * len(shape))
    rows = lambda n, w: pl.BlockSpec((n, w), lambda i: (i, 0))
    moved = 2 * (out_a.size + out_b.size + out_d.size + out_o.size) + 4 * (out_a.size + out_b.size + out_d.size + out_o.size)
    return pl.pallas_call(
        functools.partial(results_kernel, cfg),
        grid=(2,),
        out_shape=(
            sds((r, 3 * width), F32), sds((r, n_cols(cfg)), F32), sds((r, n_cols(cfg)), F32), sds((2 * chunk, width), F32),
            sds((r, width), F32), sds((GROUP, 16, 128), F32), sds((8, width), F32),
        ),
        in_specs=[
            pl.BlockSpec((GROUP, half, out_a.shape[2]), lambda i: (0, i, 0)),
            pl.BlockSpec((GROUP, half, out_b.shape[2]), lambda i: (0, i, 0)),
            pl.BlockSpec((1, chunk, width), lambda i: (i, 0, 0)),
            pl.BlockSpec((1, half, width), lambda i: (i, 0, 0)),
            whole(small.shape),
        ],
        out_specs=(
            rows(half, 3 * width), rows(half, n_cols(cfg)), rows(half, n_cols(cfg)), rows(chunk, width), rows(half, width),
            whole((GROUP, 16, 128)), whole((8, width)),
        ),
        compiler_params=pltpu.CompilerParams(vmem_limit_bytes=40 * 2**20),
        cost_estimate=pl.CostEstimate(flops=0, bytes_accessed=moved, transcendentals=0),
        name="results",
    )(out_a, out_b, out_d, out_o, small)


def n_cols(cfg):
    return cfg["ff"] * GROUP


def fits(mesh, tokens, kernel, w_gate):
    n = mesh.shape["fsdp"]
    width, length, heads, ff = tokens.shape[2], tokens.shape[1], kernel.shape[0], w_gate.shape[1]
    return (
        mesh.shape["rep"] == 2
        and n == 4 * PLANE
        and heads == 2 * GROUP
        and width == heads * 96
        and (width // n) % 32 == 0
        and ff % (2 * n * 128) == 0
        and length == SIDE
    )


def per_device_group(
    planes,
    tokens,
    doc_lengths,
    pad_counts,
    norm_in,
    w_qkv,
    kernel,
    mixing,
    norm_heads,
    w_out,
    norm_mid,
    w_gate,
    w_up,
    w_down,
    cotangent,
):
    length, width = tokens.shape[1:]
    heads, kq, kk = kernel.shape
    dh = width // heads
    n = planes * PLANE
    r = width // n
    chunk = w_down.shape[0] // 2
    ff = planes * chunk
    cfg = dict(planes=planes, dh=dh, kq=kq, kk=kk, ff=ff)
    f = lax.axis_index("fsdp")

    gain_cols = jnp.stack([norm_in, norm_mid, norm_heads], axis=1).astype(F32)
    gain_cols = jnp.pad(gain_cols, ((0, 0), (0, 125)))
    tok, ct = tokens[0], cotangent[0]
    kern = kernel.reshape(-1)

    (_, ct_all, a_all, b_all, d_all, o_all, nrm_all, qkv_all, p_all, m_all, gated_all, mid_all, resid, gains, ends) = (
        forward_call(
            cfg, tok, ct, w_qkv, w_gate, w_up, w_down, w_out, gain_cols, doc_lengths, pad_counts, kern, mixing
        )
    )
    g_res, branch_all, dw_b, sum_d, sum_first, out_red, g_mid_gain = feed_call(cfg, mid_all, ct_all, b_all, d_all, resid, gains)
    g_tokens, layer_out, out_a, out_b, out_d, out_o, small = backward_call(
        cfg, branch_all, o_all, a_all, nrm_all, qkv_all, p_all, m_all, gated_all, dw_b.reshape(n, r, 2 * ff), sum_d, sum_first, out_red,
        tok, resid, g_res, gains, ends, g_mid_gain, kern, mixing,
    )

    g_qkv, g_gate, g_up, g_down, g_out, taps, vectors = results_call(cfg, out_a, out_b, out_d, out_o, small)
    with jax.named_scope("small_results"):
        g_kernel = taps[:, :kk, : 2 * kq].transpose(0, 2, 1).reshape(heads, kq, kk)
        g_mixing = taps[:, 0:4, 127].reshape(heads, 2)
        own = lax.dynamic_slice(vectors, (0, f * r), (3, r))
        g_in, g_mid, g_heads = own[0], own[1], own[2]
    return (layer_out[None], g_tokens[None], g_in, g_qkv, g_kernel, g_mixing, g_heads, g_out, g_mid, g_gate, g_up, g_down)


def solution(mesh):
    in_specs = (
        P(("rep", "fsdp"), None, None),
        P(("rep", "fsdp"), None),
        P(("rep", "fsdp")),
        P("fsdp"),
        P("fsdp", None),
        P(),
        P(),
        P("fsdp"),
        P("fsdp", None),
        P("fsdp"),
        P("fsdp", None),
        P("fsdp", None),
        P("fsdp", None),
        P(("rep", "fsdp"), None, None),
    )
    out_specs = (
        P(("rep", "fsdp"), None, None),
        P(("rep", "fsdp"), None, None),
        P("fsdp"),
        P("fsdp", None),
        P(),
        P(),
        P("fsdp"),
        P("fsdp", None),
        P("fsdp"),
        P("fsdp", None),
        P("fsdp", None),
        P("fsdp", None),
    )

    def layer(*args):
        body = per_device
        if fits(mesh, args[0], args[5], args[10]):
            body = functools.partial(per_device_group, mesh.shape["fsdp"] // PLANE)
        return jax.shard_map(body, mesh=mesh, in_specs=in_specs, out_specs=out_specs, check_vma=False)(*args)

    return layer
```

```python
import functools

import jax
import jax.numpy as jnp
from jax import lax
from jax.experimental import pallas as pl
from jax.experimental.pallas import tpu as pltpu
from jax.sharding import PartitionSpec as P

F32 = jnp.float32
BF16 = jnp.bfloat16
NEG_FILL = -1e30
MESH = pl.DeviceIdType.MESH
PLANE = 4
GROUP = 8
SIDE = 256
SLOTS = 2
QKV = 640


class Place:
    def __init__(self, planes):
        self.planes = planes
        self.y = lax.axis_index("rep")
        self.f = lax.axis_index("fsdp")
        self.g = lax.div(self.f, PLANE)
        self.s = lax.rem(self.f, PLANE)
        self.x = lax.div(self.s, 2)
        self.c = lax.rem(self.s, 2)
        self.slot = self.y * PLANE + self.s
        self.home = self.y + self.c * (planes - 1 - 2 * self.y)
        self.pair = 2 * self.home + self.x
        self.sib = self.dev(self.y, self.x, 1 - self.c)
        self.xn = self.dev(self.y, 1 - self.x, self.c)
        self.yn = self.dev(1 - self.y, self.x, self.c)

    def dev(self, y, x, c):
        return (y, self.g * PLANE + x * 2 + c)

    def plane_dev(self, g):
        return (self.y, g * PLANE + self.s)

    def row(self, dy, dx, dc):
        y = self.y + dy - 2 * dy * self.y
        x = self.x + dx - 2 * dx * self.x
        c = self.c + dc - 2 * dc * self.c
        return y * 4 + x * 2 + c

    def greet(self):
        sem = pltpu.get_barrier_semaphore()
        n = self.planes * PLANE
        for d in range(1, n):
            pl.semaphore_signal(sem, inc=1, device_id=(self.y, lax.rem(self.f + d, n)), device_id_type=MESH)
        for s in range(PLANE):
            pl.semaphore_signal(sem, inc=1, device_id=(1 - self.y, self.g * PLANE + s), device_id_type=MESH)
        pl.semaphore_wait(sem, n - 1 + PLANE)


def meet(me, sem):
    pl.semaphore_signal(sem, inc=1, device_id=me.sib, device_id_type=MESH)
    pl.semaphore_wait(sem, 1)


def remote(src, dst, send, recv, dev):
    return pltpu.make_async_remote_copy(
        src_ref=src, dst_ref=dst, send_sem=send, recv_sem=recv, device_id=dev, device_id_type=MESH
    )


class Gather:
    SENDS = 14
    RECVS = 14

    def __init__(self, me, own, buf, send, recv, local):
        self.me, self.own, self.buf = me, own, buf
        self.send, self.recv, self.local = send, recv, local
        self.half = own.shape[0] // 2
        self.sent = []

    def _own(self, h):
        return self.own.at[pl.ds(h * self.half, self.half)]

    def _blk(self, row, h):
        return self.buf.at[row, pl.ds(h * self.half, self.half)]

    def _copy(self, i):
        own, row, h, kind, dev = self.sent[i]
        src = self._own(h) if own else self._blk(row, h)
        return remote(src, self._blk(row, h), self.send.at[i], self.recv.at[kind * 2 + h], dev)

    def _go(self, own, row, h, kind, dev):
        self.sent.append((own, row, h, kind, dev))
        self._copy(len(self.sent) - 1).start()

    def _await(self, row, h, kind):
        b = self._blk(row, h)
        remote(b, b, self.send.at[0], self.recv.at[kind * 2 + h], self.me.sib).wait_recv()

    def start(self):
        me = self.me
        self.rows = [me.row(0, 0, 1), me.row(0, 1, 0), me.row(1, 0, 0), me.row(1, 1, 0), me.row(0, 1, 1), me.row(1, 0, 1), me.row(1, 1, 1)]
        self.here = pltpu.make_async_copy(self.own, self.buf.at[me.slot], self.local)
        self.here.start()
        self._go(True, me.slot, 0, 1, me.xn)
        self._go(True, me.slot, 1, 2, me.yn)
        self._go(True, me.slot, 0, 0, me.sib)
        self._go(True, me.slot, 1, 0, me.sib)
        self._go(True, me.slot, 1, 1, me.xn)
        self._go(True, me.slot, 0, 2, me.yn)

    def relay(self):
        me, rows = self.me, self.rows
        self._await(rows[1], 0, 1)
        self._go(False, rows[1], 0, 3, me.yn)
        self._go(False, rows[1], 0, 4, me.sib)
        self._await(rows[2], 1, 2)
        self._go(False, rows[2], 1, 3, me.xn)
        self._go(False, rows[2], 1, 5, me.sib)

    def share(self):
        me, rows = self.me, self.rows
        self._await(rows[1], 1, 1)
        self._go(False, rows[1], 1, 4, me.sib)
        self._await(rows[2], 0, 2)
        self._go(False, rows[2], 0, 5, me.sib)

    def last(self):
        me, rows = self.me, self.rows
        for h in (0, 1):
            self._await(rows[3], h, 3)
            self._go(False, rows[3], h, 6, me.sib)

    def finish(self):
        for kind in (0, 4, 5, 6):
            for h in (0, 1):
                self._await(self.rows[kind], h, kind)
        for i in range(len(self.sent)):
            self._copy(i).wait_send()
        self.here.wait()


class Scatter:
    SENDS = 10
    RECVS = 10

    @staticmethod
    def scratch(rows, width, cores=True, chips=True):
        bufs = []
        if cores:
            bufs.append(pltpu.VMEM((2, rows, width), BF16))
        bufs.append(pltpu.VMEM((4, rows, width), BF16))
        if chips:
            bufs += [pltpu.VMEM((2, rows // 2, width), BF16), pltpu.VMEM((2, rows, width), BF16)]
        return bufs + [pltpu.SemaphoreType.DMA((Scatter.SENDS,)), pltpu.SemaphoreType.DMA((Scatter.RECVS,))]

    def __init__(self, me, out, red, diag, near, send, recv):
        self.me, self.out, self.red, self.diag, self.near = me, out, red, diag, near
        self.send, self.recv = send, recv
        self.half = red.shape[1] // 2

    def _sib(self, k):
        return remote(self.out.at[lax.rem(k, 2)], self.red.at[k], self.send.at[k], self.recv.at[k], self.me.sib)

    def put_sib(self, k, value):
        @pl.when(k >= 2)
        def _():
            self._sib(k - 2).wait_send()

        self.out[lax.rem(k, 2)] = value.astype(BF16)
        self._sib(k).start()

    def put_self(self, k, value):
        self._sib(k).wait_recv()
        self.red[k] = (value + self.red[k].astype(F32)).astype(BF16)

    def _copy(self, name):
        h, me = self.half, self.me
        lo, hi = pl.ds(0, h), pl.ds(h, h)
        src, dst, i, dev = {
            "da": (self.red.at[0, lo], self.diag.at[0], 4, me.xn),
            "db": (self.red.at[0, hi], self.diag.at[1], 5, me.yn),
            "xa": (self.red.at[1, lo], self.near.at[0, lo], 6, me.xn),
            "xb": (self.red.at[1, hi], self.near.at[0, hi], 7, me.xn),
            "ya": (self.red.at[2, lo], self.near.at[1, lo], 8, me.yn),
            "yb": (self.red.at[2, hi], self.near.at[1, hi], 9, me.yn),
        }[name]
        return remote(src, dst, self.send.at[i], self.recv.at[i], dev)

    def push(self, i, turn=True):
        @pl.when(i == 1)
        def _():
            self._copy("da").start()
            self._copy("db").start()

        @pl.when(i == 3)
        def _():
            self._copy("xa").start()

        @pl.when(i == 5)
        def _():
            self._copy("yb").start()
            if turn:
                self.turn()

    def ahead(self):
        self._copy("yb").start()

    def turn(self):
        h = self.half
        self._copy("db").wait_recv()
        self.red[1, h:] = (self.red[1, h:].astype(F32) + self.diag[1].astype(F32)).astype(BF16)
        self._copy("xb").start()
        self._copy("da").wait_recv()
        self.red[2, :h] = (self.red[2, :h].astype(F32) + self.diag[0].astype(F32)).astype(BF16)
        self._copy("ya").start()

    def arrive(self):
        for name in ("xa", "xb", "ya", "yb"):
            self._copy(name).wait_recv()

    def total(self, at):
        return self.red[3, at].astype(F32) + self.near[0, at].astype(F32) + self.near[1, at].astype(F32)

    def finish_cores(self):
        for k in (2, 3):
            self._sib(k).wait_send()

    def finish_chips(self):
        for name in ("da", "db", "xa", "xb", "ya", "yb"):
            self._copy(name).wait_send()


class Spread:
    def __init__(self, me, blocks, send, recv):
        self.me, self.blocks, self.send, self.recv = me, blocks, send, recv

    def _copy(self, b, t, i):
        return remote(self.blocks(b), self.blocks(b), self.send.at[i], self.recv.at[b], self.me.plane_dev(t))

    def _sends(self, b):
        last = self.me.planes - 1
        if b in (0, last):
            return [(b, 1 if b == 0 else last - 1, 0)] + [(b, t, 1) for t in sorted(range(last + 1), key=lambda t: abs(t - b))[2:]]
        other, end = (2, 0) if b == 1 else (1, 3)
        return [(b, b - 1, 0), (b, b + 1, 0), (other, end, 1)]

    def _each(self, act, steps):
        for g in range(self.me.planes):

            @pl.when(self.me.g == g)
            def _():
                for i, (b, t, step) in enumerate(self._sends(g)):
                    if step in steps:
                        act(self._copy(b, t, i))

    def near(self):
        self._each(lambda cp: cp.start(), (0,))

    def settle(self):
        inner = (self.me.g == 0) | (self.me.g == 2)

        @pl.when(inner)
        def _():
            self._copy(1, 0, 0).wait_recv()

        @pl.when(jnp.logical_not(inner))
        def _():
            self._copy(2, 0, 0).wait_recv()

    def rest(self):
        self._each(lambda cp: cp.start(), (1,))

    def arrive(self):
        for g in range(self.me.planes):

            @pl.when(self.me.g == g)
            def _():
                for b in range(self.me.planes):
                    if b not in (g, 1 if g in (0, 2) else 2):
                        self._copy(b, b, 0).wait_recv()

    def finish(self):
        self._each(lambda cp: cp.wait_send(), (0, 1))


class Collect:
    def __init__(self, me, blocks, landing, via, send, recv):
        self.me, self.blocks, self.landing, self.via, self.send, self.recv = me, blocks, landing, via, send, recv
        self.by = {(0, 3): 1, (3, 0): 2} if me.planes == 4 else {}

    def _copy(self, b, t, src, i):
        at = (b - t) % self.me.planes - 1
        return remote(src, self.landing.at[at], self.send.at[i], self.recv.at[at], self.me.plane_dev(t))

    def _plan(self, b):
        combined = [t for (s, t), by in self.by.items() if by == b]
        direct = [t for t in range(self.me.planes) if t != b and t not in combined]
        direct.sort(key=lambda t: -abs(t - b))
        return [(t, (b, t) in self.by, i) for i, t in enumerate(direct)]

    def _each(self, b, act, target=None):
        @pl.when(self.me.g == b)
        def _():
            for t, through, i in self._plan(b):
                if target not in (None, t):
                    continue
                if through:
                    z = self.me.planes
                    by = self.by[(b, t)]
                    act(remote(self.blocks(t), self.via, self.send.at[i], self.recv.at[z - 1], self.me.plane_dev(by)))
                else:
                    act(self._copy(b, t, self.blocks(t), i))

    def start(self, targets=None):
        for b in range(self.me.planes):
            self._each(b, lambda cp: cp.start(), None if targets is None else targets[b])

    def _combined(self, b, t):
        return self._copy(b, t, self.via, self.me.planes - 2)

    def combine(self, own):
        for (s, t), by in self.by.items():

            @pl.when(self.me.g == by)
            def _():
                z = self.me.planes
                remote(self.via, self.via, self.send.at[0], self.recv.at[z - 1], self.me.plane_dev(by)).wait_recv()
                for q in range(self.via.shape[0]):
                    self.via[q] = (self.via[q].astype(F32) + own(t)[q].astype(F32)).astype(BF16)
                self._combined(by, t).start()

    def clear(self):
        for s, t in self.by:

            @pl.when(self.me.g == t)
            def _():
                at = (s - t) % self.me.planes - 1
                self.landing[at] = jnp.zeros(self.landing.shape[1:], BF16)

    def total(self, out, own):
        z = self.me.planes
        for t in range(z):

            @pl.when(self.me.g == t)
            def _():
                for b in range(z):
                    if b != t and (b, t) not in self.by:
                        at = (b - t) % z - 1
                        self._copy(b, t, self.landing.at[at], 0).wait_recv()

        for q in range(out.shape[0]):
            value = own[q].astype(F32)
            for at in range(z - 1):
                value = value + self.landing[at, q].astype(F32)
            out[q] = value.astype(BF16)

    def finish(self):
        for b in range(self.me.planes):
            self._each(b, lambda cp: cp.wait_send())
        for (s, t), by in self.by.items():

            @pl.when(self.me.g == by)
            def _():
                self._combined(by, t).wait_send()


def order(me, i):
    k = lax.div(i, 2)
    dx = 1 - lax.div(k, 2)
    dy = 1 - lax.rem(k, 2)
    dc = 1 - lax.rem(i, 2)
    return me.row(dy, dx, dc), k


def strips(length, body, strip=64):
    def one(i, carry):
        body(pl.ds(pl.multiple_of(i * strip, strip), strip))
        return carry

    lax.fori_loop(0, length // strip, one, 0)


def lanes(rows, width):
    return lax.broadcasted_iota(jnp.int32, (rows, width), 1)


def nt(a, b):
    return lax.dot_general(a, b, (((1,), (1,)), ((), ())), preferred_element_type=F32)


def tn(a, b):
    return lax.dot_general(a, b, (((0,), (0,)), ((), ())), preferred_element_type=F32)


def nn(a, b):
    return jnp.dot(a, b, preferred_element_type=F32)


def head_lanes(rows, dh):
    at = lanes(rows, SIDE)
    return at < dh, (at >= dh) & (at < 2 * dh)


def allowed_mask(length, ends):
    i = lax.broadcasted_iota(jnp.int32, (length, length), 0)
    j = lax.broadcasted_iota(jnp.int32, (length, length), 1)
    return (i >= j) & (i.astype(F32) < ends)


def mix_at(mix_ref, pair, o, g):
    return mix_ref[pl.ds(2 * pair + o, 1), g : g + 1]


def mix_lanes(mix_ref, pair, g, dh):
    at = lanes(1, SIDE)
    m0, m1 = mix_at(mix_ref, pair, 0, g), mix_at(mix_ref, pair, 1, g)
    return jnp.where(at < dh, m0, jnp.where(at < 2 * dh, m1, 0.0))


def head_stats(value, dh, h0, h1):
    m0 = jnp.sum(jnp.where(h0, value, 0.0), axis=-1, keepdims=True) / dh
    m1 = jnp.sum(jnp.where(h1, value, 0.0), axis=-1, keepdims=True) / dh
    return jnp.where(h0, m0, jnp.where(h1, m1, 0.0))


def band(kern_ref, head, a, taps_q, taps_k, length, flip):
    r = lax.broadcasted_iota(jnp.int32, (length, length), 0)
    c = lax.broadcasted_iota(jnp.int32, (length, length), 1)
    diff = (c - r) if flip else (r - c)
    acc = jnp.zeros((length, length), F32)
    for b in range(taps_k):
        acc = jnp.where(diff == b - taps_k // 2, kern_ref[head, a : a + 1, b : b + 1], acc)
    return acc


def rms_norm(values_in, scaling):
    return (
        values_in
        * lax.rsqrt(jnp.mean(values_in * values_in, axis=-1, keepdims=True) + 1e-06)
        * scaling
    )


def group_norm(values_in, scaling):
    centred = values_in - jnp.mean(values_in, axis=-1, keepdims=True)
    scaled = centred * lax.rsqrt(jnp.mean(centred * centred, axis=-1, keepdims=True) + 1e-05)
    return scaled.reshape(values_in.shape[0], -1) * scaling


def convolve(scores, kernel):
    length = scores.shape[1]
    taps_query = kernel.shape[1]
    taps_key = kernel.shape[2]
    half_width = taps_key // 2
    padded = jnp.pad(scores, ((0, 0), (taps_query - 1, 0), (half_width, half_width)))
    summed = jnp.zeros_like(scores)
    for shift_q in range(taps_query):
        for shift_k in range(taps_key):
            start_q = taps_query - 1 - shift_q
            window = padded[:, start_q : start_q + length, shift_k : shift_k + length]
            summed = summed + kernel[:, shift_q, shift_k][:, None, None] * window
    return summed


def convolve_back(grad_conv, masked, kernel):
    length = masked.shape[1]
    taps_query = kernel.shape[1]
    taps_key = kernel.shape[2]
    half_width = taps_key // 2
    padded = jnp.pad(masked, ((0, 0), (taps_query - 1, 0), (half_width, half_width)))
    grad_padded = jnp.pad(grad_conv, ((0, 0), (0, taps_query - 1), (half_width, half_width)))
    grad_masked = jnp.zeros_like(masked)
    grad_taps = []
    for shift_q in range(taps_query):
        for shift_k in range(taps_key):
            start_q = taps_query - 1 - shift_q
            window = padded[:, start_q : start_q + length, shift_k : shift_k + length]
            grad_taps.append(jnp.sum(grad_conv * window, axis=(1, 2)))
            start_k = taps_key - 1 - shift_k
            back_window = grad_padded[:, shift_q : shift_q + length, start_k : start_k + length]
            grad_masked = grad_masked + kernel[:, shift_q, shift_k][:, None, None] * back_window
    grad_kern = jnp.stack(grad_taps, axis=1).reshape(kernel.shape)
    return (grad_masked, grad_kern)


def build_mask(doc_lengths, pad_count, length):
    places = jnp.arange(length, dtype=jnp.int32)
    doc_ends = jnp.cumsum(doc_lengths)
    segment = jnp.sum((places[:, None] >= doc_ends[None, :]).astype(jnp.int32), axis=1)
    live_end = length - pad_count
    same_doc = segment[:, None] == segment[None, :]
    causal = places[None, :] <= places[:, None]
    usable = (places[None, :] < live_end) | (places[None, :] == places[:, None])
    return same_doc & causal & usable


def outer_sum(left_rows, right_rows):
    return lax.dot_general(
        left_rows, right_rows, (((0,), (0,)), ((), ())), preferred_element_type=jnp.float32
    )


def back_product(grad_rows, weight_full):
    return lax.dot_general(
        grad_rows, weight_full, (((1,), (1,)), ((), ())), preferred_element_type=jnp.float32
    )


def attention_weights(norm_in, w_qkv, norm_heads, w_out):
    return (
        lax.all_gather(norm_in, "fsdp", axis=0, tiled=True),
        lax.all_gather(w_qkv, "fsdp", axis=0, tiled=True),
        lax.all_gather(norm_heads, "fsdp", axis=0, tiled=True),
        lax.all_gather(w_out, "fsdp", axis=0, tiled=True),
    )


def feed_weights(norm_mid, w_gate, w_up, w_down):
    return (
        lax.all_gather(norm_mid, "fsdp", axis=0, tiled=True),
        lax.all_gather(w_gate, "fsdp", axis=0, tiled=True),
        lax.all_gather(w_up, "fsdp", axis=0, tiled=True),
        lax.all_gather(w_down, "fsdp", axis=0, tiled=True),
    )


def per_device(
    tokens,
    doc_lengths,
    pad_counts,
    norm_in,
    w_qkv,
    kernel,
    mixing,
    norm_heads,
    w_out,
    norm_mid,
    w_gate,
    w_up,
    w_down,
    cotangent,
):
    inputs = tokens[0].astype(jnp.float32)
    length = inputs.shape[0]
    model_width = inputs.shape[1]
    head_count = kernel.shape[0]
    head_size = model_width // head_count
    pair_count = head_count // 2
    score_scale = head_size ** (-0.5)
    allowed = build_mask(doc_lengths[0], pad_counts[0], length)[None]
    kern_pairs = kernel.reshape(pair_count, 2, kernel.shape[1], kernel.shape[2])
    mix_pairs = mixing.reshape(pair_count, 2, 2)
    attn_set = attention_weights(norm_in, w_qkv, norm_heads, w_out)
    normed = rms_norm(inputs, attn_set[0].astype(jnp.float32)).astype(jnp.bfloat16)
    projected = jnp.dot(normed, attn_set[1], preferred_element_type=jnp.float32).astype(
        jnp.bfloat16
    )
    split_qkv = projected.reshape(length, 3, pair_count, 2, head_size).transpose(1, 2, 3, 0, 4)

    def pair_scores(queries, key_rows, kern_pair):
        raw_scores = (
            jnp.einsum("gie,gje->gij", queries, key_rows, preferred_element_type=jnp.float32)
            * score_scale
        )
        masked = jnp.where(allowed, raw_scores, 0.0)
        logits = jnp.where(allowed, convolve(masked, kern_pair), NEG_FILL)
        return (masked, logits)

    def pair_forward(pieces):
        queries, key_rows, value_rows, kern_pair, mix_pair = pieces
        masked, logits = pair_scores(queries, key_rows, kern_pair)
        row_peak = jnp.max(logits, axis=-1, keepdims=True)
        log_total = row_peak + jnp.log(jnp.sum(jnp.exp(logits - row_peak), axis=-1, keepdims=True))
        attn_probs = jnp.exp(logits - log_total)
        mixed_probs = jnp.einsum("og,gij->oij", mix_pair, attn_probs, precision=lax.Precision.HIGHEST)
        output = jnp.einsum(
            "oij,oje->oie", mixed_probs, value_rows.astype(jnp.float32), precision=lax.Precision.HIGHEST
        )
        return (output, log_total)

    attended_pairs, log_totals = lax.map(
        pair_forward, (split_qkv[0], split_qkv[1], split_qkv[2], kern_pairs, mix_pairs)
    )
    attended = attended_pairs.transpose(2, 0, 1, 3).reshape(length, head_count, head_size)
    gated_out = group_norm(attended, attn_set[2].astype(jnp.float32)).astype(jnp.bfloat16)
    residual = inputs + jnp.dot(gated_out, attn_set[3], preferred_element_type=jnp.float32)
    ffn_set = feed_weights(norm_mid, w_gate, w_up, w_down)
    normed_mid = rms_norm(residual, ffn_set[0].astype(jnp.float32)).astype(jnp.bfloat16)
    gate_pre = jnp.dot(normed_mid, ffn_set[1], preferred_element_type=jnp.float32)
    up_pre = jnp.dot(normed_mid, ffn_set[2], preferred_element_type=jnp.float32)
    sigmoid_gate = jax.nn.sigmoid(gate_pre)
    silu_gate = gate_pre * sigmoid_gate
    hidden = (silu_gate * up_pre).astype(jnp.bfloat16)
    layer_out = (residual + jnp.dot(hidden, ffn_set[3], preferred_element_type=jnp.float32))[None]
    ffn_again = feed_weights(norm_mid, w_gate, w_up, w_down)
    grad_y = cotangent[0]
    grad_w_down = outer_sum(hidden, grad_y)
    grad_hidden = back_product(grad_y, ffn_again[3])
    grad_gate = (
        grad_hidden * up_pre * sigmoid_gate * (1.0 + gate_pre * (1.0 - sigmoid_gate))
    ).astype(jnp.bfloat16)
    grad_up = (grad_hidden * silu_gate).astype(jnp.bfloat16)
    grad_w_gate = outer_sum(normed_mid, grad_gate)
    grad_w_up = outer_sum(normed_mid, grad_up)
    grad_mid = back_product(grad_gate, ffn_again[1]) + back_product(grad_up, ffn_again[2])
    mid_pull = jax.vjp(rms_norm, residual, ffn_again[0].astype(jnp.float32))[1]
    grad_residual_norm, grad_norm_mid = mid_pull(grad_mid)
    grad_residual = grad_y.astype(jnp.float32) + grad_residual_norm
    ffn_shards = (
        lax.psum_scatter(grad_norm_mid, "fsdp", scatter_dimension=0, tiled=True),
        lax.psum_scatter(grad_w_gate, "fsdp", scatter_dimension=0, tiled=True),
        lax.psum_scatter(grad_w_up, "fsdp", scatter_dimension=0, tiled=True),
        lax.psum_scatter(grad_w_down, "fsdp", scatter_dimension=0, tiled=True),
    )
    attn_again = attention_weights(norm_in, w_qkv, norm_heads, w_out)
    grad_branch = grad_residual.astype(jnp.bfloat16)
    grad_w_out = outer_sum(gated_out, grad_branch)
    grad_gated = back_product(grad_branch, attn_again[3])
    head_pull = jax.vjp(group_norm, attended, attn_again[2].astype(jnp.float32))[1]
    grad_attended, grad_norm_heads = head_pull(grad_gated)
    grad_att_pairs = (
        grad_attended.astype(jnp.bfloat16)
        .reshape(length, pair_count, 2, head_size)
        .transpose(1, 2, 0, 3)
    )

    def pair_backward(pieces):
        queries, key_rows, value_rows, kern_pair, mix_pair, log_total, grad_output = pieces
        masked, logits = pair_scores(queries, key_rows, kern_pair)
        attn_probs = jnp.exp(logits - log_total)
        mixed_probs = jnp.einsum("og,gij->oij", mix_pair, attn_probs, precision=lax.Precision.HIGHEST)
        grad_wide = grad_output.astype(jnp.float32)
        grad_mixed = jnp.einsum(
            "oie,oje->oij", grad_wide, value_rows.astype(jnp.float32), precision=lax.Precision.HIGHEST
        )
        grad_values = jnp.einsum("oij,oie->oje", mixed_probs, grad_wide, precision=lax.Precision.HIGHEST)
        grad_mix = jnp.einsum("oij,gij->og", grad_mixed, attn_probs, precision=lax.Precision.HIGHEST)
        grad_probs = jnp.einsum("og,oij->gij", mix_pair, grad_mixed, precision=lax.Precision.HIGHEST)
        grad_logits = attn_probs * (
            grad_probs - jnp.sum(attn_probs * grad_probs, axis=-1, keepdims=True)
        )
        grad_conv = jnp.where(allowed, grad_logits, 0.0)
        grad_masked, grad_kern = convolve_back(grad_conv, masked, kern_pair)
        grad_raw = jnp.where(allowed, grad_masked, 0.0)
        grad_query = (
            jnp.einsum("gij,gje->gie", grad_raw, key_rows.astype(jnp.float32), precision=lax.Precision.HIGHEST)
            * score_scale
        )
        grad_key = (
            jnp.einsum("gij,gie->gje", grad_raw, queries.astype(jnp.float32), precision=lax.Precision.HIGHEST)
            * score_scale
        )
        return (
            grad_query.astype(jnp.bfloat16),
            grad_key.astype(jnp.bfloat16),
            grad_values.astype(jnp.bfloat16),
            grad_kern,
            grad_mix,
        )

    grads_query, grads_key, grads_value, grad_kern_pairs, grad_mix_pairs = lax.map(
        pair_backward,
        (
            split_qkv[0],
            split_qkv[1],
            split_qkv[2],
            kern_pairs,
            mix_pairs,
            log_totals,
            grad_att_pairs,
        ),
    )
    grad_qkv = (
        jnp.stack([grads_query, grads_key, grads_value])
        .transpose(3, 0, 1, 2, 4)
        .reshape(length, 3 * model_width)
    )
    grad_w_qkv = outer_sum(normed, grad_qkv)
    grad_normed = back_product(grad_qkv, attn_again[1])
    in_pull = jax.vjp(rms_norm, inputs, attn_again[0].astype(jnp.float32))[1]
    grad_inputs_norm, grad_norm_in = in_pull(grad_normed)
    grad_tokens = (grad_residual + grad_inputs_norm)[None]
    small_sums = lax.psum(
        (grad_kern_pairs.reshape(kernel.shape), grad_mix_pairs.reshape(mixing.shape)),
        ("rep", "fsdp"),
    )
    attn_shards = (
        lax.psum_scatter(grad_norm_in, "fsdp", scatter_dimension=0, tiled=True),
        lax.psum_scatter(grad_w_qkv, "fsdp", scatter_dimension=0, tiled=True),
        lax.psum_scatter(grad_norm_heads, "fsdp", scatter_dimension=0, tiled=True),
        lax.psum_scatter(grad_w_out, "fsdp", scatter_dimension=0, tiled=True),
    )
    summed = (
        lax.psum(ffn_shards[0].astype(jnp.bfloat16), "rep").astype(jnp.float32),
        lax.psum(ffn_shards[1].astype(jnp.bfloat16), "rep").astype(jnp.float32),
        lax.psum(ffn_shards[2].astype(jnp.bfloat16), "rep").astype(jnp.float32),
        lax.psum(ffn_shards[3].astype(jnp.bfloat16), "rep").astype(jnp.float32),
        lax.psum(attn_shards[0].astype(jnp.bfloat16), "rep").astype(jnp.float32),
        lax.psum(attn_shards[1].astype(jnp.bfloat16), "rep").astype(jnp.float32),
        lax.psum(attn_shards[2].astype(jnp.bfloat16), "rep").astype(jnp.float32),
        lax.psum(attn_shards[3].astype(jnp.bfloat16), "rep").astype(jnp.float32),
    )
    return (
        layer_out,
        grad_tokens,
        summed[4],
        summed[5],
        small_sums[0],
        small_sums[1],
        summed[6],
        summed[7],
        summed[0],
        summed[1],
        summed[2],
        summed[3],
    )


def forward_kernel(cfg, *refs):
    (tok, ct, w_qkv, w_gate, w_up, w_down, w_o, kern_in, mix_in, gain_rows, docs, pads,
     tok_all, ct_all, a_all, b_all, d_all, o_all, nrm_all, qkv_all, p_all, m_all, gated_all, mid_all, resid, gains, ends,
     kern, mix, wq_v, w_a, w_b, meta, gain_v, ct_v, down_v, own_o,
     x_v, wa_v, wo_v, t_v, cat_v, shift_v, qkv_v, p_v, m_v, gated_v, meta_v, mid_v, tok_v,
     out_v, red, diag, near, rs_send, rs_recv,
     g_send, g_recv, g_loc, a_send, a_recv, ch_send, ch_recv, o_send, o_recv, meta_send, meta_recv, gain_send, gain_recv, meet_sems, loc, pack, row_in, row_out) = refs
    planes, dh, taps_q, taps_k = cfg["planes"], cfg["dh"], cfg["kq"], cfg["kk"]
    length, width = tok.shape
    per_pair = o_all.shape[0]
    scale = dh ** (-0.5)
    ff, chunk = cfg["ff"], cfg["ff"] // planes
    me = Place(planes)

    wq_in = pltpu.make_async_copy(w_qkv, wq_v, loc.at[1])
    wq_in.start()
    tok_in = pltpu.make_async_copy(tok, tok_v, loc.at[0])
    tok_in.start()
    taps_in = [pltpu.make_async_copy(kern_in, kern, loc.at[6]), pltpu.make_async_copy(mix_in, mix, loc.at[7])]
    for cp in taps_in:
        cp.start()
    o_in = pltpu.make_async_copy(w_o, own_o, loc.at[4])
    o_in.start()
    down_in = pltpu.make_async_copy(w_down.at[pl.ds(me.y * chunk, chunk)], down_v, loc.at[3])
    down_in.start()
    ct_in = pltpu.make_async_copy(ct, ct_v, loc.at[5])
    ct_in.start()

    def columns(j, s, z):
        at = pl.multiple_of(z * (2 * PLANE * chunk) + s * (2 * chunk) + me.y * chunk, 128)
        src = (w_gate, w_up)[j].at[:, pl.ds(at, chunk)]
        return pltpu.make_async_copy(src, w_b.at[s, :, pl.ds(j * ff + z * chunk, chunk)], pack.at[j, s, z])

    for j in range(2):
        for s in range(PLANE):
            for z in range(planes):
                columns(j, s, z).start()

    places = lanes(8, length).astype(F32)
    last = length * 1.0
    reach = [docs[0, 0]]
    for k in range(1, docs.shape[1]):
        reach.append(reach[-1] + docs[0, k])
    own_end = jnp.full((8, length), last, F32)
    for end in reversed(reach):
        own_end = jnp.where(places < end.astype(F32), end.astype(F32), own_end)
    meta[...] = jnp.where(places < last - pads[0].astype(F32), own_end, places + 1.0)

    wq_in.wait()
    low = lanes(w_qkv.shape[0], 128) < 64
    for s in range(PLANE):
        base = (me.y if s % 2 == 0 else planes - 1 - me.y) * (4 * dh)

        def part(j):
            blk = wq_v[:, pl.ds(pl.multiple_of(j * width + base, 128), 4 * dh)].astype(F32)
            t0, t1, t2 = blk[:, 0:128], blk[:, 128:256], blk[:, 256:384]
            if s // 2 == 0:
                return t0, t1
            t1, t2 = pltpu.roll(t1, 64, 1), pltpu.roll(t2, 64, 1)
            return jnp.where(low, t1, t2), t2

        (q0, q1), (k0, k1), (v0, v1) = part(0), part(1), part(2)
        tiles = (
            q0,
            jnp.where(low, q1, pltpu.roll(v1, 64, 1)),
            k0,
            jnp.where(low, k1, 0.0),
            v0,
        )
        for i, t in enumerate(tiles):
            w_a[s, :, i * 128 : (i + 1) * 128] = t.astype(BF16)

    down_in.wait()
    down_out = pltpu.make_async_copy(down_v, d_all.at[me.g], loc.at[3])
    down_out.start()
    o_in.wait()
    tok_in.wait()
    for cp in taps_in:
        cp.wait()
    me.greet()

    def first(src, dst_all, base):
        cps = []
        for d in range(1, PLANE):
            s = lax.rem(me.s + d, PLANE)
            cp = remote(src.at[s], dst_all.at[me.f], a_send.at[base + d], a_recv.at[base + d], (me.y, me.g * PLANE + s))
            cp.start()
            cps.append(cp)
        own = pltpu.make_async_copy(src.at[me.s], dst_all.at[me.f], a_send.at[base])
        own.start()
        return cps, own

    def first_wait(src, dst_all, base, own):
        for d in range(1, PLANE):
            s = lax.rem(me.s - d + PLANE, PLANE)
            blk = dst_all.at[me.g * PLANE + s]
            remote(blk, blk, a_send.at[base + d], a_recv.at[base + d], me.sib).wait_recv()
        own.wait()

    meta_sent = []
    for d in range(1, GROUP):
        to = lax.rem(me.slot + d, GROUP)
        cp = remote(
            meta, meta_v.at[me.slot], meta_send.at[d], meta_recv.at[d],
            (lax.div(to, PLANE), me.g * PLANE + lax.rem(to, PLANE)),
        )
        cp.start()
        meta_sent.append(cp)
    meta_here = pltpu.make_async_copy(meta, meta_v.at[me.slot], meta_send.at[0])
    meta_here.start()
    gain_here = pltpu.make_async_copy(gain_rows, gain_v.at[me.f], gain_send.at[0])
    gain_here.start()
    gain_sent = []
    for d in range(1, PLANE):
        to = lax.rem(me.s + d, PLANE)
        gain_sent.append(remote(gain_rows, gain_v.at[me.f], gain_send.at[d], gain_recv.at[d], (me.y, me.g * PLANE + to)))
        gain_sent[-1].start()
    sent_a, own_a = first(w_a, a_all, 0)
    tokens = Gather(me, tok_v, tok_all, g_send.at[0], g_recv.at[0], g_loc.at[0])
    tokens.start()

    o_y = jnp.where((me.g == 1) | (me.g == 2), 1, 0)
    o_c = jnp.where(me.g >= 2, 1, 0)
    o_here = pltpu.make_async_copy(own_o, o_all.at[me.c], o_send.at[0])
    o_sib = remote(own_o, o_all.at[me.c], o_send.at[0], o_recv.at[0], me.sib)

    @pl.when((o_y == me.y) & (o_c == me.c))
    def _():
        o_here.start()

    @pl.when((o_y == me.y) & (o_c != me.c))
    def _():
        o_sib.start()

    def o_copy(t, i):
        return remote(o_all, o_all, o_send.at[i], o_recv.at[1], me.plane_dev(t))

    o_way = ((2, 1), (2, 0), (1, 3), (1, 2))

    def o_each(act):
        for home, (first_to, then_to) in enumerate(o_way):

            @pl.when((me.g == home) & (me.home == home))
            def _():
                act(o_copy(first_to, 1))
                act(o_copy(then_to, 2))

    o_relays = ((me.home < 2) & (me.g == 2)) | ((me.home >= 2) & (me.g == 1))

    def o_from_home():
        o_here.wait()
        remote(o_all.at[1 - me.c], o_all.at[1 - me.c], o_send.at[0], o_recv.at[0], me.sib).wait_recv()

    def o_relay():
        o_copy(0, 1).wait_recv()
        o_copy(jnp.where(me.home < 2, planes - 1, 0), 1).start()

    blocks4 = lambda ref: (lambda b: ref.at[pl.ds(b * PLANE, PLANE)])
    spread_a = Spread(me, blocks4(a_all), ch_send.at[0], ch_recv.at[0])
    spread_b = Spread(me, blocks4(b_all), ch_send.at[1], ch_recv.at[1])
    spread_d = Spread(me, lambda b: d_all.at[b], ch_send.at[2], ch_recv.at[2])

    for g in range(2):
        for a in range(taps_q):
            t = band(kern, 2 * me.pair + g, a, taps_q, taps_k, length, False)
            high = t.astype(BF16)
            at = slice(a * length, (a + 1) * length)
            t_v[g, 0:length, at] = high
            t_v[g, length : 2 * length, at] = high
            t_v[g, 2 * length :, at] = (t - high.astype(F32)).astype(BF16)
    shift_v[0:8] = jnp.zeros((8, taps_q * length), F32)
    wo_v[...] = jnp.zeros(wo_v.shape, BF16)

    pl.when(me.g == me.home)(o_from_home)
    o_each(lambda cp: cp.start())
    gain_here.wait()
    for d in range(1, PLANE):
        fr = me.g * PLANE + lax.rem(me.s - d + PLANE, PLANE)
        remote(gain_rows, gain_v.at[fr], gain_send.at[d], gain_recv.at[d], me.sib).wait_recv()
    for d in range(1, planes):
        to = lax.rem(me.g + d, planes)
        part = gain_v.at[pl.ds(me.g * PLANE, PLANE)]
        gain_sent.append(remote(part, part, gain_send.at[PLANE + d], gain_recv.at[PLANE + d], me.plane_dev(to)))
        gain_sent[-1].start()
    first_wait(w_a, a_all, 0, own_a)
    spread_a.near()
    pl.when(o_relays)(o_relay)

    tokens.relay()
    for j in range(2):
        for s in range(PLANE):
            for z in range(planes):
                columns(j, s, z).wait()
    sent_b, own_b = first(w_b, b_all, PLANE)
    cots = Gather(me, ct_v, ct_all, g_send.at[1], g_recv.at[1], g_loc.at[1])
    ct_in.wait()
    cots.start()
    spread_a.settle()
    meet(me, meet_sems.at[0])
    spread_a.rest()

    down_out.wait()

    tokens.share()
    tokens.last()
    tokens.finish()
    for row in range(GROUP):
        pltpu.make_async_copy(tok_all.at[row], x_v.at[row], row_in.at[row]).start()
    first_wait(w_b, b_all, PLANE, own_b)
    for d in range(1, GROUP):
        fr = lax.rem(me.slot - d + GROUP, GROUP)
        remote(meta, meta_v.at[fr], meta_send.at[d], meta_recv.at[d], me.sib).wait_recv()
    meta_here.wait()
    ends[...] = meta_v[...]
    for d in range(1, planes):
        part = gain_v.at[pl.ds(lax.rem(me.g - d + planes, planes) * PLANE, PLANE)]
        remote(part, part, gain_send.at[PLANE + d], gain_recv.at[PLANE + d], me.sib).wait_recv()
    gains[...] = jnp.zeros(gains.shape, F32)
    lane = lanes(8, 128)
    for k in range(planes):
        v0, v1, v2, v3 = (gain_v[k * PLANE + j] for j in range(PLANE))
        v1, v2, v3 = pltpu.roll(v1, 96, 1), pltpu.roll(v2, 64, 1), pltpu.roll(v3, 32, 1)
        for j, t in enumerate((jnp.where(lane < 96, v0, v1), jnp.where(lane < 64, v1, v2), jnp.where(lane < 32, v2, v3))):
            at = k * PLANE * w_o.shape[0] + j * 128
            gains[0:2, at : at + 128] = t[0:2]
    v0, v1 = gain_v[2 * me.pair], pltpu.roll(gain_v[2 * me.pair + 1], 96, 1)
    gains[2:3, 0:128] = jnp.where(lane < 96, v0, v1)[2:3]
    gains[2:3, 128:256] = jnp.where(lane < 64, v1, 0.0)[2:3]

    def norms(i, carry):
        row, _ = order(me, i)
        pltpu.make_async_copy(tok_all.at[row], x_v.at[row], row_in.at[row]).wait()

        def norm(at):
            x = x_v[row, at].astype(F32)
            s = lax.rsqrt(jnp.mean(x * x, axis=-1, keepdims=True) + 1e-6)
            x_v[row, at] = (x * s * gains[0:1]).astype(BF16)

        strips(length, norm)
        pltpu.make_async_copy(x_v.at[row], nrm_all.at[row], row_out.at[0, row]).start()
        return carry

    lax.fori_loop(0, GROUP, norms, 0)
    spread_a.arrive()
    wa_in = pltpu.make_async_copy(a_all, wa_v, loc.at[1])
    wa_in.start()
    @pl.when((me.g != me.home) & jnp.logical_not(o_relays))
    def _():
        o_copy(0, 1).wait_recv()

    wo_in = pltpu.make_async_copy(o_all, wo_v.at[pl.ds(0, per_pair)], loc.at[2])
    wo_in.start()
    spread_d.near()
    spread_b.near()
    wa_in.wait()
    wo_in.wait()
    h0, h1 = head_lanes(length, dh)
    scatter = Scatter(me, out_v, red, diag, near, rs_send, rs_recv)

    def attention(i):
        row, k = order(me, i)
        acc = nn(x_v[row], wa_v[...].reshape(width, QKV))
        at = lanes(length, 128)
        q = jnp.where(h0 | h1, acc[:, 0:SIDE], 0.0)
        kk = jnp.where(h0 | h1, acc[:, SIDE : 2 * SIDE], 0.0)
        tail = jnp.where(at < 64, pltpu.roll(acc[:, 128:256], 64, 1), 0.0)
        v = jnp.concatenate([acc[:, 2 * SIDE : QKV], tail], axis=1)
        q, kk, v = q.astype(BF16), kk.astype(BF16), v.astype(BF16)
        qkv_v[row, :, 0:SIDE] = q
        qkv_v[row, :, SIDE : 2 * SIDE] = kk
        qkv_v[row, :, 2 * SIDE : 3 * SIDE] = v
        pltpu.make_async_copy(qkv_v.at[row], qkv_all.at[row], row_out.at[1, row]).start()
        ok = allowed_mask(length, meta_v[row, 0:1, :])
        attended = jnp.zeros((length, SIDE), F32)
        for g in range(2):
            kg = jnp.where(h0 if g == 0 else h1, kk.astype(F32), 0.0).astype(BF16)
            raw = nt(q, kg) * scale
            masked = jnp.where(ok, raw, 0.0)
            m_v[row, g] = masked.astype(BF16)
            high = masked.astype(BF16)
            cat_v[:, 0:length] = high
            cat_v[:, length : 2 * length] = (masked - high.astype(F32)).astype(BF16)
            cat_v[:, 2 * length :] = high
            shift_v[8 : 8 + length] = nn(cat_v[...], t_v[g])
            conv = shift_v[8 : 8 + length, 0:length]
            for a in range(1, taps_q):
                conv = conv + shift_v[8 - a : 8 - a + length, a * length : (a + 1) * length]
            logits = jnp.where(ok, conv, NEG_FILL)
            e = jnp.exp(logits - jnp.max(logits, axis=-1, keepdims=True))
            probs = e / jnp.sum(e, axis=-1, keepdims=True)
            high = probs.astype(BF16)
            low = (probs - high.astype(F32)).astype(BF16)
            p_v[row, g, 0] = high
            p_v[row, g, 1] = low
            attended = attended + (nn(high, v) + nn(low, v)) * mix_lanes(mix, me.pair, g, dh)
        pltpu.make_async_copy(m_v.at[row], m_all.at[row], row_out.at[2, row]).start()
        pltpu.make_async_copy(p_v.at[row], p_all.at[row], row_out.at[3, row]).start()
        centred = attended - head_stats(attended, dh, h0, h1)
        centred = jnp.where(h0 | h1, centred, 0.0)
        scaled = centred * lax.rsqrt(head_stats(centred * centred, dh, h0, h1) + 1e-5)
        gated = (scaled * gains[2:3, 0:SIDE]).astype(BF16)
        gated_v[row] = gated
        pltpu.make_async_copy(gated_v.at[row], gated_all.at[row], row_out.at[4, row]).start()
        wo = wo_v[...].reshape(wo_v.shape[0] * wo_v.shape[1], width)

    def project(i):
        row, k = order(me, i)
        wo = wo_v[...].reshape(wo_v.shape[0] * wo_v.shape[1], width)
        part = nn(gated_v[row], wo[0:SIDE])

        @pl.when(lax.rem(i, 2) == 0)
        def _():
            scatter.put_sib(k, part)

        @pl.when(lax.rem(i, 2) == 1)
        def _():
            scatter.put_self(k, part)

        scatter.push(i)

    def one(i, carry):
        attention(i)

        project(i)

        @pl.when(i == 1)
        def _():
            cots.relay()

        @pl.when(i == 4)
        def _():
            spread_d.settle()
            spread_b.settle()
            meet(me, meet_sems.at[1])
            spread_d.rest()
            spread_b.rest()

        return carry

    lax.fori_loop(0, GROUP, one, 0)
    scatter.arrive()

    def middle(at):
        res = tok_v[at].astype(F32) + scatter.total(at)
        resid[at] = res
        s = lax.rsqrt(jnp.mean(res * res, axis=-1, keepdims=True) + 1e-6)
        mid_v[at] = (res * s * gains[1:2]).astype(BF16)

    strips(length, middle)
    mids = Gather(me, mid_v, mid_all, g_send.at[2], g_recv.at[2], g_loc.at[2])
    mids.start()
    mids.relay()
    cots.share()
    cots.last()
    mids.share()
    mids.last()
    mids.finish()
    cots.finish()
    spread_d.arrive()
    spread_b.arrive()
    scatter.finish_cores()
    scatter.finish_chips()
    for sp in (spread_a, spread_b, spread_d):
        sp.finish()
    o_each(lambda cp: cp.wait_send())

    @pl.when(o_relays)
    def _():
        o_copy(0, 1).wait_send()

    @pl.when((o_y == me.y) & (o_c != me.c))
    def _():
        o_sib.wait_send()

    for cp in meta_sent + gain_sent + sent_a + sent_b:
        cp.wait_send()
    for r in range(GROUP):
        pltpu.make_async_copy(x_v.at[r], nrm_all.at[r], row_out.at[0, r]).wait()
        pltpu.make_async_copy(qkv_v.at[r], qkv_all.at[r], row_out.at[1, r]).wait()
        pltpu.make_async_copy(m_v.at[r], m_all.at[r], row_out.at[2, r]).wait()
        pltpu.make_async_copy(p_v.at[r], p_all.at[r], row_out.at[3, r]).wait()
        pltpu.make_async_copy(gated_v.at[r], gated_all.at[r], row_out.at[4, r]).wait()


def forward_call(cfg, tok, ct, w_qkv, w_gate, w_up, w_down, w_o, kern, mix, gain_rows, docs, pads):
    length, width = tok.shape
    planes, ff, r = cfg["planes"], cfg["ff"], w_qkv.shape[0]
    n = planes * PLANE
    chunk = ff // planes
    per_pair = n // GROUP
    taps = cfg["kq"] * length
    pad_rows = -(-SIDE // w_o.shape[0])
    hbm, vmem, smem = pl.BlockSpec(memory_space=pl.ANY), pl.BlockSpec(memory_space=pltpu.VMEM), pl.BlockSpec(memory_space=pltpu.SMEM)
    sds = jax.ShapeDtypeStruct
    rows = (GROUP, length)
    dma = pltpu.SemaphoreType.DMA
    v16 = lambda *shape: pltpu.VMEM(shape, BF16)
    v32 = lambda *shape: pltpu.VMEM(shape, F32)
    return pl.pallas_call(
        functools.partial(forward_kernel, cfg),
        out_shape=(
            sds(rows + (width,), BF16), sds(rows + (width,), BF16),
            sds((n, r, QKV), BF16), sds((n, r, 2 * ff), BF16), sds((planes, chunk, width), BF16),
            sds((per_pair,) + w_o.shape, BF16), sds(rows + (width,), BF16), sds(rows + (3 * SIDE,), BF16),
            sds((GROUP, 2, 2, length, length), BF16), sds((GROUP, 2, length, length), BF16), sds(rows + (SIDE,), BF16),
            sds(rows + (width,), BF16), sds((length, width), F32), sds((8, width), F32), sds((GROUP, 8, length), F32),
        ),
        in_specs=[hbm] * 9 + [vmem] + [smem] * 2,
        out_specs=(hbm,) * 12 + (vmem,) * 3,
        scratch_shapes=[
            v32(*kern.shape), v32(*mix.shape), v16(*w_qkv.shape), v16(PLANE, r, QKV), v16(PLANE, r, 2 * ff), v32(8, length), v32(n, 8, 128), v16(length, width), v16(chunk, width), v16(*w_o.shape),
            v16(*rows, width), v16(n, r, QKV), v16(pad_rows, *w_o.shape),
            v16(2, 3 * length, taps), v16(length, 3 * length), v32(length + 8, taps),
            v16(*rows, 3 * SIDE), v16(GROUP, 2, 2, length, length), v16(GROUP, 2, length, length), v16(*rows, SIDE),
            v32(GROUP, 8, length), v16(length, width), v16(length, width),
            *Scatter.scratch(length, width),
            dma((3, Gather.SENDS)), dma((3, Gather.RECVS)), dma((3,)), dma((2 * PLANE,)), dma((2 * PLANE,)),
            dma((3, planes)), dma((3, planes)), dma((3,)), dma((2,)), dma((GROUP,)), dma((GROUP,)), dma((PLANE + planes,)), dma((PLANE + planes,)), pltpu.SemaphoreType.REGULAR((2,)),
            dma((8,)), dma((2, PLANE, planes)), dma((GROUP,)), dma((5, GROUP)),
        ],
        compiler_params=pltpu.CompilerParams(collective_id=1, has_side_effects=True, vmem_limit_bytes=60 * 2**20),
        name="attention_forward",
    )(tok, ct, w_qkv, w_gate, w_up, w_down, w_o, kern, mix, gain_rows, docs, pads)


def feed_kernel(cfg, *refs):
    (mid_all, ct_all, w_b, w_d, resid, gains,
     g_res, branch_all, dw_b, sum_d, sum_first, out_red, g_mid_gain,
     mid_v, ct_v, wb_v, wd_v, hid_v, gu_v, tile_v, dd_v, zd_v, via_v, sd_v, first_v, zf_v, via_f, sf_v,
     o_out, o_red, o_send, o_recv,
     m_out, m_red, m_diag, m_near, m_send, m_recv,
     g_send, g_recv, g_loc, z_send, z_recv, loc, row_in, out_sem) = refs
    length, width = resid.shape
    ff = cfg["ff"]
    me = Place(cfg["planes"])
    wb_in = pltpu.make_async_copy(w_b, wb_v, loc.at[0])
    wb_in.start()
    wd_in = pltpu.make_async_copy(w_d, wd_v, loc.at[1])
    wd_in.start()

    def row_copies(row):
        return (
            pltpu.make_async_copy(mid_all.at[row], mid_v.at[row], row_in.at[0, row]),
            pltpu.make_async_copy(ct_all.at[row], ct_v.at[row], row_in.at[1, row]),
        )

    for i in range(2):
        for cp in row_copies(order(me, i)[0]):
            cp.start()
    me.greet()
    sum_out = Scatter(me, o_out, o_red, None, None, o_send, o_recv)
    down_sum = Collect(me, lambda b: dd_v.at[pl.ds(b, 1)], zd_v, via_v, z_send.at[0], z_recv.at[0])
    down_sum.clear()
    first_sum = Collect(me, lambda b: first_v.at[pl.ds(b, 1)], zf_v, via_f, z_send.at[1], z_recv.at[1])
    first_sum.clear()
    sum_mid = Scatter(me, m_out, m_red, m_diag, m_near, m_send, m_recv)
    wb_in.wait()
    wd_in.wait()
    for i in range(2, GROUP):
        for cp in row_copies(order(me, i)[0]):
            cp.start()

    def one(i, carry):
        row, k = order(me, i)
        for cp in row_copies(row):
            cp.wait()
        wb = wb_v[...].reshape(width, 2 * ff)
        wd = wd_v[...].reshape(ff, width)
        pre = nn(mid_v[row], wb)
        gate, up = pre[:, :ff], pre[:, ff:]
        g_hidden = nt(ct_v[row], wd)
        sig = jax.nn.sigmoid(gate)
        silu = gate * sig
        hidden = (silu * up).astype(BF16)
        hid_v[row] = hidden
        g_gate = (g_hidden * up * sig * (1.0 + gate * (1.0 - sig))).astype(BF16)
        g_up = (g_hidden * silu).astype(BF16)
        gu_v[row, :, :ff] = g_gate
        gu_v[row, :, ff:] = g_up
        mid_part = nt(gu_v[row], wb)

        @pl.when(lax.rem(i, 2) == 0)
        def _():
            sum_mid.put_sib(k, mid_part)

        @pl.when(lax.rem(i, 2) == 1)
        def _():
            sum_mid.put_self(k, mid_part)

        sum_mid.push(i)
        return carry

    lax.fori_loop(0, GROUP, one, 0)

    def output(i, carry):
        row, k = order(me, i)
        out_part = nn(hid_v[row], wd_v[...].reshape(ff, width))

        @pl.when(lax.rem(i, 2) == 0)
        def _():
            sum_out.put_sib(k, out_part)

        @pl.when(lax.rem(i, 2) == 1)
        def _():
            sum_out.put_self(k, out_part)

        return carry

    tokens = GROUP * length
    tile = SIDE

    def down(i, carry):
        at = pl.ds(pl.multiple_of(i * tile, tile), tile)
        value = tn(hid_v[:, :, at].reshape(tokens, tile), ct_v[...].reshape(tokens, width)).astype(BF16)
        per = tile // dd_v.shape[1]
        dd_v[pl.ds(i * per, per)] = value.reshape((per,) + dd_v.shape[1:])
        return carry

    lax.fori_loop(0, ff // tile, down, 0)
    down_sum.start()

    steps = width // tile

    def tile_out(i):
        slot = lax.rem(i, 2)
        at = pl.ds(pl.multiple_of(i * tile, tile), tile)
        return pltpu.make_async_copy(tile_v.at[slot], dw_b.at[at], out_sem.at[slot])

    def gate_up(i, carry):
        @pl.when(i >= 2)
        def _():
            tile_out(i - 2).wait()

        at = pl.ds(pl.multiple_of(i * tile, tile), tile)
        value = tn(mid_v[:, :, at].reshape(tokens, tile), gu_v[...].reshape(tokens, 2 * ff)).astype(BF16)
        tile_v[lax.rem(i, 2)] = value
        tile_out(i).start()
        for z in range(first_v.shape[0]):
            lo = z * PLANE * first_v.shape[1]

            @pl.when(i == lo // tile)
            def _():
                first_v[z] = value[lo % tile : lo % tile + first_v.shape[1]]

        return carry

    lax.fori_loop(0, steps, gate_up, 0)
    first_sum.start()
    g_mid_gain[...] = jnp.zeros(g_mid_gain.shape, F32)
    sum_mid.arrive()

    def middle(at):
        g_mid = sum_mid.total(at)
        res = resid[at]
        s = lax.rsqrt(jnp.mean(res * res, axis=-1, keepdims=True) + 1e-6)
        g_mid_gain[0:1] = g_mid_gain[0:1] + jnp.sum(g_mid * res * s, axis=0, keepdims=True)
        pulled = g_mid * gains[1:2]
        back = ct_v[me.slot, at].astype(F32) + s * pulled
        back = back - res * (s * s * s * jnp.mean(pulled * res, axis=-1, keepdims=True))
        g_res[at] = back
        ct_v[me.slot, at] = back.astype(BF16)

    strips(length, middle)
    branch = Gather(me, ct_v.at[me.slot], branch_all, g_send, g_recv, g_loc.at[0])
    branch.start()

    lax.fori_loop(0, GROUP, output, 0)
    red_out = pltpu.make_async_copy(o_red, out_red, out_sem.at[2])
    red_out.start()
    down_sum.combine(lambda t: dd_v.at[pl.ds(t, 1)])
    branch.relay()
    branch.share()
    first_sum.combine(lambda t: first_v.at[pl.ds(t, 1)])
    branch.last()
    down_sum.total(sd_v, dd_v.at[pl.ds(me.g, 1)])
    sd_out = pltpu.make_async_copy(sd_v.at[0], sum_d, out_sem.at[3])
    sd_out.start()
    first_sum.total(sf_v, first_v.at[pl.ds(me.g, 1)])
    sf_out = pltpu.make_async_copy(sf_v.at[0], sum_first, out_sem.at[4])
    sf_out.start()
    branch.finish()
    sum_mid.finish_cores()
    sum_mid.finish_chips()
    sum_out.finish_cores()
    down_sum.finish()
    first_sum.finish()
    tile_out(steps - 2).wait()
    tile_out(steps - 1).wait()
    red_out.wait()
    sd_out.wait()
    sf_out.wait()


def feed_call(cfg, mid_all, ct_all, w_b, w_d, resid, gains):
    length, width = resid.shape
    ff = cfg["ff"]
    hbm, vmem = pl.BlockSpec(memory_space=pl.ANY), pl.BlockSpec(memory_space=pltpu.VMEM)
    sds = jax.ShapeDtypeStruct
    dma = pltpu.SemaphoreType.DMA
    rows = (GROUP, length)
    chunk = ff // cfg["planes"]
    others = cfg["planes"] - 1
    r = w_b.shape[1]
    v16 = lambda *shape: pltpu.VMEM(shape, BF16)
    return pl.pallas_call(
        functools.partial(feed_kernel, cfg),
        out_shape=(
            sds((length, width), F32), sds(rows + (width,), BF16),
            sds((width, 2 * ff), BF16), sds((chunk, width), BF16), sds((r, 2 * ff), BF16), sds((4, length, width), BF16), sds((8, width), F32),
        ),
        in_specs=[hbm] * 4 + [vmem] * 2,
        out_specs=(vmem, hbm, hbm, hbm, hbm, hbm, vmem),
        scratch_shapes=[
            v16(*rows, width), v16(*rows, width), v16(*w_b.shape), v16(*w_d.shape), v16(*rows, ff), v16(*rows, 2 * ff),
            v16(2, SIDE, 2 * ff), v16(others + 1, chunk, width), v16(others, 1, chunk, width), v16(1, chunk, width), v16(1, chunk, width),
            v16(others + 1, r, 2 * ff), v16(others, 1, r, 2 * ff), v16(1, r, 2 * ff), v16(1, r, 2 * ff),
            *Scatter.scratch(length, width, chips=False), *Scatter.scratch(length, width),
            dma((Gather.SENDS,)), dma((Gather.RECVS,)), dma((1,)), dma((2, others + 1)), dma((2, others + 1)),
            dma((2,)), dma((2, GROUP)), dma((5,)),
        ],
        compiler_params=pltpu.CompilerParams(collective_id=2, has_side_effects=True, vmem_limit_bytes=52 * 2**20),
        name="feed_forward",
    )(mid_all, ct_all, w_b, w_d, resid, gains)


def backward_kernel(cfg, *refs):
    (branch_all, o_all, a_all, nrm_all, qkv_all, p_all, m_all, gated_all, dw_b, sum_d, sum_first, out_red, tok,
     resid, kern_in, mix_in, g_res, gains, ends, g_mid_gain,
     g_tokens, layer_out, out_a, out_b, out_d, out_o, out_small,
     kern, mix, gb_v, wo_v, wa_v, nrm_v, qkv_v, p_v, m_v, t_v, cat_v, shift_v, corr_v, gq_v, da_v, do_v, tok_v, rows_v, line_v, taps_v,
     zb_v, za_v, zo_v, via_b, via_a, via_o, sb_v, sa_v, so_v, far_b, strip_v, sd_v, small_v, small_in,
     s_out, s_red, s_diag, s_near, rs_send, rs_recv,
     l_red, l_diag, l_near, l_send, l_recv,
     z_send, z_recv, small_send, small_recv, t_send, t_recv, loc, row_in) = refs
    planes, dh, taps_q, taps_k = cfg["planes"], cfg["dh"], cfg["kq"], cfg["kk"]
    length, width = tok.shape
    scale = dh ** (-0.5)
    me = Place(planes)
    per_pair = o_all.shape[0]
    r = a_all.shape[1]
    far = jnp.where(me.g == 1, planes - 1, 0)
    loads = [
        pltpu.make_async_copy(src, dst, loc.at[i])
        for i, (src, dst) in enumerate(
            [(a_all, wa_v), (o_all, wo_v.at[pl.ds(0, per_pair)]), (tok, tok_v)]
            + [(dw_b.at[pl.ds(me.g * PLANE + 1, PLANE - 1)], sb_v.at[pl.ds(1, PLANE - 1)]), (sum_first, sb_v.at[0])]
            + [(dw_b.at[pl.ds(far * PLANE + 1, PLANE - 1)], far_b), (out_red, l_red), (sum_d, sd_v)]
        )
    ]

    span = PLANE * r

    turns = ((3, 2, 1, 0), (0, 2, 3, 1), (3, 1, 0, 2), (0, 1, 2, 3))

    def turn_of(i):
        return sum(jnp.where(me.g == b, turns[b][i], 0) for b in range(planes))

    def nrm_copy(i):
        at = pl.ds(pl.multiple_of(turn_of(i) * span, 128), span)
        return pltpu.make_async_copy(nrm_all.at[:, :, at], nrm_v.at[i % 2], loc.at[8 + i % 2])

    def row_copies(i):
        row = order(me, i)[0]
        at = lax.rem(i, SLOTS)
        cps = [pltpu.make_async_copy(branch_all.at[row], gb_v.at[row], row_in.at[0, i])]
        for j, (src, dst) in enumerate(((qkv_all, qkv_v), (p_all, p_v), (m_all, m_v))):
            cps.append(pltpu.make_async_copy(src.at[row], dst.at[at], row_in.at[j + 1, i]))
        return cps

    taps_in = [pltpu.make_async_copy(kern_in, kern, loc.at[10]), pltpu.make_async_copy(mix_in, mix, loc.at[11])]
    for cp in taps_in:
        cp.start()
    wo_v[...] = jnp.zeros(wo_v.shape, BF16)
    loads[1].start()
    loads[0].start()
    for i in range(SLOTS):
        for cp in row_copies(i):
            cp.start()
    for cp in loads[2:]:
        cp.start()
    for j in range(2):
        nrm_copy(j).start()
    for cp in taps_in:
        cp.wait()
    for g in range(2):
        for a in range(taps_q):
            t_v[g, a * length : (a + 1) * length] = band(kern, 2 * me.pair + g, a, taps_q, taps_k, length, True).astype(BF16)
    shift_v[length:] = jnp.zeros((8, length), F32)
    corr_v[...] = jnp.zeros(corr_v.shape, F32)
    rows_v[...] = jnp.zeros(rows_v.shape, F32)
    small_v[...] = jnp.zeros(small_v.shape, F32)
    me.greet()

    blocks4 = lambda ref: (lambda b: ref.at[pl.ds(b * PLANE, PLANE)])
    sum_b = Collect(me, lambda b: dw_b.at[pl.ds(b * PLANE + 1, PLANE - 1)], zb_v, via_b, z_send.at[0], z_recv.at[0])
    sum_a = Collect(me, blocks4(da_v), za_v, via_a, z_send.at[1], z_recv.at[1])
    sum_o = Collect(me, lambda b: do_v.at[pl.ds(b, 1)], zo_v, via_o, z_send.at[2], z_recv.at[2])
    send_s = []
    for d in range(1, planes):
        to = lax.rem(me.g + d, planes)
        send_s.append(remote(small_v, small_in.at[d - 1], small_send.at[d - 1], small_recv.at[d - 1], me.plane_dev(to)))
    sum_b.start()
    for group in (sum_b, sum_a, sum_o):
        group.clear()
    h0, h1 = head_lanes(length, dh)
    scatter = Scatter(me, s_out, s_red, s_diag, s_near, rs_send, rs_recv)
    layer = Scatter(me, None, l_red, l_diag, l_near, l_send, l_recv)
    loads[0].wait()
    loads[1].wait()
    loads[5].wait()
    loads[6].wait()
    layer.push(1)
    layer.push(3)
    layer.ahead()
    loads[7].wait()
    d_cp = remote(sd_v, out_d.at[me.y], t_send.at[3, 0], t_recv.at[3, 0], me.yn)
    d_cp.start()
    d_here = pltpu.make_async_copy(sd_v, out_d.at[me.y], t_send.at[3, 1])
    d_here.start()

    def one(i, carry):
        row, k = order(me, i)
        at = lax.rem(i, SLOTS)
        for cp in row_copies(i):
            cp.wait()
        wo = wo_v[...].reshape(wo_v.shape[0] * wo_v.shape[1], width)[0:SIDE]
        q, kk, v = qkv_v[at, :, 0:SIDE], qkv_v[at, :, SIDE : 2 * SIDE], qkv_v[at, :, 2 * SIDE : 3 * SIDE]
        parts = [nn(p_v[at, g, 0], v) + nn(p_v[at, g, 1], v) for g in range(2)]
        probs = [p_v[at, g, 0].astype(F32) + p_v[at, g, 1].astype(F32) for g in range(2)]
        lane_mix = [mix_lanes(mix, me.pair, g, dh) for g in range(2)]
        attended = parts[0] * lane_mix[0] + parts[1] * lane_mix[1]
        centred = jnp.where(h0 | h1, attended - head_stats(attended, dh, h0, h1), 0.0)
        inv = lax.rsqrt(head_stats(centred * centred, dh, h0, h1) + 1e-5)
        normal = centred * inv
        g_gated = nt(gb_v[row], wo)
        rows_v[0:1] = rows_v[0:1] + jnp.sum(g_gated * normal, axis=0, keepdims=True)
        u = g_gated * gains[2:3, 0:SIDE]
        g_att = inv * (u - head_stats(u, dh, h0, h1) - normal * head_stats(u * normal, dh, h0, h1))
        g_exact = jnp.where(h0 | h1, g_att, 0.0)
        g_att = g_exact.astype(BF16).astype(F32)
        ok = allowed_mask(length, ends[row, 0:1, :])
        g_q = jnp.zeros((length, SIDE), F32)
        g_k = jnp.zeros((length, SIDE), F32)
        g_v = jnp.zeros((length, SIDE), F32)
        for o in range(2):
            mixed = mix_at(mix, me.pair, o, 0) * probs[0] + mix_at(mix, me.pair, o, 1) * probs[1]
            g_v = g_v + tn(mixed.astype(BF16), jnp.where(h0 if o == 0 else h1, g_att, 0.0).astype(BF16))
        for g in range(2):
            mine = h0 if g == 0 else h1
            rows_v[1 + g : 2 + g] = rows_v[1 + g : 2 + g] + jnp.sum(g_exact * parts[g], axis=0, keepdims=True)
            g_out = (g_att * lane_mix[g]).astype(BF16)
            g_probs = nt(g_out, v)
            g_conv = probs[g] * (g_probs - jnp.sum(probs[g] * g_probs, axis=-1, keepdims=True))
            shift_v[0:length] = g_conv
            for a in range(taps_q):
                cat_v[:, a * length : (a + 1) * length] = shift_v[a : a + length].astype(BF16)
            corr_v[g] = corr_v[g] + tn(m_v[at, g], cat_v[...])
            g_raw = jnp.where(ok, nn(cat_v[...], t_v[g]), 0.0).astype(BF16)
            g_q = g_q + nn(g_raw, jnp.where(mine, kk.astype(F32), 0.0).astype(BF16))
            g_k = g_k + tn(g_raw, jnp.where(mine, q.astype(F32), 0.0).astype(BF16))
        g_q, g_k = g_q * scale, g_k * scale
        mid_tile = g_q[:, 128:256] + pltpu.roll(g_v[:, 128:256], 64, 1)
        packed = jnp.concatenate([g_q[:, 0:128], mid_tile, g_k, g_v[:, 0:128]], axis=1).astype(BF16)
        gq_v[row] = packed

        @pl.when(i + SLOTS < GROUP)
        def _():
            for cp in row_copies(i + SLOTS):
                cp.start()

        @pl.when(i == 4)
        def _():
            layer.turn()

        @pl.when(i == 5)
        def _():
            sum_b.combine(lambda t: far_b)

        return carry

    lax.fori_loop(0, GROUP, one, 0)
    for i in (2, 3, 4):
        loads[i].wait()
    gated_in = [
        pltpu.make_async_copy(gated_all.at[i], p_v.at[i // 4, i // 2 % 2, i % 2], row_in.at[0, i]) for i in range(GROUP)
    ]
    for cp in gated_in:
        cp.start()

    tokens = GROUP * length
    for cp in gated_in:
        cp.wait()
    value = tn(p_v[...].reshape(tokens, SIDE), gb_v[...].reshape(tokens, width))
    do_v[...] = value[0 : 2 * dh].astype(BF16).reshape(do_v.shape)

    sum_o.start()
    for i in range(planes):
        nrm_copy(i).wait()
        value = tn(nrm_v[i % 2].reshape(tokens, span), gq_v[...].reshape(tokens, QKV))
        da_v[pl.ds(turn_of(i) * PLANE, PLANE)] = value.astype(BF16).reshape(PLANE, r, QKV)
        sum_a.start([turns[b][i] for b in range(planes)])
        if i + 2 < planes:
            nrm_copy(i + 2).start()
    def to_slot(d):
        to = lax.rem(me.slot + d, GROUP)
        return lax.div(to, PLANE), lax.rem(to, PLANE)

    def group_copies(kind, src_of, landing):
        cps = []
        for d in range(1, GROUP):
            y, sl = to_slot(d)
            cps.append(remote(src_of(sl), landing.at[me.slot], t_send.at[kind, d], t_recv.at[kind, d], (y, me.g * PLANE + sl)))
        cps.append(pltpu.make_async_copy(src_of(me.s), landing.at[me.slot], t_send.at[kind, 0]))
        for cp in cps:
            cp.start()
        return cps

    def group_wait(kind, cps, landing):
        for d in range(1, GROUP):
            fr = lax.rem(me.slot - d + GROUP, GROUP)
            remote(landing.at[fr], landing.at[fr], t_send.at[kind, d], t_recv.at[kind, d], me.sib).wait_recv()
        for cp in cps[:-1]:
            cp.wait_send()
        cps[-1].wait()

    def back_through(i, carry):
        row, k = order(me, i)
        part = nt(gq_v[row], wa_v[...].reshape(width, QKV))

        @pl.when(lax.rem(i, 2) == 0)
        def _():
            scatter.put_sib(k, part)

        @pl.when(lax.rem(i, 2) == 1)
        def _():
            scatter.put_self(k, part)

        scatter.push(i, turn=False)
        return carry

    lax.fori_loop(0, GROUP, back_through, 0)
    scatter.turn()
    sum_b.total(sb_v.at[pl.ds(1, PLANE - 1)], sb_v.at[pl.ds(1, PLANE - 1)])
    b_cps = group_copies(0, lambda sl: sb_v.at[sl], out_b)

    sum_o.combine(lambda t: do_v.at[pl.ds(t, 1)])
    sum_a.combine(lambda t: da_v.at[pl.ds(t * PLANE, PLANE)])

    def taps(at, carry):
        g, a = lax.div(at, taps_q), lax.rem(at, taps_q)
        lanes_at = pl.ds(pl.multiple_of(a * length, length), length)
        e = corr_v[g, :, lanes_at]
        diff = lax.broadcasted_iota(jnp.int32, (length, length), 0) - lax.broadcasted_iota(jnp.int32, (length, length), 1)
        for b in range(taps_k):
            line = jnp.sum(jnp.where(diff == b - taps_k // 2, e, 0.0), axis=0, keepdims=True)
            taps_v[b : b + 1] = line[:, 0:128] + line[:, 128:256]
        each = jnp.sum(taps_v[...], axis=-1, keepdims=True)
        small_v[0] = jnp.where(lanes(16, 128) == at, each, small_v[0])
        return carry

    taps_v[...] = jnp.zeros(taps_v.shape, F32)
    lax.fori_loop(0, 2 * taps_q, taps, 0)
    base = 1
    at = lanes(1, SIDE)
    for o in range(2):
        for g in range(2):
            line = jnp.where((at >= o * dh) & (at < (o + 1) * dh), rows_v[1 + g : 2 + g], 0.0)
            small_v[base, 2 * o + g : 2 * o + g + 1] = line[:, 0:128] + line[:, 128:256]
    for j in range(2):
        small_v[base, 4 + j : 5 + j] = rows_v[0:1, j * 128 : (j + 1) * 128]

    layer.arrive()

    def result(at):
        cp = pltpu.make_async_copy(resid.at[at], strip_v, loc.at[0])
        cp.start()
        cp.wait()
        strip_v[...] = strip_v[...] + layer.total(at)
        cp = pltpu.make_async_copy(strip_v, layer_out.at[at], loc.at[0])
        cp.start()
        cp.wait()

    strips(length, result)

    scatter.arrive()

    def middle(at):
        g_normed = scatter.total(at)
        tok32 = tok_v[at].astype(F32)
        s = lax.rsqrt(jnp.mean(tok32 * tok32, axis=-1, keepdims=True) + 1e-6)
        line_v[0:1] = line_v[0:1] + jnp.sum(g_normed * tok32 * s, axis=0, keepdims=True)
        pulled = g_normed * gains[0:1]
        back = g_res[at] + s * pulled
        g_tokens[at] = back - tok32 * (s * s * s * jnp.mean(pulled * tok32, axis=-1, keepdims=True))

    line_v[...] = jnp.zeros(line_v.shape, F32)
    strips(length, middle)
    line = line_v[0:1]
    for j in range(width // 128):
        small_v[base + 1, j : j + 1] = line[:, j * 128 : (j + 1) * 128]
        small_v[base + 2, j : j + 1] = g_mid_gain[0:1, j * 128 : (j + 1) * 128]
    for cp in send_s:
        cp.start()

    sum_o.total(so_v, do_v.at[pl.ds(me.g, 1)])
    o_to = me.pair * per_pair + lax.div(me.g, 2)
    o_half = lax.rem(me.g, 2)

    def o_copy(y):
        return remote(so_v.at[0], out_o.at[o_half], t_send.at[4, y], t_recv.at[4, o_half], (y, o_to))

    o_here = pltpu.make_async_copy(so_v.at[0], out_o.at[o_half], t_send.at[4, 2])

    def o_each(act, act_here):
        for y in range(2):
            mine = (y == me.y) & (o_to == me.f)

            @pl.when(jnp.logical_not(mine))
            def _():
                act(o_copy(y))

            @pl.when(mine)
            def _():
                act_here(o_here)

    o_each(lambda cp: cp.start(), lambda cp: cp.start())
    sum_a.total(sa_v, da_v.at[pl.ds(me.g * PLANE, PLANE)])
    a_cps = group_copies(1, lambda sl: sa_v.at[sl], out_a)

    for cp in send_s:
        cp.wait_recv()
    for cp in send_s:
        cp.wait_send()
    small_v[...] = small_v[...] + sum(small_in[d] for d in range(planes - 1))
    small_cps = group_copies(2, lambda sl: small_v, out_small)

    group_wait(2, small_cps, out_small)
    d_cp.wait_send()
    remote(out_d.at[1 - me.y], out_d.at[1 - me.y], t_send.at[3, 0], t_recv.at[3, 0], me.yn).wait_recv()
    d_here.wait()
    group_wait(0, b_cps, out_b)
    src_y = jnp.where((me.g == 1) | (me.g == 2), 1, 0)
    src_s = me.x * 2 + jnp.where(me.g >= 2, 1, 0)
    for h in range(2):
        src_f = (2 * lax.rem(me.f, per_pair) + h) * PLANE + src_s

        @pl.when(jnp.logical_not((src_y == me.y) & (src_f == me.f)))
        def _():
            remote(out_o.at[h], out_o.at[h], t_send.at[4, 0], t_recv.at[4, h], me.sib).wait_recv()

    o_each(lambda cp: cp.wait_send(), lambda cp: cp.wait())
    group_wait(1, a_cps, out_a)
    for group in (sum_b, sum_a, sum_o):
        group.finish()
    scatter.finish_cores()
    scatter.finish_chips()
    layer.finish_chips()


def backward_call(cfg, *args):
    branch_all, o_all, a_all, tok = args[0], args[1], args[2], args[12]
    length, width = tok.shape
    planes, ff = cfg["planes"], cfg["ff"]
    n, r = a_all.shape[:2]
    chunk = ff // planes
    taps = cfg["kq"] * length
    pad_rows = -(-SIDE // o_all.shape[1])
    piece = 2 * cfg["dh"] // planes
    small = (4, 16, 128)
    hbm, vmem, smem = pl.BlockSpec(memory_space=pl.ANY), pl.BlockSpec(memory_space=pltpu.VMEM), pl.BlockSpec(memory_space=pltpu.SMEM)
    sds = jax.ShapeDtypeStruct
    dma = pltpu.SemaphoreType.DMA
    rows = (GROUP, length)
    others = planes - 1
    v16 = lambda *shape: pltpu.VMEM(shape, BF16)
    v32 = lambda *shape: pltpu.VMEM(shape, F32)
    b_block, a_block, o_block = (PLANE - 1, r, 2 * ff), (PLANE, r, QKV), (1, piece, width)
    return pl.pallas_call(
        functools.partial(backward_kernel, cfg),
        out_shape=(
            sds((length, width), F32), sds((length, width), F32), sds((GROUP, r, QKV), BF16), sds((GROUP, r, 2 * ff), BF16),
            sds((2, chunk, width), BF16), sds((2, piece, width), BF16), sds((GROUP,) + small, F32),
        ),
        in_specs=[hbm] * 16 + [vmem] * 4,
        out_specs=(vmem,) + (hbm,) * 6,
        scratch_shapes=[
            v32(*args[14].shape), v32(*args[15].shape), v16(*rows, width), v16(pad_rows, *o_all.shape[1:]), v16(n, r, QKV), v16(2, *rows, PLANE * r), v16(SLOTS, length, 3 * SIDE),
            v16(SLOTS, 2, 2, length, length), v16(SLOTS, 2, length, length),
            v16(2, taps, length), v16(length, taps), v32(length + 8, length), v32(2, length, taps), v16(*rows, QKV),
            v16(n, r, QKV), v16(planes, piece, width), v16(length, width), v32(8, SIDE), v32(8, width), v32(16, 128),
            v16(others, *b_block), v16(others, *a_block), v16(others, *o_block), v16(*b_block), v16(*a_block), v16(*o_block),
            v16(PLANE, r, 2 * ff), v16(*a_block), v16(*o_block), v16(*b_block), v32(64, width), v16(chunk, width),
            v32(*small), v32(others, *small),
            *Scatter.scratch(length, width), *Scatter.scratch(length, width, cores=False),
            dma((3, planes)), dma((3, planes)), dma((others,)), dma((others,)), dma((5, GROUP)), dma((5, GROUP)),
            dma((12,)), dma((4, GROUP)),
        ],
        compiler_params=pltpu.CompilerParams(collective_id=3, has_side_effects=True, vmem_limit_bytes=54 * 2**20),
        name="attention_backward",
    )(*args)


def results_kernel(cfg, a_ref, b_ref, d_ref, o_ref, small_ref, g_tok, layer, qkv_ref, gate_ref, up_ref, down_ref, out_ref,
                   taps_ref, mix_ref, in_ref, mid_ref, heads_ref, tok_ref, layer_ref, vec_v):
    planes, ff = cfg["planes"], cfg["ff"]
    rows, width = out_ref.shape
    chunk = ff // planes
    low = lanes(rows, 128) < 64

    def slot(pair):
        home, x = pair // 2, pair % 2
        y, c = (0, 1, 1, 0)[home], (0, 0, 1, 1)[home]
        return y * PLANE + x * 2 + c

    def joined(even, odd, low):
        o0, o1 = pltpu.roll(odd[0], 64, 1), pltpu.roll(odd[1], 64, 1)
        return even[0], jnp.where(low, even[1], o0), jnp.where(low, o0, o1)

    def tiles(pair, j):
        t = lambda i: a_ref[slot(pair), :, i * 128 : (i + 1) * 128].astype(F32)
        if j == 2:
            return t(4), pltpu.roll(t(1), 64, 1)
        return t(2 * j), t(2 * j + 1)

    for j in range(3):
        for two in range(GROUP // 2):
            for i, t in enumerate(joined(tiles(2 * two, j), tiles(2 * two + 1, j), low)):
                at = j * width + two * 384 + i * 128
                qkv_ref[:, at : at + 128] = t
    for z in range(planes):
        for s in range(PLANE):
            for y in range(2):
                at = ((z * PLANE + s) * 2 + y) * chunk
                src = b_ref.at[y * PLANE + s]
                gate_ref[:, at : at + chunk] = src[:, z * chunk : (z + 1) * chunk].astype(F32)
                up_ref[:, at : at + chunk] = src[:, ff + z * chunk : ff + (z + 1) * chunk].astype(F32)
    down_ref[...] = d_ref[0].astype(F32)
    out_ref[...] = o_ref[0].astype(F32)

    tok_ref[...] = g_tok[...]
    layer_ref[...] = layer[...]

    @pl.when(pl.program_id(0) == 0)
    def _():
        base = 1
        for pair in range(GROUP):
            taps = jnp.transpose(jnp.concatenate([small_ref[slot(pair), 0], jnp.zeros((112, 128), F32)], axis=0))
            for g in range(2):
                taps_ref[2 * pair + g] = taps[g * cfg["kq"] : (g + 1) * cfg["kq"], 0 : cfg["kk"]]
            mixed = jnp.sum(small_ref[slot(pair), base], axis=-1, keepdims=True)
            for o in range(2):
                for g in range(2):
                    mix_ref[2 * pair + o : 2 * pair + o + 1, g : g + 1] = mixed[2 * o + g : 2 * o + g + 1]
        vec_v[...] = jnp.zeros(vec_v.shape, F32)
        for k in range(2):
            total = small_ref[0, base + 1 + k]
            for s in range(1, GROUP):
                total = total + small_ref[s, base + 1 + k]
            for j in range(width // 128):
                vec_v[k : k + 1, j * 128 : (j + 1) * 128] = total[j : j + 1]
        line = lambda pair: tuple(small_ref[slot(pair), base, 4 + j : 5 + j] for j in range(2))
        for two in range(GROUP // 2):
            for i, t in enumerate(joined(line(2 * two), line(2 * two + 1), lanes(1, 128) < 64)):
                vec_v[2:3, two * 384 + i * 128 : two * 384 + (i + 1) * 128] = t
        own = in_ref.shape[1]
        mine = pltpu.roll(vec_v[...], lax.rem(width - lax.axis_index("fsdp") * own, width), 1)
        for k, ref in enumerate((in_ref, mid_ref, heads_ref)):
            ref[...] = mine[k : k + 1, 0:own]


def results_call(cfg, out_a, out_b, out_d, out_o, small, g_tokens, layer_out):
    r = out_a.shape[1]
    _, chunk, width = out_d.shape
    half = r // 2
    sds = jax.ShapeDtypeStruct
    whole = lambda shape: pl.BlockSpec(shape, lambda i: (0,) * len(shape))
    rows = lambda n, w: pl.BlockSpec((n, w), lambda i: (i, 0))
    moved = 2 * (out_a.size + out_b.size + out_d.size + out_o.size) + 4 * (out_a.size + out_b.size + out_d.size + out_o.size)
    return pl.pallas_call(
        functools.partial(results_kernel, cfg),
        grid=(2,),
        out_shape=(
            sds((r, 3 * width), F32), sds((r, n_cols(cfg)), F32), sds((r, n_cols(cfg)), F32), sds((2 * chunk, width), F32),
            sds((r, width), F32), sds((2 * GROUP, cfg["kq"], cfg["kk"]), F32), sds((2 * GROUP, 2), F32),
            sds((1, r), F32), sds((1, r), F32), sds((1, r), F32), sds(g_tokens.shape, F32), sds(g_tokens.shape, F32),
        ),
        in_specs=[
            pl.BlockSpec((GROUP, half, out_a.shape[2]), lambda i: (0, i, 0)),
            pl.BlockSpec((GROUP, half, out_b.shape[2]), lambda i: (0, i, 0)),
            pl.BlockSpec((1, chunk, width), lambda i: (i, 0, 0)),
            pl.BlockSpec((1, half, width), lambda i: (i, 0, 0)),
            whole(small.shape),
            rows(g_tokens.shape[0] // 2, width),
            rows(g_tokens.shape[0] // 2, width),
        ],
        scratch_shapes=[pltpu.VMEM((8, width), F32)],
        out_specs=(
            rows(half, 3 * width), rows(half, n_cols(cfg)), rows(half, n_cols(cfg)), rows(chunk, width), rows(half, width),
            whole((2 * GROUP, cfg["kq"], cfg["kk"])), whole((2 * GROUP, 2)),
            whole((1, r)), whole((1, r)), whole((1, r)), rows(g_tokens.shape[0] // 2, width), rows(g_tokens.shape[0] // 2, width),
        ),
        compiler_params=pltpu.CompilerParams(vmem_limit_bytes=60 * 2**20),
        cost_estimate=pl.CostEstimate(flops=0, bytes_accessed=moved, transcendentals=0),
        name="results",
    )(out_a, out_b, out_d, out_o, small, g_tokens, layer_out)


def n_cols(cfg):
    return cfg["ff"] * GROUP


def fits(mesh, tokens, kernel, w_gate):
    n = mesh.shape["fsdp"]
    width, length, heads, ff = tokens.shape[2], tokens.shape[1], kernel.shape[0], w_gate.shape[1]
    return (
        mesh.shape["rep"] == 2
        and n == 4 * PLANE
        and heads == 2 * GROUP
        and width == heads * 96
        and (width // n) % 32 == 0
        and ff % (2 * n * 128) == 0
        and length == SIDE
    )


def per_device_group(
    planes,
    tokens,
    doc_lengths,
    pad_counts,
    norm_in,
    w_qkv,
    kernel,
    mixing,
    norm_heads,
    w_out,
    norm_mid,
    w_gate,
    w_up,
    w_down,
    cotangent,
):
    length, width = tokens.shape[1:]
    heads, kq, kk = kernel.shape
    dh = width // heads
    n = planes * PLANE
    r = width // n
    chunk = w_down.shape[0] // 2
    ff = planes * chunk
    cfg = dict(planes=planes, dh=dh, kq=kq, kk=kk, ff=ff)

    gain_rows = jnp.pad(jnp.stack([norm_in, norm_mid, norm_heads]).astype(F32), ((0, 5), (0, 128 - r)))
    tok, ct = tokens[0], cotangent[0]

    (_, ct_all, a_all, b_all, d_all, o_all, nrm_all, qkv_all, p_all, m_all, gated_all, mid_all, resid, gains, ends) = (
        forward_call(
            cfg, tok, ct, w_qkv, w_gate, w_up, w_down, w_out, kernel, mixing, gain_rows, doc_lengths, pad_counts
        )
    )
    g_res, branch_all, dw_b, sum_d, sum_first, out_red, g_mid_gain = feed_call(cfg, mid_all, ct_all, b_all, d_all, resid, gains)
    g_tokens, layer_out, out_a, out_b, out_d, out_o, small = backward_call(
        cfg, branch_all, o_all, a_all, nrm_all, qkv_all, p_all, m_all, gated_all, dw_b.reshape(n, r, 2 * ff), sum_d, sum_first, out_red,
        tok, resid, kernel, mixing, g_res, gains, ends, g_mid_gain,
    )

    g_qkv, g_gate, g_up, g_down, g_out, g_kernel, g_mixing, g_in, g_mid, g_heads, g_tokens, layer_out = results_call(
        cfg, out_a, out_b, out_d, out_o, small, g_tokens, layer_out
    )
    return (
        layer_out[None],
        g_tokens[None],
        g_in[0],
        g_qkv,
        g_kernel,
        g_mixing,
        g_heads[0],
        g_out,
        g_mid[0],
        g_gate,
        g_up,
        g_down,
    )


def solution(mesh):
    in_specs = (
        P(("rep", "fsdp"), None, None),
        P(("rep", "fsdp"), None),
        P(("rep", "fsdp")),
        P("fsdp"),
        P("fsdp", None),
        P(),
        P(),
        P("fsdp"),
        P("fsdp", None),
        P("fsdp"),
        P("fsdp", None),
        P("fsdp", None),
        P("fsdp", None),
        P(("rep", "fsdp"), None, None),
    )
    out_specs = (
        P(("rep", "fsdp"), None, None),
        P(("rep", "fsdp"), None, None),
        P("fsdp"),
        P("fsdp", None),
        P(),
        P(),
        P("fsdp"),
        P("fsdp", None),
        P("fsdp"),
        P("fsdp", None),
        P("fsdp", None),
        P("fsdp", None),
    )

    def layer(*args):
        body = per_device
        if fits(mesh, args[0], args[5], args[10]):
            body = functools.partial(per_device_group, mesh.shape["fsdp"] // PLANE)
        return jax.shard_map(body, mesh=mesh, in_specs=in_specs, out_specs=out_specs, check_vma=False)(*args)

    return layer
```

```python
import functools

import jax
import jax.numpy as jnp
from jax import lax
from jax.experimental import pallas as pl
from jax.experimental.pallas import tpu as pltpu
from jax.sharding import PartitionSpec as P

F32 = jnp.float32
BF16 = jnp.bfloat16
NEG_FILL = -1e30
MESH = pl.DeviceIdType.MESH
PLANE = 4
GROUP = 8
SIDE = 256
FIRST = 1
SLOTS = 2
QKV = 640


class Place:
    def __init__(self, planes):
        self.planes = planes
        self.y = lax.axis_index("rep")
        self.f = lax.axis_index("fsdp")
        self.g = lax.div(self.f, PLANE)
        self.s = lax.rem(self.f, PLANE)
        self.x = lax.div(self.s, 2)
        self.c = lax.rem(self.s, 2)
        self.slot = self.y * PLANE + self.s
        self.home = self.y + self.c * (planes - 1 - 2 * self.y)
        self.pair = 2 * self.home + self.x
        self.sib = self.dev(self.y, self.x, 1 - self.c)
        self.xn = self.dev(self.y, 1 - self.x, self.c)
        self.yn = self.dev(1 - self.y, self.x, self.c)

    def dev(self, y, x, c):
        return (y, self.g * PLANE + x * 2 + c)

    def plane_dev(self, g):
        return (self.y, g * PLANE + self.s)

    def row(self, dy, dx, dc):
        y = self.y + dy - 2 * dy * self.y
        x = self.x + dx - 2 * dx * self.x
        c = self.c + dc - 2 * dc * self.c
        return y * 4 + x * 2 + c

    def greet(self):
        sem = pltpu.get_barrier_semaphore()
        n = self.planes * PLANE
        for d in range(1, n):
            pl.semaphore_signal(sem, inc=1, device_id=(self.y, lax.rem(self.f + d, n)), device_id_type=MESH)
        for s in range(PLANE):
            pl.semaphore_signal(sem, inc=1, device_id=(1 - self.y, self.g * PLANE + s), device_id_type=MESH)
        pl.semaphore_wait(sem, n - 1 + PLANE)


def meet(me, sem):
    pl.semaphore_signal(sem, inc=1, device_id=me.sib, device_id_type=MESH)
    pl.semaphore_wait(sem, 1)


def remote(src, dst, send, recv, dev):
    return pltpu.make_async_remote_copy(
        src_ref=src, dst_ref=dst, send_sem=send, recv_sem=recv, device_id=dev, device_id_type=MESH
    )


class Gather:
    SENDS = 14
    RECVS = 14

    def __init__(self, me, own, buf, send, recv, local):
        self.me, self.own, self.buf = me, own, buf
        self.send, self.recv, self.local = send, recv, local
        self.half = own.shape[0] // 2
        self.sent = []

    def _own(self, h):
        return self.own.at[pl.ds(h * self.half, self.half)]

    def _blk(self, row, h):
        return self.buf.at[row, pl.ds(h * self.half, self.half)]

    def _copy(self, i):
        own, row, h, kind, dev = self.sent[i]
        src = self._own(h) if own else self._blk(row, h)
        return remote(src, self._blk(row, h), self.send.at[i], self.recv.at[kind * 2 + h], dev)

    def _go(self, own, row, h, kind, dev):
        self.sent.append((own, row, h, kind, dev))
        self._copy(len(self.sent) - 1).start()

    def _await(self, row, h, kind):
        b = self._blk(row, h)
        remote(b, b, self.send.at[0], self.recv.at[kind * 2 + h], self.me.sib).wait_recv()

    def start(self):
        me = self.me
        self.rows = [me.row(0, 0, 1), me.row(0, 1, 0), me.row(1, 0, 0), me.row(1, 1, 0), me.row(0, 1, 1), me.row(1, 0, 1), me.row(1, 1, 1)]
        self.here = pltpu.make_async_copy(self.own, self.buf.at[me.slot], self.local)
        self.here.start()
        self._go(True, me.slot, 0, 1, me.xn)
        self._go(True, me.slot, 1, 2, me.yn)
        self._go(True, me.slot, 0, 0, me.sib)
        self._go(True, me.slot, 1, 0, me.sib)
        self._go(True, me.slot, 1, 1, me.xn)
        self._go(True, me.slot, 0, 2, me.yn)

    def relay(self):
        me, rows = self.me, self.rows
        self._await(rows[1], 0, 1)
        self._go(False, rows[1], 0, 3, me.yn)
        self._go(False, rows[1], 0, 4, me.sib)
        self._await(rows[2], 1, 2)
        self._go(False, rows[2], 1, 3, me.xn)
        self._go(False, rows[2], 1, 5, me.sib)

    def share(self):
        me, rows = self.me, self.rows
        self._await(rows[1], 1, 1)
        self._go(False, rows[1], 1, 4, me.sib)
        self._await(rows[2], 0, 2)
        self._go(False, rows[2], 0, 5, me.sib)

    def last(self):
        me, rows = self.me, self.rows
        for h in (0, 1):
            self._await(rows[3], h, 3)
            self._go(False, rows[3], h, 6, me.sib)

    def finish(self):
        for kind in (0, 4, 5, 6):
            for h in (0, 1):
                self._await(self.rows[kind], h, kind)
        for i in range(len(self.sent)):
            self._copy(i).wait_send()
        self.here.wait()


class Scatter:
    SENDS = 10
    RECVS = 10

    @staticmethod
    def scratch(rows, width, cores=True, chips=True):
        bufs = []
        if cores:
            bufs.append(pltpu.VMEM((2, rows, width), BF16))
        bufs.append(pltpu.VMEM((4, rows, width), BF16))
        if chips:
            bufs += [pltpu.VMEM((2, rows // 2, width), BF16), pltpu.VMEM((2, rows, width), BF16)]
        return bufs + [pltpu.SemaphoreType.DMA((Scatter.SENDS,)), pltpu.SemaphoreType.DMA((Scatter.RECVS,))]

    def __init__(self, me, out, red, diag, near, send, recv):
        self.me, self.out, self.red, self.diag, self.near = me, out, red, diag, near
        self.send, self.recv = send, recv
        self.half = red.shape[1] // 2

    def _sib(self, k):
        return remote(self.out.at[lax.rem(k, 2)], self.red.at[k], self.send.at[k], self.recv.at[k], self.me.sib)

    def put_sib(self, k, value):
        @pl.when(k >= 2)
        def _():
            self._sib(k - 2).wait_send()

        self.out[lax.rem(k, 2)] = value.astype(BF16)
        self._sib(k).start()

    def put_self(self, k, value):
        self._sib(k).wait_recv()
        self.red[k] = (value + self.red[k].astype(F32)).astype(BF16)

    def _copy(self, name):
        h, me = self.half, self.me
        lo, hi = pl.ds(0, h), pl.ds(h, h)
        src, dst, i, dev = {
            "da": (self.red.at[0, lo], self.diag.at[0], 4, me.xn),
            "db": (self.red.at[0, hi], self.diag.at[1], 5, me.yn),
            "xa": (self.red.at[1, lo], self.near.at[0, lo], 6, me.xn),
            "xb": (self.red.at[1, hi], self.near.at[0, hi], 7, me.xn),
            "ya": (self.red.at[2, lo], self.near.at[1, lo], 8, me.yn),
            "yb": (self.red.at[2, hi], self.near.at[1, hi], 9, me.yn),
        }[name]
        return remote(src, dst, self.send.at[i], self.recv.at[i], dev)

    def push(self, i, turn=True):
        @pl.when(i == 1)
        def _():
            self._copy("da").start()
            self._copy("db").start()

        @pl.when(i == 3)
        def _():
            self._copy("xa").start()

        @pl.when(i == 5)
        def _():
            self._copy("yb").start()
            if turn:
                self.turn()

    def ahead(self):
        self._copy("yb").start()

    def turn(self):
        h = self.half
        self._copy("db").wait_recv()
        self.red[1, h:] = (self.red[1, h:].astype(F32) + self.diag[1].astype(F32)).astype(BF16)
        self._copy("xb").start()
        self._copy("da").wait_recv()
        self.red[2, :h] = (self.red[2, :h].astype(F32) + self.diag[0].astype(F32)).astype(BF16)
        self._copy("ya").start()

    def arrive(self):
        for name in ("xa", "xb", "ya", "yb"):
            self._copy(name).wait_recv()

    def total(self, at):
        return self.red[3, at].astype(F32) + self.near[0, at].astype(F32) + self.near[1, at].astype(F32)

    def finish_cores(self):
        for k in (2, 3):
            self._sib(k).wait_send()

    def finish_chips(self):
        for name in ("da", "db", "xa", "xb", "ya", "yb"):
            self._copy(name).wait_send()


class Spread:
    def __init__(self, me, blocks, send, recv):
        self.me, self.blocks, self.send, self.recv = me, blocks, send, recv

    def _copy(self, b, t, i):
        return remote(self.blocks(b), self.blocks(b), self.send.at[i], self.recv.at[b], self.me.plane_dev(t))

    def _sends(self, b):
        last = self.me.planes - 1
        if b in (0, last):
            return [(b, 1 if b == 0 else last - 1, 0)] + [(b, t, 1) for t in sorted(range(last + 1), key=lambda t: abs(t - b))[2:]]
        other, end = (2, 0) if b == 1 else (1, 3)
        return [(b, b - 1, 0), (b, b + 1, 0), (other, end, 1)]

    def _each(self, act, steps):
        for g in range(self.me.planes):

            @pl.when(self.me.g == g)
            def _():
                for i, (b, t, step) in enumerate(self._sends(g)):
                    if step in steps:
                        act(self._copy(b, t, i))

    def near(self):
        self._each(lambda cp: cp.start(), (0,))

    def settle(self):
        inner = (self.me.g == 0) | (self.me.g == 2)

        @pl.when(inner)
        def _():
            self._copy(1, 0, 0).wait_recv()

        @pl.when(jnp.logical_not(inner))
        def _():
            self._copy(2, 0, 0).wait_recv()

    def rest(self):
        self._each(lambda cp: cp.start(), (1,))

    def arrive(self):
        for g in range(self.me.planes):

            @pl.when(self.me.g == g)
            def _():
                for b in range(self.me.planes):
                    if b not in (g, 1 if g in (0, 2) else 2):
                        self._copy(b, b, 0).wait_recv()

    def finish(self):
        self._each(lambda cp: cp.wait_send(), (0, 1))


class Collect:
    def __init__(self, me, blocks, landing, via, send, recv):
        self.me, self.blocks, self.landing, self.via, self.send, self.recv = me, blocks, landing, via, send, recv
        self.by = {(0, 3): 1, (3, 0): 2} if me.planes == 4 else {}

    def _copy(self, b, t, src, i):
        at = (b - t) % self.me.planes - 1
        return remote(src, self.landing.at[at], self.send.at[i], self.recv.at[at], self.me.plane_dev(t))

    def _plan(self, b):
        combined = [t for (s, t), by in self.by.items() if by == b]
        direct = [t for t in range(self.me.planes) if t != b and t not in combined]
        direct.sort(key=lambda t: -abs(t - b))
        return [(t, (b, t) in self.by, i) for i, t in enumerate(direct)]

    def _each(self, b, act, ways=(True, False)):
        @pl.when(self.me.g == b)
        def _():
            for t, through, i in self._plan(b):
                if through not in ways:
                    continue
                if through:
                    z = self.me.planes
                    by = self.by[(b, t)]
                    act(remote(self.blocks(t), self.via, self.send.at[i], self.recv.at[z - 1], self.me.plane_dev(by)))
                else:
                    act(self._copy(b, t, self.blocks(t), i))

    def start(self, ways=(True, False)):
        for b in range(self.me.planes):
            self._each(b, lambda cp: cp.start(), ways)

    def _combined(self, b, t):
        return self._copy(b, t, self.via, self.me.planes - 2)

    def combine(self, own):
        for (s, t), by in self.by.items():

            @pl.when(self.me.g == by)
            def _():
                z = self.me.planes
                remote(self.via, self.via, self.send.at[0], self.recv.at[z - 1], self.me.plane_dev(by)).wait_recv()
                for q in range(self.via.shape[0]):
                    self.via[q] = (self.via[q].astype(F32) + own(t)[q].astype(F32)).astype(BF16)
                self._combined(by, t).start()

    def clear(self):
        for s, t in self.by:

            @pl.when(self.me.g == t)
            def _():
                at = (s - t) % self.me.planes - 1
                self.landing[at] = jnp.zeros(self.landing.shape[1:], BF16)

    def total(self, out, own):
        z = self.me.planes
        for t in range(z):

            @pl.when(self.me.g == t)
            def _():
                for b in range(z):
                    if b != t and (b, t) not in self.by:
                        at = (b - t) % z - 1
                        self._copy(b, t, self.landing.at[at], 0).wait_recv()

        for q in range(out.shape[0]):
            value = own[q].astype(F32)
            for at in range(z - 1):
                value = value + self.landing[at, q].astype(F32)
            out[q] = value.astype(BF16)

    def finish(self):
        for b in range(self.me.planes):
            self._each(b, lambda cp: cp.wait_send())
        for (s, t), by in self.by.items():

            @pl.when(self.me.g == by)
            def _():
                self._combined(by, t).wait_send()


def order(me, i):
    k = lax.div(i, 2)
    dx = 1 - lax.div(k, 2)
    dy = 1 - lax.rem(k, 2)
    dc = 1 - lax.rem(i, 2)
    return me.row(dy, dx, dc), k


def strips(length, body, strip=64):
    def one(i, carry):
        body(pl.ds(pl.multiple_of(i * strip, strip), strip))
        return carry

    lax.fori_loop(0, length // strip, one, 0)


def lanes(rows, width):
    return lax.broadcasted_iota(jnp.int32, (rows, width), 1)


def nt(a, b):
    return lax.dot_general(a, b, (((1,), (1,)), ((), ())), preferred_element_type=F32)


def tn(a, b):
    return lax.dot_general(a, b, (((0,), (0,)), ((), ())), preferred_element_type=F32)


def nn(a, b):
    return jnp.dot(a, b, preferred_element_type=F32)


def head_lanes(rows, dh):
    at = lanes(rows, SIDE)
    return at < dh, (at >= dh) & (at < 2 * dh)


def allowed_mask(length, ends):
    i = lax.broadcasted_iota(jnp.int32, (length, length), 0)
    j = lax.broadcasted_iota(jnp.int32, (length, length), 1)
    return (i >= j) & (i.astype(F32) < ends)


def of_head(value, head):
    at = lax.broadcasted_iota(jnp.int32, value.shape, value.ndim - 1)
    return jnp.sum(jnp.where(at == head, value, 0.0), axis=-1, keepdims=True)


def pair_mixing(mix_ref, pair):
    return [[of_head(mix_ref[g : g + 1], 2 * pair + o) for g in range(2)] for o in range(2)]


def mix_lanes(mixing, g, dh):
    at = lanes(1, SIDE)
    return jnp.where(at < dh, mixing[0][g], jnp.where(at < 2 * dh, mixing[1][g], 0.0))


def head_stats(value, dh, h0, h1):
    m0 = jnp.sum(jnp.where(h0, value, 0.0), axis=-1, keepdims=True) / dh
    m1 = jnp.sum(jnp.where(h1, value, 0.0), axis=-1, keepdims=True) / dh
    return jnp.where(h0, m0, jnp.where(h1, m1, 0.0))


def bands(kern_ref, head, length, flip):
    taps_k, taps_q, _ = kern_ref.shape
    r = lax.broadcasted_iota(jnp.int32, (length, length), 0)
    c = lax.broadcasted_iota(jnp.int32, (length, length), 1)
    diff = (c - r) if flip else (r - c)
    taps = [of_head(kern_ref[b], head) for b in range(taps_k)]
    for a in range(taps_q):
        acc = jnp.zeros((length, length), F32)
        for b in range(taps_k):
            acc = jnp.where(diff == b - taps_k // 2, taps[b][a : a + 1], acc)
        yield a, acc


def rms_norm(values_in, scaling):
    return (
        values_in
        * lax.rsqrt(jnp.mean(values_in * values_in, axis=-1, keepdims=True) + 1e-06)
        * scaling
    )


def group_norm(values_in, scaling):
    centred = values_in - jnp.mean(values_in, axis=-1, keepdims=True)
    scaled = centred * lax.rsqrt(jnp.mean(centred * centred, axis=-1, keepdims=True) + 1e-05)
    return scaled.reshape(values_in.shape[0], -1) * scaling


def convolve(scores, kernel):
    length = scores.shape[1]
    taps_query = kernel.shape[1]
    taps_key = kernel.shape[2]
    half_width = taps_key // 2
    padded = jnp.pad(scores, ((0, 0), (taps_query - 1, 0), (half_width, half_width)))
    summed = jnp.zeros_like(scores)
    for shift_q in range(taps_query):
        for shift_k in range(taps_key):
            start_q = taps_query - 1 - shift_q
            window = padded[:, start_q : start_q + length, shift_k : shift_k + length]
            summed = summed + kernel[:, shift_q, shift_k][:, None, None] * window
    return summed


def convolve_back(grad_conv, masked, kernel):
    length = masked.shape[1]
    taps_query = kernel.shape[1]
    taps_key = kernel.shape[2]
    half_width = taps_key // 2
    padded = jnp.pad(masked, ((0, 0), (taps_query - 1, 0), (half_width, half_width)))
    grad_padded = jnp.pad(grad_conv, ((0, 0), (0, taps_query - 1), (half_width, half_width)))
    grad_masked = jnp.zeros_like(masked)
    grad_taps = []
    for shift_q in range(taps_query):
        for shift_k in range(taps_key):
            start_q = taps_query - 1 - shift_q
            window = padded[:, start_q : start_q + length, shift_k : shift_k + length]
            grad_taps.append(jnp.sum(grad_conv * window, axis=(1, 2)))
            start_k = taps_key - 1 - shift_k
            back_window = grad_padded[:, shift_q : shift_q + length, start_k : start_k + length]
            grad_masked = grad_masked + kernel[:, shift_q, shift_k][:, None, None] * back_window
    grad_kern = jnp.stack(grad_taps, axis=1).reshape(kernel.shape)
    return (grad_masked, grad_kern)


def build_mask(doc_lengths, pad_count, length):
    places = jnp.arange(length, dtype=jnp.int32)
    doc_ends = jnp.cumsum(doc_lengths)
    segment = jnp.sum((places[:, None] >= doc_ends[None, :]).astype(jnp.int32), axis=1)
    live_end = length - pad_count
    same_doc = segment[:, None] == segment[None, :]
    causal = places[None, :] <= places[:, None]
    usable = (places[None, :] < live_end) | (places[None, :] == places[:, None])
    return same_doc & causal & usable


def outer_sum(left_rows, right_rows):
    return lax.dot_general(
        left_rows, right_rows, (((0,), (0,)), ((), ())), preferred_element_type=jnp.float32
    )


def back_product(grad_rows, weight_full):
    return lax.dot_general(
        grad_rows, weight_full, (((1,), (1,)), ((), ())), preferred_element_type=jnp.float32
    )


def attention_weights(norm_in, w_qkv, norm_heads, w_out):
    return (
        lax.all_gather(norm_in, "fsdp", axis=0, tiled=True),
        lax.all_gather(w_qkv, "fsdp", axis=0, tiled=True),
        lax.all_gather(norm_heads, "fsdp", axis=0, tiled=True),
        lax.all_gather(w_out, "fsdp", axis=0, tiled=True),
    )


def feed_weights(norm_mid, w_gate, w_up, w_down):
    return (
        lax.all_gather(norm_mid, "fsdp", axis=0, tiled=True),
        lax.all_gather(w_gate, "fsdp", axis=0, tiled=True),
        lax.all_gather(w_up, "fsdp", axis=0, tiled=True),
        lax.all_gather(w_down, "fsdp", axis=0, tiled=True),
    )


def per_device(
    tokens,
    doc_lengths,
    pad_counts,
    norm_in,
    w_qkv,
    kernel,
    mixing,
    norm_heads,
    w_out,
    norm_mid,
    w_gate,
    w_up,
    w_down,
    cotangent,
):
    inputs = tokens[0].astype(jnp.float32)
    length = inputs.shape[0]
    model_width = inputs.shape[1]
    head_count = kernel.shape[0]
    head_size = model_width // head_count
    pair_count = head_count // 2
    score_scale = head_size ** (-0.5)
    allowed = build_mask(doc_lengths[0], pad_counts[0], length)[None]
    kern_pairs = kernel.reshape(pair_count, 2, kernel.shape[1], kernel.shape[2])
    mix_pairs = mixing.reshape(pair_count, 2, 2)
    attn_set = attention_weights(norm_in, w_qkv, norm_heads, w_out)
    normed = rms_norm(inputs, attn_set[0].astype(jnp.float32)).astype(jnp.bfloat16)
    projected = jnp.dot(normed, attn_set[1], preferred_element_type=jnp.float32).astype(
        jnp.bfloat16
    )
    split_qkv = projected.reshape(length, 3, pair_count, 2, head_size).transpose(1, 2, 3, 0, 4)

    def pair_scores(queries, key_rows, kern_pair):
        raw_scores = (
            jnp.einsum("gie,gje->gij", queries, key_rows, preferred_element_type=jnp.float32)
            * score_scale
        )
        masked = jnp.where(allowed, raw_scores, 0.0)
        logits = jnp.where(allowed, convolve(masked, kern_pair), NEG_FILL)
        return (masked, logits)

    def pair_forward(pieces):
        queries, key_rows, value_rows, kern_pair, mix_pair = pieces
        masked, logits = pair_scores(queries, key_rows, kern_pair)
        row_peak = jnp.max(logits, axis=-1, keepdims=True)
        log_total = row_peak + jnp.log(jnp.sum(jnp.exp(logits - row_peak), axis=-1, keepdims=True))
        attn_probs = jnp.exp(logits - log_total)
        mixed_probs = jnp.einsum("og,gij->oij", mix_pair, attn_probs, precision=lax.Precision.HIGHEST)
        output = jnp.einsum(
            "oij,oje->oie", mixed_probs, value_rows.astype(jnp.float32), precision=lax.Precision.HIGHEST
        )
        return (output, log_total)

    attended_pairs, log_totals = lax.map(
        pair_forward, (split_qkv[0], split_qkv[1], split_qkv[2], kern_pairs, mix_pairs)
    )
    attended = attended_pairs.transpose(2, 0, 1, 3).reshape(length, head_count, head_size)
    gated_out = group_norm(attended, attn_set[2].astype(jnp.float32)).astype(jnp.bfloat16)
    residual = inputs + jnp.dot(gated_out, attn_set[3], preferred_element_type=jnp.float32)
    ffn_set = feed_weights(norm_mid, w_gate, w_up, w_down)
    normed_mid = rms_norm(residual, ffn_set[0].astype(jnp.float32)).astype(jnp.bfloat16)
    gate_pre = jnp.dot(normed_mid, ffn_set[1], preferred_element_type=jnp.float32)
    up_pre = jnp.dot(normed_mid, ffn_set[2], preferred_element_type=jnp.float32)
    sigmoid_gate = jax.nn.sigmoid(gate_pre)
    silu_gate = gate_pre * sigmoid_gate
    hidden = (silu_gate * up_pre).astype(jnp.bfloat16)
    layer_out = (residual + jnp.dot(hidden, ffn_set[3], preferred_element_type=jnp.float32))[None]
    ffn_again = feed_weights(norm_mid, w_gate, w_up, w_down)
    grad_y = cotangent[0]
    grad_w_down = outer_sum(hidden, grad_y)
    grad_hidden = back_product(grad_y, ffn_again[3])
    grad_gate = (
        grad_hidden * up_pre * sigmoid_gate * (1.0 + gate_pre * (1.0 - sigmoid_gate))
    ).astype(jnp.bfloat16)
    grad_up = (grad_hidden * silu_gate).astype(jnp.bfloat16)
    grad_w_gate = outer_sum(normed_mid, grad_gate)
    grad_w_up = outer_sum(normed_mid, grad_up)
    grad_mid = back_product(grad_gate, ffn_again[1]) + back_product(grad_up, ffn_again[2])
    mid_pull = jax.vjp(rms_norm, residual, ffn_again[0].astype(jnp.float32))[1]
    grad_residual_norm, grad_norm_mid = mid_pull(grad_mid)
    grad_residual = grad_y.astype(jnp.float32) + grad_residual_norm
    ffn_shards = (
        lax.psum_scatter(grad_norm_mid, "fsdp", scatter_dimension=0, tiled=True),
        lax.psum_scatter(grad_w_gate, "fsdp", scatter_dimension=0, tiled=True),
        lax.psum_scatter(grad_w_up, "fsdp", scatter_dimension=0, tiled=True),
        lax.psum_scatter(grad_w_down, "fsdp", scatter_dimension=0, tiled=True),
    )
    attn_again = attention_weights(norm_in, w_qkv, norm_heads, w_out)
    grad_branch = grad_residual.astype(jnp.bfloat16)
    grad_w_out = outer_sum(gated_out, grad_branch)
    grad_gated = back_product(grad_branch, attn_again[3])
    head_pull = jax.vjp(group_norm, attended, attn_again[2].astype(jnp.float32))[1]
    grad_attended, grad_norm_heads = head_pull(grad_gated)
    grad_att_pairs = (
        grad_attended.astype(jnp.bfloat16)
        .reshape(length, pair_count, 2, head_size)
        .transpose(1, 2, 0, 3)
    )

    def pair_backward(pieces):
        queries, key_rows, value_rows, kern_pair, mix_pair, log_total, grad_output = pieces
        masked, logits = pair_scores(queries, key_rows, kern_pair)
        attn_probs = jnp.exp(logits - log_total)
        mixed_probs = jnp.einsum("og,gij->oij", mix_pair, attn_probs, precision=lax.Precision.HIGHEST)
        grad_wide = grad_output.astype(jnp.float32)
        grad_mixed = jnp.einsum(
            "oie,oje->oij", grad_wide, value_rows.astype(jnp.float32), precision=lax.Precision.HIGHEST
        )
        grad_values = jnp.einsum("oij,oie->oje", mixed_probs, grad_wide, precision=lax.Precision.HIGHEST)
        grad_mix = jnp.einsum("oij,gij->og", grad_mixed, attn_probs, precision=lax.Precision.HIGHEST)
        grad_probs = jnp.einsum("og,oij->gij", mix_pair, grad_mixed, precision=lax.Precision.HIGHEST)
        grad_logits = attn_probs * (
            grad_probs - jnp.sum(attn_probs * grad_probs, axis=-1, keepdims=True)
        )
        grad_conv = jnp.where(allowed, grad_logits, 0.0)
        grad_masked, grad_kern = convolve_back(grad_conv, masked, kern_pair)
        grad_raw = jnp.where(allowed, grad_masked, 0.0)
        grad_query = (
            jnp.einsum("gij,gje->gie", grad_raw, key_rows.astype(jnp.float32), precision=lax.Precision.HIGHEST)
            * score_scale
        )
        grad_key = (
            jnp.einsum("gij,gie->gje", grad_raw, queries.astype(jnp.float32), precision=lax.Precision.HIGHEST)
            * score_scale
        )
        return (
            grad_query.astype(jnp.bfloat16),
            grad_key.astype(jnp.bfloat16),
            grad_values.astype(jnp.bfloat16),
            grad_kern,
            grad_mix,
        )

    grads_query, grads_key, grads_value, grad_kern_pairs, grad_mix_pairs = lax.map(
        pair_backward,
        (
            split_qkv[0],
            split_qkv[1],
            split_qkv[2],
            kern_pairs,
            mix_pairs,
            log_totals,
            grad_att_pairs,
        ),
    )
    grad_qkv = (
        jnp.stack([grads_query, grads_key, grads_value])
        .transpose(3, 0, 1, 2, 4)
        .reshape(length, 3 * model_width)
    )
    grad_w_qkv = outer_sum(normed, grad_qkv)
    grad_normed = back_product(grad_qkv, attn_again[1])
    in_pull = jax.vjp(rms_norm, inputs, attn_again[0].astype(jnp.float32))[1]
    grad_inputs_norm, grad_norm_in = in_pull(grad_normed)
    grad_tokens = (grad_residual + grad_inputs_norm)[None]
    small_sums = lax.psum(
        (grad_kern_pairs.reshape(kernel.shape), grad_mix_pairs.reshape(mixing.shape)),
        ("rep", "fsdp"),
    )
    attn_shards = (
        lax.psum_scatter(grad_norm_in, "fsdp", scatter_dimension=0, tiled=True),
        lax.psum_scatter(grad_w_qkv, "fsdp", scatter_dimension=0, tiled=True),
        lax.psum_scatter(grad_norm_heads, "fsdp", scatter_dimension=0, tiled=True),
        lax.psum_scatter(grad_w_out, "fsdp", scatter_dimension=0, tiled=True),
    )
    summed = (
        lax.psum(ffn_shards[0].astype(jnp.bfloat16), "rep").astype(jnp.float32),
        lax.psum(ffn_shards[1].astype(jnp.bfloat16), "rep").astype(jnp.float32),
        lax.psum(ffn_shards[2].astype(jnp.bfloat16), "rep").astype(jnp.float32),
        lax.psum(ffn_shards[3].astype(jnp.bfloat16), "rep").astype(jnp.float32),
        lax.psum(attn_shards[0].astype(jnp.bfloat16), "rep").astype(jnp.float32),
        lax.psum(attn_shards[1].astype(jnp.bfloat16), "rep").astype(jnp.float32),
        lax.psum(attn_shards[2].astype(jnp.bfloat16), "rep").astype(jnp.float32),
        lax.psum(attn_shards[3].astype(jnp.bfloat16), "rep").astype(jnp.float32),
    )
    return (
        layer_out,
        grad_tokens,
        summed[4],
        summed[5],
        small_sums[0],
        small_sums[1],
        summed[6],
        summed[7],
        summed[0],
        summed[1],
        summed[2],
        summed[3],
    )


def forward_kernel(cfg, *refs):
    (tok, ct, w_qkv, w_gate, w_up, w_down, w_o, kern_in, mix_in, gain_rows, docs, pads,
     tok_all, ct_all, a_all, b_all, d_all, o_all, nrm_all, qkv_all, p_all, m_all, gated_all, mid_all, resid, gains, ends,
     kern, mix, wq_v, w_a, w_b, meta, gain_v, ct_v, down_v, own_o,
     x_v, wa_v, wo_v, t_v, cat_v, shift_v, qkv_v, p_v, m_v, gated_v, meta_v, mid_v, tok_v,
     out_v, red, diag, near, rs_send, rs_recv,
     g_send, g_recv, g_loc, a_send, a_recv, ch_send, ch_recv, o_send, o_recv, meta_send, meta_recv, gain_send, gain_recv, meet_sems, loc, pack, row_in, row_out) = refs
    planes, dh, taps_q, taps_k = cfg["planes"], cfg["dh"], cfg["kq"], cfg["kk"]
    length, width = tok.shape
    per_pair = o_all.shape[0]
    scale = dh ** (-0.5)
    ff, chunk = cfg["ff"], cfg["ff"] // planes
    me = Place(planes)

    wq_in = pltpu.make_async_copy(w_qkv, wq_v, loc.at[1])
    wq_in.start()
    tok_in = pltpu.make_async_copy(tok, tok_v, loc.at[0])
    tok_in.start()
    taps_in = [pltpu.make_async_copy(kern_in, kern, loc.at[6]), pltpu.make_async_copy(mix_in, mix, loc.at[7])]
    for cp in taps_in:
        cp.start()
    o_in = pltpu.make_async_copy(w_o, own_o, loc.at[4])
    o_in.start()
    down_in = pltpu.make_async_copy(w_down.at[pl.ds(me.y * chunk, chunk)], down_v, loc.at[3])
    down_in.start()
    ct_in = pltpu.make_async_copy(ct, ct_v, loc.at[5])
    ct_in.start()

    def columns(j, s, z):
        at = pl.multiple_of(z * (2 * PLANE * chunk) + s * (2 * chunk) + me.y * chunk, 128)
        src = (w_gate, w_up)[j].at[:, pl.ds(at, chunk)]
        return pltpu.make_async_copy(src, w_b.at[s, :, pl.ds(j * ff + z * chunk, chunk)], pack.at[j, s, z])

    for j in range(2):
        for s in range(PLANE):
            for z in range(planes):
                columns(j, s, z).start()

    places = lanes(8, length).astype(F32)
    last = length * 1.0
    reach = [docs[0, 0]]
    for k in range(1, docs.shape[1]):
        reach.append(reach[-1] + docs[0, k])
    own_end = jnp.full((8, length), last, F32)
    for end in reversed(reach):
        own_end = jnp.where(places < end.astype(F32), end.astype(F32), own_end)
    meta[...] = jnp.where(places < last - pads[0].astype(F32), own_end, places + 1.0)

    wq_in.wait()
    low = lanes(w_qkv.shape[0], 128) < 64
    for s in range(PLANE):
        base = (me.y if s % 2 == 0 else planes - 1 - me.y) * (4 * dh)

        def part(j):
            blk = wq_v[:, pl.ds(pl.multiple_of(j * width + base, 128), 4 * dh)].astype(F32)
            t0, t1, t2 = blk[:, 0:128], blk[:, 128:256], blk[:, 256:384]
            if s // 2 == 0:
                return t0, t1
            t1, t2 = pltpu.roll(t1, 64, 1), pltpu.roll(t2, 64, 1)
            return jnp.where(low, t1, t2), t2

        (q0, q1), (k0, k1), (v0, v1) = part(0), part(1), part(2)
        tiles = (
            q0,
            jnp.where(low, q1, pltpu.roll(v1, 64, 1)),
            k0,
            jnp.where(low, k1, 0.0),
            v0,
        )
        for i, t in enumerate(tiles):
            w_a[s, :, i * 128 : (i + 1) * 128] = t.astype(BF16)

    down_in.wait()
    down_out = pltpu.make_async_copy(down_v, d_all.at[me.g], loc.at[3])
    down_out.start()
    o_in.wait()
    tok_in.wait()
    for cp in taps_in:
        cp.wait()
    me.greet()

    def first(src, dst_all, base):
        cps = []
        for d in range(1, PLANE):
            s = lax.rem(me.s + d, PLANE)
            cp = remote(src.at[s], dst_all.at[me.f], a_send.at[base + d], a_recv.at[base + d], (me.y, me.g * PLANE + s))
            cp.start()
            cps.append(cp)
        own = pltpu.make_async_copy(src.at[me.s], dst_all.at[me.f], a_send.at[base])
        own.start()
        return cps, own

    def first_wait(src, dst_all, base, own):
        for d in range(1, PLANE):
            s = lax.rem(me.s - d + PLANE, PLANE)
            blk = dst_all.at[me.g * PLANE + s]
            remote(blk, blk, a_send.at[base + d], a_recv.at[base + d], me.sib).wait_recv()
        own.wait()

    meta_sent = []
    for d in range(1, GROUP):
        to = lax.rem(me.slot + d, GROUP)
        cp = remote(
            meta, meta_v.at[me.slot], meta_send.at[d], meta_recv.at[d],
            (lax.div(to, PLANE), me.g * PLANE + lax.rem(to, PLANE)),
        )
        cp.start()
        meta_sent.append(cp)
    meta_here = pltpu.make_async_copy(meta, meta_v.at[me.slot], meta_send.at[0])
    meta_here.start()
    gain_here = pltpu.make_async_copy(gain_rows, gain_v.at[me.f], gain_send.at[0])
    gain_here.start()
    gain_sent = []
    for d in range(1, PLANE):
        to = lax.rem(me.s + d, PLANE)
        gain_sent.append(remote(gain_rows, gain_v.at[me.f], gain_send.at[d], gain_recv.at[d], (me.y, me.g * PLANE + to)))
        gain_sent[-1].start()
    sent_a, own_a = first(w_a, a_all, 0)
    tokens = Gather(me, tok_v, tok_all, g_send.at[0], g_recv.at[0], g_loc.at[0])
    tokens.start()

    o_y = jnp.where((me.g == 1) | (me.g == 2), 1, 0)
    o_c = jnp.where(me.g >= 2, 1, 0)
    o_here = pltpu.make_async_copy(own_o, o_all.at[me.c], o_send.at[0])
    o_sib = remote(own_o, o_all.at[me.c], o_send.at[0], o_recv.at[0], me.sib)

    @pl.when((o_y == me.y) & (o_c == me.c))
    def _():
        o_here.start()

    @pl.when((o_y == me.y) & (o_c != me.c))
    def _():
        o_sib.start()

    def o_copy(t, i):
        return remote(o_all, o_all, o_send.at[i], o_recv.at[1], me.plane_dev(t))

    o_way = ((2, 1), (2, 0), (1, 3), (1, 2))

    def o_each(act):
        for home, (first_to, then_to) in enumerate(o_way):

            @pl.when((me.g == home) & (me.home == home))
            def _():
                act(o_copy(first_to, 1))
                act(o_copy(then_to, 2))

    o_relays = ((me.home < 2) & (me.g == 2)) | ((me.home >= 2) & (me.g == 1))

    def o_from_home():
        o_here.wait()
        remote(o_all.at[1 - me.c], o_all.at[1 - me.c], o_send.at[0], o_recv.at[0], me.sib).wait_recv()

    def o_relay():
        o_copy(0, 1).wait_recv()
        o_copy(jnp.where(me.home < 2, planes - 1, 0), 1).start()

    blocks4 = lambda ref: (lambda b: ref.at[pl.ds(b * PLANE, PLANE)])
    spread_a = Spread(me, blocks4(a_all), ch_send.at[0], ch_recv.at[0])
    spread_b = Spread(me, blocks4(b_all), ch_send.at[1], ch_recv.at[1])
    spread_d = Spread(me, lambda b: d_all.at[b], ch_send.at[2], ch_recv.at[2])

    for g in range(2):
        for a, t in bands(kern, 2 * me.pair + g, length, False):
            high = t.astype(BF16)
            at = slice(a * length, (a + 1) * length)
            t_v[g, 0:length, at] = high
            t_v[g, length : 2 * length, at] = high
            t_v[g, 2 * length :, at] = (t - high.astype(F32)).astype(BF16)
    shift_v[0:8] = jnp.zeros((8, taps_q * length), F32)
    wo_v[...] = jnp.zeros(wo_v.shape, BF16)

    pl.when(me.g == me.home)(o_from_home)
    o_each(lambda cp: cp.start())
    gain_here.wait()
    for d in range(1, PLANE):
        fr = me.g * PLANE + lax.rem(me.s - d + PLANE, PLANE)
        remote(gain_rows, gain_v.at[fr], gain_send.at[d], gain_recv.at[d], me.sib).wait_recv()
    for d in range(1, planes):
        to = lax.rem(me.g + d, planes)
        part = gain_v.at[pl.ds(me.g * PLANE, PLANE)]
        gain_sent.append(remote(part, part, gain_send.at[PLANE + d], gain_recv.at[PLANE + d], me.plane_dev(to)))
        gain_sent[-1].start()
    first_wait(w_a, a_all, 0, own_a)
    spread_a.near()
    pl.when(o_relays)(o_relay)

    tokens.relay()
    for j in range(2):
        for s in range(PLANE):
            for z in range(planes):
                columns(j, s, z).wait()
    sent_b, own_b = first(w_b, b_all, PLANE)
    cots = Gather(me, ct_v, ct_all, g_send.at[1], g_recv.at[1], g_loc.at[1])
    ct_in.wait()
    cots.start()
    spread_a.settle()
    meet(me, meet_sems.at[0])
    spread_a.rest()

    down_out.wait()

    tokens.share()
    tokens.last()
    tokens.finish()
    for row in range(GROUP):
        pltpu.make_async_copy(tok_all.at[row], x_v.at[row], row_in.at[row]).start()
    first_wait(w_b, b_all, PLANE, own_b)
    for d in range(1, GROUP):
        fr = lax.rem(me.slot - d + GROUP, GROUP)
        remote(meta, meta_v.at[fr], meta_send.at[d], meta_recv.at[d], me.sib).wait_recv()
    meta_here.wait()
    ends[...] = meta_v[...]
    for d in range(1, planes):
        part = gain_v.at[pl.ds(lax.rem(me.g - d + planes, planes) * PLANE, PLANE)]
        remote(part, part, gain_send.at[PLANE + d], gain_recv.at[PLANE + d], me.sib).wait_recv()
    gains[...] = jnp.zeros(gains.shape, F32)
    lane = lanes(8, 128)
    for k in range(planes):
        v0, v1, v2, v3 = (gain_v[k * PLANE + j] for j in range(PLANE))
        v1, v2, v3 = pltpu.roll(v1, 96, 1), pltpu.roll(v2, 64, 1), pltpu.roll(v3, 32, 1)
        for j, t in enumerate((jnp.where(lane < 96, v0, v1), jnp.where(lane < 64, v1, v2), jnp.where(lane < 32, v2, v3))):
            at = k * PLANE * w_o.shape[0] + j * 128
            gains[0:2, at : at + 128] = t[0:2]
    v0, v1 = gain_v[2 * me.pair], pltpu.roll(gain_v[2 * me.pair + 1], 96, 1)
    gains[2:3, 0:128] = jnp.where(lane < 96, v0, v1)[2:3]
    gains[2:3, 128:256] = jnp.where(lane < 64, v1, 0.0)[2:3]

    def norms(i, carry):
        row, _ = order(me, i)
        pltpu.make_async_copy(tok_all.at[row], x_v.at[row], row_in.at[row]).wait()

        def norm(at):
            x = x_v[row, at].astype(F32)
            s = lax.rsqrt(jnp.mean(x * x, axis=-1, keepdims=True) + 1e-6)
            x_v[row, at] = (x * s * gains[0:1]).astype(BF16)

        strips(length, norm)
        pltpu.make_async_copy(x_v.at[row], nrm_all.at[row], row_out.at[0, row]).start()
        return carry

    lax.fori_loop(0, GROUP, norms, 0)
    spread_a.arrive()
    wa_in = pltpu.make_async_copy(a_all, wa_v, loc.at[1])
    wa_in.start()
    @pl.when((me.g != me.home) & jnp.logical_not(o_relays))
    def _():
        o_copy(0, 1).wait_recv()

    wo_in = pltpu.make_async_copy(o_all, wo_v.at[pl.ds(0, per_pair)], loc.at[2])
    wo_in.start()
    spread_d.near()
    spread_b.near()
    wa_in.wait()
    wo_in.wait()
    h0, h1 = head_lanes(length, dh)
    scatter = Scatter(me, out_v, red, diag, near, rs_send, rs_recv)

    mixing = pair_mixing(mix, me.pair)

    def attention(i):
        row, k = order(me, i)
        acc = nn(x_v[row], wa_v[...].reshape(width, QKV))
        at = lanes(length, 128)
        q = jnp.where(h0 | h1, acc[:, 0:SIDE], 0.0)
        kk = jnp.where(h0 | h1, acc[:, SIDE : 2 * SIDE], 0.0)
        tail = jnp.where(at < 64, pltpu.roll(acc[:, 128:256], 64, 1), 0.0)
        v = jnp.concatenate([acc[:, 2 * SIDE : QKV], tail], axis=1)
        q, kk, v = q.astype(BF16), kk.astype(BF16), v.astype(BF16)
        qkv_v[row, :, 0:SIDE] = q
        qkv_v[row, :, SIDE : 2 * SIDE] = kk
        qkv_v[row, :, 2 * SIDE : 3 * SIDE] = v
        pltpu.make_async_copy(qkv_v.at[row], qkv_all.at[row], row_out.at[1, row]).start()
        ok = allowed_mask(length, meta_v[row, 0:1, :])
        attended = jnp.zeros((length, SIDE), F32)
        for g in range(2):
            kg = jnp.where(h0 if g == 0 else h1, kk.astype(F32), 0.0).astype(BF16)
            raw = nt(q, kg) * scale
            masked = jnp.where(ok, raw, 0.0)
            m_v[row, g] = masked.astype(BF16)
            high = masked.astype(BF16)
            cat_v[:, 0:length] = high
            cat_v[:, length : 2 * length] = (masked - high.astype(F32)).astype(BF16)
            cat_v[:, 2 * length :] = high
            shift_v[8 : 8 + length] = nn(cat_v[...], t_v[g])
            conv = shift_v[8 : 8 + length, 0:length]
            for a in range(1, taps_q):
                conv = conv + shift_v[8 - a : 8 - a + length, a * length : (a + 1) * length]
            logits = jnp.where(ok, conv, NEG_FILL)
            e = jnp.exp(logits - jnp.max(logits, axis=-1, keepdims=True))
            probs = e / jnp.sum(e, axis=-1, keepdims=True)
            high = probs.astype(BF16)
            low = (probs - high.astype(F32)).astype(BF16)
            p_v[row, g, 0] = high
            p_v[row, g, 1] = low
            attended = attended + (nn(high, v) + nn(low, v)) * mix_lanes(mixing, g, dh)
        pltpu.make_async_copy(m_v.at[row], m_all.at[row], row_out.at[2, row]).start()
        pltpu.make_async_copy(p_v.at[row], p_all.at[row], row_out.at[3, row]).start()
        centred = attended - head_stats(attended, dh, h0, h1)
        centred = jnp.where(h0 | h1, centred, 0.0)
        scaled = centred * lax.rsqrt(head_stats(centred * centred, dh, h0, h1) + 1e-5)
        gated = (scaled * gains[2:3, 0:SIDE]).astype(BF16)
        gated_v[row] = gated
        pltpu.make_async_copy(gated_v.at[row], gated_all.at[row], row_out.at[4, row]).start()
        wo = wo_v[...].reshape(wo_v.shape[0] * wo_v.shape[1], width)

    def project(i):
        row, k = order(me, i)
        wo = wo_v[...].reshape(wo_v.shape[0] * wo_v.shape[1], width)
        part = nn(gated_v[row], wo[0:SIDE])

        @pl.when(lax.rem(i, 2) == 0)
        def _():
            scatter.put_sib(k, part)

        @pl.when(lax.rem(i, 2) == 1)
        def _():
            scatter.put_self(k, part)

        scatter.push(i)

    def one(i, carry):
        attention(i)

        project(i)

        @pl.when(i == 1)
        def _():
            cots.relay()

        @pl.when(i == 4)
        def _():
            spread_d.settle()
            spread_b.settle()
            meet(me, meet_sems.at[1])
            spread_d.rest()
            spread_b.rest()

        return carry

    lax.fori_loop(0, GROUP, one, 0)
    scatter.arrive()

    def middle(at):
        res = tok_v[at].astype(F32) + scatter.total(at)
        resid[at] = res
        s = lax.rsqrt(jnp.mean(res * res, axis=-1, keepdims=True) + 1e-6)
        mid_v[at] = (res * s * gains[1:2]).astype(BF16)

    strips(length, middle)
    mids = Gather(me, mid_v, mid_all, g_send.at[2], g_recv.at[2], g_loc.at[2])
    mids.start()
    mids.relay()
    cots.share()
    cots.last()
    mids.share()
    mids.last()
    mids.finish()
    cots.finish()
    spread_d.arrive()
    spread_b.arrive()
    scatter.finish_cores()
    scatter.finish_chips()
    for sp in (spread_a, spread_b, spread_d):
        sp.finish()
    o_each(lambda cp: cp.wait_send())

    @pl.when(o_relays)
    def _():
        o_copy(0, 1).wait_send()

    @pl.when((o_y == me.y) & (o_c != me.c))
    def _():
        o_sib.wait_send()

    for cp in meta_sent + gain_sent + sent_a + sent_b:
        cp.wait_send()
    for r in range(GROUP):
        pltpu.make_async_copy(x_v.at[r], nrm_all.at[r], row_out.at[0, r]).wait()
        pltpu.make_async_copy(qkv_v.at[r], qkv_all.at[r], row_out.at[1, r]).wait()
        pltpu.make_async_copy(m_v.at[r], m_all.at[r], row_out.at[2, r]).wait()
        pltpu.make_async_copy(p_v.at[r], p_all.at[r], row_out.at[3, r]).wait()
        pltpu.make_async_copy(gated_v.at[r], gated_all.at[r], row_out.at[4, r]).wait()


def forward_call(cfg, tok, ct, w_qkv, w_gate, w_up, w_down, w_o, kern, mix, gain_rows, docs, pads):
    length, width = tok.shape
    planes, ff, r = cfg["planes"], cfg["ff"], w_qkv.shape[0]
    n = planes * PLANE
    chunk = ff // planes
    per_pair = n // GROUP
    taps = cfg["kq"] * length
    pad_rows = -(-SIDE // w_o.shape[0])
    hbm, vmem, smem = pl.BlockSpec(memory_space=pl.ANY), pl.BlockSpec(memory_space=pltpu.VMEM), pl.BlockSpec(memory_space=pltpu.SMEM)
    sds = jax.ShapeDtypeStruct
    rows = (GROUP, length)
    dma = pltpu.SemaphoreType.DMA
    v16 = lambda *shape: pltpu.VMEM(shape, BF16)
    v32 = lambda *shape: pltpu.VMEM(shape, F32)
    return pl.pallas_call(
        functools.partial(forward_kernel, cfg),
        out_shape=(
            sds(rows + (width,), BF16), sds(rows + (width,), BF16),
            sds((n, r, QKV), BF16), sds((n, r, 2 * ff), BF16), sds((planes, chunk, width), BF16),
            sds((per_pair,) + w_o.shape, BF16), sds(rows + (width,), BF16), sds(rows + (3 * SIDE,), BF16),
            sds((GROUP, 2, 2, length, length), BF16), sds((GROUP, 2, length, length), BF16), sds(rows + (SIDE,), BF16),
            sds(rows + (width,), BF16), sds((length, width), F32), sds((8, width), F32), sds((GROUP, 8, length), F32),
        ),
        in_specs=[hbm] * 9 + [vmem] + [smem] * 2,
        out_specs=(hbm,) * 12 + (vmem,) * 3,
        scratch_shapes=[
            v32(*kern.shape), v32(*mix.shape), v16(*w_qkv.shape), v16(PLANE, r, QKV), v16(PLANE, r, 2 * ff), v32(8, length), v32(n, 8, 128), v16(length, width), v16(chunk, width), v16(*w_o.shape),
            v16(*rows, width), v16(n, r, QKV), v16(pad_rows, *w_o.shape),
            v16(2, 3 * length, taps), v16(length, 3 * length), v32(length + 8, taps),
            v16(*rows, 3 * SIDE), v16(GROUP, 2, 2, length, length), v16(GROUP, 2, length, length), v16(*rows, SIDE),
            v32(GROUP, 8, length), v16(length, width), v16(length, width),
            *Scatter.scratch(length, width),
            dma((3, Gather.SENDS)), dma((3, Gather.RECVS)), dma((3,)), dma((2 * PLANE,)), dma((2 * PLANE,)),
            dma((3, planes)), dma((3, planes)), dma((3,)), dma((2,)), dma((GROUP,)), dma((GROUP,)), dma((PLANE + planes,)), dma((PLANE + planes,)), pltpu.SemaphoreType.REGULAR((2,)),
            dma((8,)), dma((2, PLANE, planes)), dma((GROUP,)), dma((5, GROUP)),
        ],
        compiler_params=pltpu.CompilerParams(collective_id=1, has_side_effects=True, vmem_limit_bytes=60 * 2**20),
        name="attention_forward",
    )(tok, ct, w_qkv, w_gate, w_up, w_down, w_o, kern, mix, gain_rows, docs, pads)


def feed_kernel(cfg, *refs):
    (mid_all, ct_all, w_b, w_d, resid, gains,
     g_res, branch_all, dw_b, sum_d, sum_first, out_red, g_mid_gain,
     mid_v, ct_v, wb_v, wd_v, hid_v, gu_v, tile_v, dd_v, zd_v, via_v, sd_v, first_v, zf_v, via_f, sf_v,
     o_out, o_red, o_send, o_recv,
     m_out, m_red, m_diag, m_near, m_send, m_recv,
     g_send, g_recv, g_loc, z_send, z_recv, loc, row_in, out_sem) = refs
    length, width = resid.shape
    ff = cfg["ff"]
    me = Place(cfg["planes"])
    wb_in = pltpu.make_async_copy(w_b, wb_v, loc.at[0])
    wb_in.start()
    wd_in = pltpu.make_async_copy(w_d, wd_v, loc.at[1])
    wd_in.start()

    def row_copies(row):
        return (
            pltpu.make_async_copy(mid_all.at[row], mid_v.at[row], row_in.at[0, row]),
            pltpu.make_async_copy(ct_all.at[row], ct_v.at[row], row_in.at[1, row]),
        )

    for i in range(2):
        for cp in row_copies(order(me, i)[0]):
            cp.start()
    me.greet()
    sum_out = Scatter(me, o_out, o_red, None, None, o_send, o_recv)
    down_sum = Collect(me, lambda b: dd_v.at[pl.ds(b, 1)], zd_v, via_v, z_send.at[0], z_recv.at[0])
    down_sum.clear()
    first_sum = Collect(me, lambda b: first_v.at[b], zf_v, via_f, z_send.at[1], z_recv.at[1])
    first_sum.clear()
    sum_mid = Scatter(me, m_out, m_red, m_diag, m_near, m_send, m_recv)
    wb_in.wait()
    wd_in.wait()
    for i in range(2, GROUP):
        for cp in row_copies(order(me, i)[0]):
            cp.start()

    def one(i, carry):
        row, k = order(me, i)
        for cp in row_copies(row):
            cp.wait()
        wb = wb_v[...].reshape(width, 2 * ff)
        wd = wd_v[...].reshape(ff, width)
        pre = nn(mid_v[row], wb)
        gate, up = pre[:, :ff], pre[:, ff:]
        g_hidden = nt(ct_v[row], wd)
        sig = jax.nn.sigmoid(gate)
        silu = gate * sig
        hid_v[row] = (silu * up).astype(BF16)
        gu_v[row, :, :ff] = (g_hidden * up * sig * (1.0 + gate * (1.0 - sig))).astype(BF16)
        gu_v[row, :, ff:] = (g_hidden * silu).astype(BF16)
        mid_part = nt(gu_v[row], wb)

        @pl.when(lax.rem(i, 2) == 0)
        def _():
            sum_mid.put_sib(k, mid_part)

        @pl.when(lax.rem(i, 2) == 1)
        def _():
            sum_mid.put_self(k, mid_part)

        sum_mid.push(i)
        return carry

    def output(i, carry):
        row, k = order(me, i)
        out_part = nn(hid_v[row], wd_v[...].reshape(ff, width))

        @pl.when(lax.rem(i, 2) == 0)
        def _():
            sum_out.put_sib(k, out_part)

        @pl.when(lax.rem(i, 2) == 1)
        def _():
            sum_out.put_self(k, out_part)

        return carry

    lax.fori_loop(0, GROUP, one, 0)

    tokens = GROUP * length
    tile = SIDE

    def down(i, carry):
        at = pl.ds(pl.multiple_of(i * tile, tile), tile)
        value = tn(hid_v[:, :, at].reshape(tokens, tile), ct_v[...].reshape(tokens, width)).astype(BF16)
        per = tile // dd_v.shape[1]
        dd_v[pl.ds(i * per, per)] = value.reshape((per,) + dd_v.shape[1:])
        return carry

    lax.fori_loop(0, ff // tile, down, 0)
    down_sum.start()

    steps = width // tile

    def tile_out(i):
        slot = lax.rem(i, 2)
        at = pl.ds(pl.multiple_of(i * tile, tile), tile)
        return pltpu.make_async_copy(tile_v.at[slot], dw_b.at[at], out_sem.at[slot])

    def gate_up(i, carry):
        @pl.when(i >= 2)
        def _():
            tile_out(i - 2).wait()

        at = pl.ds(pl.multiple_of(i * tile, tile), tile)
        value = tn(mid_v[:, :, at].reshape(tokens, tile), gu_v[...].reshape(tokens, 2 * ff)).astype(BF16)
        tile_v[lax.rem(i, 2)] = value
        tile_out(i).start()
        r = first_v.shape[2]
        for z in range(first_v.shape[0]):
            for q in range(FIRST):
                lo = (z * PLANE + q) * r
                for tile_at in range(lo // tile, (lo + r - 1) // tile + 1):
                    begin, end = max(lo, tile_at * tile), min(lo + r, (tile_at + 1) * tile)

                    @pl.when(i == tile_at)
                    def _():
                        first_v[z, q, begin - lo : end - lo] = value[begin - tile_at * tile : end - tile_at * tile]

        return carry

    lax.fori_loop(0, steps, gate_up, 0)
    first_sum.start()
    g_mid_gain[...] = jnp.zeros(g_mid_gain.shape, F32)
    sum_mid.arrive()

    def middle(at):
        g_mid = sum_mid.total(at)
        res = resid[at]
        s = lax.rsqrt(jnp.mean(res * res, axis=-1, keepdims=True) + 1e-6)
        g_mid_gain[0:1] = g_mid_gain[0:1] + jnp.sum(g_mid * res * s, axis=0, keepdims=True)
        pulled = g_mid * gains[1:2]
        back = ct_v[me.slot, at].astype(F32) + s * pulled
        back = back - res * (s * s * s * jnp.mean(pulled * res, axis=-1, keepdims=True))
        g_res[at] = back
        ct_v[me.slot, at] = back.astype(BF16)

    strips(length, middle)
    branch = Gather(me, ct_v.at[me.slot], branch_all, g_send, g_recv, g_loc.at[0])
    branch.start()

    lax.fori_loop(0, GROUP, output, 0)
    red_out = pltpu.make_async_copy(o_red, out_red, out_sem.at[2])
    red_out.start()
    down_sum.combine(lambda t: dd_v.at[pl.ds(t, 1)])
    branch.relay()
    first_sum.combine(lambda t: first_v.at[t])
    branch.share()
    branch.last()
    down_sum.total(sd_v, dd_v.at[pl.ds(me.g, 1)])
    sd_out = pltpu.make_async_copy(sd_v.at[0], sum_d, out_sem.at[3])
    sd_out.start()
    first_sum.total(sf_v, first_v.at[me.g])
    sf_out = pltpu.make_async_copy(sf_v, sum_first, out_sem.at[4])
    sf_out.start()
    branch.finish()
    sum_mid.finish_cores()
    sum_mid.finish_chips()
    sum_out.finish_cores()
    down_sum.finish()
    first_sum.finish()
    tile_out(steps - 2).wait()
    tile_out(steps - 1).wait()
    red_out.wait()
    sd_out.wait()
    sf_out.wait()


def feed_call(cfg, mid_all, ct_all, w_b, w_d, resid, gains):
    length, width = resid.shape
    ff = cfg["ff"]
    hbm, vmem = pl.BlockSpec(memory_space=pl.ANY), pl.BlockSpec(memory_space=pltpu.VMEM)
    sds = jax.ShapeDtypeStruct
    dma = pltpu.SemaphoreType.DMA
    rows = (GROUP, length)
    chunk = ff // cfg["planes"]
    others = cfg["planes"] - 1
    r = w_b.shape[1]
    v16 = lambda *shape: pltpu.VMEM(shape, BF16)
    return pl.pallas_call(
        functools.partial(feed_kernel, cfg),
        out_shape=(
            sds((length, width), F32), sds(rows + (width,), BF16),
            sds((width, 2 * ff), BF16), sds((chunk, width), BF16), sds((FIRST, r, 2 * ff), BF16), sds((4, length, width), BF16), sds((8, width), F32),
        ),
        in_specs=[hbm] * 4 + [vmem] * 2,
        out_specs=(vmem, hbm, hbm, hbm, hbm, hbm, vmem),
        scratch_shapes=[
            v16(*rows, width), v16(*rows, width), v16(*w_b.shape), v16(*w_d.shape), v16(*rows, ff), v16(*rows, 2 * ff),
            v16(2, SIDE, 2 * ff), v16(others + 1, chunk, width), v16(others, 1, chunk, width), v16(1, chunk, width), v16(1, chunk, width),
            v16(others + 1, FIRST, r, 2 * ff), v16(others, FIRST, r, 2 * ff), v16(FIRST, r, 2 * ff), v16(FIRST, r, 2 * ff),
            *Scatter.scratch(length, width, chips=False), *Scatter.scratch(length, width),
            dma((Gather.SENDS,)), dma((Gather.RECVS,)), dma((1,)), dma((2, others + 1)), dma((2, others + 1)),
            dma((2,)), dma((2, GROUP)), dma((5,)),
        ],
        compiler_params=pltpu.CompilerParams(collective_id=2, has_side_effects=True, vmem_limit_bytes=52 * 2**20),
        name="feed_forward",
    )(mid_all, ct_all, w_b, w_d, resid, gains)


def backward_kernel(cfg, *refs):
    (branch_all, o_all, a_all, nrm_all, qkv_all, p_all, m_all, gated_all, dw_b, sum_d, sum_first, out_red, tok,
     resid, kern_in, mix_in, g_res, gains, ends, g_mid_gain,
     g_tokens, layer_out, out_a, out_c, out_b, out_d, out_o, out_small, out_line,
     kern, mix, gb_v, wo_v, wa_v, nrm_v, qkv_v, p_v, m_v, t_v, cat_v, shift_v, corr_v, gq_v, da_v, dc_v, do_v, tok_v, rows_v, line_v, taps_v,
     zb_v, za_v, zc_v, zo_v, via_b, via_a, via_c, via_o, sb_v, sa_v, sc_v, so_v, far_b, strip_v, sd_v, small_v, small_in, last_v, last_in,
     s_out, s_red, s_diag, s_near, rs_send, rs_recv,
     l_red, l_diag, l_near, l_send, l_recv,
     z_send, z_recv, small_send, small_recv, line_send, line_recv, t_send, t_recv, loc, row_in) = refs
    planes, dh, taps_q, taps_k = cfg["planes"], cfg["dh"], cfg["kq"], cfg["kk"]
    length, width = tok.shape
    scale = dh ** (-0.5)
    me = Place(planes)
    per_pair = o_all.shape[0]
    r = a_all.shape[1]
    far = jnp.where(me.g == 1, planes - 1, 0)
    loads = [
        pltpu.make_async_copy(src, dst, loc.at[i])
        for i, (src, dst) in enumerate(
            [(a_all, wa_v), (o_all, wo_v.at[pl.ds(0, per_pair)]), (tok, tok_v)]
            + [(dw_b.at[pl.ds(me.g * PLANE + FIRST, PLANE - FIRST)], sb_v.at[pl.ds(FIRST, PLANE - FIRST)]), (sum_first, sb_v.at[pl.ds(0, FIRST)])]
            + [(dw_b.at[pl.ds(far * PLANE + FIRST, PLANE - FIRST)], far_b), (out_red, l_red), (sum_d, sd_v)]
        )
    ]

    span = PLANE * r

    turns = ((3, 2, 1, 0), (0, 2, 3, 1), (3, 1, 0, 2), (0, 1, 2, 3))

    def turn_of(i):
        return sum(jnp.where(me.g == b, turns[b][i], 0) for b in range(planes))

    def nrm_copy(m):
        at = pl.ds(pl.multiple_of(turn_of(m % planes) * span, 128), span)
        return pltpu.make_async_copy(nrm_all.at[:, :, at], nrm_v.at[m % 2], loc.at[8 + m % 2])

    def row_copies(i):
        row = order(me, i)[0]
        at = lax.rem(i, SLOTS)
        cps = [pltpu.make_async_copy(branch_all.at[row], gb_v.at[row], row_in.at[0, i])]
        for j, (src, dst) in enumerate(((qkv_all, qkv_v), (p_all, p_v), (m_all, m_v))):
            cps.append(pltpu.make_async_copy(src.at[row], dst.at[at], row_in.at[j + 1, i]))
        return cps

    taps_in = [pltpu.make_async_copy(kern_in, kern, loc.at[10]), pltpu.make_async_copy(mix_in, mix, loc.at[11])]
    for cp in taps_in:
        cp.start()
    wo_v[...] = jnp.zeros(wo_v.shape, BF16)
    loads[1].start()
    loads[0].start()
    for i in range(SLOTS):
        for cp in row_copies(i):
            cp.start()
    for cp in loads[2:]:
        cp.start()
    for j in range(2):
        nrm_copy(j).start()
    for cp in taps_in:
        cp.wait()
    for g in range(2):
        for a, t in bands(kern, 2 * me.pair + g, length, True):
            t_v[g, a * length : (a + 1) * length] = t.astype(BF16)
    shift_v[length:] = jnp.zeros((8, length), F32)
    corr_v[...] = jnp.zeros(corr_v.shape, F32)
    rows_v[...] = jnp.zeros(rows_v.shape, F32)
    small_v[...] = jnp.zeros(small_v.shape, F32)
    me.greet()

    blocks4 = lambda ref: (lambda b: ref.at[pl.ds(b * PLANE, PLANE)])
    sum_b = Collect(me, lambda b: dw_b.at[pl.ds(b * PLANE + FIRST, PLANE - FIRST)], zb_v, via_b, z_send.at[0], z_recv.at[0])
    sum_a = Collect(me, blocks4(da_v), za_v, via_a, z_send.at[1], z_recv.at[1])
    sum_c = Collect(me, blocks4(dc_v), zc_v, via_c, z_send.at[3], z_recv.at[3])
    sum_o = Collect(me, lambda b: do_v.at[pl.ds(b, 1)], zo_v, via_o, z_send.at[2], z_recv.at[2])
    send_s = []
    for d in range(1, planes):
        to = lax.rem(me.g + d, planes)
        send_s.append(remote(small_v, small_in.at[d - 1], small_send.at[d - 1], small_recv.at[d - 1], me.plane_dev(to)))
    send_l = []
    for d in range(1, planes):
        to = lax.rem(me.g + d, planes)
        send_l.append(remote(last_v, last_in.at[d - 1], line_send.at[d - 1], line_recv.at[d - 1], me.plane_dev(to)))
    sum_b.start()
    for group in (sum_b, sum_a, sum_c, sum_o):
        group.clear()
    h0, h1 = head_lanes(length, dh)
    scatter = Scatter(me, s_out, s_red, s_diag, s_near, rs_send, rs_recv)
    layer = Scatter(me, None, l_red, l_diag, l_near, l_send, l_recv)
    def to_slot(d):
        to = lax.rem(me.slot + d, GROUP)
        return lax.div(to, PLANE), lax.rem(to, PLANE)

    def group_copies(kind, src_of, landing, places=None):
        def one_of(d):
            y, sl = to_slot(d)
            return remote(src_of(sl), landing.at[me.slot], t_send.at[kind, d], t_recv.at[kind, d], (y, me.g * PLANE + sl))

        own = pltpu.make_async_copy(src_of(me.s), landing.at[me.slot], t_send.at[kind, 0])
        cps = [one_of(d) for d in range(1, GROUP)] + [own]
        for d, cp in enumerate(cps, 1):
            if places is None:
                cp.start()
            else:
                sl = to_slot(d % GROUP)[1]
                pl.when((sl >= places[0]) & (sl < places[1]))(cp.start)
        return cps

    def group_wait(kind, cps, landing):
        for d in range(1, GROUP):
            fr = lax.rem(me.slot - d + GROUP, GROUP)
            remote(landing.at[fr], landing.at[fr], t_send.at[kind, d], t_recv.at[kind, d], me.sib).wait_recv()
        for cp in cps[:-1]:
            cp.wait_send()
        cps[-1].wait()

    loads[0].wait()
    loads[1].wait()
    loads[5].wait()
    loads[6].wait()
    layer.push(1)
    layer.push(3)
    layer.ahead()
    loads[4].wait()
    group_copies(0, lambda sl: sb_v.at[sl], out_b, (0, FIRST))
    loads[7].wait()
    d_cp = remote(sd_v, out_d.at[me.y], t_send.at[3, 0], t_recv.at[3, 0], me.yn)
    d_cp.start()
    d_here = pltpu.make_async_copy(sd_v, out_d.at[me.y], t_send.at[3, 1])
    d_here.start()

    mixing = pair_mixing(mix, me.pair)

    def one(i, carry):
        row, k = order(me, i)
        at = lax.rem(i, SLOTS)
        for cp in row_copies(i):
            cp.wait()
        wo = wo_v[...].reshape(wo_v.shape[0] * wo_v.shape[1], width)[0:SIDE]
        q, kk, v = qkv_v[at, :, 0:SIDE], qkv_v[at, :, SIDE : 2 * SIDE], qkv_v[at, :, 2 * SIDE : 3 * SIDE]
        parts = [nn(p_v[at, g, 0], v) + nn(p_v[at, g, 1], v) for g in range(2)]
        probs = [p_v[at, g, 0].astype(F32) + p_v[at, g, 1].astype(F32) for g in range(2)]
        lane_mix = [mix_lanes(mixing, g, dh) for g in range(2)]
        attended = parts[0] * lane_mix[0] + parts[1] * lane_mix[1]
        centred = jnp.where(h0 | h1, attended - head_stats(attended, dh, h0, h1), 0.0)
        inv = lax.rsqrt(head_stats(centred * centred, dh, h0, h1) + 1e-5)
        normal = centred * inv
        g_gated = nt(gb_v[row], wo)
        rows_v[0:1] = rows_v[0:1] + jnp.sum(g_gated * normal, axis=0, keepdims=True)
        u = g_gated * gains[2:3, 0:SIDE]
        g_att = inv * (u - head_stats(u, dh, h0, h1) - normal * head_stats(u * normal, dh, h0, h1))
        g_exact = jnp.where(h0 | h1, g_att, 0.0)
        g_att = g_exact.astype(BF16).astype(F32)
        ok = allowed_mask(length, ends[row, 0:1, :])
        g_q = jnp.zeros((length, SIDE), F32)
        g_k = jnp.zeros((length, SIDE), F32)
        g_v = jnp.zeros((length, SIDE), F32)
        for o in range(2):
            mixed = mixing[o][0] * probs[0] + mixing[o][1] * probs[1]
            g_v = g_v + tn(mixed.astype(BF16), jnp.where(h0 if o == 0 else h1, g_att, 0.0).astype(BF16))
        for g in range(2):
            mine = h0 if g == 0 else h1
            rows_v[1 + g : 2 + g] = rows_v[1 + g : 2 + g] + jnp.sum(g_exact * parts[g], axis=0, keepdims=True)
            g_out = (g_att * lane_mix[g]).astype(BF16)
            g_probs = nt(g_out, v)
            g_conv = probs[g] * (g_probs - jnp.sum(probs[g] * g_probs, axis=-1, keepdims=True))
            shift_v[0:length] = g_conv
            for a in range(taps_q):
                cat_v[:, a * length : (a + 1) * length] = shift_v[a : a + length].astype(BF16)
            corr_v[g] = corr_v[g] + tn(m_v[at, g], cat_v[...])
            g_raw = jnp.where(ok, nn(cat_v[...], t_v[g]), 0.0).astype(BF16)
            g_q = g_q + nn(g_raw, jnp.where(mine, kk.astype(F32), 0.0).astype(BF16))
            g_k = g_k + tn(g_raw, jnp.where(mine, q.astype(F32), 0.0).astype(BF16))
        g_q, g_k = g_q * scale, g_k * scale
        mid_tile = g_q[:, 128:256] + pltpu.roll(g_v[:, 128:256], 64, 1)
        packed = jnp.concatenate([g_q[:, 0:128], mid_tile, g_k, g_v[:, 0:128]], axis=1).astype(BF16)
        gq_v[row] = packed
        part = nt(packed, wa_v[...].reshape(width, QKV))

        @pl.when(lax.rem(i, 2) == 0)
        def _():
            scatter.put_sib(k, part)

        @pl.when(lax.rem(i, 2) == 1)
        def _():
            scatter.put_self(k, part)

        scatter.push(i, turn=False)

        @pl.when(i + SLOTS < GROUP)
        def _():
            for cp in row_copies(i + SLOTS):
                cp.start()

        @pl.when(i == 4)
        def _():
            layer.turn()

        @pl.when(i == 5)
        def _():
            sum_b.combine(lambda t: far_b)

        return carry

    lax.fori_loop(0, GROUP, one, 0)
    for i in (2, 3):
        loads[i].wait()
    gated_in = [
        pltpu.make_async_copy(gated_all.at[i], p_v.at[i // 4, i // 2 % 2, i % 2], row_in.at[0, i]) for i in range(GROUP)
    ]
    for cp in gated_in:
        cp.start()

    def taps(at, carry):
        g, a = lax.div(at, taps_q), lax.rem(at, taps_q)
        lanes_at = pl.ds(pl.multiple_of(a * length, length), length)
        e = corr_v[g, :, lanes_at]
        diff = lax.broadcasted_iota(jnp.int32, (length, length), 0) - lax.broadcasted_iota(jnp.int32, (length, length), 1)
        for b in range(taps_k):
            line = jnp.sum(jnp.where(diff == b - taps_k // 2, e, 0.0), axis=0, keepdims=True)
            taps_v[b : b + 1] = line[:, 0:128] + line[:, 128:256]
        each = jnp.sum(taps_v[...], axis=-1, keepdims=True)
        small_v[0] = jnp.where(lanes(16, 128) == a * 2 * GROUP + 2 * me.pair + g, each, small_v[0])
        return carry

    taps_v[...] = jnp.zeros(taps_v.shape, F32)
    lax.fori_loop(0, 2 * taps_q, taps, 0)
    base = 1
    at = lanes(1, SIDE)
    for o in range(2):
        for g in range(2):
            line = jnp.where((at >= o * dh) & (at < (o + 1) * dh), rows_v[1 + g : 2 + g], 0.0)
            small_v[base, 2 * o + g : 2 * o + g + 1] = line[:, 0:128] + line[:, 128:256]
    for j in range(2):
        small_v[base, 4 + j : 5 + j] = rows_v[0:1, j * 128 : (j + 1) * 128]

    for j in range(width // 128):
        small_v[2, j : j + 1] = g_mid_gain[0:1, j * 128 : (j + 1) * 128]
    for cp in send_s:
        cp.start()

    tokens = GROUP * length
    for cp in gated_in:
        cp.wait()
    value = tn(p_v[...].reshape(tokens, SIDE), gb_v[...].reshape(tokens, width))
    do_v[...] = value[0 : 2 * dh].astype(BF16).reshape(do_v.shape)

    sum_o.start()
    for m in range(2 * planes):
        i, first_part = m % planes, m < planes
        nrm_copy(m).wait()
        at = slice(0, SIDE) if first_part else slice(SIDE, QKV)
        value = tn(nrm_v[m % 2].reshape(tokens, span), gq_v[:, :, at].reshape(tokens, at.stop - at.start))
        terms = da_v if first_part else dc_v
        terms[pl.ds(turn_of(i) * PLANE, PLANE)] = value.astype(BF16).reshape((PLANE,) + terms.shape[1:])
        if m + 2 < 2 * planes:
            nrm_copy(m + 2).start()
    for way in (True, False):
        sum_a.start((way,))
        sum_c.start((way,))
    scatter.turn()
    sum_b.total(sb_v.at[pl.ds(FIRST, PLANE - FIRST)], sb_v.at[pl.ds(FIRST, PLANE - FIRST)])
    b_cps = group_copies(0, lambda sl: sb_v.at[sl], out_b, (FIRST, PLANE))

    for cp in send_s:
        cp.wait_recv()
    for cp in send_s:
        cp.wait_send()
    small_v[...] = small_v[...] + sum(small_in[d] for d in range(planes - 1))
    small_cps = group_copies(2, lambda sl: small_v, out_small)

    sum_o.combine(lambda t: do_v.at[pl.ds(t, 1)])
    sum_a.combine(lambda t: da_v.at[pl.ds(t * PLANE, PLANE)])

    sum_c.combine(lambda t: dc_v.at[pl.ds(t * PLANE, PLANE)])

    layer.arrive()

    def result(at):
        cp = pltpu.make_async_copy(resid.at[at], strip_v, loc.at[0])
        cp.start()
        cp.wait()
        strip_v[...] = strip_v[...] + layer.total(at)
        cp = pltpu.make_async_copy(strip_v, layer_out.at[at], loc.at[0])
        cp.start()
        cp.wait()

    strips(length, result)

    scatter.arrive()

    def middle(at):
        g_normed = scatter.total(at)
        tok32 = tok_v[at].astype(F32)
        s = lax.rsqrt(jnp.mean(tok32 * tok32, axis=-1, keepdims=True) + 1e-6)
        line_v[0:1] = line_v[0:1] + jnp.sum(g_normed * tok32 * s, axis=0, keepdims=True)
        pulled = g_normed * gains[0:1]
        back = g_res[at] + s * pulled
        g_tokens[at] = back - tok32 * (s * s * s * jnp.mean(pulled * tok32, axis=-1, keepdims=True))

    line_v[...] = jnp.zeros(line_v.shape, F32)
    strips(length, middle)
    line = line_v[0:1]
    last_v[...] = jnp.zeros(last_v.shape, F32)
    for j in range(width // 128):
        last_v[j : j + 1] = line[:, j * 128 : (j + 1) * 128]
    for cp in send_l:
        cp.start()

    sum_o.total(so_v, do_v.at[pl.ds(me.g, 1)])
    o_to = me.pair * per_pair + lax.div(me.g, 2)
    o_half = lax.rem(me.g, 2)

    def o_copy(y):
        return remote(so_v.at[0], out_o.at[o_half], t_send.at[4, y], t_recv.at[4, o_half], (y, o_to))

    o_here = pltpu.make_async_copy(so_v.at[0], out_o.at[o_half], t_send.at[4, 2])

    def o_each(act, act_here):
        for y in range(2):
            mine = (y == me.y) & (o_to == me.f)

            @pl.when(jnp.logical_not(mine))
            def _():
                act(o_copy(y))

            @pl.when(mine)
            def _():
                act_here(o_here)

    o_each(lambda cp: cp.start(), lambda cp: cp.start())
    sum_a.total(sa_v, da_v.at[pl.ds(me.g * PLANE, PLANE)])
    a_cps = group_copies(1, lambda sl: sa_v.at[sl], out_a)

    sum_c.total(sc_v, dc_v.at[pl.ds(me.g * PLANE, PLANE)])
    c_cps = group_copies(5, lambda sl: sc_v.at[sl], out_c)

    for cp in send_l:
        cp.wait_recv()
    for cp in send_l:
        cp.wait_send()
    last_v[...] = last_v[...] + sum(last_in[d] for d in range(planes - 1))
    line_cps = group_copies(6, lambda sl: last_v, out_line)

    group_wait(2, small_cps, out_small)
    d_cp.wait_send()
    remote(out_d.at[1 - me.y], out_d.at[1 - me.y], t_send.at[3, 0], t_recv.at[3, 0], me.yn).wait_recv()
    d_here.wait()
    group_wait(0, b_cps, out_b)
    src_y = jnp.where((me.g == 1) | (me.g == 2), 1, 0)
    src_s = me.x * 2 + jnp.where(me.g >= 2, 1, 0)
    for h in range(2):
        src_f = (2 * lax.rem(me.f, per_pair) + h) * PLANE + src_s

        @pl.when(jnp.logical_not((src_y == me.y) & (src_f == me.f)))
        def _():
            remote(out_o.at[h], out_o.at[h], t_send.at[4, 0], t_recv.at[4, h], me.sib).wait_recv()

    o_each(lambda cp: cp.wait_send(), lambda cp: cp.wait())
    group_wait(1, a_cps, out_a)
    group_wait(5, c_cps, out_c)
    group_wait(6, line_cps, out_line)
    for group in (sum_b, sum_a, sum_c, sum_o):
        group.finish()
    scatter.finish_cores()
    scatter.finish_chips()
    layer.finish_chips()


def backward_call(cfg, *args):
    branch_all, o_all, a_all, tok = args[0], args[1], args[2], args[12]
    length, width = tok.shape
    planes, ff = cfg["planes"], cfg["ff"]
    n, r = a_all.shape[:2]
    chunk = ff // planes
    taps = cfg["kq"] * length
    pad_rows = -(-SIDE // o_all.shape[1])
    piece = 2 * cfg["dh"] // planes
    small = (3, 16, 128)
    hbm, vmem, smem = pl.BlockSpec(memory_space=pl.ANY), pl.BlockSpec(memory_space=pltpu.VMEM), pl.BlockSpec(memory_space=pltpu.SMEM)
    sds = jax.ShapeDtypeStruct
    dma = pltpu.SemaphoreType.DMA
    rows = (GROUP, length)
    others = planes - 1
    v16 = lambda *shape: pltpu.VMEM(shape, BF16)
    v32 = lambda *shape: pltpu.VMEM(shape, F32)
    b_block, o_block = (PLANE - FIRST, r, 2 * ff), (1, piece, width)
    a_block, c_block = (PLANE, r, SIDE), (PLANE, r, QKV - SIDE)
    return pl.pallas_call(
        functools.partial(backward_kernel, cfg),
        out_shape=(
            sds((length, width), F32), sds((length, width), F32), sds((GROUP, r, SIDE), BF16), sds((GROUP, r, QKV - SIDE), BF16),
            sds((GROUP, r, 2 * ff), BF16),
            sds((2, chunk, width), BF16), sds((2, piece, width), BF16), sds((GROUP,) + small, F32), sds((GROUP, 16, 128), F32),
        ),
        in_specs=[hbm] * 16 + [vmem] * 4,
        out_specs=(vmem,) + (hbm,) * 8,
        scratch_shapes=[
            v32(*args[14].shape), v32(*args[15].shape), v16(*rows, width), v16(pad_rows, *o_all.shape[1:]), v16(n, r, QKV), v16(2, *rows, PLANE * r), v16(SLOTS, length, 3 * SIDE),
            v16(SLOTS, 2, 2, length, length), v16(SLOTS, 2, length, length),
            v16(2, taps, length), v16(length, taps), v32(length + 8, length), v32(2, length, taps), v16(*rows, QKV),
            v16(n, r, SIDE), v16(n, r, QKV - SIDE), v16(planes, piece, width), v16(length, width), v32(8, SIDE), v32(8, width), v32(16, 128),
            v16(others, *b_block), v16(others, *a_block), v16(others, *c_block), v16(others, *o_block),
            v16(*b_block), v16(*a_block), v16(*c_block), v16(*o_block),
            v16(PLANE, r, 2 * ff), v16(*a_block), v16(*c_block), v16(*o_block), v16(*b_block), v32(64, width), v16(chunk, width),
            v32(*small), v32(others, *small), v32(16, 128), v32(others, 16, 128),
            *Scatter.scratch(length, width), *Scatter.scratch(length, width, cores=False),
            dma((4, planes)), dma((4, planes)), dma((others,)), dma((others,)), dma((others,)), dma((others,)), dma((7, GROUP)), dma((7, GROUP)),
            dma((12,)), dma((4, GROUP)),
        ],
        compiler_params=pltpu.CompilerParams(collective_id=3, has_side_effects=True, vmem_limit_bytes=54 * 2**20),
        name="attention_backward",
    )(*args)


def results_kernel(cfg, a_ref, c_ref, b_ref, d_ref, o_ref, small_ref, line_ref, g_tok, layer, qkv_ref, gate_ref, up_ref, down_ref, out_ref,
                   taps_ref, mix_ref, in_ref, mid_ref, heads_ref, tok_ref, layer_ref, vec_v):
    planes, ff = cfg["planes"], cfg["ff"]
    rows, width = out_ref.shape
    chunk = ff // planes
    low = lanes(rows, 128) < 64

    def slot(pair):
        home, x = pair // 2, pair % 2
        y, c = (0, 1, 1, 0)[home], (0, 0, 1, 1)[home]
        return y * PLANE + x * 2 + c

    def joined(even, odd, low):
        o0, o1 = pltpu.roll(odd[0], 64, 1), pltpu.roll(odd[1], 64, 1)
        return even[0], jnp.where(low, even[1], o0), jnp.where(low, o0, o1)

    def tiles(pair, j):
        def t(i):
            ref, i = (a_ref, i) if i < 2 else (c_ref, i - 2)
            return ref[slot(pair), :, i * 128 : (i + 1) * 128].astype(F32)

        if j == 2:
            return t(4), pltpu.roll(t(1), 64, 1)
        return t(2 * j), t(2 * j + 1)

    for j in range(3):
        for two in range(GROUP // 2):
            for i, t in enumerate(joined(tiles(2 * two, j), tiles(2 * two + 1, j), low)):
                at = j * width + two * 384 + i * 128
                qkv_ref[:, at : at + 128] = t
    for z in range(planes):
        for s in range(PLANE):
            for y in range(2):
                at = ((z * PLANE + s) * 2 + y) * chunk
                src = b_ref.at[y * PLANE + s]
                gate_ref[:, at : at + chunk] = src[:, z * chunk : (z + 1) * chunk].astype(F32)
                up_ref[:, at : at + chunk] = src[:, ff + z * chunk : ff + (z + 1) * chunk].astype(F32)
    down_ref[...] = d_ref[0].astype(F32)
    out_ref[...] = o_ref[0].astype(F32)

    tok_ref[...] = g_tok[...]
    layer_ref[...] = layer[...]

    @pl.when(pl.program_id(0) == 0)
    def _():
        base = 1
        heads = 2 * GROUP
        taps = small_ref[0, 0]
        for s in range(1, GROUP):
            taps = taps + small_ref[s, 0]
        for k in range(cfg["kk"]):
            for q in range(cfg["kq"]):
                taps_ref[k, q : q + 1] = taps[k : k + 1, q * heads : (q + 1) * heads]
        mixed = [jnp.sum(small_ref[slot(pair), base], axis=-1, keepdims=True) for pair in range(GROUP)]
        for g in range(2):
            line = jnp.zeros((1, heads), F32)
            for pair in range(GROUP):
                for o in range(2):
                    k = 2 * o + g
                    line = jnp.where(lanes(1, heads) == 2 * pair + o, mixed[pair][k : k + 1], line)
            mix_ref[g : g + 1] = line
        vec_v[...] = jnp.zeros(vec_v.shape, F32)
        for k, part in enumerate((lambda s: line_ref[s], lambda s: small_ref[s, base + 1])):
            total = part(0)
            for s in range(1, GROUP):
                total = total + part(s)
            for j in range(width // 128):
                vec_v[k : k + 1, j * 128 : (j + 1) * 128] = total[j : j + 1]
        line = lambda pair: tuple(small_ref[slot(pair), base, 4 + j : 5 + j] for j in range(2))
        for two in range(GROUP // 2):
            for i, t in enumerate(joined(line(2 * two), line(2 * two + 1), lanes(1, 128) < 64)):
                vec_v[2:3, two * 384 + i * 128 : two * 384 + (i + 1) * 128] = t
        own = in_ref.shape[1]
        mine = pltpu.roll(vec_v[...], lax.rem(width - lax.axis_index("fsdp") * own, width), 1)
        for k, ref in enumerate((in_ref, mid_ref, heads_ref)):
            ref[...] = mine[k : k + 1, 0:own]


def results_call(cfg, out_a, out_c, out_b, out_d, out_o, small, line, g_tokens, layer_out):
    r = out_a.shape[1]
    _, chunk, width = out_d.shape
    half = r // 2
    sds = jax.ShapeDtypeStruct
    whole = lambda shape: pl.BlockSpec(shape, lambda i: (0,) * len(shape))
    rows = lambda n, w: pl.BlockSpec((n, w), lambda i: (i, 0))
    moved = 6 * (out_a.size + out_c.size + out_b.size + out_d.size + out_o.size) + 16 * g_tokens.size
    return pl.pallas_call(
        functools.partial(results_kernel, cfg),
        grid=(2,),
        out_shape=(
            sds((r, 3 * width), F32), sds((r, n_cols(cfg)), F32), sds((r, n_cols(cfg)), F32), sds((2 * chunk, width), F32),
            sds((r, width), F32), sds((cfg["kk"], cfg["kq"], 2 * GROUP), F32), sds((2, 2 * GROUP), F32),
            sds((1, r), F32), sds((1, r), F32), sds((1, r), F32), sds(g_tokens.shape, F32), sds(g_tokens.shape, F32),
        ),
        in_specs=[
            pl.BlockSpec((GROUP, half, out_a.shape[2]), lambda i: (0, i, 0)),
            pl.BlockSpec((GROUP, half, out_c.shape[2]), lambda i: (0, i, 0)),
            pl.BlockSpec((GROUP, half, out_b.shape[2]), lambda i: (0, i, 0)),
            pl.BlockSpec((1, chunk, width), lambda i: (i, 0, 0)),
            pl.BlockSpec((1, half, width), lambda i: (i, 0, 0)),
            whole(small.shape),
            whole(line.shape),
            rows(g_tokens.shape[0] // 2, width),
            rows(g_tokens.shape[0] // 2, width),
        ],
        scratch_shapes=[pltpu.VMEM((8, width), F32)],
        out_specs=(
            rows(half, 3 * width), rows(half, n_cols(cfg)), rows(half, n_cols(cfg)), rows(chunk, width), rows(half, width),
            whole((cfg["kk"], cfg["kq"], 2 * GROUP)), whole((2, 2 * GROUP)),
            whole((1, r)), whole((1, r)), whole((1, r)), rows(g_tokens.shape[0] // 2, width), rows(g_tokens.shape[0] // 2, width),
        ),
        compiler_params=pltpu.CompilerParams(vmem_limit_bytes=60 * 2**20),
        cost_estimate=pl.CostEstimate(flops=0, bytes_accessed=moved, transcendentals=0),
        name="results",
    )(out_a, out_c, out_b, out_d, out_o, small, line, g_tokens, layer_out)


def n_cols(cfg):
    return cfg["ff"] * GROUP


def fits(mesh, tokens, kernel, w_gate):
    n = mesh.shape["fsdp"]
    width, length, heads, ff = tokens.shape[2], tokens.shape[1], kernel.shape[0], w_gate.shape[1]
    return (
        mesh.shape["rep"] == 2
        and n == 4 * PLANE
        and heads == 2 * GROUP
        and width == heads * 96
        and (width // n) % 32 == 0
        and ff % (2 * n * 128) == 0
        and length == SIDE
    )


def per_device_group(
    planes,
    tokens,
    doc_lengths,
    pad_counts,
    norm_in,
    w_qkv,
    kernel,
    mixing,
    norm_heads,
    w_out,
    norm_mid,
    w_gate,
    w_up,
    w_down,
    cotangent,
):
    length, width = tokens.shape[1:]
    heads, kq, kk = kernel.shape
    dh = width // heads
    n = planes * PLANE
    r = width // n
    chunk = w_down.shape[0] // 2
    ff = planes * chunk
    cfg = dict(planes=planes, dh=dh, kq=kq, kk=kk, ff=ff)

    gain_rows = jnp.pad(jnp.stack([norm_in, norm_mid, norm_heads]).astype(F32), ((0, 5), (0, 128 - r)))
    tok, ct = tokens[0], cotangent[0]
    kern, mix = kernel.transpose(2, 1, 0), mixing.T

    (_, ct_all, a_all, b_all, d_all, o_all, nrm_all, qkv_all, p_all, m_all, gated_all, mid_all, resid, gains, ends) = (
        forward_call(
            cfg, tok, ct, w_qkv, w_gate, w_up, w_down, w_out, kern, mix, gain_rows, doc_lengths, pad_counts
        )
    )
    g_res, branch_all, dw_b, sum_d, sum_first, out_red, g_mid_gain = feed_call(cfg, mid_all, ct_all, b_all, d_all, resid, gains)
    g_tokens, layer_out, out_a, out_c, out_b, out_d, out_o, small, line = backward_call(
        cfg, branch_all, o_all, a_all, nrm_all, qkv_all, p_all, m_all, gated_all, dw_b.reshape(n, r, 2 * ff), sum_d, sum_first, out_red,
        tok, resid, kern, mix, g_res, gains, ends, g_mid_gain,
    )

    g_qkv, g_gate, g_up, g_down, g_out, g_kernel, g_mixing, g_in, g_mid, g_heads, g_tokens, layer_out = results_call(
        cfg, out_a, out_c, out_b, out_d, out_o, small, line, g_tokens, layer_out
    )
    return (
        layer_out[None],
        g_tokens[None],
        g_in[0],
        g_qkv,
        g_kernel.transpose(2, 1, 0),
        g_mixing.T,
        g_heads[0],
        g_out,
        g_mid[0],
        g_gate,
        g_up,
        g_down,
    )


def solution(mesh):
    in_specs = (
        P(("rep", "fsdp"), None, None),
        P(("rep", "fsdp"), None),
        P(("rep", "fsdp")),
        P("fsdp"),
        P("fsdp", None),
        P(),
        P(),
        P("fsdp"),
        P("fsdp", None),
        P("fsdp"),
        P("fsdp", None),
        P("fsdp", None),
        P("fsdp", None),
        P(("rep", "fsdp"), None, None),
    )
    out_specs = (
        P(("rep", "fsdp"), None, None),
        P(("rep", "fsdp"), None, None),
        P("fsdp"),
        P("fsdp", None),
        P(),
        P(),
        P("fsdp"),
        P("fsdp", None),
        P("fsdp"),
        P("fsdp", None),
        P("fsdp", None),
        P("fsdp", None),
    )

    def layer(*args):
        body = per_device
        if fits(mesh, args[0], args[5], args[10]):
            body = functools.partial(per_device_group, mesh.shape["fsdp"] // PLANE)
        return jax.shard_map(body, mesh=mesh, in_specs=in_specs, out_specs=out_specs, check_vma=False)(*args)

    return layer
```

```python
import functools

import jax
import jax.numpy as jnp
from jax import lax
from jax.experimental import pallas as pl
from jax.experimental.pallas import tpu as pltpu
from jax.sharding import PartitionSpec as P

F32 = jnp.float32
BF16 = jnp.bfloat16
NEG_FILL = -1e30
MESH = pl.DeviceIdType.MESH
PLANE = 4
GROUP = 8
SIDE = 256
FIRST = 1
SLOTS = 2
QKV = 640


class Place:
    def __init__(self, planes):
        self.planes = planes
        self.y = lax.axis_index("rep")
        self.f = lax.axis_index("fsdp")
        self.g = lax.div(self.f, PLANE)
        self.s = lax.rem(self.f, PLANE)
        self.x = lax.div(self.s, 2)
        self.c = lax.rem(self.s, 2)
        self.slot = self.y * PLANE + self.s
        self.home = self.y + self.c * (planes - 1 - 2 * self.y)
        self.pair = 2 * self.home + self.x
        self.sib = self.dev(self.y, self.x, 1 - self.c)
        self.xn = self.dev(self.y, 1 - self.x, self.c)
        self.yn = self.dev(1 - self.y, self.x, self.c)

    def dev(self, y, x, c):
        return (y, self.g * PLANE + x * 2 + c)

    def plane_dev(self, g):
        return (self.y, g * PLANE + self.s)

    def row(self, dy, dx, dc):
        y = self.y + dy - 2 * dy * self.y
        x = self.x + dx - 2 * dx * self.x
        c = self.c + dc - 2 * dc * self.c
        return y * 4 + x * 2 + c

    def hail(self):
        sem = pltpu.get_barrier_semaphore()
        n = self.planes * PLANE
        for d in range(1, n):
            pl.semaphore_signal(sem, inc=1, device_id=(self.y, lax.rem(self.f + d, n)), device_id_type=MESH)
        for s in range(PLANE):
            pl.semaphore_signal(sem, inc=1, device_id=(1 - self.y, self.g * PLANE + s), device_id_type=MESH)

    def await_all(self):
        pl.semaphore_wait(pltpu.get_barrier_semaphore(), self.planes * PLANE - 1 + PLANE)


def meet(me, sem):
    pl.semaphore_signal(sem, inc=1, device_id=me.sib, device_id_type=MESH)
    pl.semaphore_wait(sem, 1)


def remote(src, dst, send, recv, dev):
    return pltpu.make_async_remote_copy(
        src_ref=src, dst_ref=dst, send_sem=send, recv_sem=recv, device_id=dev, device_id_type=MESH
    )


class Gather:
    SENDS = 14
    RECVS = 14

    def __init__(self, me, own, buf, send, recv, local):
        self.me, self.own, self.buf = me, own, buf
        self.send, self.recv, self.local = send, recv, local
        self.half = own.shape[0] // 2
        self.sent = []

    def _own(self, h):
        return self.own.at[pl.ds(h * self.half, self.half)]

    def _blk(self, row, h):
        return self.buf.at[row, pl.ds(h * self.half, self.half)]

    def _copy(self, i):
        own, row, h, kind, dev = self.sent[i]
        src = self._own(h) if own else self._blk(row, h)
        return remote(src, self._blk(row, h), self.send.at[i], self.recv.at[kind * 2 + h], dev)

    def _go(self, own, row, h, kind, dev):
        self.sent.append((own, row, h, kind, dev))
        self._copy(len(self.sent) - 1).start()

    def _await(self, row, h, kind):
        b = self._blk(row, h)
        remote(b, b, self.send.at[0], self.recv.at[kind * 2 + h], self.me.sib).wait_recv()

    def start(self):
        me = self.me
        self.rows = [me.row(0, 0, 1), me.row(0, 1, 0), me.row(1, 0, 0), me.row(1, 1, 0), me.row(0, 1, 1), me.row(1, 0, 1), me.row(1, 1, 1)]
        self.here = pltpu.make_async_copy(self.own, self.buf.at[me.slot], self.local)
        self.here.start()
        self._go(True, me.slot, 0, 1, me.xn)
        self._go(True, me.slot, 1, 2, me.yn)
        self._go(True, me.slot, 0, 0, me.sib)
        self._go(True, me.slot, 1, 0, me.sib)
        self._go(True, me.slot, 1, 1, me.xn)
        self._go(True, me.slot, 0, 2, me.yn)

    def relay(self):
        me, rows = self.me, self.rows
        self._await(rows[1], 0, 1)
        self._go(False, rows[1], 0, 3, me.yn)
        self._go(False, rows[1], 0, 4, me.sib)
        self._await(rows[2], 1, 2)
        self._go(False, rows[2], 1, 3, me.xn)
        self._go(False, rows[2], 1, 5, me.sib)

    def share(self):
        me, rows = self.me, self.rows
        self._await(rows[1], 1, 1)
        self._go(False, rows[1], 1, 4, me.sib)
        self._await(rows[2], 0, 2)
        self._go(False, rows[2], 0, 5, me.sib)

    def last(self):
        me, rows = self.me, self.rows
        for h in (0, 1):
            self._await(rows[3], h, 3)
            self._go(False, rows[3], h, 6, me.sib)

    def finish(self):
        for kind in (0, 4, 5, 6):
            for h in (0, 1):
                self._await(self.rows[kind], h, kind)
        for i in range(len(self.sent)):
            self._copy(i).wait_send()
        self.here.wait()


class Scatter:
    SENDS = 10
    RECVS = 10

    @staticmethod
    def scratch(rows, width, cores=True, chips=True):
        bufs = []
        if cores:
            bufs.append(pltpu.VMEM((2, rows, width), BF16))
        bufs.append(pltpu.VMEM((4, rows, width), BF16))
        if chips:
            bufs += [pltpu.VMEM((2, rows // 2, width), BF16), pltpu.VMEM((2, rows, width), BF16)]
        return bufs + [pltpu.SemaphoreType.DMA((Scatter.SENDS,)), pltpu.SemaphoreType.DMA((Scatter.RECVS,))]

    def __init__(self, me, out, red, diag, near, send, recv):
        self.me, self.out, self.red, self.diag, self.near = me, out, red, diag, near
        self.send, self.recv = send, recv
        self.half = red.shape[1] // 2

    def _sib(self, k):
        return remote(self.out.at[lax.rem(k, 2)], self.red.at[k], self.send.at[k], self.recv.at[k], self.me.sib)

    def put_sib(self, k, value):
        @pl.when(k >= 2)
        def _():
            self._sib(k - 2).wait_send()

        self.out[lax.rem(k, 2)] = value.astype(BF16)
        self._sib(k).start()

    def put_self(self, k, value):
        self._sib(k).wait_recv()
        self.red[k] = (value + self.red[k].astype(F32)).astype(BF16)

    def _copy(self, name):
        h, me = self.half, self.me
        lo, hi = pl.ds(0, h), pl.ds(h, h)
        src, dst, i, dev = {
            "da": (self.red.at[0, lo], self.diag.at[0], 4, me.xn),
            "db": (self.red.at[0, hi], self.diag.at[1], 5, me.yn),
            "xa": (self.red.at[1, lo], self.near.at[0, lo], 6, me.xn),
            "xb": (self.red.at[1, hi], self.near.at[0, hi], 7, me.xn),
            "ya": (self.red.at[2, lo], self.near.at[1, lo], 8, me.yn),
            "yb": (self.red.at[2, hi], self.near.at[1, hi], 9, me.yn),
        }[name]
        return remote(src, dst, self.send.at[i], self.recv.at[i], dev)

    def push(self, i, turn=True):
        @pl.when(i == 1)
        def _():
            self._copy("da").start()
            self._copy("db").start()

        @pl.when(i == 3)
        def _():
            self._copy("xa").start()

        @pl.when(i == 5)
        def _():
            self._copy("yb").start()
            if turn:
                self.turn()

    def ahead(self):
        self._copy("yb").start()

    def turn(self):
        h = self.half
        self._copy("db").wait_recv()
        self.red[1, h:] = (self.red[1, h:].astype(F32) + self.diag[1].astype(F32)).astype(BF16)
        self._copy("xb").start()
        self._copy("da").wait_recv()
        self.red[2, :h] = (self.red[2, :h].astype(F32) + self.diag[0].astype(F32)).astype(BF16)
        self._copy("ya").start()

    def arrive(self):
        for name in ("xa", "xb", "ya", "yb"):
            self._copy(name).wait_recv()

    def total(self, at):
        return self.red[3, at].astype(F32) + self.near[0, at].astype(F32) + self.near[1, at].astype(F32)

    def finish_cores(self):
        for k in (2, 3):
            self._sib(k).wait_send()

    def finish_chips(self):
        for name in ("da", "db", "xa", "xb", "ya", "yb"):
            self._copy(name).wait_send()


class Spread:
    def __init__(self, me, blocks, send, recv):
        self.me, self.blocks, self.send, self.recv = me, blocks, send, recv

    def _copy(self, b, t, i):
        return remote(self.blocks(b), self.blocks(b), self.send.at[i], self.recv.at[b], self.me.plane_dev(t))

    def _sends(self, b):
        last = self.me.planes - 1
        if b in (0, last):
            return [(b, 1 if b == 0 else last - 1, 0)] + [(b, t, 1) for t in sorted(range(last + 1), key=lambda t: abs(t - b))[2:]]
        other, end = (2, 0) if b == 1 else (1, 3)
        return [(b, b - 1, 0), (b, b + 1, 0), (other, end, 1)]

    def _each(self, act, steps):
        for g in range(self.me.planes):

            @pl.when(self.me.g == g)
            def _():
                for i, (b, t, step) in enumerate(self._sends(g)):
                    if step in steps:
                        act(self._copy(b, t, i))

    def near(self):
        self._each(lambda cp: cp.start(), (0,))

    def settle(self):
        inner = (self.me.g == 0) | (self.me.g == 2)

        @pl.when(inner)
        def _():
            self._copy(1, 0, 0).wait_recv()

        @pl.when(jnp.logical_not(inner))
        def _():
            self._copy(2, 0, 0).wait_recv()

    def rest(self):
        self._each(lambda cp: cp.start(), (1,))

    def arrive(self):
        for g in range(self.me.planes):

            @pl.when(self.me.g == g)
            def _():
                for b in range(self.me.planes):
                    if b not in (g, 1 if g in (0, 2) else 2):
                        self._copy(b, b, 0).wait_recv()

    def finish(self):
        self._each(lambda cp: cp.wait_send(), (0, 1))


class Collect:
    def __init__(self, me, blocks, landing, via, send, recv):
        self.me, self.blocks, self.landing, self.via, self.send, self.recv = me, blocks, landing, via, send, recv
        self.by = {(0, 3): 1, (3, 0): 2} if me.planes == 4 else {}

    def _copy(self, b, t, src, i):
        at = (b - t) % self.me.planes - 1
        return remote(src, self.landing.at[at], self.send.at[i], self.recv.at[at], self.me.plane_dev(t))

    def _plan(self, b):
        combined = [t for (s, t), by in self.by.items() if by == b]
        direct = [t for t in range(self.me.planes) if t != b and t not in combined]
        direct.sort(key=lambda t: -abs(t - b))
        return [(t, (b, t) in self.by, i) for i, t in enumerate(direct)]

    def _each(self, b, act, ways=(True, False)):
        @pl.when(self.me.g == b)
        def _():
            for t, through, i in self._plan(b):
                if through not in ways:
                    continue
                if through:
                    z = self.me.planes
                    by = self.by[(b, t)]
                    act(remote(self.blocks(t), self.via, self.send.at[i], self.recv.at[z - 1], self.me.plane_dev(by)))
                else:
                    act(self._copy(b, t, self.blocks(t), i))

    def start(self, ways=(True, False)):
        for b in range(self.me.planes):
            self._each(b, lambda cp: cp.start(), ways)

    def _combined(self, b, t):
        return self._copy(b, t, self.via, self.me.planes - 2)

    def combine(self, own):
        for (s, t), by in self.by.items():

            @pl.when(self.me.g == by)
            def _():
                z = self.me.planes
                remote(self.via, self.via, self.send.at[0], self.recv.at[z - 1], self.me.plane_dev(by)).wait_recv()
                for q in range(self.via.shape[0]):
                    self.via[q] = (self.via[q].astype(F32) + own(t)[q].astype(F32)).astype(BF16)
                self._combined(by, t).start()

    def clear(self):
        for s, t in self.by:

            @pl.when(self.me.g == t)
            def _():
                at = (s - t) % self.me.planes - 1
                self.landing[at] = jnp.zeros(self.landing.shape[1:], BF16)

    def total(self, out, own):
        z = self.me.planes
        for t in range(z):

            @pl.when(self.me.g == t)
            def _():
                for b in range(z):
                    if b != t and (b, t) not in self.by:
                        at = (b - t) % z - 1
                        self._copy(b, t, self.landing.at[at], 0).wait_recv()

        for q in range(out.shape[0]):
            value = own[q].astype(F32)
            for at in range(z - 1):
                value = value + self.landing[at, q].astype(F32)
            out[q] = value.astype(BF16)

    def finish(self):
        for b in range(self.me.planes):
            self._each(b, lambda cp: cp.wait_send())
        for (s, t), by in self.by.items():

            @pl.when(self.me.g == by)
            def _():
                self._combined(by, t).wait_send()


def order(me, i):
    k = lax.div(i, 2)
    dx = 1 - lax.div(k, 2)
    dy = 1 - lax.rem(k, 2)
    dc = 1 - lax.rem(i, 2)
    return me.row(dy, dx, dc), k


def strips(length, body, strip=64):
    def one(i, carry):
        body(pl.ds(pl.multiple_of(i * strip, strip), strip))
        return carry

    lax.fori_loop(0, length // strip, one, 0)


def lanes(rows, width):
    return lax.broadcasted_iota(jnp.int32, (rows, width), 1)


def nt(a, b):
    return lax.dot_general(a, b, (((1,), (1,)), ((), ())), preferred_element_type=F32)


def tn(a, b):
    return lax.dot_general(a, b, (((0,), (0,)), ((), ())), preferred_element_type=F32)


def nn(a, b):
    return jnp.dot(a, b, preferred_element_type=F32)


def head_lanes(rows, dh):
    at = lanes(rows, SIDE)
    return at < dh, (at >= dh) & (at < 2 * dh)


def allowed_mask(length, ends):
    i = lax.broadcasted_iota(jnp.int32, (length, length), 0)
    j = lax.broadcasted_iota(jnp.int32, (length, length), 1)
    return (i >= j) & (i.astype(F32) < ends)


def of_head(value, head):
    at = lax.broadcasted_iota(jnp.int32, value.shape, value.ndim - 1)
    return jnp.sum(jnp.where(at == head, value, 0.0), axis=-1, keepdims=True)


def pair_mixing(mix_ref, pair):
    return [[of_head(mix_ref[g : g + 1], 2 * pair + o) for g in range(2)] for o in range(2)]


def mix_lanes(mixing, g, dh):
    at = lanes(1, SIDE)
    return jnp.where(at < dh, mixing[0][g], jnp.where(at < 2 * dh, mixing[1][g], 0.0))


def head_stats(value, dh, h0, h1):
    m0 = jnp.sum(jnp.where(h0, value, 0.0), axis=-1, keepdims=True) / dh
    m1 = jnp.sum(jnp.where(h1, value, 0.0), axis=-1, keepdims=True) / dh
    return jnp.where(h0, m0, jnp.where(h1, m1, 0.0))


def bands(kern_ref, head, length, flip):
    taps_k, taps_q, _ = kern_ref.shape
    r = lax.broadcasted_iota(jnp.int32, (length, length), 0)
    c = lax.broadcasted_iota(jnp.int32, (length, length), 1)
    diff = (c - r) if flip else (r - c)
    taps = [of_head(kern_ref[b], head) for b in range(taps_k)]
    for a in range(taps_q):
        acc = jnp.zeros((length, length), F32)
        for b in range(taps_k):
            acc = jnp.where(diff == b - taps_k // 2, taps[b][a : a + 1], acc)
        yield a, acc


def rms_norm(values_in, scaling):
    return (
        values_in
        * lax.rsqrt(jnp.mean(values_in * values_in, axis=-1, keepdims=True) + 1e-06)
        * scaling
    )


def group_norm(values_in, scaling):
    centred = values_in - jnp.mean(values_in, axis=-1, keepdims=True)
    scaled = centred * lax.rsqrt(jnp.mean(centred * centred, axis=-1, keepdims=True) + 1e-05)
    return scaled.reshape(values_in.shape[0], -1) * scaling


def convolve(scores, kernel):
    length = scores.shape[1]
    taps_query = kernel.shape[1]
    taps_key = kernel.shape[2]
    half_width = taps_key // 2
    padded = jnp.pad(scores, ((0, 0), (taps_query - 1, 0), (half_width, half_width)))
    summed = jnp.zeros_like(scores)
    for shift_q in range(taps_query):
        for shift_k in range(taps_key):
            start_q = taps_query - 1 - shift_q
            window = padded[:, start_q : start_q + length, shift_k : shift_k + length]
            summed = summed + kernel[:, shift_q, shift_k][:, None, None] * window
    return summed


def convolve_back(grad_conv, masked, kernel):
    length = masked.shape[1]
    taps_query = kernel.shape[1]
    taps_key = kernel.shape[2]
    half_width = taps_key // 2
    padded = jnp.pad(masked, ((0, 0), (taps_query - 1, 0), (half_width, half_width)))
    grad_padded = jnp.pad(grad_conv, ((0, 0), (0, taps_query - 1), (half_width, half_width)))
    grad_masked = jnp.zeros_like(masked)
    grad_taps = []
    for shift_q in range(taps_query):
        for shift_k in range(taps_key):
            start_q = taps_query - 1 - shift_q
            window = padded[:, start_q : start_q + length, shift_k : shift_k + length]
            grad_taps.append(jnp.sum(grad_conv * window, axis=(1, 2)))
            start_k = taps_key - 1 - shift_k
            back_window = grad_padded[:, shift_q : shift_q + length, start_k : start_k + length]
            grad_masked = grad_masked + kernel[:, shift_q, shift_k][:, None, None] * back_window
    grad_kern = jnp.stack(grad_taps, axis=1).reshape(kernel.shape)
    return (grad_masked, grad_kern)


def build_mask(doc_lengths, pad_count, length):
    places = jnp.arange(length, dtype=jnp.int32)
    doc_ends = jnp.cumsum(doc_lengths)
    segment = jnp.sum((places[:, None] >= doc_ends[None, :]).astype(jnp.int32), axis=1)
    live_end = length - pad_count
    same_doc = segment[:, None] == segment[None, :]
    causal = places[None, :] <= places[:, None]
    usable = (places[None, :] < live_end) | (places[None, :] == places[:, None])
    return same_doc & causal & usable


def outer_sum(left_rows, right_rows):
    return lax.dot_general(
        left_rows, right_rows, (((0,), (0,)), ((), ())), preferred_element_type=jnp.float32
    )


def back_product(grad_rows, weight_full):
    return lax.dot_general(
        grad_rows, weight_full, (((1,), (1,)), ((), ())), preferred_element_type=jnp.float32
    )


def attention_weights(norm_in, w_qkv, norm_heads, w_out):
    return (
        lax.all_gather(norm_in, "fsdp", axis=0, tiled=True),
        lax.all_gather(w_qkv, "fsdp", axis=0, tiled=True),
        lax.all_gather(norm_heads, "fsdp", axis=0, tiled=True),
        lax.all_gather(w_out, "fsdp", axis=0, tiled=True),
    )


def feed_weights(norm_mid, w_gate, w_up, w_down):
    return (
        lax.all_gather(norm_mid, "fsdp", axis=0, tiled=True),
        lax.all_gather(w_gate, "fsdp", axis=0, tiled=True),
        lax.all_gather(w_up, "fsdp", axis=0, tiled=True),
        lax.all_gather(w_down, "fsdp", axis=0, tiled=True),
    )


def per_device(
    tokens,
    doc_lengths,
    pad_counts,
    norm_in,
    w_qkv,
    kernel,
    mixing,
    norm_heads,
    w_out,
    norm_mid,
    w_gate,
    w_up,
    w_down,
    cotangent,
):
    inputs = tokens[0].astype(jnp.float32)
    length = inputs.shape[0]
    model_width = inputs.shape[1]
    head_count = kernel.shape[0]
    head_size = model_width // head_count
    pair_count = head_count // 2
    score_scale = head_size ** (-0.5)
    allowed = build_mask(doc_lengths[0], pad_counts[0], length)[None]
    kern_pairs = kernel.reshape(pair_count, 2, kernel.shape[1], kernel.shape[2])
    mix_pairs = mixing.reshape(pair_count, 2, 2)
    attn_set = attention_weights(norm_in, w_qkv, norm_heads, w_out)
    normed = rms_norm(inputs, attn_set[0].astype(jnp.float32)).astype(jnp.bfloat16)
    projected = jnp.dot(normed, attn_set[1], preferred_element_type=jnp.float32).astype(
        jnp.bfloat16
    )
    split_qkv = projected.reshape(length, 3, pair_count, 2, head_size).transpose(1, 2, 3, 0, 4)

    def pair_scores(queries, key_rows, kern_pair):
        raw_scores = (
            jnp.einsum("gie,gje->gij", queries, key_rows, preferred_element_type=jnp.float32)
            * score_scale
        )
        masked = jnp.where(allowed, raw_scores, 0.0)
        logits = jnp.where(allowed, convolve(masked, kern_pair), NEG_FILL)
        return (masked, logits)

    def pair_forward(pieces):
        queries, key_rows, value_rows, kern_pair, mix_pair = pieces
        masked, logits = pair_scores(queries, key_rows, kern_pair)
        row_peak = jnp.max(logits, axis=-1, keepdims=True)
        log_total = row_peak + jnp.log(jnp.sum(jnp.exp(logits - row_peak), axis=-1, keepdims=True))
        attn_probs = jnp.exp(logits - log_total)
        mixed_probs = jnp.einsum("og,gij->oij", mix_pair, attn_probs, precision=lax.Precision.HIGHEST)
        output = jnp.einsum(
            "oij,oje->oie", mixed_probs, value_rows.astype(jnp.float32), precision=lax.Precision.HIGHEST
        )
        return (output, log_total)

    attended_pairs, log_totals = lax.map(
        pair_forward, (split_qkv[0], split_qkv[1], split_qkv[2], kern_pairs, mix_pairs)
    )
    attended = attended_pairs.transpose(2, 0, 1, 3).reshape(length, head_count, head_size)
    gated_out = group_norm(attended, attn_set[2].astype(jnp.float32)).astype(jnp.bfloat16)
    residual = inputs + jnp.dot(gated_out, attn_set[3], preferred_element_type=jnp.float32)
    ffn_set = feed_weights(norm_mid, w_gate, w_up, w_down)
    normed_mid = rms_norm(residual, ffn_set[0].astype(jnp.float32)).astype(jnp.bfloat16)
    gate_pre = jnp.dot(normed_mid, ffn_set[1], preferred_element_type=jnp.float32)
    up_pre = jnp.dot(normed_mid, ffn_set[2], preferred_element_type=jnp.float32)
    sigmoid_gate = jax.nn.sigmoid(gate_pre)
    silu_gate = gate_pre * sigmoid_gate
    hidden = (silu_gate * up_pre).astype(jnp.bfloat16)
    layer_out = (residual + jnp.dot(hidden, ffn_set[3], preferred_element_type=jnp.float32))[None]
    ffn_again = feed_weights(norm_mid, w_gate, w_up, w_down)
    grad_y = cotangent[0]
    grad_w_down = outer_sum(hidden, grad_y)
    grad_hidden = back_product(grad_y, ffn_again[3])
    grad_gate = (
        grad_hidden * up_pre * sigmoid_gate * (1.0 + gate_pre * (1.0 - sigmoid_gate))
    ).astype(jnp.bfloat16)
    grad_up = (grad_hidden * silu_gate).astype(jnp.bfloat16)
    grad_w_gate = outer_sum(normed_mid, grad_gate)
    grad_w_up = outer_sum(normed_mid, grad_up)
    grad_mid = back_product(grad_gate, ffn_again[1]) + back_product(grad_up, ffn_again[2])
    mid_pull = jax.vjp(rms_norm, residual, ffn_again[0].astype(jnp.float32))[1]
    grad_residual_norm, grad_norm_mid = mid_pull(grad_mid)
    grad_residual = grad_y.astype(jnp.float32) + grad_residual_norm
    ffn_shards = (
        lax.psum_scatter(grad_norm_mid, "fsdp", scatter_dimension=0, tiled=True),
        lax.psum_scatter(grad_w_gate, "fsdp", scatter_dimension=0, tiled=True),
        lax.psum_scatter(grad_w_up, "fsdp", scatter_dimension=0, tiled=True),
        lax.psum_scatter(grad_w_down, "fsdp", scatter_dimension=0, tiled=True),
    )
    attn_again = attention_weights(norm_in, w_qkv, norm_heads, w_out)
    grad_branch = grad_residual.astype(jnp.bfloat16)
    grad_w_out = outer_sum(gated_out, grad_branch)
    grad_gated = back_product(grad_branch, attn_again[3])
    head_pull = jax.vjp(group_norm, attended, attn_again[2].astype(jnp.float32))[1]
    grad_attended, grad_norm_heads = head_pull(grad_gated)
    grad_att_pairs = (
        grad_attended.astype(jnp.bfloat16)
        .reshape(length, pair_count, 2, head_size)
        .transpose(1, 2, 0, 3)
    )

    def pair_backward(pieces):
        queries, key_rows, value_rows, kern_pair, mix_pair, log_total, grad_output = pieces
        masked, logits = pair_scores(queries, key_rows, kern_pair)
        attn_probs = jnp.exp(logits - log_total)
        mixed_probs = jnp.einsum("og,gij->oij", mix_pair, attn_probs, precision=lax.Precision.HIGHEST)
        grad_wide = grad_output.astype(jnp.float32)
        grad_mixed = jnp.einsum(
            "oie,oje->oij", grad_wide, value_rows.astype(jnp.float32), precision=lax.Precision.HIGHEST
        )
        grad_values = jnp.einsum("oij,oie->oje", mixed_probs, grad_wide, precision=lax.Precision.HIGHEST)
        grad_mix = jnp.einsum("oij,gij->og", grad_mixed, attn_probs, precision=lax.Precision.HIGHEST)
        grad_probs = jnp.einsum("og,oij->gij", mix_pair, grad_mixed, precision=lax.Precision.HIGHEST)
        grad_logits = attn_probs * (
            grad_probs - jnp.sum(attn_probs * grad_probs, axis=-1, keepdims=True)
        )
        grad_conv = jnp.where(allowed, grad_logits, 0.0)
        grad_masked, grad_kern = convolve_back(grad_conv, masked, kern_pair)
        grad_raw = jnp.where(allowed, grad_masked, 0.0)
        grad_query = (
            jnp.einsum("gij,gje->gie", grad_raw, key_rows.astype(jnp.float32), precision=lax.Precision.HIGHEST)
            * score_scale
        )
        grad_key = (
            jnp.einsum("gij,gie->gje", grad_raw, queries.astype(jnp.float32), precision=lax.Precision.HIGHEST)
            * score_scale
        )
        return (
            grad_query.astype(jnp.bfloat16),
            grad_key.astype(jnp.bfloat16),
            grad_values.astype(jnp.bfloat16),
            grad_kern,
            grad_mix,
        )

    grads_query, grads_key, grads_value, grad_kern_pairs, grad_mix_pairs = lax.map(
        pair_backward,
        (
            split_qkv[0],
            split_qkv[1],
            split_qkv[2],
            kern_pairs,
            mix_pairs,
            log_totals,
            grad_att_pairs,
        ),
    )
    grad_qkv = (
        jnp.stack([grads_query, grads_key, grads_value])
        .transpose(3, 0, 1, 2, 4)
        .reshape(length, 3 * model_width)
    )
    grad_w_qkv = outer_sum(normed, grad_qkv)
    grad_normed = back_product(grad_qkv, attn_again[1])
    in_pull = jax.vjp(rms_norm, inputs, attn_again[0].astype(jnp.float32))[1]
    grad_inputs_norm, grad_norm_in = in_pull(grad_normed)
    grad_tokens = (grad_residual + grad_inputs_norm)[None]
    small_sums = lax.psum(
        (grad_kern_pairs.reshape(kernel.shape), grad_mix_pairs.reshape(mixing.shape)),
        ("rep", "fsdp"),
    )
    attn_shards = (
        lax.psum_scatter(grad_norm_in, "fsdp", scatter_dimension=0, tiled=True),
        lax.psum_scatter(grad_w_qkv, "fsdp", scatter_dimension=0, tiled=True),
        lax.psum_scatter(grad_norm_heads, "fsdp", scatter_dimension=0, tiled=True),
        lax.psum_scatter(grad_w_out, "fsdp", scatter_dimension=0, tiled=True),
    )
    summed = (
        lax.psum(ffn_shards[0].astype(jnp.bfloat16), "rep").astype(jnp.float32),
        lax.psum(ffn_shards[1].astype(jnp.bfloat16), "rep").astype(jnp.float32),
        lax.psum(ffn_shards[2].astype(jnp.bfloat16), "rep").astype(jnp.float32),
        lax.psum(ffn_shards[3].astype(jnp.bfloat16), "rep").astype(jnp.float32),
        lax.psum(attn_shards[0].astype(jnp.bfloat16), "rep").astype(jnp.float32),
        lax.psum(attn_shards[1].astype(jnp.bfloat16), "rep").astype(jnp.float32),
        lax.psum(attn_shards[2].astype(jnp.bfloat16), "rep").astype(jnp.float32),
        lax.psum(attn_shards[3].astype(jnp.bfloat16), "rep").astype(jnp.float32),
    )
    return (
        layer_out,
        grad_tokens,
        summed[4],
        summed[5],
        small_sums[0],
        small_sums[1],
        summed[6],
        summed[7],
        summed[0],
        summed[1],
        summed[2],
        summed[3],
    )


def forward_kernel(cfg, *refs):
    (tok, ct, w_qkv, w_gate, w_up, w_down, w_o, kern_in, mix_in, gain_rows, docs, pads,
     tok_all, ct_all, a_all, b_all, d_all, o_all, nrm_all, qkv_all, p_all, m_all, gated_all, mid_all, resid, ends,
     gains, kern, mix, wq_v, w_a, w_b, meta, gain_v, ct_v, down_v, own_o,
     x_v, wa_v, wo_v, t_v, cat_v, shift_v, qkv_v, p_v, m_v, gated_v, meta_v, mid_v, tok_v,
     out_v, red, diag, near, rs_send, rs_recv,
     g_send, g_recv, g_loc, a_send, a_recv, ch_send, ch_recv, o_send, o_recv, meta_send, meta_recv, gain_send, gain_recv, meet_sems, loc, pack, row_in, row_out) = refs
    planes, dh, taps_q, taps_k = cfg["planes"], cfg["dh"], cfg["kq"], cfg["kk"]
    length, width = tok.shape
    per_pair = o_all.shape[0]
    scale = dh ** (-0.5)
    ff, chunk = cfg["ff"], cfg["ff"] // planes
    me = Place(planes)

    me.hail()

    wq_in = pltpu.make_async_copy(w_qkv, wq_v, loc.at[1])
    wq_in.start()
    tok_in = pltpu.make_async_copy(tok, tok_v, loc.at[0])
    tok_in.start()
    taps_in = [pltpu.make_async_copy(kern_in, kern, loc.at[6]), pltpu.make_async_copy(mix_in, mix, loc.at[7])]
    for cp in taps_in:
        cp.start()
    o_in = pltpu.make_async_copy(w_o, own_o, loc.at[4])
    o_in.start()
    down_in = pltpu.make_async_copy(w_down.at[pl.ds(me.y * chunk, chunk)], down_v, loc.at[3])
    down_in.start()
    ct_in = pltpu.make_async_copy(ct, ct_v, loc.at[5])
    ct_in.start()

    def columns(j, s, z):
        at = pl.multiple_of(z * (2 * PLANE * chunk) + s * (2 * chunk) + me.y * chunk, 128)
        src = (w_gate, w_up)[j].at[:, pl.ds(at, chunk)]
        return pltpu.make_async_copy(src, w_b.at[s, :, pl.ds(j * ff + z * chunk, chunk)], pack.at[j, s, z])

    for j in range(2):
        for s in range(PLANE):
            for z in range(planes):
                columns(j, s, z).start()

    places = lanes(8, length).astype(F32)
    last = length * 1.0
    reach = [docs[0, 0]]
    for k in range(1, docs.shape[1]):
        reach.append(reach[-1] + docs[0, k])
    own_end = jnp.full((8, length), last, F32)
    for end in reversed(reach):
        own_end = jnp.where(places < end.astype(F32), end.astype(F32), own_end)
    meta[...] = jnp.where(places < last - pads[0].astype(F32), own_end, places + 1.0)

    wq_in.wait()
    low = lanes(w_qkv.shape[0], 128) < 64
    for s in range(PLANE):
        base = (me.y if s % 2 == 0 else planes - 1 - me.y) * (4 * dh)

        def part(j):
            blk = wq_v[:, pl.ds(pl.multiple_of(j * width + base, 128), 4 * dh)].astype(F32)
            t0, t1, t2 = blk[:, 0:128], blk[:, 128:256], blk[:, 256:384]
            if s // 2 == 0:
                return t0, t1
            t1, t2 = pltpu.roll(t1, 64, 1), pltpu.roll(t2, 64, 1)
            return jnp.where(low, t1, t2), t2

        (q0, q1), (k0, k1), (v0, v1) = part(0), part(1), part(2)
        tiles = (
            q0,
            jnp.where(low, q1, pltpu.roll(v1, 64, 1)),
            k0,
            jnp.where(low, k1, 0.0),
            v0,
        )
        for i, t in enumerate(tiles):
            w_a[s, :, i * 128 : (i + 1) * 128] = t.astype(BF16)

    down_in.wait()
    down_out = pltpu.make_async_copy(down_v, d_all.at[me.g], loc.at[3])
    down_out.start()
    o_in.wait()
    tok_in.wait()
    for cp in taps_in:
        cp.wait()
    me.await_all()

    def first(src, dst_all, base):
        cps = []
        for d in range(1, PLANE):
            s = lax.rem(me.s + d, PLANE)
            cp = remote(src.at[s], dst_all.at[me.f], a_send.at[base + d], a_recv.at[base + d], (me.y, me.g * PLANE + s))
            cp.start()
            cps.append(cp)
        own = pltpu.make_async_copy(src.at[me.s], dst_all.at[me.f], a_send.at[base])
        own.start()
        return cps, own

    def first_wait(src, dst_all, base, own):
        for d in range(1, PLANE):
            s = lax.rem(me.s - d + PLANE, PLANE)
            blk = dst_all.at[me.g * PLANE + s]
            remote(blk, blk, a_send.at[base + d], a_recv.at[base + d], me.sib).wait_recv()
        own.wait()

    meta_sent = []
    for d in range(1, GROUP):
        to = lax.rem(me.slot + d, GROUP)
        cp = remote(
            meta, meta_v.at[me.slot], meta_send.at[d], meta_recv.at[d],
            (lax.div(to, PLANE), me.g * PLANE + lax.rem(to, PLANE)),
        )
        cp.start()
        meta_sent.append(cp)
    meta_here = pltpu.make_async_copy(meta, meta_v.at[me.slot], meta_send.at[0])
    meta_here.start()
    gain_here = pltpu.make_async_copy(gain_rows, gain_v.at[me.f], gain_send.at[0])
    gain_here.start()
    gain_sent = []
    for d in range(1, PLANE):
        to = lax.rem(me.s + d, PLANE)
        gain_sent.append(remote(gain_rows, gain_v.at[me.f], gain_send.at[d], gain_recv.at[d], (me.y, me.g * PLANE + to)))
        gain_sent[-1].start()
    sent_a, own_a = first(w_a, a_all, 0)
    tokens = Gather(me, tok_v, tok_all, g_send.at[0], g_recv.at[0], g_loc.at[0])
    tokens.start()

    o_y = jnp.where((me.g == 1) | (me.g == 2), 1, 0)
    o_c = jnp.where(me.g >= 2, 1, 0)
    o_here = pltpu.make_async_copy(own_o, o_all.at[me.c], o_send.at[0])
    o_sib = remote(own_o, o_all.at[me.c], o_send.at[0], o_recv.at[0], me.sib)

    @pl.when((o_y == me.y) & (o_c == me.c))
    def _():
        o_here.start()

    @pl.when((o_y == me.y) & (o_c != me.c))
    def _():
        o_sib.start()

    def o_copy(t, i):
        return remote(o_all, o_all, o_send.at[i], o_recv.at[1], me.plane_dev(t))

    o_way = ((2, 1), (2, 0), (1, 3), (1, 2))

    def o_each(act):
        for home, (first_to, then_to) in enumerate(o_way):

            @pl.when((me.g == home) & (me.home == home))
            def _():
                act(o_copy(first_to, 1))
                act(o_copy(then_to, 2))

    o_relays = ((me.home < 2) & (me.g == 2)) | ((me.home >= 2) & (me.g == 1))

    def o_from_home():
        o_here.wait()
        remote(o_all.at[1 - me.c], o_all.at[1 - me.c], o_send.at[0], o_recv.at[0], me.sib).wait_recv()

    def o_relay():
        o_copy(0, 1).wait_recv()
        o_copy(jnp.where(me.home < 2, planes - 1, 0), 1).start()

    blocks4 = lambda ref: (lambda b: ref.at[pl.ds(b * PLANE, PLANE)])
    spread_a = Spread(me, blocks4(a_all), ch_send.at[0], ch_recv.at[0])
    spread_b = Spread(me, blocks4(b_all), ch_send.at[1], ch_recv.at[1])
    spread_d = Spread(me, lambda b: d_all.at[b], ch_send.at[2], ch_recv.at[2])

    for g in range(2):
        for a, t in bands(kern, 2 * me.pair + g, length, False):
            high = t.astype(BF16)
            at = slice(a * length, (a + 1) * length)
            t_v[g, 0:length, at] = high
            t_v[g, length : 2 * length, at] = high
            t_v[g, 2 * length :, at] = (t - high.astype(F32)).astype(BF16)
    shift_v[0:8] = jnp.zeros((8, taps_q * length), F32)
    wo_v[...] = jnp.zeros(wo_v.shape, BF16)

    pl.when(me.g == me.home)(o_from_home)
    o_each(lambda cp: cp.start())
    gain_here.wait()
    for d in range(1, PLANE):
        fr = me.g * PLANE + lax.rem(me.s - d + PLANE, PLANE)
        remote(gain_rows, gain_v.at[fr], gain_send.at[d], gain_recv.at[d], me.sib).wait_recv()
    for d in range(1, planes):
        to = lax.rem(me.g + d, planes)
        part = gain_v.at[pl.ds(me.g * PLANE, PLANE)]
        gain_sent.append(remote(part, part, gain_send.at[PLANE + d], gain_recv.at[PLANE + d], me.plane_dev(to)))
        gain_sent[-1].start()
    first_wait(w_a, a_all, 0, own_a)
    spread_a.near()
    pl.when(o_relays)(o_relay)

    tokens.relay()
    for j in range(2):
        for s in range(PLANE):
            for z in range(planes):
                columns(j, s, z).wait()
    sent_b, own_b = first(w_b, b_all, PLANE)
    cots = Gather(me, ct_v, ct_all, g_send.at[1], g_recv.at[1], g_loc.at[1])
    ct_in.wait()
    cots.start()
    spread_a.settle()
    meet(me, meet_sems.at[0])
    spread_a.rest()

    down_out.wait()

    tokens.share()
    tokens.last()
    tokens.finish()
    for row in range(GROUP):
        pltpu.make_async_copy(tok_all.at[row], x_v.at[row], row_in.at[row]).start()
    first_wait(w_b, b_all, PLANE, own_b)
    for d in range(1, GROUP):
        fr = lax.rem(me.slot - d + GROUP, GROUP)
        remote(meta, meta_v.at[fr], meta_send.at[d], meta_recv.at[d], me.sib).wait_recv()
    meta_here.wait()
    ends[...] = meta_v[...]
    for d in range(1, planes):
        part = gain_v.at[pl.ds(lax.rem(me.g - d + planes, planes) * PLANE, PLANE)]
        remote(part, part, gain_send.at[PLANE + d], gain_recv.at[PLANE + d], me.sib).wait_recv()
    gains[...] = jnp.zeros(gains.shape, F32)
    lane = lanes(8, 128)
    for k in range(planes):
        v0, v1, v2, v3 = (gain_v[k * PLANE + j] for j in range(PLANE))
        v1, v2, v3 = pltpu.roll(v1, 96, 1), pltpu.roll(v2, 64, 1), pltpu.roll(v3, 32, 1)
        for j, t in enumerate((jnp.where(lane < 96, v0, v1), jnp.where(lane < 64, v1, v2), jnp.where(lane < 32, v2, v3))):
            at = k * PLANE * w_o.shape[0] + j * 128
            gains[0:2, at : at + 128] = t[0:2]
    v0, v1 = gain_v[2 * me.pair], pltpu.roll(gain_v[2 * me.pair + 1], 96, 1)
    gains[2:3, 0:128] = jnp.where(lane < 96, v0, v1)[2:3]
    gains[2:3, 128:256] = jnp.where(lane < 64, v1, 0.0)[2:3]

    resid[length:] = gains[...]

    def norms(i, carry):
        row, _ = order(me, i)
        pltpu.make_async_copy(tok_all.at[row], x_v.at[row], row_in.at[row]).wait()

        def norm(at):
            x = x_v[row, at].astype(F32)
            s = lax.rsqrt(jnp.mean(x * x, axis=-1, keepdims=True) + 1e-6)
            x_v[row, at] = (x * s * gains[0:1]).astype(BF16)

        strips(length, norm)
        pltpu.make_async_copy(x_v.at[row], nrm_all.at[row], row_out.at[0, row]).start()
        return carry

    lax.fori_loop(0, GROUP, norms, 0)
    spread_a.arrive()
    wa_in = pltpu.make_async_copy(a_all, wa_v, loc.at[1])
    wa_in.start()
    @pl.when((me.g != me.home) & jnp.logical_not(o_relays))
    def _():
        o_copy(0, 1).wait_recv()

    wo_in = pltpu.make_async_copy(o_all, wo_v.at[pl.ds(0, per_pair)], loc.at[2])
    wo_in.start()
    spread_d.near()
    spread_b.near()
    wa_in.wait()
    wo_in.wait()
    h0, h1 = head_lanes(length, dh)
    scatter = Scatter(me, out_v, red, diag, near, rs_send, rs_recv)

    mixing = pair_mixing(mix, me.pair)

    def attention(i):
        row, k = order(me, i)
        acc = nn(x_v[row], wa_v[...].reshape(width, QKV))
        at = lanes(length, 128)
        q = jnp.where(h0 | h1, acc[:, 0:SIDE], 0.0)
        kk = jnp.where(h0 | h1, acc[:, SIDE : 2 * SIDE], 0.0)
        tail = jnp.where(at < 64, pltpu.roll(acc[:, 128:256], 64, 1), 0.0)
        v = jnp.concatenate([acc[:, 2 * SIDE : QKV], tail], axis=1)
        q, kk, v = q.astype(BF16), kk.astype(BF16), v.astype(BF16)
        qkv_v[row, :, 0:SIDE] = q
        qkv_v[row, :, SIDE : 2 * SIDE] = kk
        qkv_v[row, :, 2 * SIDE : 3 * SIDE] = v
        pltpu.make_async_copy(qkv_v.at[row], qkv_all.at[row], row_out.at[1, row]).start()
        ok = allowed_mask(length, meta_v[row, 0:1, :])
        attended = jnp.zeros((length, SIDE), F32)
        for g in range(2):
            kg = jnp.where(h0 if g == 0 else h1, kk.astype(F32), 0.0).astype(BF16)
            raw = nt(q, kg) * scale
            masked = jnp.where(ok, raw, 0.0)
            m_v[row, g] = masked.astype(BF16)
            high = masked.astype(BF16)
            cat_v[:, 0:length] = high
            cat_v[:, length : 2 * length] = (masked - high.astype(F32)).astype(BF16)
            cat_v[:, 2 * length :] = high
            shift_v[8 : 8 + length] = nn(cat_v[...], t_v[g])
            conv = shift_v[8 : 8 + length, 0:length]
            for a in range(1, taps_q):
                conv = conv + shift_v[8 - a : 8 - a + length, a * length : (a + 1) * length]
            logits = jnp.where(ok, conv, NEG_FILL)
            e = jnp.exp(logits - jnp.max(logits, axis=-1, keepdims=True))
            probs = e / jnp.sum(e, axis=-1, keepdims=True)
            high = probs.astype(BF16)
            low = (probs - high.astype(F32)).astype(BF16)
            p_v[row, g, 0] = high
            p_v[row, g, 1] = low
            attended = attended + (nn(high, v) + nn(low, v)) * mix_lanes(mixing, g, dh)
        pltpu.make_async_copy(m_v.at[row], m_all.at[row], row_out.at[2, row]).start()
        pltpu.make_async_copy(p_v.at[row], p_all.at[row], row_out.at[3, row]).start()
        centred = attended - head_stats(attended, dh, h0, h1)
        centred = jnp.where(h0 | h1, centred, 0.0)
        scaled = centred * lax.rsqrt(head_stats(centred * centred, dh, h0, h1) + 1e-5)
        gated = (scaled * gains[2:3, 0:SIDE]).astype(BF16)
        gated_v[row] = gated
        pltpu.make_async_copy(gated_v.at[row], gated_all.at[row], row_out.at[4, row]).start()
        wo = wo_v[...].reshape(wo_v.shape[0] * wo_v.shape[1], width)

    def project(i):
        row, k = order(me, i)
        wo = wo_v[...].reshape(wo_v.shape[0] * wo_v.shape[1], width)
        part = nn(gated_v[row], wo[0:SIDE])

        @pl.when(lax.rem(i, 2) == 0)
        def _():
            scatter.put_sib(k, part)

        @pl.when(lax.rem(i, 2) == 1)
        def _():
            scatter.put_self(k, part)

        scatter.push(i)

    def one(i, carry):
        attention(i)

        project(i)

        @pl.when(i == 1)
        def _():
            cots.relay()

        @pl.when(i == 4)
        def _():
            spread_d.settle()
            spread_b.settle()
            meet(me, meet_sems.at[1])
            spread_d.rest()
            spread_b.rest()

        return carry

    lax.fori_loop(0, GROUP, one, 0)
    scatter.arrive()

    def middle(at):
        res = tok_v[at].astype(F32) + scatter.total(at)
        resid[at] = res
        s = lax.rsqrt(jnp.mean(res * res, axis=-1, keepdims=True) + 1e-6)
        mid_v[at] = (res * s * gains[1:2]).astype(BF16)

    strips(length, middle)
    mids = Gather(me, mid_v, mid_all, g_send.at[2], g_recv.at[2], g_loc.at[2])
    mids.start()
    mids.relay()
    cots.share()
    cots.last()
    mids.share()
    mids.last()
    mids.finish()
    cots.finish()
    spread_d.arrive()
    spread_b.arrive()
    scatter.finish_cores()
    scatter.finish_chips()
    for sp in (spread_a, spread_b, spread_d):
        sp.finish()
    o_each(lambda cp: cp.wait_send())

    @pl.when(o_relays)
    def _():
        o_copy(0, 1).wait_send()

    @pl.when((o_y == me.y) & (o_c != me.c))
    def _():
        o_sib.wait_send()

    for cp in meta_sent + gain_sent + sent_a + sent_b:
        cp.wait_send()
    for r in range(GROUP):
        pltpu.make_async_copy(x_v.at[r], nrm_all.at[r], row_out.at[0, r]).wait()
        pltpu.make_async_copy(qkv_v.at[r], qkv_all.at[r], row_out.at[1, r]).wait()
        pltpu.make_async_copy(m_v.at[r], m_all.at[r], row_out.at[2, r]).wait()
        pltpu.make_async_copy(p_v.at[r], p_all.at[r], row_out.at[3, r]).wait()
        pltpu.make_async_copy(gated_v.at[r], gated_all.at[r], row_out.at[4, r]).wait()


def forward_call(cfg, tok, ct, w_qkv, w_gate, w_up, w_down, w_o, kern, mix, gain_rows, docs, pads):
    length, width = tok.shape
    planes, ff, r = cfg["planes"], cfg["ff"], w_qkv.shape[0]
    n = planes * PLANE
    chunk = ff // planes
    per_pair = n // GROUP
    taps = cfg["kq"] * length
    pad_rows = -(-SIDE // w_o.shape[0])
    hbm, vmem, smem = pl.BlockSpec(memory_space=pl.ANY), pl.BlockSpec(memory_space=pltpu.VMEM), pl.BlockSpec(memory_space=pltpu.SMEM)
    sds = jax.ShapeDtypeStruct
    rows = (GROUP, length)
    dma = pltpu.SemaphoreType.DMA
    v16 = lambda *shape: pltpu.VMEM(shape, BF16)
    v32 = lambda *shape: pltpu.VMEM(shape, F32)
    return pl.pallas_call(
        functools.partial(forward_kernel, cfg),
        out_shape=(
            sds(rows + (width,), BF16), sds(rows + (width,), BF16),
            sds((n, r, QKV), BF16), sds((n, r, 2 * ff), BF16), sds((planes, chunk, width), BF16),
            sds((per_pair,) + w_o.shape, BF16), sds(rows + (width,), BF16), sds(rows + (3 * SIDE,), BF16),
            sds((GROUP, 2, 2, length, length), BF16), sds((GROUP, 2, length, length), BF16), sds(rows + (SIDE,), BF16),
            sds(rows + (width,), BF16), sds((length + 8, width), F32), sds((GROUP, 8, length), F32),
        ),
        in_specs=[hbm] * 9 + [vmem] + [smem] * 2,
        out_specs=(hbm,) * 12 + (vmem,) * 2,
        scratch_shapes=[
            v32(8, width), v32(*kern.shape), v32(*mix.shape), v16(*w_qkv.shape), v16(PLANE, r, QKV), v16(PLANE, r, 2 * ff), v32(8, length), v32(n, 8, 128), v16(length, width), v16(chunk, width), v16(*w_o.shape),
            v16(*rows, width), v16(n, r, QKV), v16(pad_rows, *w_o.shape),
            v16(2, 3 * length, taps), v16(length, 3 * length), v32(length + 8, taps),
            v16(*rows, 3 * SIDE), v16(GROUP, 2, 2, length, length), v16(GROUP, 2, length, length), v16(*rows, SIDE),
            v32(GROUP, 8, length), v16(length, width), v16(length, width),
            *Scatter.scratch(length, width),
            dma((3, Gather.SENDS)), dma((3, Gather.RECVS)), dma((3,)), dma((2 * PLANE,)), dma((2 * PLANE,)),
            dma((3, planes)), dma((3, planes)), dma((3,)), dma((2,)), dma((GROUP,)), dma((GROUP,)), dma((PLANE + planes,)), dma((PLANE + planes,)), pltpu.SemaphoreType.REGULAR((2,)),
            dma((8,)), dma((2, PLANE, planes)), dma((GROUP,)), dma((5, GROUP)),
        ],
        compiler_params=pltpu.CompilerParams(collective_id=1, has_side_effects=True, vmem_limit_bytes=60 * 2**20),
        name="attention_forward",
    )(tok, ct, w_qkv, w_gate, w_up, w_down, w_o, kern, mix, gain_rows, docs, pads)


def feed_kernel(cfg, *refs):
    (mid_all, ct_all, w_b, w_d, resid,
     g_res, branch_all, dw_b, out_red,
     mid_v, ct_v, wb_v, wd_v, hid_v, gu_v, tile_v, dd_v, zd_v, via_v, sd_v, first_v, zf_v, via_f, sf_v, flat_v,
     o_out, o_red, o_send, o_recv,
     m_out, m_red, m_diag, m_near, m_send, m_recv,
     g_send, g_recv, g_loc, z_send, z_recv, loc, row_in, out_sem) = refs
    length, width = ct_all.shape[1:]
    ff = cfg["ff"]
    gain = slice(length + 1, length + 2)
    me = Place(cfg["planes"])
    me.hail()
    wb_in = pltpu.make_async_copy(w_b, wb_v, loc.at[0])
    wb_in.start()
    wd_in = pltpu.make_async_copy(w_d, wd_v, loc.at[1])
    wd_in.start()

    def row_copies(row):
        return (
            pltpu.make_async_copy(mid_all.at[row], mid_v.at[row], row_in.at[0, row]),
            pltpu.make_async_copy(ct_all.at[row], ct_v.at[row], row_in.at[1, row]),
        )

    for i in range(2):
        for cp in row_copies(order(me, i)[0]):
            cp.start()
    me.await_all()
    sum_out = Scatter(me, o_out, o_red, None, None, o_send, o_recv)
    down_sum = Collect(me, lambda b: dd_v.at[pl.ds(b, 1)], zd_v, via_v, z_send.at[0], z_recv.at[0])
    down_sum.clear()
    first_sum = Collect(me, lambda b: first_v.at[b], zf_v, via_f, z_send.at[1], z_recv.at[1])
    first_sum.clear()
    sum_mid = Scatter(me, m_out, m_red, m_diag, m_near, m_send, m_recv)
    wb_in.wait()
    wd_in.wait()
    for i in range(2, GROUP):
        for cp in row_copies(order(me, i)[0]):
            cp.start()

    def one(i, carry):
        row, k = order(me, i)
        for cp in row_copies(row):
            cp.wait()
        wb = wb_v[...].reshape(width, 2 * ff)
        wd = wd_v[...].reshape(ff, width)
        pre = nn(mid_v[row], wb)
        gate, up = pre[:, :ff], pre[:, ff:]
        g_hidden = nt(ct_v[row], wd)
        sig = jax.nn.sigmoid(gate)
        silu = gate * sig
        hid_v[row] = (silu * up).astype(BF16)
        gu_v[row, :, :ff] = (g_hidden * up * sig * (1.0 + gate * (1.0 - sig))).astype(BF16)
        gu_v[row, :, ff:] = (g_hidden * silu).astype(BF16)
        mid_part = nt(gu_v[row], wb)

        @pl.when(lax.rem(i, 2) == 0)
        def _():
            sum_mid.put_sib(k, mid_part)

        @pl.when(lax.rem(i, 2) == 1)
        def _():
            sum_mid.put_self(k, mid_part)

        sum_mid.push(i)
        return carry

    def output(i, carry):
        row, k = order(me, i)
        out_part = nn(hid_v[row], wd_v[...].reshape(ff, width))

        @pl.when(lax.rem(i, 2) == 0)
        def _():
            sum_out.put_sib(k, out_part)

        @pl.when(lax.rem(i, 2) == 1)
        def _():
            sum_out.put_self(k, out_part)

        return carry

    lax.fori_loop(0, GROUP, one, 0)

    tokens = GROUP * length
    tile = SIDE

    def down(i, carry):
        at = pl.ds(pl.multiple_of(i * tile, tile), tile)
        value = tn(hid_v[:, :, at].reshape(tokens, tile), ct_v[...].reshape(tokens, width)).astype(BF16)
        per = tile // dd_v.shape[1]
        dd_v[pl.ds(i * per, per)] = value.reshape((per,) + dd_v.shape[1:])
        return carry

    lax.fori_loop(0, ff // tile, down, 0)
    down_sum.start()

    steps = width // tile

    def tile_out(i):
        slot = lax.rem(i, 2)
        at = pl.ds(pl.multiple_of(i * tile, tile), tile)
        return pltpu.make_async_copy(tile_v.at[slot], dw_b.at[at], out_sem.at[slot])

    def gate_up(i, carry):
        @pl.when(i >= 2)
        def _():
            tile_out(i - 2).wait()

        at = pl.ds(pl.multiple_of(i * tile, tile), tile)
        value = tn(mid_v[:, :, at].reshape(tokens, tile), gu_v[...].reshape(tokens, 2 * ff)).astype(BF16)
        tile_v[lax.rem(i, 2)] = value
        tile_out(i).start()
        r = first_v.shape[2]
        for z in range(first_v.shape[0]):
            for q in range(FIRST):
                lo = (z * PLANE + q) * r
                for tile_at in range(lo // tile, (lo + r - 1) // tile + 1):
                    begin, end = max(lo, tile_at * tile), min(lo + r, (tile_at + 1) * tile)

                    @pl.when(i == tile_at)
                    def _():
                        first_v[z, q, begin - lo : end - lo] = value[begin - tile_at * tile : end - tile_at * tile]

        return carry

    lax.fori_loop(0, steps, gate_up, 0)
    first_sum.start()
    g_res[length:] = jnp.zeros((8, width), F32)
    sum_mid.arrive()

    def middle(at):
        g_mid = sum_mid.total(at)
        res = resid[at]
        s = lax.rsqrt(jnp.mean(res * res, axis=-1, keepdims=True) + 1e-6)
        g_res[length : length + 1] = g_res[length : length + 1] + jnp.sum(g_mid * res * s, axis=0, keepdims=True)
        pulled = g_mid * resid[gain]
        back = ct_v[me.slot, at].astype(F32) + s * pulled
        back = back - res * (s * s * s * jnp.mean(pulled * res, axis=-1, keepdims=True))
        g_res[at] = back
        ct_v[me.slot, at] = back.astype(BF16)

    strips(length, middle)
    branch = Gather(me, ct_v.at[me.slot], branch_all, g_send, g_recv, g_loc.at[0])
    branch.start()

    lax.fori_loop(0, GROUP, output, 0)
    red_out = pltpu.make_async_copy(o_red, out_red.at[pl.ds(0, 4)], out_sem.at[2])
    red_out.start()
    down_sum.combine(lambda t: dd_v.at[pl.ds(t, 1)])
    branch.relay()
    first_sum.combine(lambda t: first_v.at[t])
    branch.share()
    branch.last()
    down_sum.total(sd_v, dd_v.at[pl.ds(me.g, 1)])
    sd_out = pltpu.make_async_copy(sd_v.at[0], out_red.at[4, pl.ds(0, sd_v.shape[1])], out_sem.at[3])
    sd_out.start()
    first_sum.total(sf_v, first_v.at[me.g])
    flat_v[...] = sf_v[...].reshape(flat_v.shape)
    r = sf_v.shape[1]
    own_rows = pl.ds(pl.multiple_of(me.g * (PLANE * r), 16), FIRST * r)
    tile_out(steps - 2).wait()
    tile_out(steps - 1).wait()
    sf_out = pltpu.make_async_copy(flat_v, dw_b.at[own_rows], out_sem.at[4])
    sf_out.start()
    branch.finish()
    sum_mid.finish_cores()
    sum_mid.finish_chips()
    sum_out.finish_cores()
    down_sum.finish()
    first_sum.finish()
    red_out.wait()
    sd_out.wait()
    sf_out.wait()


def feed_call(cfg, mid_all, ct_all, w_b, w_d, resid):
    length, width = ct_all.shape[1:]
    ff = cfg["ff"]
    hbm, vmem = pl.BlockSpec(memory_space=pl.ANY), pl.BlockSpec(memory_space=pltpu.VMEM)
    sds = jax.ShapeDtypeStruct
    dma = pltpu.SemaphoreType.DMA
    rows = (GROUP, length)
    chunk = ff // cfg["planes"]
    others = cfg["planes"] - 1
    r = w_b.shape[1]
    v16 = lambda *shape: pltpu.VMEM(shape, BF16)
    return pl.pallas_call(
        functools.partial(feed_kernel, cfg),
        out_shape=(
            sds((length + 8, width), F32), sds(rows + (width,), BF16),
            sds((width, 2 * ff), BF16), sds((5, length, width), BF16),
        ),
        in_specs=[hbm] * 4 + [vmem],
        out_specs=(vmem, hbm, hbm, hbm),
        scratch_shapes=[
            v16(*rows, width), v16(*rows, width), v16(*w_b.shape), v16(*w_d.shape), v16(*rows, ff), v16(*rows, 2 * ff),
            v16(2, SIDE, 2 * ff), v16(others + 1, chunk, width), v16(others, 1, chunk, width), v16(1, chunk, width), v16(1, chunk, width),
            v16(others + 1, FIRST, r, 2 * ff), v16(others, FIRST, r, 2 * ff), v16(FIRST, r, 2 * ff), v16(FIRST, r, 2 * ff), v16(FIRST * r, 2 * ff),
            *Scatter.scratch(length, width, chips=False), *Scatter.scratch(length, width),
            dma((Gather.SENDS,)), dma((Gather.RECVS,)), dma((1,)), dma((2, others + 1)), dma((2, others + 1)),
            dma((2,)), dma((2, GROUP)), dma((5,)),
        ],
        compiler_params=pltpu.CompilerParams(collective_id=2, has_side_effects=True, vmem_limit_bytes=52 * 2**20),
        name="feed_forward",
    )(mid_all, ct_all, w_b, w_d, resid)


def backward_kernel(cfg, *refs):
    (branch_all, o_all, a_all, nrm_all, qkv_all, p_all, m_all, gated_all, dw_b, out_red, tok,
     resid, kern_in, mix_in, g_res, ends,
     g_tokens, layer_out, out_a, out_c, out_b, out_d, out_o, out_small, out_line,
     gains, kern, mix, gb_v, wo_v, wa_v, nrm_v, qkv_v, p_v, m_v, t_v, cat_v, shift_v, corr_v, gq_v, da_v, dc_v, do_v, tok_v, rows_v, line_v, taps_v,
     zb_v, za_v, zc_v, zo_v, via_b, via_a, via_c, via_o, sb_v, sa_v, sc_v, so_v, far_b, strip_v, sd_v, small_v, small_in, last_v, last_in,
     s_out, s_red, s_diag, s_near, rs_send, rs_recv,
     l_red, l_diag, l_near, l_send, l_recv,
     z_send, z_recv, small_send, small_recv, line_send, line_recv, t_send, t_recv, loc, row_in) = refs
    planes, dh, taps_q, taps_k = cfg["planes"], cfg["dh"], cfg["kq"], cfg["kk"]
    length, width = tok.shape
    scale = dh ** (-0.5)
    me = Place(planes)
    per_pair = o_all.shape[0]
    r = a_all.shape[1]
    far = jnp.where(me.g == 1, planes - 1, 0)
    loads = [
        pltpu.make_async_copy(src, dst, loc.at[i])
        for i, (src, dst) in enumerate(
            [(a_all, wa_v), (o_all, wo_v.at[pl.ds(0, per_pair)]), (tok, tok_v)]
            + [(dw_b.at[pl.ds(me.g * PLANE, PLANE)], sb_v), (resid.at[pl.ds(length, 8)], gains)]
            + [(dw_b.at[pl.ds(far * PLANE + FIRST, PLANE - FIRST)], far_b), (out_red.at[pl.ds(0, 4)], l_red), (out_red.at[4, pl.ds(0, sd_v.shape[0])], sd_v)]
        )
    ]

    span = PLANE * r

    turns = ((3, 2, 1, 0), (0, 2, 3, 1), (3, 1, 0, 2), (0, 1, 2, 3))

    def turn_of(i):
        return sum(jnp.where(me.g == b, turns[b][i], 0) for b in range(planes))

    def nrm_copy(m):
        at = pl.ds(pl.multiple_of(turn_of(m % planes) * span, 128), span)
        return pltpu.make_async_copy(nrm_all.at[:, :, at], nrm_v.at[m % 2], loc.at[8 + m % 2])

    def row_copies(i):
        row = order(me, i)[0]
        at = lax.rem(i, SLOTS)
        cps = [pltpu.make_async_copy(branch_all.at[row], gb_v.at[row], row_in.at[0, i])]
        for j, (src, dst) in enumerate(((qkv_all, qkv_v), (p_all, p_v), (m_all, m_v))):
            cps.append(pltpu.make_async_copy(src.at[row], dst.at[at], row_in.at[j + 1, i]))
        return cps

    me.hail()
    taps_in = [pltpu.make_async_copy(kern_in, kern, loc.at[10]), pltpu.make_async_copy(mix_in, mix, loc.at[11])]
    for cp in taps_in:
        cp.start()
    wo_v[...] = jnp.zeros(wo_v.shape, BF16)
    loads[1].start()
    loads[0].start()
    for i in range(SLOTS):
        for cp in row_copies(i):
            cp.start()
    for cp in loads[2:]:
        cp.start()
    for j in range(2):
        nrm_copy(j).start()
    for cp in taps_in:
        cp.wait()
    for g in range(2):
        for a, t in bands(kern, 2 * me.pair + g, length, True):
            t_v[g, a * length : (a + 1) * length] = t.astype(BF16)
    shift_v[length:] = jnp.zeros((8, length), F32)
    corr_v[...] = jnp.zeros(corr_v.shape, F32)
    rows_v[...] = jnp.zeros(rows_v.shape, F32)
    small_v[...] = jnp.zeros(small_v.shape, F32)
    me.await_all()

    blocks4 = lambda ref: (lambda b: ref.at[pl.ds(b * PLANE, PLANE)])
    sum_b = Collect(me, lambda b: dw_b.at[pl.ds(b * PLANE + FIRST, PLANE - FIRST)], zb_v, via_b, z_send.at[0], z_recv.at[0])
    sum_a = Collect(me, blocks4(da_v), za_v, via_a, z_send.at[1], z_recv.at[1])
    sum_c = Collect(me, blocks4(dc_v), zc_v, via_c, z_send.at[3], z_recv.at[3])
    sum_o = Collect(me, lambda b: do_v.at[pl.ds(b, 1)], zo_v, via_o, z_send.at[2], z_recv.at[2])
    send_s = []
    for d in range(1, planes):
        to = lax.rem(me.g + d, planes)
        send_s.append(remote(small_v, small_in.at[d - 1], small_send.at[d - 1], small_recv.at[d - 1], me.plane_dev(to)))
    send_l = []
    for d in range(1, planes):
        to = lax.rem(me.g + d, planes)
        send_l.append(remote(last_v, last_in.at[d - 1], line_send.at[d - 1], line_recv.at[d - 1], me.plane_dev(to)))
    sum_b.start()
    for group in (sum_b, sum_a, sum_c, sum_o):
        group.clear()
    h0, h1 = head_lanes(length, dh)
    scatter = Scatter(me, s_out, s_red, s_diag, s_near, rs_send, rs_recv)
    layer = Scatter(me, None, l_red, l_diag, l_near, l_send, l_recv)
    def to_slot(d):
        to = lax.rem(me.slot + d, GROUP)
        return lax.div(to, PLANE), lax.rem(to, PLANE)

    def group_copies(kind, src_of, landing, places=None):
        def one_of(d):
            y, sl = to_slot(d)
            return remote(src_of(sl), landing.at[me.slot], t_send.at[kind, d], t_recv.at[kind, d], (y, me.g * PLANE + sl))

        own = pltpu.make_async_copy(src_of(me.s), landing.at[me.slot], t_send.at[kind, 0])
        cps = [one_of(d) for d in range(1, GROUP)] + [own]
        for d, cp in enumerate(cps, 1):
            if places is None:
                cp.start()
            else:
                sl = to_slot(d % GROUP)[1]
                pl.when((sl >= places[0]) & (sl < places[1]))(cp.start)
        return cps

    def group_wait(kind, cps, landing):
        for d in range(1, GROUP):
            fr = lax.rem(me.slot - d + GROUP, GROUP)
            remote(landing.at[fr], landing.at[fr], t_send.at[kind, d], t_recv.at[kind, d], me.sib).wait_recv()
        for cp in cps[:-1]:
            cp.wait_send()
        cps[-1].wait()

    loads[0].wait()
    loads[1].wait()
    loads[5].wait()
    loads[6].wait()
    layer.push(1)
    layer.push(3)
    layer.ahead()
    loads[3].wait()
    loads[4].wait()
    group_copies(0, lambda sl: sb_v.at[sl], out_b, (0, FIRST))
    loads[7].wait()
    d_cp = remote(sd_v, out_d.at[me.y], t_send.at[3, 0], t_recv.at[3, 0], me.yn)
    d_cp.start()
    d_here = pltpu.make_async_copy(sd_v, out_d.at[me.y], t_send.at[3, 1])
    d_here.start()

    mixing = pair_mixing(mix, me.pair)

    def one(i, carry):
        row, k = order(me, i)
        at = lax.rem(i, SLOTS)
        for cp in row_copies(i):
            cp.wait()
        wo = wo_v[...].reshape(wo_v.shape[0] * wo_v.shape[1], width)[0:SIDE]
        q, kk, v = qkv_v[at, :, 0:SIDE], qkv_v[at, :, SIDE : 2 * SIDE], qkv_v[at, :, 2 * SIDE : 3 * SIDE]
        parts = [nn(p_v[at, g, 0], v) + nn(p_v[at, g, 1], v) for g in range(2)]
        probs = [p_v[at, g, 0].astype(F32) + p_v[at, g, 1].astype(F32) for g in range(2)]
        lane_mix = [mix_lanes(mixing, g, dh) for g in range(2)]
        attended = parts[0] * lane_mix[0] + parts[1] * lane_mix[1]
        centred = jnp.where(h0 | h1, attended - head_stats(attended, dh, h0, h1), 0.0)
        inv = lax.rsqrt(head_stats(centred * centred, dh, h0, h1) + 1e-5)
        normal = centred * inv
        g_gated = nt(gb_v[row], wo)
        rows_v[0:1] = rows_v[0:1] + jnp.sum(g_gated * normal, axis=0, keepdims=True)
        u = g_gated * gains[2:3, 0:SIDE]
        g_att = inv * (u - head_stats(u, dh, h0, h1) - normal * head_stats(u * normal, dh, h0, h1))
        g_exact = jnp.where(h0 | h1, g_att, 0.0)
        g_att = g_exact.astype(BF16).astype(F32)
        ok = allowed_mask(length, ends[row, 0:1, :])
        g_q = jnp.zeros((length, SIDE), F32)
        g_k = jnp.zeros((length, SIDE), F32)
        g_v = jnp.zeros((length, SIDE), F32)
        for o in range(2):
            mixed = mixing[o][0] * probs[0] + mixing[o][1] * probs[1]
            g_v = g_v + tn(mixed.astype(BF16), jnp.where(h0 if o == 0 else h1, g_att, 0.0).astype(BF16))
        for g in range(2):
            mine = h0 if g == 0 else h1
            rows_v[1 + g : 2 + g] = rows_v[1 + g : 2 + g] + jnp.sum(g_exact * parts[g], axis=0, keepdims=True)
            g_out = (g_att * lane_mix[g]).astype(BF16)
            g_probs = nt(g_out, v)
            g_conv = probs[g] * (g_probs - jnp.sum(probs[g] * g_probs, axis=-1, keepdims=True))
            shift_v[0:length] = g_conv
            for a in range(taps_q):
                cat_v[:, a * length : (a + 1) * length] = shift_v[a : a + length].astype(BF16)
            corr_v[g] = corr_v[g] + tn(m_v[at, g], cat_v[...])
            g_raw = jnp.where(ok, nn(cat_v[...], t_v[g]), 0.0).astype(BF16)
            g_q = g_q + nn(g_raw, jnp.where(mine, kk.astype(F32), 0.0).astype(BF16))
            g_k = g_k + tn(g_raw, jnp.where(mine, q.astype(F32), 0.0).astype(BF16))
        g_q, g_k = g_q * scale, g_k * scale
        mid_tile = g_q[:, 128:256] + pltpu.roll(g_v[:, 128:256], 64, 1)
        packed = jnp.concatenate([g_q[:, 0:128], mid_tile, g_k, g_v[:, 0:128]], axis=1).astype(BF16)
        gq_v[row] = packed
        part = nt(packed, wa_v[...].reshape(width, QKV))

        @pl.when(lax.rem(i, 2) == 0)
        def _():
            scatter.put_sib(k, part)

        @pl.when(lax.rem(i, 2) == 1)
        def _():
            scatter.put_self(k, part)

        scatter.push(i, turn=False)

        @pl.when(i + SLOTS < GROUP)
        def _():
            for cp in row_copies(i + SLOTS):
                cp.start()

        @pl.when(i == 4)
        def _():
            layer.turn()

        @pl.when(i == 5)
        def _():
            sum_b.combine(lambda t: far_b)

        return carry

    lax.fori_loop(0, GROUP, one, 0)
    loads[2].wait()
    gated_in = [
        pltpu.make_async_copy(gated_all.at[i], p_v.at[i // 4, i // 2 % 2, i % 2], row_in.at[0, i]) for i in range(GROUP)
    ]
    for cp in gated_in:
        cp.start()

    def taps(at, carry):
        g, a = lax.div(at, taps_q), lax.rem(at, taps_q)
        lanes_at = pl.ds(pl.multiple_of(a * length, length), length)
        e = corr_v[g, :, lanes_at]
        diff = lax.broadcasted_iota(jnp.int32, (length, length), 0) - lax.broadcasted_iota(jnp.int32, (length, length), 1)
        for b in range(taps_k):
            line = jnp.sum(jnp.where(diff == b - taps_k // 2, e, 0.0), axis=0, keepdims=True)
            taps_v[b : b + 1] = line[:, 0:128] + line[:, 128:256]
        each = jnp.sum(taps_v[...], axis=-1, keepdims=True)
        small_v[0] = jnp.where(lanes(16, 128) == a * 2 * GROUP + 2 * me.pair + g, each, small_v[0])
        return carry

    taps_v[...] = jnp.zeros(taps_v.shape, F32)
    lax.fori_loop(0, 2 * taps_q, taps, 0)
    base = 1
    at = lanes(1, SIDE)
    for o in range(2):
        for g in range(2):
            line = jnp.where((at >= o * dh) & (at < (o + 1) * dh), rows_v[1 + g : 2 + g], 0.0)
            small_v[base, 2 * o + g : 2 * o + g + 1] = line[:, 0:128] + line[:, 128:256]
    for j in range(2):
        small_v[base, 4 + j : 5 + j] = rows_v[0:1, j * 128 : (j + 1) * 128]

    for j in range(width // 128):
        small_v[2, j : j + 1] = g_res[length : length + 1, j * 128 : (j + 1) * 128]
    for cp in send_s:
        cp.start()

    tokens = GROUP * length
    for cp in gated_in:
        cp.wait()
    value = tn(p_v[...].reshape(tokens, SIDE), gb_v[...].reshape(tokens, width))
    do_v[...] = value[0 : 2 * dh].astype(BF16).reshape(do_v.shape)

    sum_o.start()
    for m in range(2 * planes):
        i, first_part = m % planes, m < planes
        nrm_copy(m).wait()
        at = slice(0, SIDE) if first_part else slice(SIDE, QKV)
        value = tn(nrm_v[m % 2].reshape(tokens, span), gq_v[:, :, at].reshape(tokens, at.stop - at.start))
        terms = da_v if first_part else dc_v
        terms[pl.ds(turn_of(i) * PLANE, PLANE)] = value.astype(BF16).reshape((PLANE,) + terms.shape[1:])
        if m + 2 < 2 * planes:
            nrm_copy(m + 2).start()
    for way in (True, False):
        sum_a.start((way,))
        sum_c.start((way,))
    scatter.turn()
    sum_b.total(sb_v.at[pl.ds(FIRST, PLANE - FIRST)], sb_v.at[pl.ds(FIRST, PLANE - FIRST)])
    b_cps = group_copies(0, lambda sl: sb_v.at[sl], out_b, (FIRST, PLANE))

    for cp in send_s:
        cp.wait_recv()
    for cp in send_s:
        cp.wait_send()
    small_v[...] = small_v[...] + sum(small_in[d] for d in range(planes - 1))
    small_cps = group_copies(2, lambda sl: small_v, out_small)

    sum_o.combine(lambda t: do_v.at[pl.ds(t, 1)])
    sum_a.combine(lambda t: da_v.at[pl.ds(t * PLANE, PLANE)])

    sum_c.combine(lambda t: dc_v.at[pl.ds(t * PLANE, PLANE)])

    layer.arrive()

    def result(at):
        cp = pltpu.make_async_copy(resid.at[at], strip_v, loc.at[0])
        cp.start()
        cp.wait()
        strip_v[...] = strip_v[...] + layer.total(at)
        cp = pltpu.make_async_copy(strip_v, layer_out.at[at], loc.at[0])
        cp.start()
        cp.wait()

    strips(length, result)

    scatter.arrive()

    def middle(at):
        g_normed = scatter.total(at)
        tok32 = tok_v[at].astype(F32)
        s = lax.rsqrt(jnp.mean(tok32 * tok32, axis=-1, keepdims=True) + 1e-6)
        line_v[0:1] = line_v[0:1] + jnp.sum(g_normed * tok32 * s, axis=0, keepdims=True)
        pulled = g_normed * gains[0:1]
        back = g_res[at] + s * pulled
        g_tokens[at] = back - tok32 * (s * s * s * jnp.mean(pulled * tok32, axis=-1, keepdims=True))

    line_v[...] = jnp.zeros(line_v.shape, F32)
    strips(length, middle)
    line = line_v[0:1]
    last_v[...] = jnp.zeros(last_v.shape, F32)
    for j in range(width // 128):
        last_v[j : j + 1] = line[:, j * 128 : (j + 1) * 128]
    for cp in send_l:
        cp.start()

    sum_o.total(so_v, do_v.at[pl.ds(me.g, 1)])
    o_to = me.pair * per_pair + lax.div(me.g, 2)
    o_half = lax.rem(me.g, 2)

    def o_copy(y):
        return remote(so_v.at[0], out_o.at[o_half], t_send.at[4, y], t_recv.at[4, o_half], (y, o_to))

    o_here = pltpu.make_async_copy(so_v.at[0], out_o.at[o_half], t_send.at[4, 2])

    def o_each(act, act_here):
        for y in range(2):
            mine = (y == me.y) & (o_to == me.f)

            @pl.when(jnp.logical_not(mine))
            def _():
                act(o_copy(y))

            @pl.when(mine)
            def _():
                act_here(o_here)

    o_each(lambda cp: cp.start(), lambda cp: cp.start())
    sum_a.total(sa_v, da_v.at[pl.ds(me.g * PLANE, PLANE)])
    a_cps = group_copies(1, lambda sl: sa_v.at[sl], out_a)

    sum_c.total(sc_v, dc_v.at[pl.ds(me.g * PLANE, PLANE)])
    c_cps = group_copies(5, lambda sl: sc_v.at[sl], out_c)

    for cp in send_l:
        cp.wait_recv()
    for cp in send_l:
        cp.wait_send()
    last_v[...] = last_v[...] + sum(last_in[d] for d in range(planes - 1))
    line_cps = group_copies(6, lambda sl: last_v, out_line)

    group_wait(2, small_cps, out_small)
    d_cp.wait_send()
    remote(out_d.at[1 - me.y], out_d.at[1 - me.y], t_send.at[3, 0], t_recv.at[3, 0], me.yn).wait_recv()
    d_here.wait()
    group_wait(0, b_cps, out_b)
    src_y = jnp.where((me.g == 1) | (me.g == 2), 1, 0)
    src_s = me.x * 2 + jnp.where(me.g >= 2, 1, 0)
    for h in range(2):
        src_f = (2 * lax.rem(me.f, per_pair) + h) * PLANE + src_s

        @pl.when(jnp.logical_not((src_y == me.y) & (src_f == me.f)))
        def _():
            remote(out_o.at[h], out_o.at[h], t_send.at[4, 0], t_recv.at[4, h], me.sib).wait_recv()

    o_each(lambda cp: cp.wait_send(), lambda cp: cp.wait())
    group_wait(1, a_cps, out_a)
    group_wait(5, c_cps, out_c)
    group_wait(6, line_cps, out_line)
    for group in (sum_b, sum_a, sum_c, sum_o):
        group.finish()
    scatter.finish_cores()
    scatter.finish_chips()
    layer.finish_chips()


def backward_call(cfg, *args):
    branch_all, o_all, a_all, tok = args[0], args[1], args[2], args[10]
    length, width = tok.shape
    planes, ff = cfg["planes"], cfg["ff"]
    n, r = a_all.shape[:2]
    chunk = ff // planes
    taps = cfg["kq"] * length
    pad_rows = -(-SIDE // o_all.shape[1])
    piece = 2 * cfg["dh"] // planes
    small = (3, 16, 128)
    hbm, vmem, smem = pl.BlockSpec(memory_space=pl.ANY), pl.BlockSpec(memory_space=pltpu.VMEM), pl.BlockSpec(memory_space=pltpu.SMEM)
    sds = jax.ShapeDtypeStruct
    dma = pltpu.SemaphoreType.DMA
    rows = (GROUP, length)
    others = planes - 1
    v16 = lambda *shape: pltpu.VMEM(shape, BF16)
    v32 = lambda *shape: pltpu.VMEM(shape, F32)
    b_block, o_block = (PLANE - FIRST, r, 2 * ff), (1, piece, width)
    a_block, c_block = (PLANE, r, SIDE), (PLANE, r, QKV - SIDE)
    return pl.pallas_call(
        functools.partial(backward_kernel, cfg),
        out_shape=(
            sds((length, width), F32), sds((length, width), F32), sds((GROUP, r, SIDE), BF16), sds((GROUP, r, QKV - SIDE), BF16),
            sds((GROUP, r, 2 * ff), BF16),
            sds((2, chunk, width), BF16), sds((2, piece, width), BF16), sds((GROUP,) + small, F32), sds((GROUP, 16, 128), F32),
        ),
        in_specs=[hbm] * 14 + [vmem] * 2,
        out_specs=(vmem,) + (hbm,) * 8,
        scratch_shapes=[
            v32(8, width), v32(*args[12].shape), v32(*args[13].shape), v16(*rows, width), v16(pad_rows, *o_all.shape[1:]), v16(n, r, QKV), v16(2, *rows, PLANE * r), v16(SLOTS, length, 3 * SIDE),
            v16(SLOTS, 2, 2, length, length), v16(SLOTS, 2, length, length),
            v16(2, taps, length), v16(length, taps), v32(length + 8, length), v32(2, length, taps), v16(*rows, QKV),
            v16(n, r, SIDE), v16(n, r, QKV - SIDE), v16(planes, piece, width), v16(length, width), v32(8, SIDE), v32(8, width), v32(16, 128),
            v16(others, *b_block), v16(others, *a_block), v16(others, *c_block), v16(others, *o_block),
            v16(*b_block), v16(*a_block), v16(*c_block), v16(*o_block),
            v16(PLANE, r, 2 * ff), v16(*a_block), v16(*c_block), v16(*o_block), v16(*b_block), v32(64, width), v16(chunk, width),
            v32(*small), v32(others, *small), v32(16, 128), v32(others, 16, 128),
            *Scatter.scratch(length, width), *Scatter.scratch(length, width, cores=False),
            dma((4, planes)), dma((4, planes)), dma((others,)), dma((others,)), dma((others,)), dma((others,)), dma((7, GROUP)), dma((7, GROUP)),
            dma((12,)), dma((4, GROUP)),
        ],
        compiler_params=pltpu.CompilerParams(collective_id=3, has_side_effects=True, vmem_limit_bytes=54 * 2**20),
        name="attention_backward",
    )(*args)


def results_kernel(cfg, a_ref, c_ref, b_ref, d_ref, o_ref, small_ref, line_ref, g_tok, layer, qkv_ref, gate_ref, up_ref, down_ref, out_ref,
                   taps_ref, mix_ref, in_ref, mid_ref, heads_ref, tok_ref, layer_ref, vec_v):
    planes, ff = cfg["planes"], cfg["ff"]
    rows, width = out_ref.shape
    chunk = ff // planes
    low = lanes(rows, 128) < 64

    def slot(pair):
        home, x = pair // 2, pair % 2
        y, c = (0, 1, 1, 0)[home], (0, 0, 1, 1)[home]
        return y * PLANE + x * 2 + c

    def joined(even, odd, low):
        o0, o1 = pltpu.roll(odd[0], 64, 1), pltpu.roll(odd[1], 64, 1)
        return even[0], jnp.where(low, even[1], o0), jnp.where(low, o0, o1)

    def tiles(pair, j):
        def t(i):
            ref, i = (a_ref, i) if i < 2 else (c_ref, i - 2)
            return ref[slot(pair), :, i * 128 : (i + 1) * 128].astype(F32)

        if j == 2:
            return t(4), pltpu.roll(t(1), 64, 1)
        return t(2 * j), t(2 * j + 1)

    for j in range(3):
        for two in range(GROUP // 2):
            for i, t in enumerate(joined(tiles(2 * two, j), tiles(2 * two + 1, j), low)):
                at = j * width + two * 384 + i * 128
                qkv_ref[:, at : at + 128] = t
    for z in range(planes):
        for s in range(PLANE):
            for y in range(2):
                at = ((z * PLANE + s) * 2 + y) * chunk
                src = b_ref.at[y * PLANE + s]
                gate_ref[:, at : at + chunk] = src[:, z * chunk : (z + 1) * chunk].astype(F32)
                up_ref[:, at : at + chunk] = src[:, ff + z * chunk : ff + (z + 1) * chunk].astype(F32)
    down_ref[...] = d_ref[0].astype(F32)
    out_ref[...] = o_ref[0].astype(F32)

    tok_ref[...] = g_tok[...]
    layer_ref[...] = layer[...]

    @pl.when(pl.program_id(0) == 0)
    def _():
        base = 1
        heads = 2 * GROUP
        taps = small_ref[0, 0]
        for s in range(1, GROUP):
            taps = taps + small_ref[s, 0]
        for k in range(cfg["kk"]):
            for q in range(cfg["kq"]):
                taps_ref[k, q : q + 1] = taps[k : k + 1, q * heads : (q + 1) * heads]
        mixed = [jnp.sum(small_ref[slot(pair), base], axis=-1, keepdims=True) for pair in range(GROUP)]
        for g in range(2):
            line = jnp.zeros((1, heads), F32)
            for pair in range(GROUP):
                for o in range(2):
                    k = 2 * o + g
                    line = jnp.where(lanes(1, heads) == 2 * pair + o, mixed[pair][k : k + 1], line)
            mix_ref[g : g + 1] = line
        vec_v[...] = jnp.zeros(vec_v.shape, F32)
        for k, part in enumerate((lambda s: line_ref[s], lambda s: small_ref[s, base + 1])):
            total = part(0)
            for s in range(1, GROUP):
                total = total + part(s)
            for j in range(width // 128):
                vec_v[k : k + 1, j * 128 : (j + 1) * 128] = total[j : j + 1]
        line = lambda pair: tuple(small_ref[slot(pair), base, 4 + j : 5 + j] for j in range(2))
        for two in range(GROUP // 2):
            for i, t in enumerate(joined(line(2 * two), line(2 * two + 1), lanes(1, 128) < 64)):
                vec_v[2:3, two * 384 + i * 128 : two * 384 + (i + 1) * 128] = t
        own = in_ref.shape[1]
        mine = pltpu.roll(vec_v[...], lax.rem(width - lax.axis_index("fsdp") * own, width), 1)
        for k, ref in enumerate((in_ref, mid_ref, heads_ref)):
            ref[...] = mine[k : k + 1, 0:own]


def results_call(cfg, out_a, out_c, out_b, out_d, out_o, small, line, g_tokens, layer_out):
    r = out_a.shape[1]
    _, chunk, width = out_d.shape
    half = r // 2
    step = 16
    steps = r // step
    quarter = g_tokens.shape[0] // 4
    sds = jax.ShapeDtypeStruct
    whole = lambda shape: pl.BlockSpec(shape, lambda i: (0,) * len(shape))
    rows = lambda n, w: pl.BlockSpec((n, w), lambda i: (i, 0))
    few = lambda n, w, count: pl.BlockSpec((n, w), lambda i: (jnp.minimum(i, count - 1), 0))
    moved = 6 * (out_a.size + out_c.size + out_b.size + out_d.size + out_o.size) + 16 * g_tokens.size
    return pl.pallas_call(
        functools.partial(results_kernel, cfg),
        grid=(steps,),
        out_shape=(
            sds((r, 3 * width), F32), sds((r, n_cols(cfg)), F32), sds((r, n_cols(cfg)), F32), sds((2 * chunk, width), F32),
            sds((r, width), F32), sds((cfg["kk"], cfg["kq"], 2 * GROUP), F32), sds((2, 2 * GROUP), F32),
            sds((1, r), F32), sds((1, r), F32), sds((1, r), F32), sds(g_tokens.shape, F32), sds(g_tokens.shape, F32),
        ),
        in_specs=[
            pl.BlockSpec((GROUP, step, out_a.shape[2]), lambda i: (0, i, 0)),
            pl.BlockSpec((GROUP, step, out_c.shape[2]), lambda i: (0, i, 0)),
            pl.BlockSpec((GROUP, step, out_b.shape[2]), lambda i: (0, i, 0)),
            pl.BlockSpec((1, chunk, width), lambda i: (jnp.minimum(i, 1), 0, 0)),
            pl.BlockSpec((1, step, width), lambda i: (lax.div(i, half // step), lax.rem(i, half // step), 0)),
            whole(small.shape),
            whole(line.shape),
            few(quarter, width, 4),
            few(quarter, width, 4),
        ],
        scratch_shapes=[pltpu.VMEM((8, width), F32)],
        out_specs=(
            rows(step, 3 * width), rows(step, n_cols(cfg)), rows(step, n_cols(cfg)), few(chunk, width, 2), rows(step, width),
            whole((cfg["kk"], cfg["kq"], 2 * GROUP)), whole((2, 2 * GROUP)),
            whole((1, r)), whole((1, r)), whole((1, r)), few(quarter, width, 4), few(quarter, width, 4),
        ),
        compiler_params=pltpu.CompilerParams(vmem_limit_bytes=60 * 2**20),
        cost_estimate=pl.CostEstimate(flops=0, bytes_accessed=moved, transcendentals=0),
        name="results",
    )(out_a, out_c, out_b, out_d, out_o, small, line, g_tokens, layer_out)


def n_cols(cfg):
    return cfg["ff"] * GROUP


def fits(mesh, tokens, kernel, w_gate):
    n = mesh.shape["fsdp"]
    width, length, heads, ff = tokens.shape[2], tokens.shape[1], kernel.shape[0], w_gate.shape[1]
    return (
        mesh.shape["rep"] == 2
        and n == 4 * PLANE
        and heads == 2 * GROUP
        and width == heads * 96
        and (width // n) % 32 == 0
        and ff % (2 * n * 128) == 0
        and length == SIDE
    )


def per_device_group(
    planes,
    tokens,
    doc_lengths,
    pad_counts,
    norm_in,
    w_qkv,
    kernel,
    mixing,
    norm_heads,
    w_out,
    norm_mid,
    w_gate,
    w_up,
    w_down,
    cotangent,
):
    length, width = tokens.shape[1:]
    heads, kq, kk = kernel.shape
    dh = width // heads
    n = planes * PLANE
    r = width // n
    chunk = w_down.shape[0] // 2
    ff = planes * chunk
    cfg = dict(planes=planes, dh=dh, kq=kq, kk=kk, ff=ff)

    gain_rows = jnp.pad(jnp.stack([norm_in, norm_mid, norm_heads]).astype(F32), ((0, 5), (0, 128 - r)))
    tok, ct = tokens[0], cotangent[0]
    kern, mix = kernel.transpose(2, 1, 0), mixing.T

    (_, ct_all, a_all, b_all, d_all, o_all, nrm_all, qkv_all, p_all, m_all, gated_all, mid_all, resid, ends) = (
        forward_call(
            cfg, tok, ct, w_qkv, w_gate, w_up, w_down, w_out, kern, mix, gain_rows, doc_lengths, pad_counts
        )
    )
    g_res, branch_all, dw_b, out_red = feed_call(cfg, mid_all, ct_all, b_all, d_all, resid)
    g_tokens, layer_out, out_a, out_c, out_b, out_d, out_o, small, line = backward_call(
        cfg, branch_all, o_all, a_all, nrm_all, qkv_all, p_all, m_all, gated_all, dw_b.reshape(n, r, 2 * ff), out_red,
        tok, resid, kern, mix, g_res, ends,
    )

    g_qkv, g_gate, g_up, g_down, g_out, g_kernel, g_mixing, g_in, g_mid, g_heads, g_tokens, layer_out = results_call(
        cfg, out_a, out_c, out_b, out_d, out_o, small, line, g_tokens, layer_out
    )
    return (
        layer_out[None],
        g_tokens[None],
        g_in[0],
        g_qkv,
        g_kernel.transpose(2, 1, 0),
        g_mixing.T,
        g_heads[0],
        g_out,
        g_mid[0],
        g_gate,
        g_up,
        g_down,
    )


def solution(mesh):
    in_specs = (
        P(("rep", "fsdp"), None, None),
        P(("rep", "fsdp"), None),
        P(("rep", "fsdp")),
        P("fsdp"),
        P("fsdp", None),
        P(),
        P(),
        P("fsdp"),
        P("fsdp", None),
        P("fsdp"),
        P("fsdp", None),
        P("fsdp", None),
        P("fsdp", None),
        P(("rep", "fsdp"), None, None),
    )
    out_specs = (
        P(("rep", "fsdp"), None, None),
        P(("rep", "fsdp"), None, None),
        P("fsdp"),
        P("fsdp", None),
        P(),
        P(),
        P("fsdp"),
        P("fsdp", None),
        P("fsdp"),
        P("fsdp", None),
        P("fsdp", None),
        P("fsdp", None),
    )

    def layer(*args):
        body = per_device
        if fits(mesh, args[0], args[5], args[10]):
            body = functools.partial(per_device_group, mesh.shape["fsdp"] // PLANE)
        return jax.shard_map(body, mesh=mesh, in_specs=in_specs, out_specs=out_specs, check_vma=False)(*args)

    return layer
```

```python
import functools

import jax
import jax.numpy as jnp
from jax import lax
from jax.experimental import pallas as pl
from jax.experimental.pallas import tpu as pltpu
from jax.sharding import PartitionSpec as P

F32 = jnp.float32
BF16 = jnp.bfloat16
NEG_FILL = -1e30
MESH = pl.DeviceIdType.MESH
PLANE = 4
GROUP = 8
SIDE = 256
FIRST = 1
SLOTS = 2
QKV = 640


class Place:
    def __init__(self, planes):
        self.planes = planes
        self.y = lax.axis_index("rep")
        self.f = lax.axis_index("fsdp")
        self.g = lax.div(self.f, PLANE)
        self.s = lax.rem(self.f, PLANE)
        self.x = lax.div(self.s, 2)
        self.c = lax.rem(self.s, 2)
        self.slot = self.y * PLANE + self.s
        self.home = self.y + self.c * (planes - 1 - 2 * self.y)
        self.pair = 2 * self.home + self.x
        self.sib = self.dev(self.y, self.x, 1 - self.c)
        self.xn = self.dev(self.y, 1 - self.x, self.c)
        self.yn = self.dev(1 - self.y, self.x, self.c)

    def dev(self, y, x, c):
        return (y, self.g * PLANE + x * 2 + c)

    def plane_dev(self, g):
        return (self.y, g * PLANE + self.s)

    def row(self, dy, dx, dc):
        y = self.y + dy - 2 * dy * self.y
        x = self.x + dx - 2 * dx * self.x
        c = self.c + dc - 2 * dc * self.c
        return y * 4 + x * 2 + c

    def hail(self):
        sem = pltpu.get_barrier_semaphore()
        n = self.planes * PLANE
        for d in range(1, n):
            pl.semaphore_signal(sem, inc=1, device_id=(self.y, lax.rem(self.f + d, n)), device_id_type=MESH)
        for s in range(PLANE):
            pl.semaphore_signal(sem, inc=1, device_id=(1 - self.y, self.g * PLANE + s), device_id_type=MESH)

    def await_all(self):
        pl.semaphore_wait(pltpu.get_barrier_semaphore(), self.planes * PLANE - 1 + PLANE)


def meet(me, sem):
    pl.semaphore_signal(sem, inc=1, device_id=me.sib, device_id_type=MESH)
    pl.semaphore_wait(sem, 1)


def remote(src, dst, send, recv, dev):
    return pltpu.make_async_remote_copy(
        src_ref=src, dst_ref=dst, send_sem=send, recv_sem=recv, device_id=dev, device_id_type=MESH
    )


class Gather:
    SENDS = 14
    RECVS = 14

    def __init__(self, me, own, buf, send, recv, local):
        self.me, self.own, self.buf = me, own, buf
        self.send, self.recv, self.local = send, recv, local
        self.half = own.shape[0] // 2
        self.sent = []

    def _own(self, h):
        return self.own.at[pl.ds(h * self.half, self.half)]

    def _blk(self, row, h):
        return self.buf.at[row, pl.ds(h * self.half, self.half)]

    def _copy(self, i):
        own, row, h, kind, dev = self.sent[i]
        src = self._own(h) if own else self._blk(row, h)
        return remote(src, self._blk(row, h), self.send.at[i], self.recv.at[kind * 2 + h], dev)

    def _go(self, own, row, h, kind, dev):
        self.sent.append((own, row, h, kind, dev))
        self._copy(len(self.sent) - 1).start()

    def _await(self, row, h, kind):
        b = self._blk(row, h)
        remote(b, b, self.send.at[0], self.recv.at[kind * 2 + h], self.me.sib).wait_recv()

    def start(self):
        me = self.me
        self.rows = [me.row(0, 0, 1), me.row(0, 1, 0), me.row(1, 0, 0), me.row(1, 1, 0), me.row(0, 1, 1), me.row(1, 0, 1), me.row(1, 1, 1)]
        self.here = pltpu.make_async_copy(self.own, self.buf.at[me.slot], self.local)
        self.here.start()
        self._go(True, me.slot, 0, 1, me.xn)
        self._go(True, me.slot, 1, 2, me.yn)
        self._go(True, me.slot, 0, 0, me.sib)
        self._go(True, me.slot, 1, 0, me.sib)
        self._go(True, me.slot, 1, 1, me.xn)
        self._go(True, me.slot, 0, 2, me.yn)

    def relay(self):
        me, rows = self.me, self.rows
        self._await(rows[1], 0, 1)
        self._go(False, rows[1], 0, 3, me.yn)
        self._go(False, rows[1], 0, 4, me.sib)
        self._await(rows[2], 1, 2)
        self._go(False, rows[2], 1, 3, me.xn)
        self._go(False, rows[2], 1, 5, me.sib)

    def share(self):
        me, rows = self.me, self.rows
        self._await(rows[1], 1, 1)
        self._go(False, rows[1], 1, 4, me.sib)
        self._await(rows[2], 0, 2)
        self._go(False, rows[2], 0, 5, me.sib)

    def last(self):
        me, rows = self.me, self.rows
        for h in (0, 1):
            self._await(rows[3], h, 3)
            self._go(False, rows[3], h, 6, me.sib)

    def finish(self):
        for kind in (0, 4, 5, 6):
            for h in (0, 1):
                self._await(self.rows[kind], h, kind)
        for i in range(len(self.sent)):
            self._copy(i).wait_send()
        self.here.wait()


class Scatter:
    SENDS = 10
    RECVS = 10

    @staticmethod
    def scratch(rows, width, cores=True, chips=True):
        bufs = []
        if cores:
            bufs.append(pltpu.VMEM((2, rows, width), BF16))
        bufs.append(pltpu.VMEM((4, rows, width), BF16))
        if chips:
            bufs += [pltpu.VMEM((2, rows // 2, width), BF16), pltpu.VMEM((2, rows, width), BF16)]
        return bufs + [pltpu.SemaphoreType.DMA((Scatter.SENDS,)), pltpu.SemaphoreType.DMA((Scatter.RECVS,))]

    def __init__(self, me, out, red, diag, near, send, recv):
        self.me, self.out, self.red, self.diag, self.near = me, out, red, diag, near
        self.send, self.recv = send, recv
        self.half = red.shape[1] // 2

    def _sib(self, k):
        return remote(self.out.at[lax.rem(k, 2)], self.red.at[k], self.send.at[k], self.recv.at[k], self.me.sib)

    def put_sib(self, k, value):
        @pl.when(k >= 2)
        def _():
            self._sib(k - 2).wait_send()

        self.out[lax.rem(k, 2)] = value.astype(BF16)
        self._sib(k).start()

    def put_self(self, k, value):
        self._sib(k).wait_recv()
        self.red[k] = (value + self.red[k].astype(F32)).astype(BF16)

    def _copy(self, name):
        h, me = self.half, self.me
        lo, hi = pl.ds(0, h), pl.ds(h, h)
        src, dst, i, dev = {
            "da": (self.red.at[0, lo], self.diag.at[0], 4, me.xn),
            "db": (self.red.at[0, hi], self.diag.at[1], 5, me.yn),
            "xa": (self.red.at[1, lo], self.near.at[0, lo], 6, me.xn),
            "xb": (self.red.at[1, hi], self.near.at[0, hi], 7, me.xn),
            "ya": (self.red.at[2, lo], self.near.at[1, lo], 8, me.yn),
            "yb": (self.red.at[2, hi], self.near.at[1, hi], 9, me.yn),
        }[name]
        return remote(src, dst, self.send.at[i], self.recv.at[i], dev)

    def push(self, i, turn=True):
        @pl.when(i == 1)
        def _():
            self._copy("da").start()
            self._copy("db").start()

        @pl.when(i == 3)
        def _():
            self._copy("xa").start()

        @pl.when(i == 5)
        def _():
            self._copy("yb").start()
            if turn:
                self.turn()

    def ahead(self):
        self._copy("yb").start()

    def turn(self):
        h = self.half
        self._copy("db").wait_recv()
        self.red[1, h:] = (self.red[1, h:].astype(F32) + self.diag[1].astype(F32)).astype(BF16)
        self._copy("xb").start()
        self._copy("da").wait_recv()
        self.red[2, :h] = (self.red[2, :h].astype(F32) + self.diag[0].astype(F32)).astype(BF16)
        self._copy("ya").start()

    def arrive(self):
        for name in ("xa", "xb", "ya", "yb"):
            self._copy(name).wait_recv()

    def total(self, at):
        return self.red[3, at].astype(F32) + self.near[0, at].astype(F32) + self.near[1, at].astype(F32)

    def finish_cores(self):
        for k in (2, 3):
            self._sib(k).wait_send()

    def finish_chips(self):
        for name in ("da", "db", "xa", "xb", "ya", "yb"):
            self._copy(name).wait_send()


class Spread:
    def __init__(self, me, blocks, send, recv):
        self.me, self.blocks, self.send, self.recv = me, blocks, send, recv

    def _copy(self, b, t, i):
        return remote(self.blocks(b), self.blocks(b), self.send.at[i], self.recv.at[b], self.me.plane_dev(t))

    def _sends(self, b):
        last = self.me.planes - 1
        if b in (0, last):
            return [(b, 1 if b == 0 else last - 1, 0)] + [(b, t, 1) for t in sorted(range(last + 1), key=lambda t: abs(t - b))[2:]]
        other, end = (2, 0) if b == 1 else (1, 3)
        return [(b, b - 1, 0), (b, b + 1, 0), (other, end, 1)]

    def _each(self, act, steps):
        for g in range(self.me.planes):

            @pl.when(self.me.g == g)
            def _():
                for i, (b, t, step) in enumerate(self._sends(g)):
                    if step in steps:
                        act(self._copy(b, t, i))

    def near(self):
        self._each(lambda cp: cp.start(), (0,))

    def settle(self):
        inner = (self.me.g == 0) | (self.me.g == 2)

        @pl.when(inner)
        def _():
            self._copy(1, 0, 0).wait_recv()

        @pl.when(jnp.logical_not(inner))
        def _():
            self._copy(2, 0, 0).wait_recv()

    def rest(self):
        self._each(lambda cp: cp.start(), (1,))

    def arrive(self):
        for g in range(self.me.planes):

            @pl.when(self.me.g == g)
            def _():
                for b in range(self.me.planes):
                    if b not in (g, 1 if g in (0, 2) else 2):
                        self._copy(b, b, 0).wait_recv()

    def finish(self):
        self._each(lambda cp: cp.wait_send(), (0, 1))


class Collect:
    def __init__(self, me, blocks, landing, via, send, recv):
        self.me, self.blocks, self.landing, self.via, self.send, self.recv = me, blocks, landing, via, send, recv
        self.by = {(0, 3): 1, (3, 0): 2} if me.planes == 4 else {}

    def _copy(self, b, t, src, i):
        at = (b - t) % self.me.planes - 1
        return remote(src, self.landing.at[at], self.send.at[i], self.recv.at[at], self.me.plane_dev(t))

    def _plan(self, b):
        combined = [t for (s, t), by in self.by.items() if by == b]
        direct = [t for t in range(self.me.planes) if t != b and t not in combined]
        direct.sort(key=lambda t: -abs(t - b))
        return [(t, (b, t) in self.by, i) for i, t in enumerate(direct)]

    def _each(self, b, act, ways=(True, False)):
        @pl.when(self.me.g == b)
        def _():
            for t, through, i in self._plan(b):
                if through not in ways:
                    continue
                if through:
                    z = self.me.planes
                    by = self.by[(b, t)]
                    act(remote(self.blocks(t), self.via, self.send.at[i], self.recv.at[z - 1], self.me.plane_dev(by)))
                else:
                    act(self._copy(b, t, self.blocks(t), i))

    def start(self, ways=(True, False)):
        for b in range(self.me.planes):
            self._each(b, lambda cp: cp.start(), ways)

    def _combined(self, b, t):
        return self._copy(b, t, self.via, self.me.planes - 2)

    def combine(self, own):
        for (s, t), by in self.by.items():

            @pl.when(self.me.g == by)
            def _():
                z = self.me.planes
                remote(self.via, self.via, self.send.at[0], self.recv.at[z - 1], self.me.plane_dev(by)).wait_recv()
                for q in range(self.via.shape[0]):
                    self.via[q] = (self.via[q].astype(F32) + own(t)[q].astype(F32)).astype(BF16)
                self._combined(by, t).start()

    def clear(self):
        for s, t in self.by:

            @pl.when(self.me.g == t)
            def _():
                at = (s - t) % self.me.planes - 1
                self.landing[at] = jnp.zeros(self.landing.shape[1:], BF16)

    def total(self, out, own):
        z = self.me.planes
        for t in range(z):

            @pl.when(self.me.g == t)
            def _():
                for b in range(z):
                    if b != t and (b, t) not in self.by:
                        at = (b - t) % z - 1
                        self._copy(b, t, self.landing.at[at], 0).wait_recv()

        for q in range(out.shape[0]):
            value = own[q].astype(F32)
            for at in range(z - 1):
                value = value + self.landing[at, q].astype(F32)
            out[q] = value.astype(BF16)

    def finish(self):
        for b in range(self.me.planes):
            self._each(b, lambda cp: cp.wait_send())
        for (s, t), by in self.by.items():

            @pl.when(self.me.g == by)
            def _():
                self._combined(by, t).wait_send()


def order(me, i):
    k = lax.div(i, 2)
    dx = 1 - lax.div(k, 2)
    dy = 1 - lax.rem(k, 2)
    dc = 1 - lax.rem(i, 2)
    return me.row(dy, dx, dc), k


def strips(length, body, strip=64):
    def one(i, carry):
        body(pl.ds(pl.multiple_of(i * strip, strip), strip))
        return carry

    lax.fori_loop(0, length // strip, one, 0)


def lanes(rows, width):
    return lax.broadcasted_iota(jnp.int32, (rows, width), 1)


def nt(a, b):
    return lax.dot_general(a, b, (((1,), (1,)), ((), ())), preferred_element_type=F32)


def tn(a, b):
    return lax.dot_general(a, b, (((0,), (0,)), ((), ())), preferred_element_type=F32)


def nn(a, b):
    return jnp.dot(a, b, preferred_element_type=F32)


def head_lanes(rows, dh):
    at = lanes(rows, SIDE)
    return at < dh, (at >= dh) & (at < 2 * dh)


def allowed_mask(length, ends):
    i = lax.broadcasted_iota(jnp.int32, (length, length), 0)
    j = lax.broadcasted_iota(jnp.int32, (length, length), 1)
    return (i >= j) & (i.astype(F32) < ends)


def of_head(value, head):
    at = lax.broadcasted_iota(jnp.int32, value.shape, value.ndim - 1)
    return jnp.sum(jnp.where(at == head, value, 0.0), axis=-1, keepdims=True)


def pair_mixing(mix_ref, pair):
    return [[of_head(mix_ref[g : g + 1], 2 * pair + o) for g in range(2)] for o in range(2)]


def mix_lanes(mixing, g, dh):
    at = lanes(1, SIDE)
    return jnp.where(at < dh, mixing[0][g], jnp.where(at < 2 * dh, mixing[1][g], 0.0))


def head_stats(value, dh, h0, h1):
    m0 = jnp.sum(jnp.where(h0, value, 0.0), axis=-1, keepdims=True) / dh
    m1 = jnp.sum(jnp.where(h1, value, 0.0), axis=-1, keepdims=True) / dh
    return jnp.where(h0, m0, jnp.where(h1, m1, 0.0))


def bands(kern_ref, head, length, flip):
    taps_k, taps_q, _ = kern_ref.shape
    r = lax.broadcasted_iota(jnp.int32, (length, length), 0)
    c = lax.broadcasted_iota(jnp.int32, (length, length), 1)
    diff = (c - r) if flip else (r - c)
    taps = [of_head(kern_ref[b], head) for b in range(taps_k)]
    for a in range(taps_q):
        acc = jnp.zeros((length, length), F32)
        for b in range(taps_k):
            acc = jnp.where(diff == b - taps_k // 2, taps[b][a : a + 1], acc)
        yield a, acc


def rms_norm(values_in, scaling):
    return (
        values_in
        * lax.rsqrt(jnp.mean(values_in * values_in, axis=-1, keepdims=True) + 1e-06)
        * scaling
    )


def group_norm(values_in, scaling):
    centred = values_in - jnp.mean(values_in, axis=-1, keepdims=True)
    scaled = centred * lax.rsqrt(jnp.mean(centred * centred, axis=-1, keepdims=True) + 1e-05)
    return scaled.reshape(values_in.shape[0], -1) * scaling


def convolve(scores, kernel):
    length = scores.shape[1]
    taps_query = kernel.shape[1]
    taps_key = kernel.shape[2]
    half_width = taps_key // 2
    padded = jnp.pad(scores, ((0, 0), (taps_query - 1, 0), (half_width, half_width)))
    summed = jnp.zeros_like(scores)
    for shift_q in range(taps_query):
        for shift_k in range(taps_key):
            start_q = taps_query - 1 - shift_q
            window = padded[:, start_q : start_q + length, shift_k : shift_k + length]
            summed = summed + kernel[:, shift_q, shift_k][:, None, None] * window
    return summed


def convolve_back(grad_conv, masked, kernel):
    length = masked.shape[1]
    taps_query = kernel.shape[1]
    taps_key = kernel.shape[2]
    half_width = taps_key // 2
    padded = jnp.pad(masked, ((0, 0), (taps_query - 1, 0), (half_width, half_width)))
    grad_padded = jnp.pad(grad_conv, ((0, 0), (0, taps_query - 1), (half_width, half_width)))
    grad_masked = jnp.zeros_like(masked)
    grad_taps = []
    for shift_q in range(taps_query):
        for shift_k in range(taps_key):
            start_q = taps_query - 1 - shift_q
            window = padded[:, start_q : start_q + length, shift_k : shift_k + length]
            grad_taps.append(jnp.sum(grad_conv * window, axis=(1, 2)))
            start_k = taps_key - 1 - shift_k
            back_window = grad_padded[:, shift_q : shift_q + length, start_k : start_k + length]
            grad_masked = grad_masked + kernel[:, shift_q, shift_k][:, None, None] * back_window
    grad_kern = jnp.stack(grad_taps, axis=1).reshape(kernel.shape)
    return (grad_masked, grad_kern)


def build_mask(doc_lengths, pad_count, length):
    places = jnp.arange(length, dtype=jnp.int32)
    doc_ends = jnp.cumsum(doc_lengths)
    segment = jnp.sum((places[:, None] >= doc_ends[None, :]).astype(jnp.int32), axis=1)
    live_end = length - pad_count
    same_doc = segment[:, None] == segment[None, :]
    causal = places[None, :] <= places[:, None]
    usable = (places[None, :] < live_end) | (places[None, :] == places[:, None])
    return same_doc & causal & usable


def outer_sum(left_rows, right_rows):
    return lax.dot_general(
        left_rows, right_rows, (((0,), (0,)), ((), ())), preferred_element_type=jnp.float32
    )


def back_product(grad_rows, weight_full):
    return lax.dot_general(
        grad_rows, weight_full, (((1,), (1,)), ((), ())), preferred_element_type=jnp.float32
    )


def attention_weights(norm_in, w_qkv, norm_heads, w_out):
    return (
        lax.all_gather(norm_in, "fsdp", axis=0, tiled=True),
        lax.all_gather(w_qkv, "fsdp", axis=0, tiled=True),
        lax.all_gather(norm_heads, "fsdp", axis=0, tiled=True),
        lax.all_gather(w_out, "fsdp", axis=0, tiled=True),
    )


def feed_weights(norm_mid, w_gate, w_up, w_down):
    return (
        lax.all_gather(norm_mid, "fsdp", axis=0, tiled=True),
        lax.all_gather(w_gate, "fsdp", axis=0, tiled=True),
        lax.all_gather(w_up, "fsdp", axis=0, tiled=True),
        lax.all_gather(w_down, "fsdp", axis=0, tiled=True),
    )


def per_device(
    tokens,
    doc_lengths,
    pad_counts,
    norm_in,
    w_qkv,
    kernel,
    mixing,
    norm_heads,
    w_out,
    norm_mid,
    w_gate,
    w_up,
    w_down,
    cotangent,
):
    inputs = tokens[0].astype(jnp.float32)
    length = inputs.shape[0]
    model_width = inputs.shape[1]
    head_count = kernel.shape[0]
    head_size = model_width // head_count
    pair_count = head_count // 2
    score_scale = head_size ** (-0.5)
    allowed = build_mask(doc_lengths[0], pad_counts[0], length)[None]
    kern_pairs = kernel.reshape(pair_count, 2, kernel.shape[1], kernel.shape[2])
    mix_pairs = mixing.reshape(pair_count, 2, 2)
    attn_set = attention_weights(norm_in, w_qkv, norm_heads, w_out)
    normed = rms_norm(inputs, attn_set[0].astype(jnp.float32)).astype(jnp.bfloat16)
    projected = jnp.dot(normed, attn_set[1], preferred_element_type=jnp.float32).astype(
        jnp.bfloat16
    )
    split_qkv = projected.reshape(length, 3, pair_count, 2, head_size).transpose(1, 2, 3, 0, 4)

    def pair_scores(queries, key_rows, kern_pair):
        raw_scores = (
            jnp.einsum("gie,gje->gij", queries, key_rows, preferred_element_type=jnp.float32)
            * score_scale
        )
        masked = jnp.where(allowed, raw_scores, 0.0)
        logits = jnp.where(allowed, convolve(masked, kern_pair), NEG_FILL)
        return (masked, logits)

    def pair_forward(pieces):
        queries, key_rows, value_rows, kern_pair, mix_pair = pieces
        masked, logits = pair_scores(queries, key_rows, kern_pair)
        row_peak = jnp.max(logits, axis=-1, keepdims=True)
        log_total = row_peak + jnp.log(jnp.sum(jnp.exp(logits - row_peak), axis=-1, keepdims=True))
        attn_probs = jnp.exp(logits - log_total)
        mixed_probs = jnp.einsum("og,gij->oij", mix_pair, attn_probs, precision=lax.Precision.HIGHEST)
        output = jnp.einsum(
            "oij,oje->oie", mixed_probs, value_rows.astype(jnp.float32), precision=lax.Precision.HIGHEST
        )
        return (output, log_total)

    attended_pairs, log_totals = lax.map(
        pair_forward, (split_qkv[0], split_qkv[1], split_qkv[2], kern_pairs, mix_pairs)
    )
    attended = attended_pairs.transpose(2, 0, 1, 3).reshape(length, head_count, head_size)
    gated_out = group_norm(attended, attn_set[2].astype(jnp.float32)).astype(jnp.bfloat16)
    residual = inputs + jnp.dot(gated_out, attn_set[3], preferred_element_type=jnp.float32)
    ffn_set = feed_weights(norm_mid, w_gate, w_up, w_down)
    normed_mid = rms_norm(residual, ffn_set[0].astype(jnp.float32)).astype(jnp.bfloat16)
    gate_pre = jnp.dot(normed_mid, ffn_set[1], preferred_element_type=jnp.float32)
    up_pre = jnp.dot(normed_mid, ffn_set[2], preferred_element_type=jnp.float32)
    sigmoid_gate = jax.nn.sigmoid(gate_pre)
    silu_gate = gate_pre * sigmoid_gate
    hidden = (silu_gate * up_pre).astype(jnp.bfloat16)
    layer_out = (residual + jnp.dot(hidden, ffn_set[3], preferred_element_type=jnp.float32))[None]
    ffn_again = feed_weights(norm_mid, w_gate, w_up, w_down)
    grad_y = cotangent[0]
    grad_w_down = outer_sum(hidden, grad_y)
    grad_hidden = back_product(grad_y, ffn_again[3])
    grad_gate = (
        grad_hidden * up_pre * sigmoid_gate * (1.0 + gate_pre * (1.0 - sigmoid_gate))
    ).astype(jnp.bfloat16)
    grad_up = (grad_hidden * silu_gate).astype(jnp.bfloat16)
    grad_w_gate = outer_sum(normed_mid, grad_gate)
    grad_w_up = outer_sum(normed_mid, grad_up)
    grad_mid = back_product(grad_gate, ffn_again[1]) + back_product(grad_up, ffn_again[2])
    mid_pull = jax.vjp(rms_norm, residual, ffn_again[0].astype(jnp.float32))[1]
    grad_residual_norm, grad_norm_mid = mid_pull(grad_mid)
    grad_residual = grad_y.astype(jnp.float32) + grad_residual_norm
    ffn_shards = (
        lax.psum_scatter(grad_norm_mid, "fsdp", scatter_dimension=0, tiled=True),
        lax.psum_scatter(grad_w_gate, "fsdp", scatter_dimension=0, tiled=True),
        lax.psum_scatter(grad_w_up, "fsdp", scatter_dimension=0, tiled=True),
        lax.psum_scatter(grad_w_down, "fsdp", scatter_dimension=0, tiled=True),
    )
    attn_again = attention_weights(norm_in, w_qkv, norm_heads, w_out)
    grad_branch = grad_residual.astype(jnp.bfloat16)
    grad_w_out = outer_sum(gated_out, grad_branch)
    grad_gated = back_product(grad_branch, attn_again[3])
    head_pull = jax.vjp(group_norm, attended, attn_again[2].astype(jnp.float32))[1]
    grad_attended, grad_norm_heads = head_pull(grad_gated)
    grad_att_pairs = (
        grad_attended.astype(jnp.bfloat16)
        .reshape(length, pair_count, 2, head_size)
        .transpose(1, 2, 0, 3)
    )

    def pair_backward(pieces):
        queries, key_rows, value_rows, kern_pair, mix_pair, log_total, grad_output = pieces
        masked, logits = pair_scores(queries, key_rows, kern_pair)
        attn_probs = jnp.exp(logits - log_total)
        mixed_probs = jnp.einsum("og,gij->oij", mix_pair, attn_probs, precision=lax.Precision.HIGHEST)
        grad_wide = grad_output.astype(jnp.float32)
        grad_mixed = jnp.einsum(
            "oie,oje->oij", grad_wide, value_rows.astype(jnp.float32), precision=lax.Precision.HIGHEST
        )
        grad_values = jnp.einsum("oij,oie->oje", mixed_probs, grad_wide, precision=lax.Precision.HIGHEST)
        grad_mix = jnp.einsum("oij,gij->og", grad_mixed, attn_probs, precision=lax.Precision.HIGHEST)
        grad_probs = jnp.einsum("og,oij->gij", mix_pair, grad_mixed, precision=lax.Precision.HIGHEST)
        grad_logits = attn_probs * (
            grad_probs - jnp.sum(attn_probs * grad_probs, axis=-1, keepdims=True)
        )
        grad_conv = jnp.where(allowed, grad_logits, 0.0)
        grad_masked, grad_kern = convolve_back(grad_conv, masked, kern_pair)
        grad_raw = jnp.where(allowed, grad_masked, 0.0)
        grad_query = (
            jnp.einsum("gij,gje->gie", grad_raw, key_rows.astype(jnp.float32), precision=lax.Precision.HIGHEST)
            * score_scale
        )
        grad_key = (
            jnp.einsum("gij,gie->gje", grad_raw, queries.astype(jnp.float32), precision=lax.Precision.HIGHEST)
            * score_scale
        )
        return (
            grad_query.astype(jnp.bfloat16),
            grad_key.astype(jnp.bfloat16),
            grad_values.astype(jnp.bfloat16),
            grad_kern,
            grad_mix,
        )

    grads_query, grads_key, grads_value, grad_kern_pairs, grad_mix_pairs = lax.map(
        pair_backward,
        (
            split_qkv[0],
            split_qkv[1],
            split_qkv[2],
            kern_pairs,
            mix_pairs,
            log_totals,
            grad_att_pairs,
        ),
    )
    grad_qkv = (
        jnp.stack([grads_query, grads_key, grads_value])
        .transpose(3, 0, 1, 2, 4)
        .reshape(length, 3 * model_width)
    )
    grad_w_qkv = outer_sum(normed, grad_qkv)
    grad_normed = back_product(grad_qkv, attn_again[1])
    in_pull = jax.vjp(rms_norm, inputs, attn_again[0].astype(jnp.float32))[1]
    grad_inputs_norm, grad_norm_in = in_pull(grad_normed)
    grad_tokens = (grad_residual + grad_inputs_norm)[None]
    small_sums = lax.psum(
        (grad_kern_pairs.reshape(kernel.shape), grad_mix_pairs.reshape(mixing.shape)),
        ("rep", "fsdp"),
    )
    attn_shards = (
        lax.psum_scatter(grad_norm_in, "fsdp", scatter_dimension=0, tiled=True),
        lax.psum_scatter(grad_w_qkv, "fsdp", scatter_dimension=0, tiled=True),
        lax.psum_scatter(grad_norm_heads, "fsdp", scatter_dimension=0, tiled=True),
        lax.psum_scatter(grad_w_out, "fsdp", scatter_dimension=0, tiled=True),
    )
    summed = (
        lax.psum(ffn_shards[0].astype(jnp.bfloat16), "rep").astype(jnp.float32),
        lax.psum(ffn_shards[1].astype(jnp.bfloat16), "rep").astype(jnp.float32),
        lax.psum(ffn_shards[2].astype(jnp.bfloat16), "rep").astype(jnp.float32),
        lax.psum(ffn_shards[3].astype(jnp.bfloat16), "rep").astype(jnp.float32),
        lax.psum(attn_shards[0].astype(jnp.bfloat16), "rep").astype(jnp.float32),
        lax.psum(attn_shards[1].astype(jnp.bfloat16), "rep").astype(jnp.float32),
        lax.psum(attn_shards[2].astype(jnp.bfloat16), "rep").astype(jnp.float32),
        lax.psum(attn_shards[3].astype(jnp.bfloat16), "rep").astype(jnp.float32),
    )
    return (
        layer_out,
        grad_tokens,
        summed[4],
        summed[5],
        small_sums[0],
        small_sums[1],
        summed[6],
        summed[7],
        summed[0],
        summed[1],
        summed[2],
        summed[3],
    )


def forward_kernel(cfg, *refs):
    (tok, ct, w_qkv, w_gate, w_up, w_down, w_o, kern_in, mix_in, gain_rows, docs, pads,
     tok_all, ct_all, a_all, b_all, d_all, o_all, nrm_all, qkv_all, p_all, m_all, gated_all, mid_all, resid, ends,
     gains, kern, mix, wq_v, w_a, w_b, meta, gain_v, ct_v, down_v, own_o,
     x_v, wa_v, wo_v, t_v, cat_v, shift_v, qkv_v, p_v, m_v, gated_v, meta_v, mid_v, tok_v,
     out_v, red, diag, near, rs_send, rs_recv,
     g_send, g_recv, g_loc, a_send, a_recv, ch_send, ch_recv, o_send, o_recv, meta_send, meta_recv, gain_send, gain_recv, meet_sems, loc, pack, row_in, row_out) = refs
    planes, dh, taps_q, taps_k = cfg["planes"], cfg["dh"], cfg["kq"], cfg["kk"]
    length, width = tok.shape
    per_pair = o_all.shape[0]
    scale = dh ** (-0.5)
    ff, chunk = cfg["ff"], cfg["ff"] // planes
    me = Place(planes)

    me.hail()

    wq_in = pltpu.make_async_copy(w_qkv, wq_v, loc.at[1])
    wq_in.start()
    tok_in = pltpu.make_async_copy(tok, tok_v, loc.at[0])
    tok_in.start()
    taps_in = [pltpu.make_async_copy(kern_in, kern, loc.at[6]), pltpu.make_async_copy(mix_in, mix, loc.at[7])]
    for cp in taps_in:
        cp.start()
    o_in = pltpu.make_async_copy(w_o, own_o, loc.at[4])
    o_in.start()
    down_in = pltpu.make_async_copy(w_down.at[pl.ds(me.y * chunk, chunk)], down_v, loc.at[3])
    down_in.start()
    ct_in = pltpu.make_async_copy(ct, ct_v, loc.at[5])
    ct_in.start()

    def columns(j, s, z):
        at = pl.multiple_of(z * (2 * PLANE * chunk) + s * (2 * chunk) + me.y * chunk, 128)
        src = (w_gate, w_up)[j].at[:, pl.ds(at, chunk)]
        return pltpu.make_async_copy(src, w_b.at[s, :, pl.ds(j * ff + z * chunk, chunk)], pack.at[j, s, z])

    for j in range(2):
        for s in range(PLANE):
            for z in range(planes):
                columns(j, s, z).start()

    places = lanes(8, length).astype(F32)
    last = length * 1.0
    reach = [docs[0, 0]]
    for k in range(1, docs.shape[1]):
        reach.append(reach[-1] + docs[0, k])
    own_end = jnp.full((8, length), last, F32)
    for end in reversed(reach):
        own_end = jnp.where(places < end.astype(F32), end.astype(F32), own_end)
    meta[...] = jnp.where(places < last - pads[0].astype(F32), own_end, places + 1.0)

    wq_in.wait()
    low = lanes(w_qkv.shape[0], 128) < 64
    for s in range(PLANE):
        base = (me.y if s % 2 == 0 else planes - 1 - me.y) * (4 * dh)

        def part(j):
            blk = wq_v[:, pl.ds(pl.multiple_of(j * width + base, 128), 4 * dh)].astype(F32)
            t0, t1, t2 = blk[:, 0:128], blk[:, 128:256], blk[:, 256:384]
            if s // 2 == 0:
                return t0, t1
            t1, t2 = pltpu.roll(t1, 64, 1), pltpu.roll(t2, 64, 1)
            return jnp.where(low, t1, t2), t2

        (q0, q1), (k0, k1), (v0, v1) = part(0), part(1), part(2)
        tiles = (
            q0,
            jnp.where(low, q1, pltpu.roll(v1, 64, 1)),
            k0,
            jnp.where(low, k1, 0.0),
            v0,
        )
        for i, t in enumerate(tiles):
            w_a[s, :, i * 128 : (i + 1) * 128] = t.astype(BF16)

    down_in.wait()
    down_out = pltpu.make_async_copy(down_v, d_all.at[me.g], loc.at[3])
    down_out.start()
    o_in.wait()
    tok_in.wait()
    for cp in taps_in:
        cp.wait()
    me.await_all()

    def first(src, dst_all, base):
        cps = []
        for d in range(1, PLANE):
            s = lax.rem(me.s + d, PLANE)
            cp = remote(src.at[s], dst_all.at[me.f], a_send.at[base + d], a_recv.at[base + d], (me.y, me.g * PLANE + s))
            cp.start()
            cps.append(cp)
        own = pltpu.make_async_copy(src.at[me.s], dst_all.at[me.f], a_send.at[base])
        own.start()
        return cps, own

    def first_wait(src, dst_all, base, own):
        for d in range(1, PLANE):
            s = lax.rem(me.s - d + PLANE, PLANE)
            blk = dst_all.at[me.g * PLANE + s]
            remote(blk, blk, a_send.at[base + d], a_recv.at[base + d], me.sib).wait_recv()
        own.wait()

    meta_sent = []
    for d in range(1, GROUP):
        to = lax.rem(me.slot + d, GROUP)
        cp = remote(
            meta, meta_v.at[me.slot], meta_send.at[d], meta_recv.at[d],
            (lax.div(to, PLANE), me.g * PLANE + lax.rem(to, PLANE)),
        )
        cp.start()
        meta_sent.append(cp)
    meta_here = pltpu.make_async_copy(meta, meta_v.at[me.slot], meta_send.at[0])
    meta_here.start()
    gain_here = pltpu.make_async_copy(gain_rows, gain_v.at[me.f], gain_send.at[0])
    gain_here.start()
    gain_sent = []
    for d in range(1, PLANE):
        to = lax.rem(me.s + d, PLANE)
        gain_sent.append(remote(gain_rows, gain_v.at[me.f], gain_send.at[d], gain_recv.at[d], (me.y, me.g * PLANE + to)))
        gain_sent[-1].start()
    sent_a, own_a = first(w_a, a_all, 0)
    tokens = Gather(me, tok_v, tok_all, g_send.at[0], g_recv.at[0], g_loc.at[0])
    tokens.start()

    o_y = jnp.where((me.g == 1) | (me.g == 2), 1, 0)
    o_c = jnp.where(me.g >= 2, 1, 0)
    o_here = pltpu.make_async_copy(own_o, o_all.at[me.c], o_send.at[0])
    o_sib = remote(own_o, o_all.at[me.c], o_send.at[0], o_recv.at[0], me.sib)

    @pl.when((o_y == me.y) & (o_c == me.c))
    def _():
        o_here.start()

    @pl.when((o_y == me.y) & (o_c != me.c))
    def _():
        o_sib.start()

    def o_copy(t, i):
        return remote(o_all, o_all, o_send.at[i], o_recv.at[1], me.plane_dev(t))

    o_way = ((2, 1), (2, 0), (1, 3), (1, 2))

    def o_each(act):
        for home, (first_to, then_to) in enumerate(o_way):

            @pl.when((me.g == home) & (me.home == home))
            def _():
                act(o_copy(first_to, 1))
                act(o_copy(then_to, 2))

    o_relays = ((me.home < 2) & (me.g == 2)) | ((me.home >= 2) & (me.g == 1))

    def o_from_home():
        o_here.wait()
        remote(o_all.at[1 - me.c], o_all.at[1 - me.c], o_send.at[0], o_recv.at[0], me.sib).wait_recv()

    def o_relay():
        o_copy(0, 1).wait_recv()
        o_copy(jnp.where(me.home < 2, planes - 1, 0), 1).start()

    blocks4 = lambda ref: (lambda b: ref.at[pl.ds(b * PLANE, PLANE)])
    spread_a = Spread(me, blocks4(a_all), ch_send.at[0], ch_recv.at[0])
    spread_b = Spread(me, blocks4(b_all), ch_send.at[1], ch_recv.at[1])
    spread_d = Spread(me, lambda b: d_all.at[b], ch_send.at[2], ch_recv.at[2])

    for g in range(2):
        for a, t in bands(kern, 2 * me.pair + g, length, False):
            high = t.astype(BF16)
            at = slice(a * length, (a + 1) * length)
            t_v[g, 0:length, at] = high
            t_v[g, length : 2 * length, at] = high
            t_v[g, 2 * length :, at] = (t - high.astype(F32)).astype(BF16)
    shift_v[0:8] = jnp.zeros((8, taps_q * length), F32)
    wo_v[...] = jnp.zeros(wo_v.shape, BF16)

    pl.when(me.g == me.home)(o_from_home)
    o_each(lambda cp: cp.start())
    gain_here.wait()
    for d in range(1, PLANE):
        fr = me.g * PLANE + lax.rem(me.s - d + PLANE, PLANE)
        remote(gain_rows, gain_v.at[fr], gain_send.at[d], gain_recv.at[d], me.sib).wait_recv()
    for d in range(1, planes):
        to = lax.rem(me.g + d, planes)
        part = gain_v.at[pl.ds(me.g * PLANE, PLANE)]
        gain_sent.append(remote(part, part, gain_send.at[PLANE + d], gain_recv.at[PLANE + d], me.plane_dev(to)))
        gain_sent[-1].start()
    first_wait(w_a, a_all, 0, own_a)
    spread_a.near()
    pl.when(o_relays)(o_relay)

    tokens.relay()
    for j in range(2):
        for s in range(PLANE):
            for z in range(planes):
                columns(j, s, z).wait()
    sent_b, own_b = first(w_b, b_all, PLANE)
    cots = Gather(me, ct_v, ct_all, g_send.at[1], g_recv.at[1], g_loc.at[1])
    ct_in.wait()
    cots.start()
    spread_a.settle()
    meet(me, meet_sems.at[0])
    spread_a.rest()

    down_out.wait()

    tokens.share()
    tokens.last()
    tokens.finish()
    for row in range(GROUP):
        pltpu.make_async_copy(tok_all.at[row], x_v.at[row], row_in.at[row]).start()
    first_wait(w_b, b_all, PLANE, own_b)
    for d in range(1, GROUP):
        fr = lax.rem(me.slot - d + GROUP, GROUP)
        remote(meta, meta_v.at[fr], meta_send.at[d], meta_recv.at[d], me.sib).wait_recv()
    meta_here.wait()
    ends[...] = meta_v[...]
    for d in range(1, planes):
        part = gain_v.at[pl.ds(lax.rem(me.g - d + planes, planes) * PLANE, PLANE)]
        remote(part, part, gain_send.at[PLANE + d], gain_recv.at[PLANE + d], me.sib).wait_recv()
    gains[...] = jnp.zeros(gains.shape, F32)
    lane = lanes(8, 128)
    for k in range(planes):
        v0, v1, v2, v3 = (gain_v[k * PLANE + j] for j in range(PLANE))
        v1, v2, v3 = pltpu.roll(v1, 96, 1), pltpu.roll(v2, 64, 1), pltpu.roll(v3, 32, 1)
        for j, t in enumerate((jnp.where(lane < 96, v0, v1), jnp.where(lane < 64, v1, v2), jnp.where(lane < 32, v2, v3))):
            at = k * PLANE * w_o.shape[0] + j * 128
            gains[0:2, at : at + 128] = t[0:2]
    v0, v1 = gain_v[2 * me.pair], pltpu.roll(gain_v[2 * me.pair + 1], 96, 1)
    gains[2:3, 0:128] = jnp.where(lane < 96, v0, v1)[2:3]
    gains[2:3, 128:256] = jnp.where(lane < 64, v1, 0.0)[2:3]

    resid[length:] = gains[...]

    def norms(i, carry):
        row, _ = order(me, i)
        pltpu.make_async_copy(tok_all.at[row], x_v.at[row], row_in.at[row]).wait()

        def norm(at):
            x = x_v[row, at].astype(F32)
            s = lax.rsqrt(jnp.mean(x * x, axis=-1, keepdims=True) + 1e-6)
            x_v[row, at] = (x * s * gains[0:1]).astype(BF16)

        strips(length, norm)
        pltpu.make_async_copy(x_v.at[row], nrm_all.at[row], row_out.at[0, row]).start()
        return carry

    lax.fori_loop(0, GROUP, norms, 0)
    spread_a.arrive()
    wa_in = pltpu.make_async_copy(a_all, wa_v, loc.at[1])
    wa_in.start()
    @pl.when((me.g != me.home) & jnp.logical_not(o_relays))
    def _():
        o_copy(0, 1).wait_recv()

    wo_in = pltpu.make_async_copy(o_all, wo_v.at[pl.ds(0, per_pair)], loc.at[2])
    wo_in.start()
    spread_d.near()
    spread_b.near()
    wa_in.wait()
    wo_in.wait()
    h0, h1 = head_lanes(length, dh)
    scatter = Scatter(me, out_v, red, diag, near, rs_send, rs_recv)

    mixing = pair_mixing(mix, me.pair)

    def attention(i):
        row, k = order(me, i)
        acc = nn(x_v[row], wa_v[...].reshape(width, QKV))
        at = lanes(length, 128)
        q = jnp.where(h0 | h1, acc[:, 0:SIDE], 0.0)
        kk = jnp.where(h0 | h1, acc[:, SIDE : 2 * SIDE], 0.0)
        tail = jnp.where(at < 64, pltpu.roll(acc[:, 128:256], 64, 1), 0.0)
        v = jnp.concatenate([acc[:, 2 * SIDE : QKV], tail], axis=1)
        q, kk, v = q.astype(BF16), kk.astype(BF16), v.astype(BF16)
        qkv_v[row, :, 0:SIDE] = q
        qkv_v[row, :, SIDE : 2 * SIDE] = kk
        qkv_v[row, :, 2 * SIDE : 3 * SIDE] = v
        pltpu.make_async_copy(qkv_v.at[row], qkv_all.at[row], row_out.at[1, row]).start()
        ok = allowed_mask(length, meta_v[row, 0:1, :])
        attended = jnp.zeros((length, SIDE), F32)
        for g in range(2):
            kg = jnp.where(h0 if g == 0 else h1, kk.astype(F32), 0.0).astype(BF16)
            raw = nt(q, kg) * scale
            masked = jnp.where(ok, raw, 0.0)
            m_v[row, g] = masked.astype(BF16)
            high = masked.astype(BF16)
            cat_v[:, 0:length] = high
            cat_v[:, length : 2 * length] = (masked - high.astype(F32)).astype(BF16)
            cat_v[:, 2 * length :] = high
            shift_v[8 : 8 + length] = nn(cat_v[...], t_v[g])
            conv = shift_v[8 : 8 + length, 0:length]
            for a in range(1, taps_q):
                conv = conv + shift_v[8 - a : 8 - a + length, a * length : (a + 1) * length]
            logits = jnp.where(ok, conv, NEG_FILL)
            e = jnp.exp(logits - jnp.max(logits, axis=-1, keepdims=True))
            probs = e / jnp.sum(e, axis=-1, keepdims=True)
            high = probs.astype(BF16)
            low = (probs - high.astype(F32)).astype(BF16)
            p_v[row, g, 0] = high
            p_v[row, g, 1] = low
            attended = attended + (nn(high, v) + nn(low, v)) * mix_lanes(mixing, g, dh)
        pltpu.make_async_copy(m_v.at[row], m_all.at[row], row_out.at[2, row]).start()
        pltpu.make_async_copy(p_v.at[row], p_all.at[row], row_out.at[3, row]).start()
        centred = attended - head_stats(attended, dh, h0, h1)
        centred = jnp.where(h0 | h1, centred, 0.0)
        scaled = centred * lax.rsqrt(head_stats(centred * centred, dh, h0, h1) + 1e-5)
        gated = (scaled * gains[2:3, 0:SIDE]).astype(BF16)
        gated_v[row] = gated
        pltpu.make_async_copy(gated_v.at[row], gated_all.at[row], row_out.at[4, row]).start()
        wo = wo_v[...].reshape(wo_v.shape[0] * wo_v.shape[1], width)

    def project(i):
        row, k = order(me, i)
        wo = wo_v[...].reshape(wo_v.shape[0] * wo_v.shape[1], width)
        part = nn(gated_v[row], wo[0:SIDE])

        @pl.when(lax.rem(i, 2) == 0)
        def _():
            scatter.put_sib(k, part)

        @pl.when(lax.rem(i, 2) == 1)
        def _():
            scatter.put_self(k, part)

        scatter.push(i)

    def one(i, carry):
        attention(i)

        project(i)

        @pl.when(i == 1)
        def _():
            cots.relay()

        @pl.when(i == 4)
        def _():
            spread_d.settle()
            spread_b.settle()
            meet(me, meet_sems.at[1])
            spread_d.rest()
            spread_b.rest()

        return carry

    lax.fori_loop(0, GROUP, one, 0)
    scatter.arrive()

    def middle(at):
        res = tok_v[at].astype(F32) + scatter.total(at)
        resid[at] = res
        s = lax.rsqrt(jnp.mean(res * res, axis=-1, keepdims=True) + 1e-6)
        mid_v[at] = (res * s * gains[1:2]).astype(BF16)

    strips(length, middle)
    mids = Gather(me, mid_v, mid_all, g_send.at[2], g_recv.at[2], g_loc.at[2])
    mids.start()
    mids.relay()
    cots.share()
    cots.last()
    mids.share()
    mids.last()
    mids.finish()
    cots.finish()
    spread_d.arrive()
    spread_b.arrive()
    scatter.finish_cores()
    scatter.finish_chips()
    for sp in (spread_a, spread_b, spread_d):
        sp.finish()
    o_each(lambda cp: cp.wait_send())

    @pl.when(o_relays)
    def _():
        o_copy(0, 1).wait_send()

    @pl.when((o_y == me.y) & (o_c != me.c))
    def _():
        o_sib.wait_send()

    for cp in meta_sent + gain_sent + sent_a + sent_b:
        cp.wait_send()
    for r in range(GROUP):
        pltpu.make_async_copy(x_v.at[r], nrm_all.at[r], row_out.at[0, r]).wait()
        pltpu.make_async_copy(qkv_v.at[r], qkv_all.at[r], row_out.at[1, r]).wait()
        pltpu.make_async_copy(m_v.at[r], m_all.at[r], row_out.at[2, r]).wait()
        pltpu.make_async_copy(p_v.at[r], p_all.at[r], row_out.at[3, r]).wait()
        pltpu.make_async_copy(gated_v.at[r], gated_all.at[r], row_out.at[4, r]).wait()


def forward_call(cfg, tok, ct, w_qkv, w_gate, w_up, w_down, w_o, kern, mix, gain_rows, docs, pads):
    length, width = tok.shape
    planes, ff, r = cfg["planes"], cfg["ff"], w_qkv.shape[0]
    n = planes * PLANE
    chunk = ff // planes
    per_pair = n // GROUP
    taps = cfg["kq"] * length
    pad_rows = -(-SIDE // w_o.shape[0])
    hbm, vmem, smem = pl.BlockSpec(memory_space=pl.ANY), pl.BlockSpec(memory_space=pltpu.VMEM), pl.BlockSpec(memory_space=pltpu.SMEM)
    sds = jax.ShapeDtypeStruct
    rows = (GROUP, length)
    dma = pltpu.SemaphoreType.DMA
    v16 = lambda *shape: pltpu.VMEM(shape, BF16)
    v32 = lambda *shape: pltpu.VMEM(shape, F32)
    return pl.pallas_call(
        functools.partial(forward_kernel, cfg),
        out_shape=(
            sds(rows + (width,), BF16), sds(rows + (width,), BF16),
            sds((n, r, QKV), BF16), sds((n, r, 2 * ff), BF16), sds((planes, chunk, width), BF16),
            sds((per_pair,) + w_o.shape, BF16), sds(rows + (width,), BF16), sds(rows + (3 * SIDE,), BF16),
            sds((GROUP, 2, 2, length, length), BF16), sds((GROUP, 2, length, length), BF16), sds(rows + (SIDE,), BF16),
            sds(rows + (width,), BF16), sds((length + 8, width), F32), sds((GROUP, 8, length), F32),
        ),
        in_specs=[hbm] * 9 + [vmem] + [smem] * 2,
        out_specs=(hbm,) * 12 + (vmem,) * 2,
        scratch_shapes=[
            v32(8, width), v32(*kern.shape), v32(*mix.shape), v16(*w_qkv.shape), v16(PLANE, r, QKV), v16(PLANE, r, 2 * ff), v32(8, length), v32(n, 8, 128), v16(length, width), v16(chunk, width), v16(*w_o.shape),
            v16(*rows, width), v16(n, r, QKV), v16(pad_rows, *w_o.shape),
            v16(2, 3 * length, taps), v16(length, 3 * length), v32(length + 8, taps),
            v16(*rows, 3 * SIDE), v16(GROUP, 2, 2, length, length), v16(GROUP, 2, length, length), v16(*rows, SIDE),
            v32(GROUP, 8, length), v16(length, width), v16(length, width),
            *Scatter.scratch(length, width),
            dma((3, Gather.SENDS)), dma((3, Gather.RECVS)), dma((3,)), dma((2 * PLANE,)), dma((2 * PLANE,)),
            dma((3, planes)), dma((3, planes)), dma((3,)), dma((2,)), dma((GROUP,)), dma((GROUP,)), dma((PLANE + planes,)), dma((PLANE + planes,)), pltpu.SemaphoreType.REGULAR((2,)),
            dma((8,)), dma((2, PLANE, planes)), dma((GROUP,)), dma((5, GROUP)),
        ],
        compiler_params=pltpu.CompilerParams(collective_id=1, has_side_effects=True, vmem_limit_bytes=60 * 2**20),
        name="attention_forward",
    )(tok, ct, w_qkv, w_gate, w_up, w_down, w_o, kern, mix, gain_rows, docs, pads)


def feed_kernel(cfg, *refs):
    (mid_all, ct_all, w_b, w_d, resid,
     g_res, branch_all, dw_b, out_red,
     mid_v, ct_v, wb_v, wd_v, hid_v, gu_v, tile_v, dd_v, zd_v, via_v, sd_v, first_v, zf_v, via_f, sf_v, flat_v,
     o_out, o_red, o_send, o_recv,
     m_out, m_red, m_diag, m_near, m_send, m_recv,
     g_send, g_recv, g_loc, z_send, z_recv, loc, row_in, out_sem) = refs
    length, width = ct_all.shape[1:]
    ff = cfg["ff"]
    gain = slice(length + 1, length + 2)
    me = Place(cfg["planes"])
    me.hail()
    wb_in = pltpu.make_async_copy(w_b, wb_v, loc.at[0])
    wb_in.start()
    wd_in = pltpu.make_async_copy(w_d, wd_v, loc.at[1])
    wd_in.start()

    def row_copies(row):
        return (
            pltpu.make_async_copy(mid_all.at[row], mid_v.at[row], row_in.at[0, row]),
            pltpu.make_async_copy(ct_all.at[row], ct_v.at[row], row_in.at[1, row]),
        )

    for i in range(2):
        for cp in row_copies(order(me, i)[0]):
            cp.start()
    me.await_all()
    sum_out = Scatter(me, o_out, o_red, None, None, o_send, o_recv)
    down_sum = Collect(me, lambda b: dd_v.at[pl.ds(b, 1)], zd_v, via_v, z_send.at[0], z_recv.at[0])
    down_sum.clear()
    first_sum = Collect(me, lambda b: first_v.at[b], zf_v, via_f, z_send.at[1], z_recv.at[1])
    first_sum.clear()
    sum_mid = Scatter(me, m_out, m_red, m_diag, m_near, m_send, m_recv)
    wb_in.wait()
    wd_in.wait()
    for i in range(2, GROUP):
        for cp in row_copies(order(me, i)[0]):
            cp.start()

    def one(i, carry):
        row, k = order(me, i)
        for cp in row_copies(row):
            cp.wait()
        wb = wb_v[...].reshape(width, 2 * ff)
        wd = wd_v[...].reshape(ff, width)
        pre = nn(mid_v[row], wb)
        gate, up = pre[:, :ff], pre[:, ff:]
        g_hidden = nt(ct_v[row], wd)
        sig = jax.nn.sigmoid(gate)
        silu = gate * sig
        hid_v[row] = (silu * up).astype(BF16)
        gu_v[row, :, :ff] = (g_hidden * up * sig * (1.0 + gate * (1.0 - sig))).astype(BF16)
        gu_v[row, :, ff:] = (g_hidden * silu).astype(BF16)
        mid_part = nt(gu_v[row], wb)

        @pl.when(lax.rem(i, 2) == 0)
        def _():
            sum_mid.put_sib(k, mid_part)

        @pl.when(lax.rem(i, 2) == 1)
        def _():
            sum_mid.put_self(k, mid_part)

        sum_mid.push(i)
        return carry

    def output(i, carry):
        row, k = order(me, i)
        out_part = nn(hid_v[row], wd_v[...].reshape(ff, width))

        @pl.when(lax.rem(i, 2) == 0)
        def _():
            sum_out.put_sib(k, out_part)

        @pl.when(lax.rem(i, 2) == 1)
        def _():
            sum_out.put_self(k, out_part)

        return carry

    lax.fori_loop(0, GROUP, one, 0)

    tokens = GROUP * length
    tile = SIDE

    def down(i, carry):
        at = pl.ds(pl.multiple_of(i * tile, tile), tile)
        value = tn(hid_v[:, :, at].reshape(tokens, tile), ct_v[...].reshape(tokens, width)).astype(BF16)
        per = tile // dd_v.shape[1]
        dd_v[pl.ds(i * per, per)] = value.reshape((per,) + dd_v.shape[1:])
        return carry

    lax.fori_loop(0, ff // tile, down, 0)
    down_sum.start()

    steps = width // tile

    def tile_out(i):
        slot = lax.rem(i, 2)
        at = pl.ds(pl.multiple_of(i * tile, tile), tile)
        return pltpu.make_async_copy(tile_v.at[slot], dw_b.at[at], out_sem.at[slot])

    def gate_up(i, carry):
        @pl.when(i >= 2)
        def _():
            tile_out(i - 2).wait()

        at = pl.ds(pl.multiple_of(i * tile, tile), tile)
        value = tn(mid_v[:, :, at].reshape(tokens, tile), gu_v[...].reshape(tokens, 2 * ff)).astype(BF16)
        tile_v[lax.rem(i, 2)] = value
        tile_out(i).start()
        r = first_v.shape[2]
        for z in range(first_v.shape[0]):
            for q in range(FIRST):
                lo = (z * PLANE + q) * r
                for tile_at in range(lo // tile, (lo + r - 1) // tile + 1):
                    begin, end = max(lo, tile_at * tile), min(lo + r, (tile_at + 1) * tile)

                    @pl.when(i == tile_at)
                    def _():
                        first_v[z, q, begin - lo : end - lo] = value[begin - tile_at * tile : end - tile_at * tile]

        return carry

    lax.fori_loop(0, steps, gate_up, 0)
    first_sum.start()
    g_res[length:] = jnp.zeros((8, width), F32)
    sum_mid.arrive()

    def middle(at):
        g_mid = sum_mid.total(at)
        res = resid[at]
        s = lax.rsqrt(jnp.mean(res * res, axis=-1, keepdims=True) + 1e-6)
        g_res[length : length + 1] = g_res[length : length + 1] + jnp.sum(g_mid * res * s, axis=0, keepdims=True)
        pulled = g_mid * resid[gain]
        back = ct_v[me.slot, at].astype(F32) + s * pulled
        back = back - res * (s * s * s * jnp.mean(pulled * res, axis=-1, keepdims=True))
        g_res[at] = back
        ct_v[me.slot, at] = back.astype(BF16)

    strips(length, middle)
    branch = Gather(me, ct_v.at[me.slot], branch_all, g_send, g_recv, g_loc.at[0])
    branch.start()

    lax.fori_loop(0, GROUP, output, 0)
    red_out = pltpu.make_async_copy(o_red, out_red.at[pl.ds(0, 4)], out_sem.at[2])
    red_out.start()
    down_sum.combine(lambda t: dd_v.at[pl.ds(t, 1)])
    branch.relay()
    first_sum.combine(lambda t: first_v.at[t])
    branch.share()
    branch.last()
    down_sum.total(sd_v, dd_v.at[pl.ds(me.g, 1)])
    sd_out = pltpu.make_async_copy(sd_v.at[0], out_red.at[4, pl.ds(0, sd_v.shape[1])], out_sem.at[3])
    sd_out.start()
    first_sum.total(sf_v, first_v.at[me.g])
    flat_v[...] = sf_v[...].reshape(flat_v.shape)
    r = sf_v.shape[1]
    own_rows = pl.ds(pl.multiple_of(me.g * (PLANE * r), 16), FIRST * r)
    tile_out(steps - 2).wait()
    tile_out(steps - 1).wait()
    sf_out = pltpu.make_async_copy(flat_v, dw_b.at[own_rows], out_sem.at[4])
    sf_out.start()
    branch.finish()
    sum_mid.finish_cores()
    sum_mid.finish_chips()
    sum_out.finish_cores()
    down_sum.finish()
    first_sum.finish()
    red_out.wait()
    sd_out.wait()
    sf_out.wait()


def feed_call(cfg, mid_all, ct_all, w_b, w_d, resid):
    length, width = ct_all.shape[1:]
    ff = cfg["ff"]
    hbm, vmem = pl.BlockSpec(memory_space=pl.ANY), pl.BlockSpec(memory_space=pltpu.VMEM)
    sds = jax.ShapeDtypeStruct
    dma = pltpu.SemaphoreType.DMA
    rows = (GROUP, length)
    chunk = ff // cfg["planes"]
    others = cfg["planes"] - 1
    r = w_b.shape[1]
    v16 = lambda *shape: pltpu.VMEM(shape, BF16)
    return pl.pallas_call(
        functools.partial(feed_kernel, cfg),
        out_shape=(
            sds((length + 8, width), F32), sds(rows + (width,), BF16),
            sds((width, 2 * ff), BF16), sds((5, length, width), BF16),
        ),
        in_specs=[hbm] * 4 + [vmem],
        out_specs=(vmem, hbm, hbm, hbm),
        scratch_shapes=[
            v16(*rows, width), v16(*rows, width), v16(*w_b.shape), v16(*w_d.shape), v16(*rows, ff), v16(*rows, 2 * ff),
            v16(2, SIDE, 2 * ff), v16(others + 1, chunk, width), v16(others, 1, chunk, width), v16(1, chunk, width), v16(1, chunk, width),
            v16(others + 1, FIRST, r, 2 * ff), v16(others, FIRST, r, 2 * ff), v16(FIRST, r, 2 * ff), v16(FIRST, r, 2 * ff), v16(FIRST * r, 2 * ff),
            *Scatter.scratch(length, width, chips=False), *Scatter.scratch(length, width),
            dma((Gather.SENDS,)), dma((Gather.RECVS,)), dma((1,)), dma((2, others + 1)), dma((2, others + 1)),
            dma((2,)), dma((2, GROUP)), dma((5,)),
        ],
        compiler_params=pltpu.CompilerParams(collective_id=2, has_side_effects=True, vmem_limit_bytes=63 * 2**20),
        name="feed_forward",
    )(mid_all, ct_all, w_b, w_d, resid)


def backward_kernel(cfg, *refs):
    (branch_all, o_all, a_all, nrm_all, qkv_all, p_all, m_all, gated_all, dw_b, out_red, tok,
     resid, kern_in, mix_in, g_res, ends,
     g_tokens, layer_out, out_a, out_c, out_b, out_d, out_o, out_small, out_line,
     gains, kern, mix, gb_v, wo_v, wa_v, nrm_v, qkv_v, p_v, m_v, t_v, cat_v, shift_v, corr_v, gq_v, da_v, dc_v, do_v, tok_v, rows_v, line_v, taps_v,
     zb_v, za_v, zc_v, zo_v, via_b, via_a, via_c, via_o, sb_v, sa_v, sc_v, so_v, far_b, strip_v, sd_v, small_v, small_in, last_v, last_in,
     s_out, s_red, s_diag, s_near, rs_send, rs_recv,
     l_red, l_diag, l_near, l_send, l_recv,
     z_send, z_recv, small_send, small_recv, line_send, line_recv, t_send, t_recv, loc, row_in) = refs
    planes, dh, taps_q, taps_k = cfg["planes"], cfg["dh"], cfg["kq"], cfg["kk"]
    length, width = tok.shape
    scale = dh ** (-0.5)
    me = Place(planes)
    per_pair = o_all.shape[0]
    r = a_all.shape[1]
    far = jnp.where(me.g == 1, planes - 1, 0)
    loads = [
        pltpu.make_async_copy(src, dst, loc.at[i])
        for i, (src, dst) in enumerate(
            [(a_all, wa_v), (o_all, wo_v.at[pl.ds(0, per_pair)]), (tok, tok_v)]
            + [(dw_b.at[pl.ds(me.g * PLANE, PLANE)], sb_v), (resid.at[pl.ds(length, 8)], gains)]
            + [(dw_b.at[pl.ds(far * PLANE + FIRST, PLANE - FIRST)], far_b), (out_red.at[pl.ds(0, 4)], l_red), (out_red.at[4, pl.ds(0, sd_v.shape[0])], sd_v)]
        )
    ]

    span = PLANE * r

    turns = ((3, 2, 1, 0), (0, 2, 3, 1), (3, 1, 0, 2), (0, 1, 2, 3))

    def turn_of(i):
        return sum(jnp.where(me.g == b, turns[b][i], 0) for b in range(planes))

    def nrm_copy(m):
        at = pl.ds(pl.multiple_of(turn_of(m % planes) * span, 128), span)
        return pltpu.make_async_copy(nrm_all.at[:, :, at], nrm_v.at[m % 2], loc.at[8 + m % 2])

    def row_copies(i):
        row = order(me, i)[0]
        at = lax.rem(i, SLOTS)
        cps = [pltpu.make_async_copy(branch_all.at[row], gb_v.at[row], row_in.at[0, i])]
        for j, (src, dst) in enumerate(((qkv_all, qkv_v), (p_all, p_v), (m_all, m_v))):
            cps.append(pltpu.make_async_copy(src.at[row], dst.at[at], row_in.at[j + 1, i]))
        return cps

    me.hail()
    taps_in = [pltpu.make_async_copy(kern_in, kern, loc.at[10]), pltpu.make_async_copy(mix_in, mix, loc.at[11])]
    for cp in taps_in:
        cp.start()
    wo_v[...] = jnp.zeros(wo_v.shape, BF16)
    loads[1].start()
    loads[0].start()
    for i in range(SLOTS):
        for cp in row_copies(i):
            cp.start()
    for cp in loads[2:]:
        cp.start()
    for j in range(2):
        nrm_copy(j).start()
    for cp in taps_in:
        cp.wait()
    for g in range(2):
        for a, t in bands(kern, 2 * me.pair + g, length, True):
            t_v[g, a * length : (a + 1) * length] = t.astype(BF16)
    shift_v[length:] = jnp.zeros((8, length), F32)
    corr_v[...] = jnp.zeros(corr_v.shape, F32)
    rows_v[...] = jnp.zeros(rows_v.shape, F32)
    small_v[...] = jnp.zeros(small_v.shape, F32)
    me.await_all()

    blocks4 = lambda ref: (lambda b: ref.at[pl.ds(b * PLANE, PLANE)])
    sum_b = Collect(me, lambda b: dw_b.at[pl.ds(b * PLANE + FIRST, PLANE - FIRST)], zb_v, via_b, z_send.at[0], z_recv.at[0])
    sum_a = Collect(me, blocks4(da_v), za_v, via_a, z_send.at[1], z_recv.at[1])
    sum_c = Collect(me, blocks4(dc_v), zc_v, via_c, z_send.at[3], z_recv.at[3])
    sum_o = Collect(me, lambda b: do_v.at[pl.ds(b, 1)], zo_v, via_o, z_send.at[2], z_recv.at[2])
    send_s = []
    for d in range(1, planes):
        to = lax.rem(me.g + d, planes)
        send_s.append(remote(small_v, small_in.at[d - 1], small_send.at[d - 1], small_recv.at[d - 1], me.plane_dev(to)))
    send_l = []
    for d in range(1, planes):
        to = lax.rem(me.g + d, planes)
        send_l.append(remote(last_v, last_in.at[d - 1], line_send.at[d - 1], line_recv.at[d - 1], me.plane_dev(to)))
    sum_b.start()
    for group in (sum_b, sum_a, sum_c, sum_o):
        group.clear()
    h0, h1 = head_lanes(length, dh)
    scatter = Scatter(me, s_out, s_red, s_diag, s_near, rs_send, rs_recv)
    layer = Scatter(me, None, l_red, l_diag, l_near, l_send, l_recv)
    def to_slot(d):
        to = lax.rem(me.slot + d, GROUP)
        return lax.div(to, PLANE), lax.rem(to, PLANE)

    def group_copies(kind, src_of, landing, places=None):
        def one_of(d):
            y, sl = to_slot(d)
            return remote(src_of(sl), landing.at[me.slot], t_send.at[kind, d], t_recv.at[kind, d], (y, me.g * PLANE + sl))

        own = pltpu.make_async_copy(src_of(me.s), landing.at[me.slot], t_send.at[kind, 0])
        cps = [one_of(d) for d in range(1, GROUP)] + [own]
        for d, cp in enumerate(cps, 1):
            if places is None:
                cp.start()
            else:
                sl = to_slot(d % GROUP)[1]
                pl.when((sl >= places[0]) & (sl < places[1]))(cp.start)
        return cps

    def group_wait(kind, cps, landing):
        for d in range(1, GROUP):
            fr = lax.rem(me.slot - d + GROUP, GROUP)
            remote(landing.at[fr], landing.at[fr], t_send.at[kind, d], t_recv.at[kind, d], me.sib).wait_recv()
        for cp in cps[:-1]:
            cp.wait_send()
        cps[-1].wait()

    loads[0].wait()
    loads[1].wait()
    loads[5].wait()
    loads[6].wait()
    layer.push(1)
    layer.push(3)
    layer.ahead()
    loads[3].wait()
    loads[4].wait()
    group_copies(0, lambda sl: sb_v.at[sl], out_b, (0, FIRST))
    loads[7].wait()
    d_cp = remote(sd_v, out_d.at[me.y], t_send.at[3, 0], t_recv.at[3, 0], me.yn)
    d_cp.start()
    d_here = pltpu.make_async_copy(sd_v, out_d.at[me.y], t_send.at[3, 1])
    d_here.start()

    mixing = pair_mixing(mix, me.pair)

    def one(i, carry):
        row, k = order(me, i)
        at = lax.rem(i, SLOTS)
        for cp in row_copies(i):
            cp.wait()
        wo = wo_v[...].reshape(wo_v.shape[0] * wo_v.shape[1], width)[0:SIDE]
        q, kk, v = qkv_v[at, :, 0:SIDE], qkv_v[at, :, SIDE : 2 * SIDE], qkv_v[at, :, 2 * SIDE : 3 * SIDE]
        parts = [nn(p_v[at, g, 0], v) + nn(p_v[at, g, 1], v) for g in range(2)]
        probs = [p_v[at, g, 0].astype(F32) + p_v[at, g, 1].astype(F32) for g in range(2)]
        lane_mix = [mix_lanes(mixing, g, dh) for g in range(2)]
        attended = parts[0] * lane_mix[0] + parts[1] * lane_mix[1]
        centred = jnp.where(h0 | h1, attended - head_stats(attended, dh, h0, h1), 0.0)
        inv = lax.rsqrt(head_stats(centred * centred, dh, h0, h1) + 1e-5)
        normal = centred * inv
        g_gated = nt(gb_v[row], wo)
        rows_v[0:1] = rows_v[0:1] + jnp.sum(g_gated * normal, axis=0, keepdims=True)
        u = g_gated * gains[2:3, 0:SIDE]
        g_att = inv * (u - head_stats(u, dh, h0, h1) - normal * head_stats(u * normal, dh, h0, h1))
        g_exact = jnp.where(h0 | h1, g_att, 0.0)
        g_att = g_exact.astype(BF16).astype(F32)
        ok = allowed_mask(length, ends[row, 0:1, :])
        g_q = jnp.zeros((length, SIDE), F32)
        g_k = jnp.zeros((length, SIDE), F32)
        g_v = jnp.zeros((length, SIDE), F32)
        for o in range(2):
            mixed = mixing[o][0] * probs[0] + mixing[o][1] * probs[1]
            g_v = g_v + tn(mixed.astype(BF16), jnp.where(h0 if o == 0 else h1, g_att, 0.0).astype(BF16))
        for g in range(2):
            mine = h0 if g == 0 else h1
            rows_v[1 + g : 2 + g] = rows_v[1 + g : 2 + g] + jnp.sum(g_exact * parts[g], axis=0, keepdims=True)
            g_out = (g_att * lane_mix[g]).astype(BF16)
            g_probs = nt(g_out, v)
            g_conv = probs[g] * (g_probs - jnp.sum(probs[g] * g_probs, axis=-1, keepdims=True))
            shift_v[0:length] = g_conv
            for a in range(taps_q):
                cat_v[:, a * length : (a + 1) * length] = shift_v[a : a + length].astype(BF16)
            corr_v[g] = corr_v[g] + tn(m_v[at, g], cat_v[...])
            g_raw = jnp.where(ok, nn(cat_v[...], t_v[g]), 0.0).astype(BF16)
            g_q = g_q + nn(g_raw, jnp.where(mine, kk.astype(F32), 0.0).astype(BF16))
            g_k = g_k + tn(g_raw, jnp.where(mine, q.astype(F32), 0.0).astype(BF16))
        g_q, g_k = g_q * scale, g_k * scale
        mid_tile = g_q[:, 128:256] + pltpu.roll(g_v[:, 128:256], 64, 1)
        packed = jnp.concatenate([g_q[:, 0:128], mid_tile, g_k, g_v[:, 0:128]], axis=1).astype(BF16)
        gq_v[row] = packed
        part = nt(packed, wa_v[...].reshape(width, QKV))

        @pl.when(lax.rem(i, 2) == 0)
        def _():
            scatter.put_sib(k, part)

        @pl.when(lax.rem(i, 2) == 1)
        def _():
            scatter.put_self(k, part)

        scatter.push(i, turn=False)

        @pl.when(i + SLOTS < GROUP)
        def _():
            for cp in row_copies(i + SLOTS):
                cp.start()

        @pl.when(i == 4)
        def _():
            layer.turn()

        @pl.when(i == 5)
        def _():
            sum_b.combine(lambda t: far_b)

        return carry

    lax.fori_loop(0, GROUP, one, 0)
    loads[2].wait()
    gated_in = [
        pltpu.make_async_copy(gated_all.at[i], p_v.at[i // 4, i // 2 % 2, i % 2], row_in.at[0, i]) for i in range(GROUP)
    ]
    for cp in gated_in:
        cp.start()

    def taps(at, carry):
        g, a = lax.div(at, taps_q), lax.rem(at, taps_q)
        lanes_at = pl.ds(pl.multiple_of(a * length, length), length)
        e = corr_v[g, :, lanes_at]
        diff = lax.broadcasted_iota(jnp.int32, (length, length), 0) - lax.broadcasted_iota(jnp.int32, (length, length), 1)
        for b in range(taps_k):
            line = jnp.sum(jnp.where(diff == b - taps_k // 2, e, 0.0), axis=0, keepdims=True)
            taps_v[b : b + 1] = line[:, 0:128] + line[:, 128:256]
        each = jnp.sum(taps_v[...], axis=-1, keepdims=True)
        small_v[0] = jnp.where(lanes(16, 128) == a * 2 * GROUP + 2 * me.pair + g, each, small_v[0])
        return carry

    taps_v[...] = jnp.zeros(taps_v.shape, F32)
    lax.fori_loop(0, 2 * taps_q, taps, 0)
    base = 1
    at = lanes(1, SIDE)
    for o in range(2):
        for g in range(2):
            line = jnp.where((at >= o * dh) & (at < (o + 1) * dh), rows_v[1 + g : 2 + g], 0.0)
            small_v[base, 2 * o + g : 2 * o + g + 1] = line[:, 0:128] + line[:, 128:256]
    for j in range(2):
        small_v[base, 4 + j : 5 + j] = rows_v[0:1, j * 128 : (j + 1) * 128]

    for j in range(width // 128):
        small_v[2, j : j + 1] = g_res[length : length + 1, j * 128 : (j + 1) * 128]
    for cp in send_s:
        cp.start()

    tokens = GROUP * length
    for cp in gated_in:
        cp.wait()
    value = tn(p_v[...].reshape(tokens, SIDE), gb_v[...].reshape(tokens, width))
    do_v[...] = value[0 : 2 * dh].astype(BF16).reshape(do_v.shape)

    sum_o.start()
    for m in range(2 * planes):
        i, first_part = m % planes, m < planes
        nrm_copy(m).wait()
        at = slice(0, SIDE) if first_part else slice(SIDE, QKV)
        value = tn(nrm_v[m % 2].reshape(tokens, span), gq_v[:, :, at].reshape(tokens, at.stop - at.start))
        terms = da_v if first_part else dc_v
        terms[pl.ds(turn_of(i) * PLANE, PLANE)] = value.astype(BF16).reshape((PLANE,) + terms.shape[1:])
        if m + 2 < 2 * planes:
            nrm_copy(m + 2).start()
    for way in (True, False):
        sum_a.start((way,))
        sum_c.start((way,))
    scatter.turn()
    sum_b.total(sb_v.at[pl.ds(FIRST, PLANE - FIRST)], sb_v.at[pl.ds(FIRST, PLANE - FIRST)])
    b_cps = group_copies(0, lambda sl: sb_v.at[sl], out_b, (FIRST, PLANE))

    for cp in send_s:
        cp.wait_recv()
    for cp in send_s:
        cp.wait_send()
    small_v[...] = small_v[...] + sum(small_in[d] for d in range(planes - 1))
    small_cps = group_copies(2, lambda sl: small_v, out_small)

    sum_o.combine(lambda t: do_v.at[pl.ds(t, 1)])
    sum_a.combine(lambda t: da_v.at[pl.ds(t * PLANE, PLANE)])

    sum_c.combine(lambda t: dc_v.at[pl.ds(t * PLANE, PLANE)])

    layer.arrive()

    def result(at):
        cp = pltpu.make_async_copy(resid.at[at], strip_v, loc.at[0])
        cp.start()
        cp.wait()
        strip_v[...] = strip_v[...] + layer.total(at)
        cp = pltpu.make_async_copy(strip_v, layer_out.at[at], loc.at[0])
        cp.start()
        cp.wait()

    strips(length, result)

    scatter.arrive()

    def middle(at):
        g_normed = scatter.total(at)
        tok32 = tok_v[at].astype(F32)
        s = lax.rsqrt(jnp.mean(tok32 * tok32, axis=-1, keepdims=True) + 1e-6)
        line_v[0:1] = line_v[0:1] + jnp.sum(g_normed * tok32 * s, axis=0, keepdims=True)
        pulled = g_normed * gains[0:1]
        back = g_res[at] + s * pulled
        g_tokens[at] = back - tok32 * (s * s * s * jnp.mean(pulled * tok32, axis=-1, keepdims=True))

    line_v[...] = jnp.zeros(line_v.shape, F32)
    strips(length, middle)
    line = line_v[0:1]
    last_v[...] = jnp.zeros(last_v.shape, F32)
    for j in range(width // 128):
        last_v[j : j + 1] = line[:, j * 128 : (j + 1) * 128]
    for cp in send_l:
        cp.start()

    sum_o.total(so_v, do_v.at[pl.ds(me.g, 1)])
    o_to = me.pair * per_pair + lax.div(me.g, 2)
    o_half = lax.rem(me.g, 2)

    def o_copy(y):
        return remote(so_v.at[0], out_o.at[o_half], t_send.at[4, y], t_recv.at[4, o_half], (y, o_to))

    o_here = pltpu.make_async_copy(so_v.at[0], out_o.at[o_half], t_send.at[4, 2])

    def o_each(act, act_here):
        for y in range(2):
            mine = (y == me.y) & (o_to == me.f)

            @pl.when(jnp.logical_not(mine))
            def _():
                act(o_copy(y))

            @pl.when(mine)
            def _():
                act_here(o_here)

    o_each(lambda cp: cp.start(), lambda cp: cp.start())
    sum_a.total(sa_v, da_v.at[pl.ds(me.g * PLANE, PLANE)])
    a_cps = group_copies(1, lambda sl: sa_v.at[sl], out_a)

    sum_c.total(sc_v, dc_v.at[pl.ds(me.g * PLANE, PLANE)])
    c_cps = group_copies(5, lambda sl: sc_v.at[sl], out_c)

    for cp in send_l:
        cp.wait_recv()
    for cp in send_l:
        cp.wait_send()
    last_v[...] = last_v[...] + sum(last_in[d] for d in range(planes - 1))
    line_cps = group_copies(6, lambda sl: last_v, out_line)

    group_wait(2, small_cps, out_small)
    d_cp.wait_send()
    remote(out_d.at[1 - me.y], out_d.at[1 - me.y], t_send.at[3, 0], t_recv.at[3, 0], me.yn).wait_recv()
    d_here.wait()
    group_wait(0, b_cps, out_b)
    src_y = jnp.where((me.g == 1) | (me.g == 2), 1, 0)
    src_s = me.x * 2 + jnp.where(me.g >= 2, 1, 0)
    for h in range(2):
        src_f = (2 * lax.rem(me.f, per_pair) + h) * PLANE + src_s

        @pl.when(jnp.logical_not((src_y == me.y) & (src_f == me.f)))
        def _():
            remote(out_o.at[h], out_o.at[h], t_send.at[4, 0], t_recv.at[4, h], me.sib).wait_recv()

    o_each(lambda cp: cp.wait_send(), lambda cp: cp.wait())
    group_wait(1, a_cps, out_a)
    group_wait(5, c_cps, out_c)
    group_wait(6, line_cps, out_line)
    for group in (sum_b, sum_a, sum_c, sum_o):
        group.finish()
    scatter.finish_cores()
    scatter.finish_chips()
    layer.finish_chips()


def backward_call(cfg, *args):
    branch_all, o_all, a_all, tok = args[0], args[1], args[2], args[10]
    length, width = tok.shape
    planes, ff = cfg["planes"], cfg["ff"]
    n, r = a_all.shape[:2]
    chunk = ff // planes
    taps = cfg["kq"] * length
    pad_rows = -(-SIDE // o_all.shape[1])
    piece = 2 * cfg["dh"] // planes
    small = (3, 16, 128)
    hbm, vmem, smem = pl.BlockSpec(memory_space=pl.ANY), pl.BlockSpec(memory_space=pltpu.VMEM), pl.BlockSpec(memory_space=pltpu.SMEM)
    sds = jax.ShapeDtypeStruct
    dma = pltpu.SemaphoreType.DMA
    rows = (GROUP, length)
    others = planes - 1
    v16 = lambda *shape: pltpu.VMEM(shape, BF16)
    v32 = lambda *shape: pltpu.VMEM(shape, F32)
    b_block, o_block = (PLANE - FIRST, r, 2 * ff), (1, piece, width)
    a_block, c_block = (PLANE, r, SIDE), (PLANE, r, QKV - SIDE)
    return pl.pallas_call(
        functools.partial(backward_kernel, cfg),
        out_shape=(
            sds((length, width), F32), sds((length, width), F32), sds((GROUP, r, SIDE), BF16), sds((GROUP, r, QKV - SIDE), BF16),
            sds((GROUP, r, 2 * ff), BF16),
            sds((2, chunk, width), BF16), sds((2, piece, width), BF16), sds((GROUP,) + small, F32), sds((GROUP, 16, 128), F32),
        ),
        in_specs=[hbm] * 14 + [vmem] * 2,
        out_specs=(vmem,) + (hbm,) * 8,
        scratch_shapes=[
            v32(8, width), v32(*args[12].shape), v32(*args[13].shape), v16(*rows, width), v16(pad_rows, *o_all.shape[1:]), v16(n, r, QKV), v16(2, *rows, PLANE * r), v16(SLOTS, length, 3 * SIDE),
            v16(SLOTS, 2, 2, length, length), v16(SLOTS, 2, length, length),
            v16(2, taps, length), v16(length, taps), v32(length + 8, length), v32(2, length, taps), v16(*rows, QKV),
            v16(n, r, SIDE), v16(n, r, QKV - SIDE), v16(planes, piece, width), v16(length, width), v32(8, SIDE), v32(8, width), v32(16, 128),
            v16(others, *b_block), v16(others, *a_block), v16(others, *c_block), v16(others, *o_block),
            v16(*b_block), v16(*a_block), v16(*c_block), v16(*o_block),
            v16(PLANE, r, 2 * ff), v16(*a_block), v16(*c_block), v16(*o_block), v16(*b_block), v32(64, width), v16(chunk, width),
            v32(*small), v32(others, *small), v32(16, 128), v32(others, 16, 128),
            *Scatter.scratch(length, width), *Scatter.scratch(length, width, cores=False),
            dma((4, planes)), dma((4, planes)), dma((others,)), dma((others,)), dma((others,)), dma((others,)), dma((7, GROUP)), dma((7, GROUP)),
            dma((12,)), dma((4, GROUP)),
        ],
        compiler_params=pltpu.CompilerParams(collective_id=3, has_side_effects=True, vmem_limit_bytes=54 * 2**20),
        name="attention_backward",
    )(*args)


def results_kernel(cfg, a_ref, c_ref, b_ref, d_ref, o_ref, small_ref, line_ref, g_tok, layer, qkv_ref, gate_ref, up_ref, down_ref, out_ref,
                   taps_ref, mix_ref, in_ref, mid_ref, heads_ref, tok_ref, layer_ref, vec_v):
    planes, ff = cfg["planes"], cfg["ff"]
    rows, width = out_ref.shape
    chunk = ff // planes
    low = lanes(rows, 128) < 64

    def slot(pair):
        home, x = pair // 2, pair % 2
        y, c = (0, 1, 1, 0)[home], (0, 0, 1, 1)[home]
        return y * PLANE + x * 2 + c

    def joined(even, odd, low):
        o0, o1 = pltpu.roll(odd[0], 64, 1), pltpu.roll(odd[1], 64, 1)
        return even[0], jnp.where(low, even[1], o0), jnp.where(low, o0, o1)

    def tiles(pair, j):
        def t(i):
            ref, i = (a_ref, i) if i < 2 else (c_ref, i - 2)
            return ref[slot(pair), :, i * 128 : (i + 1) * 128].astype(F32)

        if j == 2:
            return t(4), pltpu.roll(t(1), 64, 1)
        return t(2 * j), t(2 * j + 1)

    for j in range(3):
        for two in range(GROUP // 2):
            for i, t in enumerate(joined(tiles(2 * two, j), tiles(2 * two + 1, j), low)):
                at = j * width + two * 384 + i * 128
                qkv_ref[:, at : at + 128] = t
    for z in range(planes):
        for s in range(PLANE):
            for y in range(2):
                at = ((z * PLANE + s) * 2 + y) * chunk
                src = b_ref.at[y * PLANE + s]
                gate_ref[:, at : at + chunk] = src[:, z * chunk : (z + 1) * chunk].astype(F32)
                up_ref[:, at : at + chunk] = src[:, ff + z * chunk : ff + (z + 1) * chunk].astype(F32)
    down_ref[...] = d_ref[0].astype(F32)
    out_ref[...] = o_ref[0].astype(F32)

    tok_ref[...] = g_tok[...]
    layer_ref[...] = layer[...]

    @pl.when(pl.program_id(0) == 0)
    def _():
        base = 1
        heads = 2 * GROUP
        taps = small_ref[0, 0]
        for s in range(1, GROUP):
            taps = taps + small_ref[s, 0]
        for k in range(cfg["kk"]):
            for q in range(cfg["kq"]):
                taps_ref[k, q : q + 1] = taps[k : k + 1, q * heads : (q + 1) * heads]
        mixed = [jnp.sum(small_ref[slot(pair), base], axis=-1, keepdims=True) for pair in range(GROUP)]
        for g in range(2):
            line = jnp.zeros((1, heads), F32)
            for pair in range(GROUP):
                for o in range(2):
                    k = 2 * o + g
                    line = jnp.where(lanes(1, heads) == 2 * pair + o, mixed[pair][k : k + 1], line)
            mix_ref[g : g + 1] = line
        vec_v[...] = jnp.zeros(vec_v.shape, F32)
        for k, part in enumerate((lambda s: line_ref[s], lambda s: small_ref[s, base + 1])):
            total = part(0)
            for s in range(1, GROUP):
                total = total + part(s)
            for j in range(width // 128):
                vec_v[k : k + 1, j * 128 : (j + 1) * 128] = total[j : j + 1]
        line = lambda pair: tuple(small_ref[slot(pair), base, 4 + j : 5 + j] for j in range(2))
        for two in range(GROUP // 2):
            for i, t in enumerate(joined(line(2 * two), line(2 * two + 1), lanes(1, 128) < 64)):
                vec_v[2:3, two * 384 + i * 128 : two * 384 + (i + 1) * 128] = t
        own = in_ref.shape[1]
        mine = pltpu.roll(vec_v[...], lax.rem(width - lax.axis_index("fsdp") * own, width), 1)
        for k, ref in enumerate((in_ref, mid_ref, heads_ref)):
            ref[...] = mine[k : k + 1, 0:own]


def results_call(cfg, out_a, out_c, out_b, out_d, out_o, small, line, g_tokens, layer_out):
    r = out_a.shape[1]
    _, chunk, width = out_d.shape
    half = r // 2
    sds = jax.ShapeDtypeStruct
    whole = lambda shape: pl.BlockSpec(shape, lambda i: (0,) * len(shape))
    rows = lambda n, w: pl.BlockSpec((n, w), lambda i: (i, 0))
    moved = 6 * (out_a.size + out_c.size + out_b.size + out_d.size + out_o.size) + 16 * g_tokens.size
    return pl.pallas_call(
        functools.partial(results_kernel, cfg),
        grid=(2,),
        out_shape=(
            sds((r, 3 * width), F32), sds((r, n_cols(cfg)), F32), sds((r, n_cols(cfg)), F32), sds((2 * chunk, width), F32),
            sds((r, width), F32), sds((cfg["kk"], cfg["kq"], 2 * GROUP), F32), sds((2, 2 * GROUP), F32),
            sds((1, r), F32), sds((1, r), F32), sds((1, r), F32), sds(g_tokens.shape, F32), sds(g_tokens.shape, F32),
        ),
        in_specs=[
            pl.BlockSpec((GROUP, half, out_a.shape[2]), lambda i: (0, i, 0)),
            pl.BlockSpec((GROUP, half, out_c.shape[2]), lambda i: (0, i, 0)),
            pl.BlockSpec((GROUP, half, out_b.shape[2]), lambda i: (0, i, 0)),
            pl.BlockSpec((1, chunk, width), lambda i: (i, 0, 0)),
            pl.BlockSpec((1, half, width), lambda i: (i, 0, 0)),
            whole(small.shape),
            whole(line.shape),
            rows(g_tokens.shape[0] // 2, width),
            rows(g_tokens.shape[0] // 2, width),
        ],
        scratch_shapes=[pltpu.VMEM((8, width), F32)],
        out_specs=(
            rows(half, 3 * width), rows(half, n_cols(cfg)), rows(half, n_cols(cfg)), rows(chunk, width), rows(half, width),
            whole((cfg["kk"], cfg["kq"], 2 * GROUP)), whole((2, 2 * GROUP)),
            whole((1, r)), whole((1, r)), whole((1, r)), rows(g_tokens.shape[0] // 2, width), rows(g_tokens.shape[0] // 2, width),
        ),
        compiler_params=pltpu.CompilerParams(vmem_limit_bytes=60 * 2**20),
        cost_estimate=pl.CostEstimate(flops=0, bytes_accessed=moved, transcendentals=0),
        name="results",
    )(out_a, out_c, out_b, out_d, out_o, small, line, g_tokens, layer_out)


def n_cols(cfg):
    return cfg["ff"] * GROUP


def fits(mesh, tokens, kernel, w_gate):
    n = mesh.shape["fsdp"]
    width, length, heads, ff = tokens.shape[2], tokens.shape[1], kernel.shape[0], w_gate.shape[1]
    return (
        mesh.shape["rep"] == 2
        and n == 4 * PLANE
        and heads == 2 * GROUP
        and width == heads * 96
        and (width // n) % 32 == 0
        and ff % (2 * n * 128) == 0
        and length == SIDE
    )


def per_device_group(
    planes,
    tokens,
    doc_lengths,
    pad_counts,
    norm_in,
    w_qkv,
    kernel,
    mixing,
    norm_heads,
    w_out,
    norm_mid,
    w_gate,
    w_up,
    w_down,
    cotangent,
):
    length, width = tokens.shape[1:]
    heads, kq, kk = kernel.shape
    dh = width // heads
    n = planes * PLANE
    r = width // n
    chunk = w_down.shape[0] // 2
    ff = planes * chunk
    cfg = dict(planes=planes, dh=dh, kq=kq, kk=kk, ff=ff)

    gain_rows = jnp.pad(jnp.stack([norm_in, norm_mid, norm_heads]).astype(F32), ((0, 5), (0, 128 - r)))
    tok, ct = tokens[0], cotangent[0]
    kern, mix = kernel.transpose(2, 1, 0), mixing.T

    (_, ct_all, a_all, b_all, d_all, o_all, nrm_all, qkv_all, p_all, m_all, gated_all, mid_all, resid, ends) = (
        forward_call(
            cfg, tok, ct, w_qkv, w_gate, w_up, w_down, w_out, kern, mix, gain_rows, doc_lengths, pad_counts
        )
    )
    g_res, branch_all, dw_b, out_red = feed_call(cfg, mid_all, ct_all, b_all, d_all, resid)
    g_tokens, layer_out, out_a, out_c, out_b, out_d, out_o, small, line = backward_call(
        cfg, branch_all, o_all, a_all, nrm_all, qkv_all, p_all, m_all, gated_all, dw_b.reshape(n, r, 2 * ff), out_red,
        tok, resid, kern, mix, g_res, ends,
    )

    g_qkv, g_gate, g_up, g_down, g_out, g_kernel, g_mixing, g_in, g_mid, g_heads, g_tokens, layer_out = results_call(
        cfg, out_a, out_c, out_b, out_d, out_o, small, line, g_tokens, layer_out
    )
    return (
        layer_out[None],
        g_tokens[None],
        g_in[0],
        g_qkv,
        g_kernel.transpose(2, 1, 0),
        g_mixing.T,
        g_heads[0],
        g_out,
        g_mid[0],
        g_gate,
        g_up,
        g_down,
    )


def solution(mesh):
    in_specs = (
        P(("rep", "fsdp"), None, None),
        P(("rep", "fsdp"), None),
        P(("rep", "fsdp")),
        P("fsdp"),
        P("fsdp", None),
        P(),
        P(),
        P("fsdp"),
        P("fsdp", None),
        P("fsdp"),
        P("fsdp", None),
        P("fsdp", None),
        P("fsdp", None),
        P(("rep", "fsdp"), None, None),
    )
    out_specs = (
        P(("rep", "fsdp"), None, None),
        P(("rep", "fsdp"), None, None),
        P("fsdp"),
        P("fsdp", None),
        P(),
        P(),
        P("fsdp"),
        P("fsdp", None),
        P("fsdp"),
        P("fsdp", None),
        P("fsdp", None),
        P("fsdp", None),
    )

    def layer(*args):
        body = per_device
        if fits(mesh, args[0], args[5], args[10]):
            body = functools.partial(per_device_group, mesh.shape["fsdp"] // PLANE)
        return jax.shard_map(body, mesh=mesh, in_specs=in_specs, out_specs=out_specs, check_vma=False)(*args)

    return layer
```

```python
import functools

import jax
import jax.numpy as jnp
from jax import lax
from jax.experimental import pallas as pl
from jax.experimental.pallas import tpu as pltpu
from jax.sharding import PartitionSpec as P

F32 = jnp.float32
BF16 = jnp.bfloat16
NEG_FILL = -1e30
MESH = pl.DeviceIdType.MESH
PLANE = 4
GROUP = 8
SIDE = 256
FIRST = 1
SLOTS = 2
QKV = 640


class Place:
    def __init__(self, planes):
        self.planes = planes
        self.y = lax.axis_index("rep")
        self.f = lax.axis_index("fsdp")
        self.g = lax.div(self.f, PLANE)
        self.s = lax.rem(self.f, PLANE)
        self.x = lax.div(self.s, 2)
        self.c = lax.rem(self.s, 2)
        self.slot = self.y * PLANE + self.s
        self.home = self.y + self.c * (planes - 1 - 2 * self.y)
        self.pair = 2 * self.home + self.x
        self.sib = self.dev(self.y, self.x, 1 - self.c)
        self.xn = self.dev(self.y, 1 - self.x, self.c)
        self.yn = self.dev(1 - self.y, self.x, self.c)

    def dev(self, y, x, c):
        return (y, self.g * PLANE + x * 2 + c)

    def plane_dev(self, g):
        return (self.y, g * PLANE + self.s)

    def row(self, dy, dx, dc):
        y = self.y + dy - 2 * dy * self.y
        x = self.x + dx - 2 * dx * self.x
        c = self.c + dc - 2 * dc * self.c
        return y * 4 + x * 2 + c

    def hail(self):
        sem = pltpu.get_barrier_semaphore()
        n = self.planes * PLANE
        for d in range(1, n):
            pl.semaphore_signal(sem, inc=1, device_id=(self.y, lax.rem(self.f + d, n)), device_id_type=MESH)
        for s in range(PLANE):
            pl.semaphore_signal(sem, inc=1, device_id=(1 - self.y, self.g * PLANE + s), device_id_type=MESH)

    def await_all(self):
        pl.semaphore_wait(pltpu.get_barrier_semaphore(), self.planes * PLANE - 1 + PLANE)


def meet(me, sem):
    pl.semaphore_signal(sem, inc=1, device_id=me.sib, device_id_type=MESH)
    pl.semaphore_wait(sem, 1)


def remote(src, dst, send, recv, dev):
    return pltpu.make_async_remote_copy(
        src_ref=src, dst_ref=dst, send_sem=send, recv_sem=recv, device_id=dev, device_id_type=MESH
    )


class Gather:
    SENDS = 14
    RECVS = 14

    def __init__(self, me, own, buf, send, recv, local):
        self.me, self.own, self.buf = me, own, buf
        self.send, self.recv, self.local = send, recv, local
        self.half = own.shape[0] // 2
        self.sent = []

    def _own(self, h):
        return self.own.at[pl.ds(h * self.half, self.half)]

    def _blk(self, row, h):
        return self.buf.at[row, pl.ds(h * self.half, self.half)]

    def _copy(self, i):
        own, row, h, kind, dev = self.sent[i]
        src = self._own(h) if own else self._blk(row, h)
        return remote(src, self._blk(row, h), self.send.at[i], self.recv.at[kind * 2 + h], dev)

    def _go(self, own, row, h, kind, dev):
        self.sent.append((own, row, h, kind, dev))
        self._copy(len(self.sent) - 1).start()

    def _await(self, row, h, kind):
        b = self._blk(row, h)
        remote(b, b, self.send.at[0], self.recv.at[kind * 2 + h], self.me.sib).wait_recv()

    def start(self):
        me = self.me
        self.rows = [me.row(0, 0, 1), me.row(0, 1, 0), me.row(1, 0, 0), me.row(1, 1, 0), me.row(0, 1, 1), me.row(1, 0, 1), me.row(1, 1, 1)]
        self.here = pltpu.make_async_copy(self.own, self.buf.at[me.slot], self.local)
        self.here.start()
        self._go(True, me.slot, 0, 1, me.xn)
        self._go(True, me.slot, 1, 2, me.yn)
        self._go(True, me.slot, 0, 0, me.sib)
        self._go(True, me.slot, 1, 0, me.sib)
        self._go(True, me.slot, 1, 1, me.xn)
        self._go(True, me.slot, 0, 2, me.yn)

    def relay(self):
        me, rows = self.me, self.rows
        self._await(rows[1], 0, 1)
        self._go(False, rows[1], 0, 3, me.yn)
        self._go(False, rows[1], 0, 4, me.sib)
        self._await(rows[2], 1, 2)
        self._go(False, rows[2], 1, 3, me.xn)
        self._go(False, rows[2], 1, 5, me.sib)

    def share(self):
        me, rows = self.me, self.rows
        self._await(rows[1], 1, 1)
        self._go(False, rows[1], 1, 4, me.sib)
        self._await(rows[2], 0, 2)
        self._go(False, rows[2], 0, 5, me.sib)

    def last(self):
        me, rows = self.me, self.rows
        for h in (0, 1):
            self._await(rows[3], h, 3)
            self._go(False, rows[3], h, 6, me.sib)

    def finish(self):
        for kind in (0, 4, 5, 6):
            for h in (0, 1):
                self._await(self.rows[kind], h, kind)
        for i in range(len(self.sent)):
            self._copy(i).wait_send()
        self.here.wait()


class Scatter:
    SENDS = 10
    RECVS = 10

    @staticmethod
    def scratch(rows, width, cores=True, chips=True):
        bufs = []
        if cores:
            bufs.append(pltpu.VMEM((2, rows, width), BF16))
        bufs.append(pltpu.VMEM((4, rows, width), BF16))
        if chips:
            bufs += [pltpu.VMEM((2, rows // 2, width), BF16), pltpu.VMEM((2, rows, width), BF16)]
        return bufs + [pltpu.SemaphoreType.DMA((Scatter.SENDS,)), pltpu.SemaphoreType.DMA((Scatter.RECVS,))]

    def __init__(self, me, out, red, diag, near, send, recv):
        self.me, self.out, self.red, self.diag, self.near = me, out, red, diag, near
        self.send, self.recv = send, recv
        self.half = red.shape[1] // 2

    def _sib(self, k):
        return remote(self.out.at[lax.rem(k, 2)], self.red.at[k], self.send.at[k], self.recv.at[k], self.me.sib)

    def put_sib(self, k, value):
        @pl.when(k >= 2)
        def _():
            self._sib(k - 2).wait_send()

        self.out[lax.rem(k, 2)] = value.astype(BF16)
        self._sib(k).start()

    def put_self(self, k, value):
        self._sib(k).wait_recv()
        self.red[k] = (value + self.red[k].astype(F32)).astype(BF16)

    def _copy(self, name):
        h, me = self.half, self.me
        lo, hi = pl.ds(0, h), pl.ds(h, h)
        src, dst, i, dev = {
            "da": (self.red.at[0, lo], self.diag.at[0], 4, me.xn),
            "db": (self.red.at[0, hi], self.diag.at[1], 5, me.yn),
            "xa": (self.red.at[1, lo], self.near.at[0, lo], 6, me.xn),
            "xb": (self.red.at[1, hi], self.near.at[0, hi], 7, me.xn),
            "ya": (self.red.at[2, lo], self.near.at[1, lo], 8, me.yn),
            "yb": (self.red.at[2, hi], self.near.at[1, hi], 9, me.yn),
        }[name]
        return remote(src, dst, self.send.at[i], self.recv.at[i], dev)

    def push(self, i, turn=True):
        @pl.when(i == 1)
        def _():
            self._copy("da").start()
            self._copy("db").start()

        @pl.when(i == 3)
        def _():
            self._copy("xa").start()

        @pl.when(i == 5)
        def _():
            self._copy("yb").start()
            if turn:
                self.turn()

    def ahead(self):
        self._copy("yb").start()

    def turn(self):
        h = self.half
        self._copy("db").wait_recv()
        self.red[1, h:] = (self.red[1, h:].astype(F32) + self.diag[1].astype(F32)).astype(BF16)
        self._copy("xb").start()
        self._copy("da").wait_recv()
        self.red[2, :h] = (self.red[2, :h].astype(F32) + self.diag[0].astype(F32)).astype(BF16)
        self._copy("ya").start()

    def arrive(self):
        for name in ("xa", "xb", "ya", "yb"):
            self._copy(name).wait_recv()

    def total(self, at):
        return self.red[3, at].astype(F32) + self.near[0, at].astype(F32) + self.near[1, at].astype(F32)

    def finish_cores(self):
        for k in (2, 3):
            self._sib(k).wait_send()

    def finish_chips(self):
        for name in ("da", "db", "xa", "xb", "ya", "yb"):
            self._copy(name).wait_send()


class Spread:
    def __init__(self, me, blocks, send, recv):
        self.me, self.blocks, self.send, self.recv = me, blocks, send, recv

    def _copy(self, b, t, i):
        return remote(self.blocks(b), self.blocks(b), self.send.at[i], self.recv.at[b], self.me.plane_dev(t))

    def _sends(self, b):
        last = self.me.planes - 1
        if b in (0, last):
            return [(b, 1 if b == 0 else last - 1, 0)] + [(b, t, 1) for t in sorted(range(last + 1), key=lambda t: abs(t - b))[2:]]
        other, end = (2, 0) if b == 1 else (1, 3)
        return [(b, b - 1, 0), (b, b + 1, 0), (other, end, 1)]

    def _each(self, act, steps):
        for g in range(self.me.planes):

            @pl.when(self.me.g == g)
            def _():
                for i, (b, t, step) in enumerate(self._sends(g)):
                    if step in steps:
                        act(self._copy(b, t, i))

    def near(self):
        self._each(lambda cp: cp.start(), (0,))

    def settle(self):
        inner = (self.me.g == 0) | (self.me.g == 2)

        @pl.when(inner)
        def _():
            self._copy(1, 0, 0).wait_recv()

        @pl.when(jnp.logical_not(inner))
        def _():
            self._copy(2, 0, 0).wait_recv()

    def rest(self):
        self._each(lambda cp: cp.start(), (1,))

    def arrive(self):
        for g in range(self.me.planes):

            @pl.when(self.me.g == g)
            def _():
                for b in range(self.me.planes):
                    if b not in (g, 1 if g in (0, 2) else 2):
                        self._copy(b, b, 0).wait_recv()

    def finish(self):
        self._each(lambda cp: cp.wait_send(), (0, 1))


class Collect:
    def __init__(self, me, blocks, landing, via, send, recv):
        self.me, self.blocks, self.landing, self.via, self.send, self.recv = me, blocks, landing, via, send, recv
        self.by = {(0, 3): 1, (3, 0): 2} if me.planes == 4 else {}

    def _copy(self, b, t, src, i):
        at = (b - t) % self.me.planes - 1
        return remote(src, self.landing.at[at], self.send.at[i], self.recv.at[at], self.me.plane_dev(t))

    def _plan(self, b):
        combined = [t for (s, t), by in self.by.items() if by == b]
        direct = [t for t in range(self.me.planes) if t != b and t not in combined]
        direct.sort(key=lambda t: -abs(t - b))
        return [(t, (b, t) in self.by, i) for i, t in enumerate(direct)]

    def _each(self, b, act, ways=(True, False)):
        @pl.when(self.me.g == b)
        def _():
            for t, through, i in self._plan(b):
                if through not in ways:
                    continue
                if through:
                    z = self.me.planes
                    by = self.by[(b, t)]
                    act(remote(self.blocks(t), self.via, self.send.at[i], self.recv.at[z - 1], self.me.plane_dev(by)))
                else:
                    act(self._copy(b, t, self.blocks(t), i))

    def start(self, ways=(True, False)):
        for b in range(self.me.planes):
            self._each(b, lambda cp: cp.start(), ways)

    def _combined(self, b, t):
        return self._copy(b, t, self.via, self.me.planes - 2)

    def combine(self, own):
        for (s, t), by in self.by.items():

            @pl.when(self.me.g == by)
            def _():
                z = self.me.planes
                remote(self.via, self.via, self.send.at[0], self.recv.at[z - 1], self.me.plane_dev(by)).wait_recv()
                for q in range(self.via.shape[0]):
                    self.via[q] = (self.via[q].astype(F32) + own(t)[q].astype(F32)).astype(BF16)
                self._combined(by, t).start()

    def clear(self):
        for s, t in self.by:

            @pl.when(self.me.g == t)
            def _():
                at = (s - t) % self.me.planes - 1
                self.landing[at] = jnp.zeros(self.landing.shape[1:], BF16)

    def total(self, out, own):
        z = self.me.planes
        for t in range(z):

            @pl.when(self.me.g == t)
            def _():
                for b in range(z):
                    if b != t and (b, t) not in self.by:
                        at = (b - t) % z - 1
                        self._copy(b, t, self.landing.at[at], 0).wait_recv()

        for q in range(out.shape[0]):
            value = own[q].astype(F32)
            for at in range(z - 1):
                value = value + self.landing[at, q].astype(F32)
            out[q] = value.astype(BF16)

    def finish(self):
        for b in range(self.me.planes):
            self._each(b, lambda cp: cp.wait_send())
        for (s, t), by in self.by.items():

            @pl.when(self.me.g == by)
            def _():
                self._combined(by, t).wait_send()


def order(me, i):
    k = lax.div(i, 2)
    dx = 1 - lax.div(k, 2)
    dy = 1 - lax.rem(k, 2)
    dc = 1 - lax.rem(i, 2)
    return me.row(dy, dx, dc), k


def strips(length, body, strip=64):
    def one(i, carry):
        body(pl.ds(pl.multiple_of(i * strip, strip), strip))
        return carry

    lax.fori_loop(0, length // strip, one, 0)


def lanes(rows, width):
    return lax.broadcasted_iota(jnp.int32, (rows, width), 1)


def nt(a, b):
    return lax.dot_general(a, b, (((1,), (1,)), ((), ())), preferred_element_type=F32)


def tn(a, b):
    return lax.dot_general(a, b, (((0,), (0,)), ((), ())), preferred_element_type=F32)


def nn(a, b):
    return jnp.dot(a, b, preferred_element_type=F32)


def head_lanes(rows, dh):
    at = lanes(rows, SIDE)
    return at < dh, (at >= dh) & (at < 2 * dh)


def allowed_mask(length, ends):
    i = lax.broadcasted_iota(jnp.int32, (length, length), 0)
    j = lax.broadcasted_iota(jnp.int32, (length, length), 1)
    return (i >= j) & (i.astype(F32) < ends)


def of_head(value, head):
    at = lax.broadcasted_iota(jnp.int32, value.shape, value.ndim - 1)
    return jnp.sum(jnp.where(at == head, value, 0.0), axis=-1, keepdims=True)


def pair_mixing(mix_ref, pair):
    return [[of_head(mix_ref[g : g + 1], 2 * pair + o) for g in range(2)] for o in range(2)]


def mix_lanes(mixing, g, dh):
    at = lanes(1, SIDE)
    return jnp.where(at < dh, mixing[0][g], jnp.where(at < 2 * dh, mixing[1][g], 0.0))


def head_stats(value, dh, h0, h1):
    m0 = jnp.sum(jnp.where(h0, value, 0.0), axis=-1, keepdims=True) / dh
    m1 = jnp.sum(jnp.where(h1, value, 0.0), axis=-1, keepdims=True) / dh
    return jnp.where(h0, m0, jnp.where(h1, m1, 0.0))


def bands(kern_ref, head, length, flip):
    taps_k, taps_q, _ = kern_ref.shape
    r = lax.broadcasted_iota(jnp.int32, (length, length), 0)
    c = lax.broadcasted_iota(jnp.int32, (length, length), 1)
    diff = (c - r) if flip else (r - c)
    taps = [of_head(kern_ref[b], head) for b in range(taps_k)]
    for a in range(taps_q):
        acc = jnp.zeros((length, length), F32)
        for b in range(taps_k):
            acc = jnp.where(diff == b - taps_k // 2, taps[b][a : a + 1], acc)
        yield a, acc


def rms_norm(values_in, scaling):
    return (
        values_in
        * lax.rsqrt(jnp.mean(values_in * values_in, axis=-1, keepdims=True) + 1e-06)
        * scaling
    )


def group_norm(values_in, scaling):
    centred = values_in - jnp.mean(values_in, axis=-1, keepdims=True)
    scaled = centred * lax.rsqrt(jnp.mean(centred * centred, axis=-1, keepdims=True) + 1e-05)
    return scaled.reshape(values_in.shape[0], -1) * scaling


def convolve(scores, kernel):
    length = scores.shape[1]
    taps_query = kernel.shape[1]
    taps_key = kernel.shape[2]
    half_width = taps_key // 2
    padded = jnp.pad(scores, ((0, 0), (taps_query - 1, 0), (half_width, half_width)))
    summed = jnp.zeros_like(scores)
    for shift_q in range(taps_query):
        for shift_k in range(taps_key):
            start_q = taps_query - 1 - shift_q
            window = padded[:, start_q : start_q + length, shift_k : shift_k + length]
            summed = summed + kernel[:, shift_q, shift_k][:, None, None] * window
    return summed


def convolve_back(grad_conv, masked, kernel):
    length = masked.shape[1]
    taps_query = kernel.shape[1]
    taps_key = kernel.shape[2]
    half_width = taps_key // 2
    padded = jnp.pad(masked, ((0, 0), (taps_query - 1, 0), (half_width, half_width)))
    grad_padded = jnp.pad(grad_conv, ((0, 0), (0, taps_query - 1), (half_width, half_width)))
    grad_masked = jnp.zeros_like(masked)
    grad_taps = []
    for shift_q in range(taps_query):
        for shift_k in range(taps_key):
            start_q = taps_query - 1 - shift_q
            window = padded[:, start_q : start_q + length, shift_k : shift_k + length]
            grad_taps.append(jnp.sum(grad_conv * window, axis=(1, 2)))
            start_k = taps_key - 1 - shift_k
            back_window = grad_padded[:, shift_q : shift_q + length, start_k : start_k + length]
            grad_masked = grad_masked + kernel[:, shift_q, shift_k][:, None, None] * back_window
    grad_kern = jnp.stack(grad_taps, axis=1).reshape(kernel.shape)
    return (grad_masked, grad_kern)


def build_mask(doc_lengths, pad_count, length):
    places = jnp.arange(length, dtype=jnp.int32)
    doc_ends = jnp.cumsum(doc_lengths)
    segment = jnp.sum((places[:, None] >= doc_ends[None, :]).astype(jnp.int32), axis=1)
    live_end = length - pad_count
    same_doc = segment[:, None] == segment[None, :]
    causal = places[None, :] <= places[:, None]
    usable = (places[None, :] < live_end) | (places[None, :] == places[:, None])
    return same_doc & causal & usable


def outer_sum(left_rows, right_rows):
    return lax.dot_general(
        left_rows, right_rows, (((0,), (0,)), ((), ())), preferred_element_type=jnp.float32
    )


def back_product(grad_rows, weight_full):
    return lax.dot_general(
        grad_rows, weight_full, (((1,), (1,)), ((), ())), preferred_element_type=jnp.float32
    )


def attention_weights(norm_in, w_qkv, norm_heads, w_out):
    return (
        lax.all_gather(norm_in, "fsdp", axis=0, tiled=True),
        lax.all_gather(w_qkv, "fsdp", axis=0, tiled=True),
        lax.all_gather(norm_heads, "fsdp", axis=0, tiled=True),
        lax.all_gather(w_out, "fsdp", axis=0, tiled=True),
    )


def feed_weights(norm_mid, w_gate, w_up, w_down):
    return (
        lax.all_gather(norm_mid, "fsdp", axis=0, tiled=True),
        lax.all_gather(w_gate, "fsdp", axis=0, tiled=True),
        lax.all_gather(w_up, "fsdp", axis=0, tiled=True),
        lax.all_gather(w_down, "fsdp", axis=0, tiled=True),
    )


def per_device(
    tokens,
    doc_lengths,
    pad_counts,
    norm_in,
    w_qkv,
    kernel,
    mixing,
    norm_heads,
    w_out,
    norm_mid,
    w_gate,
    w_up,
    w_down,
    cotangent,
):
    inputs = tokens[0].astype(jnp.float32)
    length = inputs.shape[0]
    model_width = inputs.shape[1]
    head_count = kernel.shape[0]
    head_size = model_width // head_count
    pair_count = head_count // 2
    score_scale = head_size ** (-0.5)
    allowed = build_mask(doc_lengths[0], pad_counts[0], length)[None]
    kern_pairs = kernel.reshape(pair_count, 2, kernel.shape[1], kernel.shape[2])
    mix_pairs = mixing.reshape(pair_count, 2, 2)
    attn_set = attention_weights(norm_in, w_qkv, norm_heads, w_out)
    normed = rms_norm(inputs, attn_set[0].astype(jnp.float32)).astype(jnp.bfloat16)
    projected = jnp.dot(normed, attn_set[1], preferred_element_type=jnp.float32).astype(
        jnp.bfloat16
    )
    split_qkv = projected.reshape(length, 3, pair_count, 2, head_size).transpose(1, 2, 3, 0, 4)

    def pair_scores(queries, key_rows, kern_pair):
        raw_scores = (
            jnp.einsum("gie,gje->gij", queries, key_rows, preferred_element_type=jnp.float32)
            * score_scale
        )
        masked = jnp.where(allowed, raw_scores, 0.0)
        logits = jnp.where(allowed, convolve(masked, kern_pair), NEG_FILL)
        return (masked, logits)

    def pair_forward(pieces):
        queries, key_rows, value_rows, kern_pair, mix_pair = pieces
        masked, logits = pair_scores(queries, key_rows, kern_pair)
        row_peak = jnp.max(logits, axis=-1, keepdims=True)
        log_total = row_peak + jnp.log(jnp.sum(jnp.exp(logits - row_peak), axis=-1, keepdims=True))
        attn_probs = jnp.exp(logits - log_total)
        mixed_probs = jnp.einsum("og,gij->oij", mix_pair, attn_probs, precision=lax.Precision.HIGHEST)
        output = jnp.einsum(
            "oij,oje->oie", mixed_probs, value_rows.astype(jnp.float32), precision=lax.Precision.HIGHEST
        )
        return (output, log_total)

    attended_pairs, log_totals = lax.map(
        pair_forward, (split_qkv[0], split_qkv[1], split_qkv[2], kern_pairs, mix_pairs)
    )
    attended = attended_pairs.transpose(2, 0, 1, 3).reshape(length, head_count, head_size)
    gated_out = group_norm(attended, attn_set[2].astype(jnp.float32)).astype(jnp.bfloat16)
    residual = inputs + jnp.dot(gated_out, attn_set[3], preferred_element_type=jnp.float32)
    ffn_set = feed_weights(norm_mid, w_gate, w_up, w_down)
    normed_mid = rms_norm(residual, ffn_set[0].astype(jnp.float32)).astype(jnp.bfloat16)
    gate_pre = jnp.dot(normed_mid, ffn_set[1], preferred_element_type=jnp.float32)
    up_pre = jnp.dot(normed_mid, ffn_set[2], preferred_element_type=jnp.float32)
    sigmoid_gate = jax.nn.sigmoid(gate_pre)
    silu_gate = gate_pre * sigmoid_gate
    hidden = (silu_gate * up_pre).astype(jnp.bfloat16)
    layer_out = (residual + jnp.dot(hidden, ffn_set[3], preferred_element_type=jnp.float32))[None]
    ffn_again = feed_weights(norm_mid, w_gate, w_up, w_down)
    grad_y = cotangent[0]
    grad_w_down = outer_sum(hidden, grad_y)
    grad_hidden = back_product(grad_y, ffn_again[3])
    grad_gate = (
        grad_hidden * up_pre * sigmoid_gate * (1.0 + gate_pre * (1.0 - sigmoid_gate))
    ).astype(jnp.bfloat16)
    grad_up = (grad_hidden * silu_gate).astype(jnp.bfloat16)
    grad_w_gate = outer_sum(normed_mid, grad_gate)
    grad_w_up = outer_sum(normed_mid, grad_up)
    grad_mid = back_product(grad_gate, ffn_again[1]) + back_product(grad_up, ffn_again[2])
    mid_pull = jax.vjp(rms_norm, residual, ffn_again[0].astype(jnp.float32))[1]
    grad_residual_norm, grad_norm_mid = mid_pull(grad_mid)
    grad_residual = grad_y.astype(jnp.float32) + grad_residual_norm
    ffn_shards = (
        lax.psum_scatter(grad_norm_mid, "fsdp", scatter_dimension=0, tiled=True),
        lax.psum_scatter(grad_w_gate, "fsdp", scatter_dimension=0, tiled=True),
        lax.psum_scatter(grad_w_up, "fsdp", scatter_dimension=0, tiled=True),
        lax.psum_scatter(grad_w_down, "fsdp", scatter_dimension=0, tiled=True),
    )
    attn_again = attention_weights(norm_in, w_qkv, norm_heads, w_out)
    grad_branch = grad_residual.astype(jnp.bfloat16)
    grad_w_out = outer_sum(gated_out, grad_branch)
    grad_gated = back_product(grad_branch, attn_again[3])
    head_pull = jax.vjp(group_norm, attended, attn_again[2].astype(jnp.float32))[1]
    grad_attended, grad_norm_heads = head_pull(grad_gated)
    grad_att_pairs = (
        grad_attended.astype(jnp.bfloat16)
        .reshape(length, pair_count, 2, head_size)
        .transpose(1, 2, 0, 3)
    )

    def pair_backward(pieces):
        queries, key_rows, value_rows, kern_pair, mix_pair, log_total, grad_output = pieces
        masked, logits = pair_scores(queries, key_rows, kern_pair)
        attn_probs = jnp.exp(logits - log_total)
        mixed_probs = jnp.einsum("og,gij->oij", mix_pair, attn_probs, precision=lax.Precision.HIGHEST)
        grad_wide = grad_output.astype(jnp.float32)
        grad_mixed = jnp.einsum(
            "oie,oje->oij", grad_wide, value_rows.astype(jnp.float32), precision=lax.Precision.HIGHEST
        )
        grad_values = jnp.einsum("oij,oie->oje", mixed_probs, grad_wide, precision=lax.Precision.HIGHEST)
        grad_mix = jnp.einsum("oij,gij->og", grad_mixed, attn_probs, precision=lax.Precision.HIGHEST)
        grad_probs = jnp.einsum("og,oij->gij", mix_pair, grad_mixed, precision=lax.Precision.HIGHEST)
        grad_logits = attn_probs * (
            grad_probs - jnp.sum(attn_probs * grad_probs, axis=-1, keepdims=True)
        )
        grad_conv = jnp.where(allowed, grad_logits, 0.0)
        grad_masked, grad_kern = convolve_back(grad_conv, masked, kern_pair)
        grad_raw = jnp.where(allowed, grad_masked, 0.0)
        grad_query = (
            jnp.einsum("gij,gje->gie", grad_raw, key_rows.astype(jnp.float32), precision=lax.Precision.HIGHEST)
            * score_scale
        )
        grad_key = (
            jnp.einsum("gij,gie->gje", grad_raw, queries.astype(jnp.float32), precision=lax.Precision.HIGHEST)
            * score_scale
        )
        return (
            grad_query.astype(jnp.bfloat16),
            grad_key.astype(jnp.bfloat16),
            grad_values.astype(jnp.bfloat16),
            grad_kern,
            grad_mix,
        )

    grads_query, grads_key, grads_value, grad_kern_pairs, grad_mix_pairs = lax.map(
        pair_backward,
        (
            split_qkv[0],
            split_qkv[1],
            split_qkv[2],
            kern_pairs,
            mix_pairs,
            log_totals,
            grad_att_pairs,
        ),
    )
    grad_qkv = (
        jnp.stack([grads_query, grads_key, grads_value])
        .transpose(3, 0, 1, 2, 4)
        .reshape(length, 3 * model_width)
    )
    grad_w_qkv = outer_sum(normed, grad_qkv)
    grad_normed = back_product(grad_qkv, attn_again[1])
    in_pull = jax.vjp(rms_norm, inputs, attn_again[0].astype(jnp.float32))[1]
    grad_inputs_norm, grad_norm_in = in_pull(grad_normed)
    grad_tokens = (grad_residual + grad_inputs_norm)[None]
    small_sums = lax.psum(
        (grad_kern_pairs.reshape(kernel.shape), grad_mix_pairs.reshape(mixing.shape)),
        ("rep", "fsdp"),
    )
    attn_shards = (
        lax.psum_scatter(grad_norm_in, "fsdp", scatter_dimension=0, tiled=True),
        lax.psum_scatter(grad_w_qkv, "fsdp", scatter_dimension=0, tiled=True),
        lax.psum_scatter(grad_norm_heads, "fsdp", scatter_dimension=0, tiled=True),
        lax.psum_scatter(grad_w_out, "fsdp", scatter_dimension=0, tiled=True),
    )
    summed = (
        lax.psum(ffn_shards[0].astype(jnp.bfloat16), "rep").astype(jnp.float32),
        lax.psum(ffn_shards[1].astype(jnp.bfloat16), "rep").astype(jnp.float32),
        lax.psum(ffn_shards[2].astype(jnp.bfloat16), "rep").astype(jnp.float32),
        lax.psum(ffn_shards[3].astype(jnp.bfloat16), "rep").astype(jnp.float32),
        lax.psum(attn_shards[0].astype(jnp.bfloat16), "rep").astype(jnp.float32),
        lax.psum(attn_shards[1].astype(jnp.bfloat16), "rep").astype(jnp.float32),
        lax.psum(attn_shards[2].astype(jnp.bfloat16), "rep").astype(jnp.float32),
        lax.psum(attn_shards[3].astype(jnp.bfloat16), "rep").astype(jnp.float32),
    )
    return (
        layer_out,
        grad_tokens,
        summed[4],
        summed[5],
        small_sums[0],
        small_sums[1],
        summed[6],
        summed[7],
        summed[0],
        summed[1],
        summed[2],
        summed[3],
    )


def forward_kernel(cfg, *refs):
    (tok, ct, w_qkv, w_gate, w_up, w_down, w_o, kern_in, mix_in, gain_rows, docs, pads,
     tok_all, ct_all, a_all, b_all, d_all, o_all, nrm_all, qkv_all, p_all, m_all, gated_all, mid_all, resid, ends,
     gains, kern, mix, wq_v, w_a, w_b, meta, gain_v, ct_v, down_v, own_o,
     x_v, wa_v, wo_v, t_v, cat_v, shift_v, qkv_v, p_v, m_v, gated_v, meta_v, mid_v, tok_v,
     out_v, red, diag, near, rs_send, rs_recv,
     g_send, g_recv, g_loc, a_send, a_recv, ch_send, ch_recv, o_send, o_recv, meta_send, meta_recv, gain_send, gain_recv, meet_sems, loc, pack, row_in, row_out) = refs
    planes, dh, taps_q, taps_k = cfg["planes"], cfg["dh"], cfg["kq"], cfg["kk"]
    length, width = tok.shape
    per_pair = o_all.shape[0]
    scale = dh ** (-0.5)
    ff, chunk = cfg["ff"], cfg["ff"] // planes
    me = Place(planes)

    me.hail()

    wq_in = pltpu.make_async_copy(w_qkv, wq_v, loc.at[1])
    wq_in.start()
    tok_in = pltpu.make_async_copy(tok, tok_v, loc.at[0])
    tok_in.start()
    taps_in = [pltpu.make_async_copy(kern_in, kern, loc.at[6]), pltpu.make_async_copy(mix_in, mix, loc.at[7])]
    for cp in taps_in:
        cp.start()
    o_in = pltpu.make_async_copy(w_o, own_o, loc.at[4])
    o_in.start()
    down_in = pltpu.make_async_copy(w_down.at[pl.ds(me.y * chunk, chunk)], down_v, loc.at[3])
    down_in.start()
    ct_in = pltpu.make_async_copy(ct, ct_v, loc.at[5])
    ct_in.start()

    def columns(j, s, z):
        at = pl.multiple_of(z * (2 * PLANE * chunk) + s * (2 * chunk) + me.y * chunk, 128)
        src = (w_gate, w_up)[j].at[:, pl.ds(at, chunk)]
        return pltpu.make_async_copy(src, w_b.at[s, :, pl.ds(j * ff + z * chunk, chunk)], pack.at[j, s, z])

    for j in range(2):
        for s in range(PLANE):
            for z in range(planes):
                columns(j, s, z).start()

    places = lanes(8, length).astype(F32)
    last = length * 1.0
    reach = [docs[0, 0]]
    for k in range(1, docs.shape[1]):
        reach.append(reach[-1] + docs[0, k])
    own_end = jnp.full((8, length), last, F32)
    for end in reversed(reach):
        own_end = jnp.where(places < end.astype(F32), end.astype(F32), own_end)
    meta[...] = jnp.where(places < last - pads[0].astype(F32), own_end, places + 1.0)

    wq_in.wait()
    low = lanes(w_qkv.shape[0], 128) < 64
    for s in range(PLANE):
        base = (me.y if s % 2 == 0 else planes - 1 - me.y) * (4 * dh)

        def part(j):
            blk = wq_v[:, pl.ds(pl.multiple_of(j * width + base, 128), 4 * dh)].astype(F32)
            t0, t1, t2 = blk[:, 0:128], blk[:, 128:256], blk[:, 256:384]
            if s // 2 == 0:
                return t0, t1
            t1, t2 = pltpu.roll(t1, 64, 1), pltpu.roll(t2, 64, 1)
            return jnp.where(low, t1, t2), t2

        (q0, q1), (k0, k1), (v0, v1) = part(0), part(1), part(2)
        tiles = (
            q0,
            jnp.where(low, q1, pltpu.roll(v1, 64, 1)),
            k0,
            jnp.where(low, k1, 0.0),
            v0,
        )
        for i, t in enumerate(tiles):
            w_a[s, :, i * 128 : (i + 1) * 128] = t.astype(BF16)

    down_in.wait()
    down_out = pltpu.make_async_copy(down_v, d_all.at[me.g], loc.at[3])
    down_out.start()
    o_in.wait()
    tok_in.wait()
    for cp in taps_in:
        cp.wait()
    me.await_all()

    def first(src, dst_all, base):
        cps = []
        for d in range(1, PLANE):
            s = lax.rem(me.s + d, PLANE)
            cp = remote(src.at[s], dst_all.at[me.f], a_send.at[base + d], a_recv.at[base + d], (me.y, me.g * PLANE + s))
            cp.start()
            cps.append(cp)
        own = pltpu.make_async_copy(src.at[me.s], dst_all.at[me.f], a_send.at[base])
        own.start()
        return cps, own

    def first_wait(src, dst_all, base, own):
        for d in range(1, PLANE):
            s = lax.rem(me.s - d + PLANE, PLANE)
            blk = dst_all.at[me.g * PLANE + s]
            remote(blk, blk, a_send.at[base + d], a_recv.at[base + d], me.sib).wait_recv()
        own.wait()

    meta_sent = []
    for d in range(1, GROUP):
        to = lax.rem(me.slot + d, GROUP)
        cp = remote(
            meta, meta_v.at[me.slot], meta_send.at[d], meta_recv.at[d],
            (lax.div(to, PLANE), me.g * PLANE + lax.rem(to, PLANE)),
        )
        cp.start()
        meta_sent.append(cp)
    meta_here = pltpu.make_async_copy(meta, meta_v.at[me.slot], meta_send.at[0])
    meta_here.start()
    gain_here = pltpu.make_async_copy(gain_rows, gain_v.at[me.f], gain_send.at[0])
    gain_here.start()
    gain_sent = []
    for d in range(1, PLANE):
        to = lax.rem(me.s + d, PLANE)
        gain_sent.append(remote(gain_rows, gain_v.at[me.f], gain_send.at[d], gain_recv.at[d], (me.y, me.g * PLANE + to)))
        gain_sent[-1].start()
    sent_a, own_a = first(w_a, a_all, 0)
    tokens = Gather(me, tok_v, tok_all, g_send.at[0], g_recv.at[0], g_loc.at[0])
    tokens.start()

    o_y = jnp.where((me.g == 1) | (me.g == 2), 1, 0)
    o_c = jnp.where(me.g >= 2, 1, 0)
    o_here = pltpu.make_async_copy(own_o, o_all.at[me.c], o_send.at[0])
    o_sib = remote(own_o, o_all.at[me.c], o_send.at[0], o_recv.at[0], me.sib)

    @pl.when((o_y == me.y) & (o_c == me.c))
    def _():
        o_here.start()

    @pl.when((o_y == me.y) & (o_c != me.c))
    def _():
        o_sib.start()

    def o_copy(t, i):
        return remote(o_all, o_all, o_send.at[i], o_recv.at[1], me.plane_dev(t))

    o_way = ((2, 1), (2, 0), (1, 3), (1, 2))

    def o_each(act):
        for home, (first_to, then_to) in enumerate(o_way):

            @pl.when((me.g == home) & (me.home == home))
            def _():
                act(o_copy(first_to, 1))
                act(o_copy(then_to, 2))

    o_relays = ((me.home < 2) & (me.g == 2)) | ((me.home >= 2) & (me.g == 1))

    def o_from_home():
        o_here.wait()
        remote(o_all.at[1 - me.c], o_all.at[1 - me.c], o_send.at[0], o_recv.at[0], me.sib).wait_recv()

    def o_relay():
        o_copy(0, 1).wait_recv()
        o_copy(jnp.where(me.home < 2, planes - 1, 0), 1).start()

    blocks4 = lambda ref: (lambda b: ref.at[pl.ds(b * PLANE, PLANE)])
    spread_a = Spread(me, blocks4(a_all), ch_send.at[0], ch_recv.at[0])
    spread_b = Spread(me, blocks4(b_all), ch_send.at[1], ch_recv.at[1])
    spread_d = Spread(me, lambda b: d_all.at[b], ch_send.at[2], ch_recv.at[2])

    for g in range(2):
        for a, t in bands(kern, 2 * me.pair + g, length, False):
            high = t.astype(BF16)
            at = slice(a * length, (a + 1) * length)
            t_v[g, 0:length, at] = high
            t_v[g, length : 2 * length, at] = high
            t_v[g, 2 * length :, at] = (t - high.astype(F32)).astype(BF16)
    shift_v[0:8] = jnp.zeros((8, taps_q * length), F32)
    wo_v[...] = jnp.zeros(wo_v.shape, BF16)

    pl.when(me.g == me.home)(o_from_home)
    o_each(lambda cp: cp.start())
    gain_here.wait()
    for d in range(1, PLANE):
        fr = me.g * PLANE + lax.rem(me.s - d + PLANE, PLANE)
        remote(gain_rows, gain_v.at[fr], gain_send.at[d], gain_recv.at[d], me.sib).wait_recv()
    for d in range(1, planes):
        to = lax.rem(me.g + d, planes)
        part = gain_v.at[pl.ds(me.g * PLANE, PLANE)]
        gain_sent.append(remote(part, part, gain_send.at[PLANE + d], gain_recv.at[PLANE + d], me.plane_dev(to)))
        gain_sent[-1].start()
    first_wait(w_a, a_all, 0, own_a)
    spread_a.near()
    pl.when(o_relays)(o_relay)

    tokens.relay()
    for j in range(2):
        for s in range(PLANE):
            for z in range(planes):
                columns(j, s, z).wait()
    sent_b, own_b = first(w_b, b_all, PLANE)
    cots = Gather(me, ct_v, ct_all, g_send.at[1], g_recv.at[1], g_loc.at[1])
    ct_in.wait()
    cots.start()
    spread_a.settle()
    meet(me, meet_sems.at[0])
    spread_a.rest()

    down_out.wait()

    tokens.share()
    tokens.last()
    tokens.finish()
    for row in range(GROUP):
        pltpu.make_async_copy(tok_all.at[row], x_v.at[row], row_in.at[row]).start()
    first_wait(w_b, b_all, PLANE, own_b)
    for d in range(1, GROUP):
        fr = lax.rem(me.slot - d + GROUP, GROUP)
        remote(meta, meta_v.at[fr], meta_send.at[d], meta_recv.at[d], me.sib).wait_recv()
    meta_here.wait()
    ends[...] = meta_v[...]
    for d in range(1, planes):
        part = gain_v.at[pl.ds(lax.rem(me.g - d + planes, planes) * PLANE, PLANE)]
        remote(part, part, gain_send.at[PLANE + d], gain_recv.at[PLANE + d], me.sib).wait_recv()
    gains[...] = jnp.zeros(gains.shape, F32)
    lane = lanes(8, 128)
    for k in range(planes):
        v0, v1, v2, v3 = (gain_v[k * PLANE + j] for j in range(PLANE))
        v1, v2, v3 = pltpu.roll(v1, 96, 1), pltpu.roll(v2, 64, 1), pltpu.roll(v3, 32, 1)
        for j, t in enumerate((jnp.where(lane < 96, v0, v1), jnp.where(lane < 64, v1, v2), jnp.where(lane < 32, v2, v3))):
            at = k * PLANE * w_o.shape[0] + j * 128
            gains[0:2, at : at + 128] = t[0:2]
    v0, v1 = gain_v[2 * me.pair], pltpu.roll(gain_v[2 * me.pair + 1], 96, 1)
    gains[2:3, 0:128] = jnp.where(lane < 96, v0, v1)[2:3]
    gains[2:3, 128:256] = jnp.where(lane < 64, v1, 0.0)[2:3]

    resid[length:] = gains[...]

    def norms(i, carry):
        row, _ = order(me, i)
        pltpu.make_async_copy(tok_all.at[row], x_v.at[row], row_in.at[row]).wait()

        def norm(at):
            x = x_v[row, at].astype(F32)
            s = lax.rsqrt(jnp.mean(x * x, axis=-1, keepdims=True) + 1e-6)
            x_v[row, at] = (x * s * gains[0:1]).astype(BF16)

        strips(length, norm)
        pltpu.make_async_copy(x_v.at[row], nrm_all.at[row], row_out.at[0, row]).start()
        return carry

    lax.fori_loop(0, GROUP, norms, 0)
    spread_a.arrive()
    wa_in = pltpu.make_async_copy(a_all, wa_v, loc.at[1])
    wa_in.start()
    @pl.when((me.g != me.home) & jnp.logical_not(o_relays))
    def _():
        o_copy(0, 1).wait_recv()

    wo_in = pltpu.make_async_copy(o_all, wo_v.at[pl.ds(0, per_pair)], loc.at[2])
    wo_in.start()
    spread_d.near()
    spread_b.near()
    wa_in.wait()
    wo_in.wait()
    h0, h1 = head_lanes(length, dh)
    scatter = Scatter(me, out_v, red, diag, near, rs_send, rs_recv)

    mixing = pair_mixing(mix, me.pair)

    def attention(i):
        row, k = order(me, i)
        acc = nn(x_v[row], wa_v[...].reshape(width, QKV))
        at = lanes(length, 128)
        q = jnp.where(h0 | h1, acc[:, 0:SIDE], 0.0)
        kk = jnp.where(h0 | h1, acc[:, SIDE : 2 * SIDE], 0.0)
        tail = jnp.where(at < 64, pltpu.roll(acc[:, 128:256], 64, 1), 0.0)
        v = jnp.concatenate([acc[:, 2 * SIDE : QKV], tail], axis=1)
        q, kk, v = q.astype(BF16), kk.astype(BF16), v.astype(BF16)
        qkv_v[row, :, 0:SIDE] = q
        qkv_v[row, :, SIDE : 2 * SIDE] = kk
        qkv_v[row, :, 2 * SIDE : 3 * SIDE] = v
        pltpu.make_async_copy(qkv_v.at[row], qkv_all.at[row], row_out.at[1, row]).start()
        ok = allowed_mask(length, meta_v[row, 0:1, :])
        attended = jnp.zeros((length, SIDE), F32)
        for g in range(2):
            kg = jnp.where(h0 if g == 0 else h1, kk.astype(F32), 0.0).astype(BF16)
            raw = nt(q, kg) * scale
            masked = jnp.where(ok, raw, 0.0)
            m_v[row, g] = masked.astype(BF16)
            high = masked.astype(BF16)
            cat_v[:, 0:length] = high
            cat_v[:, length : 2 * length] = (masked - high.astype(F32)).astype(BF16)
            cat_v[:, 2 * length :] = high
            shift_v[8 : 8 + length] = nn(cat_v[...], t_v[g])
            conv = shift_v[8 : 8 + length, 0:length]
            for a in range(1, taps_q):
                conv = conv + shift_v[8 - a : 8 - a + length, a * length : (a + 1) * length]
            logits = jnp.where(ok, conv, NEG_FILL)
            e = jnp.exp(logits - jnp.max(logits, axis=-1, keepdims=True))
            probs = e / jnp.sum(e, axis=-1, keepdims=True)
            high = probs.astype(BF16)
            low = (probs - high.astype(F32)).astype(BF16)
            p_v[row, g, 0] = high
            p_v[row, g, 1] = low
            attended = attended + (nn(high, v) + nn(low, v)) * mix_lanes(mixing, g, dh)
        pltpu.make_async_copy(m_v.at[row], m_all.at[row], row_out.at[2, row]).start()
        pltpu.make_async_copy(p_v.at[row], p_all.at[row], row_out.at[3, row]).start()
        centred = attended - head_stats(attended, dh, h0, h1)
        centred = jnp.where(h0 | h1, centred, 0.0)
        scaled = centred * lax.rsqrt(head_stats(centred * centred, dh, h0, h1) + 1e-5)
        gated = (scaled * gains[2:3, 0:SIDE]).astype(BF16)
        gated_v[row] = gated
        pltpu.make_async_copy(gated_v.at[row], gated_all.at[row], row_out.at[4, row]).start()
        wo = wo_v[...].reshape(wo_v.shape[0] * wo_v.shape[1], width)

    def project(i):
        row, k = order(me, i)
        wo = wo_v[...].reshape(wo_v.shape[0] * wo_v.shape[1], width)
        part = nn(gated_v[row], wo[0:SIDE])

        @pl.when(lax.rem(i, 2) == 0)
        def _():
            scatter.put_sib(k, part)

        @pl.when(lax.rem(i, 2) == 1)
        def _():
            scatter.put_self(k, part)

        scatter.push(i)

    def one(i, carry):
        attention(i)

        project(i)

        @pl.when(i == 1)
        def _():
            cots.relay()

        @pl.when(i == 5)
        def _():
            spread_d.settle()
            spread_b.settle()
            meet(me, meet_sems.at[1])
            spread_d.rest()
            spread_b.rest()

        return carry

    lax.fori_loop(0, GROUP, one, 0)
    scatter.arrive()

    def middle(at):
        res = tok_v[at].astype(F32) + scatter.total(at)
        resid[at] = res
        s = lax.rsqrt(jnp.mean(res * res, axis=-1, keepdims=True) + 1e-6)
        mid_v[at] = (res * s * gains[1:2]).astype(BF16)

    strips(length, middle)
    mids = Gather(me, mid_v, mid_all, g_send.at[2], g_recv.at[2], g_loc.at[2])
    mids.start()
    mids.relay()
    cots.share()
    cots.last()
    mids.share()
    mids.last()
    mids.finish()
    cots.finish()
    spread_d.arrive()
    spread_b.arrive()
    scatter.finish_cores()
    scatter.finish_chips()
    for sp in (spread_a, spread_b, spread_d):
        sp.finish()
    o_each(lambda cp: cp.wait_send())

    @pl.when(o_relays)
    def _():
        o_copy(0, 1).wait_send()

    @pl.when((o_y == me.y) & (o_c != me.c))
    def _():
        o_sib.wait_send()

    for cp in meta_sent + gain_sent + sent_a + sent_b:
        cp.wait_send()
    for r in range(GROUP):
        pltpu.make_async_copy(x_v.at[r], nrm_all.at[r], row_out.at[0, r]).wait()
        pltpu.make_async_copy(qkv_v.at[r], qkv_all.at[r], row_out.at[1, r]).wait()
        pltpu.make_async_copy(m_v.at[r], m_all.at[r], row_out.at[2, r]).wait()
        pltpu.make_async_copy(p_v.at[r], p_all.at[r], row_out.at[3, r]).wait()
        pltpu.make_async_copy(gated_v.at[r], gated_all.at[r], row_out.at[4, r]).wait()


def forward_call(cfg, tok, ct, w_qkv, w_gate, w_up, w_down, w_o, kern, mix, gain_rows, docs, pads):
    length, width = tok.shape
    planes, ff, r = cfg["planes"], cfg["ff"], w_qkv.shape[0]
    n = planes * PLANE
    chunk = ff // planes
    per_pair = n // GROUP
    taps = cfg["kq"] * length
    pad_rows = -(-SIDE // w_o.shape[0])
    hbm, vmem, smem = pl.BlockSpec(memory_space=pl.ANY), pl.BlockSpec(memory_space=pltpu.VMEM), pl.BlockSpec(memory_space=pltpu.SMEM)
    sds = jax.ShapeDtypeStruct
    rows = (GROUP, length)
    dma = pltpu.SemaphoreType.DMA
    v16 = lambda *shape: pltpu.VMEM(shape, BF16)
    v32 = lambda *shape: pltpu.VMEM(shape, F32)
    return pl.pallas_call(
        functools.partial(forward_kernel, cfg),
        out_shape=(
            sds(rows + (width,), BF16), sds(rows + (width,), BF16),
            sds((n, r, QKV), BF16), sds((n, r, 2 * ff), BF16), sds((planes, chunk, width), BF16),
            sds((per_pair,) + w_o.shape, BF16), sds(rows + (width,), BF16), sds(rows + (3 * SIDE,), BF16),
            sds((GROUP, 2, 2, length, length), BF16), sds((GROUP, 2, length, length), BF16), sds(rows + (SIDE,), BF16),
            sds(rows + (width,), BF16), sds((length + 8, width), F32), sds((GROUP, 8, length), F32),
        ),
        in_specs=[hbm] * 9 + [vmem] + [smem] * 2,
        out_specs=(hbm,) * 12 + (vmem,) * 2,
        scratch_shapes=[
            v32(8, width), v32(*kern.shape), v32(*mix.shape), v16(*w_qkv.shape), v16(PLANE, r, QKV), v16(PLANE, r, 2 * ff), v32(8, length), v32(n, 8, 128), v16(length, width), v16(chunk, width), v16(*w_o.shape),
            v16(*rows, width), v16(n, r, QKV), v16(pad_rows, *w_o.shape),
            v16(2, 3 * length, taps), v16(length, 3 * length), v32(length + 8, taps),
            v16(*rows, 3 * SIDE), v16(GROUP, 2, 2, length, length), v16(GROUP, 2, length, length), v16(*rows, SIDE),
            v32(GROUP, 8, length), v16(length, width), v16(length, width),
            *Scatter.scratch(length, width),
            dma((3, Gather.SENDS)), dma((3, Gather.RECVS)), dma((3,)), dma((2 * PLANE,)), dma((2 * PLANE,)),
            dma((3, planes)), dma((3, planes)), dma((3,)), dma((2,)), dma((GROUP,)), dma((GROUP,)), dma((PLANE + planes,)), dma((PLANE + planes,)), pltpu.SemaphoreType.REGULAR((2,)),
            dma((8,)), dma((2, PLANE, planes)), dma((GROUP,)), dma((5, GROUP)),
        ],
        compiler_params=pltpu.CompilerParams(collective_id=1, has_side_effects=True, vmem_limit_bytes=60 * 2**20),
        name="attention_forward",
    )(tok, ct, w_qkv, w_gate, w_up, w_down, w_o, kern, mix, gain_rows, docs, pads)


def feed_kernel(cfg, *refs):
    (mid_all, ct_all, w_b, w_d, resid,
     g_res, branch_all, dw_b, out_red,
     mid_v, ct_v, wb_v, wd_v, hid_v, gu_v, tile_v, dd_v, zd_v, via_v, sd_v, first_v, zf_v, via_f, sf_v, flat_v,
     o_out, o_red, o_send, o_recv,
     m_out, m_red, m_diag, m_near, m_send, m_recv,
     g_send, g_recv, g_loc, z_send, z_recv, loc, row_in, out_sem) = refs
    length, width = ct_all.shape[1:]
    ff = cfg["ff"]
    gain = slice(length + 1, length + 2)
    me = Place(cfg["planes"])
    me.hail()
    wb_in = pltpu.make_async_copy(w_b, wb_v, loc.at[0])
    wb_in.start()
    wd_in = pltpu.make_async_copy(w_d, wd_v, loc.at[1])
    wd_in.start()

    def row_copies(row):
        return (
            pltpu.make_async_copy(mid_all.at[row], mid_v.at[row], row_in.at[0, row]),
            pltpu.make_async_copy(ct_all.at[row], ct_v.at[row], row_in.at[1, row]),
        )

    for i in range(2):
        for cp in row_copies(order(me, i)[0]):
            cp.start()
    me.await_all()
    sum_out = Scatter(me, o_out, o_red, None, None, o_send, o_recv)
    down_sum = Collect(me, lambda b: dd_v.at[pl.ds(b, 1)], zd_v, via_v, z_send.at[0], z_recv.at[0])
    down_sum.clear()
    first_sum = Collect(me, lambda b: first_v.at[b], zf_v, via_f, z_send.at[1], z_recv.at[1])
    first_sum.clear()
    sum_mid = Scatter(me, m_out, m_red, m_diag, m_near, m_send, m_recv)
    wb_in.wait()
    wd_in.wait()
    for i in range(2, GROUP):
        for cp in row_copies(order(me, i)[0]):
            cp.start()

    def one(i, carry):
        row, k = order(me, i)
        for cp in row_copies(row):
            cp.wait()
        wb = wb_v[...].reshape(width, 2 * ff)
        wd = wd_v[...].reshape(ff, width)
        pre = nn(mid_v[row], wb)
        gate, up = pre[:, :ff], pre[:, ff:]
        g_hidden = nt(ct_v[row], wd)
        sig = jax.nn.sigmoid(gate)
        silu = gate * sig
        hid_v[row] = (silu * up).astype(BF16)
        gu_v[row, :, :ff] = (g_hidden * up * sig * (1.0 + gate * (1.0 - sig))).astype(BF16)
        gu_v[row, :, ff:] = (g_hidden * silu).astype(BF16)
        mid_part = nt(gu_v[row], wb)

        @pl.when(lax.rem(i, 2) == 0)
        def _():
            sum_mid.put_sib(k, mid_part)

        @pl.when(lax.rem(i, 2) == 1)
        def _():
            sum_mid.put_self(k, mid_part)

        sum_mid.push(i)
        return carry

    def output(i, carry):
        row, k = order(me, i)
        out_part = nn(hid_v[row], wd_v[...].reshape(ff, width))

        @pl.when(lax.rem(i, 2) == 0)
        def _():
            sum_out.put_sib(k, out_part)

        @pl.when(lax.rem(i, 2) == 1)
        def _():
            sum_out.put_self(k, out_part)

        return carry

    lax.fori_loop(0, GROUP, one, 0)

    tokens = GROUP * length
    tile = SIDE

    def down(i, carry):
        at = pl.ds(pl.multiple_of(i * tile, tile), tile)
        value = tn(hid_v[:, :, at].reshape(tokens, tile), ct_v[...].reshape(tokens, width)).astype(BF16)
        per = tile // dd_v.shape[1]
        dd_v[pl.ds(i * per, per)] = value.reshape((per,) + dd_v.shape[1:])
        return carry

    lax.fori_loop(0, ff // tile, down, 0)
    down_sum.start()

    steps = width // tile

    def tile_out(i):
        slot = lax.rem(i, 2)
        at = pl.ds(pl.multiple_of(i * tile, tile), tile)
        return pltpu.make_async_copy(tile_v.at[slot], dw_b.at[at], out_sem.at[slot])

    def gate_up(i, carry):
        @pl.when(i >= 2)
        def _():
            tile_out(i - 2).wait()

        at = pl.ds(pl.multiple_of(i * tile, tile), tile)
        value = tn(mid_v[:, :, at].reshape(tokens, tile), gu_v[...].reshape(tokens, 2 * ff)).astype(BF16)
        tile_v[lax.rem(i, 2)] = value
        tile_out(i).start()
        r = first_v.shape[2]
        for z in range(first_v.shape[0]):
            for q in range(FIRST):
                lo = (z * PLANE + q) * r
                for tile_at in range(lo // tile, (lo + r - 1) // tile + 1):
                    begin, end = max(lo, tile_at * tile), min(lo + r, (tile_at + 1) * tile)

                    @pl.when(i == tile_at)
                    def _():
                        first_v[z, q, begin - lo : end - lo] = value[begin - tile_at * tile : end - tile_at * tile]

        return carry

    lax.fori_loop(0, steps, gate_up, 0)
    first_sum.start()
    g_res[length:] = jnp.zeros((8, width), F32)
    sum_mid.arrive()

    def middle(at):
        g_mid = sum_mid.total(at)
        res = resid[at]
        s = lax.rsqrt(jnp.mean(res * res, axis=-1, keepdims=True) + 1e-6)
        g_res[length : length + 1] = g_res[length : length + 1] + jnp.sum(g_mid * res * s, axis=0, keepdims=True)
        pulled = g_mid * resid[gain]
        back = ct_v[me.slot, at].astype(F32) + s * pulled
        back = back - res * (s * s * s * jnp.mean(pulled * res, axis=-1, keepdims=True))
        g_res[at] = back
        ct_v[me.slot, at] = back.astype(BF16)

    strips(length, middle)
    branch = Gather(me, ct_v.at[me.slot], branch_all, g_send, g_recv, g_loc.at[0])
    branch.start()

    lax.fori_loop(0, GROUP, output, 0)
    red_out = pltpu.make_async_copy(o_red, out_red.at[pl.ds(0, 4)], out_sem.at[2])
    red_out.start()
    down_sum.combine(lambda t: dd_v.at[pl.ds(t, 1)])
    branch.relay()
    first_sum.combine(lambda t: first_v.at[t])
    branch.share()
    branch.last()
    down_sum.total(sd_v, dd_v.at[pl.ds(me.g, 1)])
    sd_out = pltpu.make_async_copy(sd_v.at[0], out_red.at[4, pl.ds(0, sd_v.shape[1])], out_sem.at[3])
    sd_out.start()
    first_sum.total(sf_v, first_v.at[me.g])
    flat_v[...] = sf_v[...].reshape(flat_v.shape)
    r = sf_v.shape[1]
    own_rows = pl.ds(pl.multiple_of(me.g * (PLANE * r), 16), FIRST * r)
    tile_out(steps - 2).wait()
    tile_out(steps - 1).wait()
    sf_out = pltpu.make_async_copy(flat_v, dw_b.at[own_rows], out_sem.at[4])
    sf_out.start()
    branch.finish()
    sum_mid.finish_cores()
    sum_mid.finish_chips()
    sum_out.finish_cores()
    down_sum.finish()
    first_sum.finish()
    red_out.wait()
    sd_out.wait()
    sf_out.wait()


def feed_call(cfg, mid_all, ct_all, w_b, w_d, resid):
    length, width = ct_all.shape[1:]
    ff = cfg["ff"]
    hbm, vmem = pl.BlockSpec(memory_space=pl.ANY), pl.BlockSpec(memory_space=pltpu.VMEM)
    sds = jax.ShapeDtypeStruct
    dma = pltpu.SemaphoreType.DMA
    rows = (GROUP, length)
    chunk = ff // cfg["planes"]
    others = cfg["planes"] - 1
    r = w_b.shape[1]
    v16 = lambda *shape: pltpu.VMEM(shape, BF16)
    return pl.pallas_call(
        functools.partial(feed_kernel, cfg),
        out_shape=(
            sds((length + 8, width), F32), sds(rows + (width,), BF16),
            sds((width, 2 * ff), BF16), sds((5, length, width), BF16),
        ),
        in_specs=[hbm] * 4 + [vmem],
        out_specs=(vmem, hbm, hbm, hbm),
        scratch_shapes=[
            v16(*rows, width), v16(*rows, width), v16(*w_b.shape), v16(*w_d.shape), v16(*rows, ff), v16(*rows, 2 * ff),
            v16(2, SIDE, 2 * ff), v16(others + 1, chunk, width), v16(others, 1, chunk, width), v16(1, chunk, width), v16(1, chunk, width),
            v16(others + 1, FIRST, r, 2 * ff), v16(others, FIRST, r, 2 * ff), v16(FIRST, r, 2 * ff), v16(FIRST, r, 2 * ff), v16(FIRST * r, 2 * ff),
            *Scatter.scratch(length, width, chips=False), *Scatter.scratch(length, width),
            dma((Gather.SENDS,)), dma((Gather.RECVS,)), dma((1,)), dma((2, others + 1)), dma((2, others + 1)),
            dma((2,)), dma((2, GROUP)), dma((5,)),
        ],
        compiler_params=pltpu.CompilerParams(collective_id=2, has_side_effects=True, vmem_limit_bytes=63 * 2**20),
        name="feed_forward",
    )(mid_all, ct_all, w_b, w_d, resid)


def backward_kernel(cfg, *refs):
    (branch_all, o_all, a_all, nrm_all, qkv_all, p_all, m_all, gated_all, dw_b, out_red, tok,
     resid, kern_in, mix_in, g_res, ends,
     g_tokens, layer_out, out_a, out_c, out_b, out_d, out_o, out_small, out_line,
     gains, kern, mix, gb_v, wo_v, wa_v, nrm_v, qkv_v, p_v, m_v, t_v, cat_v, shift_v, corr_v, gq_v, da_v, dc_v, do_v, tok_v, rows_v, line_v, taps_v,
     zb_v, za_v, zc_v, zo_v, via_b, via_a, via_c, via_o, sb_v, sa_v, sc_v, so_v, far_b, strip_v, sd_v, small_v, small_in, last_v, last_in,
     s_out, s_red, s_diag, s_near, rs_send, rs_recv,
     l_red, l_diag, l_near, l_send, l_recv,
     z_send, z_recv, small_send, small_recv, line_send, line_recv, t_send, t_recv, loc, row_in) = refs
    planes, dh, taps_q, taps_k = cfg["planes"], cfg["dh"], cfg["kq"], cfg["kk"]
    length, width = tok.shape
    scale = dh ** (-0.5)
    me = Place(planes)
    per_pair = o_all.shape[0]
    r = a_all.shape[1]
    far = jnp.where(me.g == 1, planes - 1, 0)
    loads = [
        pltpu.make_async_copy(src, dst, loc.at[i])
        for i, (src, dst) in enumerate(
            [(a_all, wa_v), (o_all, wo_v.at[pl.ds(0, per_pair)]), (tok, tok_v)]
            + [(dw_b.at[pl.ds(me.g * PLANE, PLANE)], sb_v), (resid.at[pl.ds(length, 8)], gains)]
            + [(dw_b.at[pl.ds(far * PLANE + FIRST, PLANE - FIRST)], far_b), (out_red.at[pl.ds(0, 4)], l_red), (out_red.at[4, pl.ds(0, sd_v.shape[0])], sd_v)]
        )
    ]

    span = PLANE * r

    turns = ((3, 2, 1, 0), (0, 2, 3, 1), (3, 1, 0, 2), (0, 1, 2, 3))

    def turn_of(i):
        return sum(jnp.where(me.g == b, turns[b][i], 0) for b in range(planes))

    def nrm_copy(m):
        at = pl.ds(pl.multiple_of(turn_of(m % planes) * span, 128), span)
        return pltpu.make_async_copy(nrm_all.at[:, :, at], nrm_v.at[m % 2], loc.at[8 + m % 2])

    def row_copies(i):
        row = order(me, i)[0]
        at = lax.rem(i, SLOTS)
        cps = [pltpu.make_async_copy(branch_all.at[row], gb_v.at[row], row_in.at[0, i])]
        for j, (src, dst) in enumerate(((qkv_all, qkv_v), (p_all, p_v), (m_all, m_v))):
            cps.append(pltpu.make_async_copy(src.at[row], dst.at[at], row_in.at[j + 1, i]))
        return cps

    me.hail()
    taps_in = [pltpu.make_async_copy(kern_in, kern, loc.at[10]), pltpu.make_async_copy(mix_in, mix, loc.at[11])]
    for cp in taps_in:
        cp.start()
    wo_v[...] = jnp.zeros(wo_v.shape, BF16)
    loads[1].start()
    loads[0].start()
    for i in range(SLOTS):
        for cp in row_copies(i):
            cp.start()
    for cp in loads[2:]:
        cp.start()
    for j in range(2):
        nrm_copy(j).start()
    for cp in taps_in:
        cp.wait()
    for g in range(2):
        for a, t in bands(kern, 2 * me.pair + g, length, True):
            t_v[g, a * length : (a + 1) * length] = t.astype(BF16)
    shift_v[length:] = jnp.zeros((8, length), F32)
    corr_v[...] = jnp.zeros(corr_v.shape, F32)
    rows_v[...] = jnp.zeros(rows_v.shape, F32)
    small_v[...] = jnp.zeros(small_v.shape, F32)
    me.await_all()

    blocks4 = lambda ref: (lambda b: ref.at[pl.ds(b * PLANE, PLANE)])
    sum_b = Collect(me, lambda b: dw_b.at[pl.ds(b * PLANE + FIRST, PLANE - FIRST)], zb_v, via_b, z_send.at[0], z_recv.at[0])
    sum_a = Collect(me, blocks4(da_v), za_v, via_a, z_send.at[1], z_recv.at[1])
    sum_c = Collect(me, blocks4(dc_v), zc_v, via_c, z_send.at[3], z_recv.at[3])
    sum_o = Collect(me, lambda b: do_v.at[pl.ds(b, 1)], zo_v, via_o, z_send.at[2], z_recv.at[2])
    send_s = []
    for d in range(1, planes):
        to = lax.rem(me.g + d, planes)
        send_s.append(remote(small_v, small_in.at[d - 1], small_send.at[d - 1], small_recv.at[d - 1], me.plane_dev(to)))
    send_l = []
    for d in range(1, planes):
        to = lax.rem(me.g + d, planes)
        send_l.append(remote(last_v, last_in.at[d - 1], line_send.at[d - 1], line_recv.at[d - 1], me.plane_dev(to)))
    sum_b.start()
    for group in (sum_b, sum_a, sum_c, sum_o):
        group.clear()
    h0, h1 = head_lanes(length, dh)
    scatter = Scatter(me, s_out, s_red, s_diag, s_near, rs_send, rs_recv)
    layer = Scatter(me, None, l_red, l_diag, l_near, l_send, l_recv)
    def to_slot(d):
        to = lax.rem(me.slot + d, GROUP)
        return lax.div(to, PLANE), lax.rem(to, PLANE)

    def group_copies(kind, src_of, landing, places=None):
        def one_of(d):
            y, sl = to_slot(d)
            return remote(src_of(sl), landing.at[me.slot], t_send.at[kind, d], t_recv.at[kind, d], (y, me.g * PLANE + sl))

        own = pltpu.make_async_copy(src_of(me.s), landing.at[me.slot], t_send.at[kind, 0])
        cps = [one_of(d) for d in range(1, GROUP)] + [own]
        for d, cp in enumerate(cps, 1):
            if places is None:
                cp.start()
            else:
                sl = to_slot(d % GROUP)[1]
                pl.when((sl >= places[0]) & (sl < places[1]))(cp.start)
        return cps

    def group_wait(kind, cps, landing):
        for d in range(1, GROUP):
            fr = lax.rem(me.slot - d + GROUP, GROUP)
            remote(landing.at[fr], landing.at[fr], t_send.at[kind, d], t_recv.at[kind, d], me.sib).wait_recv()
        for cp in cps[:-1]:
            cp.wait_send()
        cps[-1].wait()

    loads[0].wait()
    loads[1].wait()
    loads[5].wait()
    loads[6].wait()
    layer.push(1)
    layer.push(3)
    layer.ahead()
    loads[3].wait()
    loads[4].wait()
    group_copies(0, lambda sl: sb_v.at[sl], out_b, (0, FIRST))
    loads[7].wait()
    d_cp = remote(sd_v, out_d.at[me.y], t_send.at[3, 0], t_recv.at[3, 0], me.yn)
    d_cp.start()
    d_here = pltpu.make_async_copy(sd_v, out_d.at[me.y], t_send.at[3, 1])
    d_here.start()

    mixing = pair_mixing(mix, me.pair)

    def one(i, carry):
        row, k = order(me, i)
        at = lax.rem(i, SLOTS)
        for cp in row_copies(i):
            cp.wait()
        wo = wo_v[...].reshape(wo_v.shape[0] * wo_v.shape[1], width)[0:SIDE]
        q, kk, v = qkv_v[at, :, 0:SIDE], qkv_v[at, :, SIDE : 2 * SIDE], qkv_v[at, :, 2 * SIDE : 3 * SIDE]
        parts = [nn(p_v[at, g, 0], v) + nn(p_v[at, g, 1], v) for g in range(2)]
        probs = [p_v[at, g, 0].astype(F32) + p_v[at, g, 1].astype(F32) for g in range(2)]
        lane_mix = [mix_lanes(mixing, g, dh) for g in range(2)]
        attended = parts[0] * lane_mix[0] + parts[1] * lane_mix[1]
        centred = jnp.where(h0 | h1, attended - head_stats(attended, dh, h0, h1), 0.0)
        inv = lax.rsqrt(head_stats(centred * centred, dh, h0, h1) + 1e-5)
        normal = centred * inv
        g_gated = nt(gb_v[row], wo)
        rows_v[0:1] = rows_v[0:1] + jnp.sum(g_gated * normal, axis=0, keepdims=True)
        u = g_gated * gains[2:3, 0:SIDE]
        g_att = inv * (u - head_stats(u, dh, h0, h1) - normal * head_stats(u * normal, dh, h0, h1))
        g_exact = jnp.where(h0 | h1, g_att, 0.0)
        g_att = g_exact.astype(BF16).astype(F32)
        ok = allowed_mask(length, ends[row, 0:1, :])
        g_q = jnp.zeros((length, SIDE), F32)
        g_k = jnp.zeros((length, SIDE), F32)
        g_v = jnp.zeros((length, SIDE), F32)
        for o in range(2):
            mixed = mixing[o][0] * probs[0] + mixing[o][1] * probs[1]
            g_v = g_v + tn(mixed.astype(BF16), jnp.where(h0 if o == 0 else h1, g_att, 0.0).astype(BF16))
        for g in range(2):
            mine = h0 if g == 0 else h1
            rows_v[1 + g : 2 + g] = rows_v[1 + g : 2 + g] + jnp.sum(g_exact * parts[g], axis=0, keepdims=True)
            g_out = (g_att * lane_mix[g]).astype(BF16)
            g_probs = nt(g_out, v)
            g_conv = probs[g] * (g_probs - jnp.sum(probs[g] * g_probs, axis=-1, keepdims=True))
            shift_v[0:length] = g_conv
            for a in range(taps_q):
                cat_v[:, a * length : (a + 1) * length] = shift_v[a : a + length].astype(BF16)
            corr_v[g] = corr_v[g] + tn(m_v[at, g], cat_v[...])
            g_raw = jnp.where(ok, nn(cat_v[...], t_v[g]), 0.0).astype(BF16)
            g_q = g_q + nn(g_raw, jnp.where(mine, kk.astype(F32), 0.0).astype(BF16))
            g_k = g_k + tn(g_raw, jnp.where(mine, q.astype(F32), 0.0).astype(BF16))
        g_q, g_k = g_q * scale, g_k * scale
        mid_tile = g_q[:, 128:256] + pltpu.roll(g_v[:, 128:256], 64, 1)
        packed = jnp.concatenate([g_q[:, 0:128], mid_tile, g_k, g_v[:, 0:128]], axis=1).astype(BF16)
        gq_v[row] = packed
        part = nt(packed, wa_v[...].reshape(width, QKV))

        @pl.when(lax.rem(i, 2) == 0)
        def _():
            scatter.put_sib(k, part)

        @pl.when(lax.rem(i, 2) == 1)
        def _():
            scatter.put_self(k, part)

        scatter.push(i, turn=False)

        @pl.when(i + SLOTS < GROUP)
        def _():
            for cp in row_copies(i + SLOTS):
                cp.start()

        @pl.when(i == 4)
        def _():
            layer.turn()

        @pl.when(i == 5)
        def _():
            sum_b.combine(lambda t: far_b)

        return carry

    lax.fori_loop(0, GROUP, one, 0)
    loads[2].wait()
    gated_in = [
        pltpu.make_async_copy(gated_all.at[i], p_v.at[i // 4, i // 2 % 2, i % 2], row_in.at[0, i]) for i in range(GROUP)
    ]
    for cp in gated_in:
        cp.start()

    tokens = GROUP * length
    for cp in gated_in:
        cp.wait()
    value = tn(p_v[...].reshape(tokens, SIDE), gb_v[...].reshape(tokens, width))
    do_v[...] = value[0 : 2 * dh].astype(BF16).reshape(do_v.shape)

    sum_o.start()
    def taps(at, carry):
        g, a = lax.div(at, taps_q), lax.rem(at, taps_q)
        lanes_at = pl.ds(pl.multiple_of(a * length, length), length)
        e = corr_v[g, :, lanes_at]
        diff = lax.broadcasted_iota(jnp.int32, (length, length), 0) - lax.broadcasted_iota(jnp.int32, (length, length), 1)
        for b in range(taps_k):
            line = jnp.sum(jnp.where(diff == b - taps_k // 2, e, 0.0), axis=0, keepdims=True)
            taps_v[b : b + 1] = line[:, 0:128] + line[:, 128:256]
        each = jnp.sum(taps_v[...], axis=-1, keepdims=True)
        small_v[0] = jnp.where(lanes(16, 128) == a * 2 * GROUP + 2 * me.pair + g, each, small_v[0])
        return carry

    taps_v[...] = jnp.zeros(taps_v.shape, F32)
    lax.fori_loop(0, 2 * taps_q, taps, 0)
    base = 1
    at = lanes(1, SIDE)
    for o in range(2):
        for g in range(2):
            line = jnp.where((at >= o * dh) & (at < (o + 1) * dh), rows_v[1 + g : 2 + g], 0.0)
            small_v[base, 2 * o + g : 2 * o + g + 1] = line[:, 0:128] + line[:, 128:256]
    for j in range(2):
        small_v[base, 4 + j : 5 + j] = rows_v[0:1, j * 128 : (j + 1) * 128]

    for j in range(width // 128):
        small_v[2, j : j + 1] = g_res[length : length + 1, j * 128 : (j + 1) * 128]
    for cp in send_s:
        cp.start()

    for m in range(2 * planes):
        i, narrow = m % planes, m >= planes
        nrm_copy(m).wait()
        at = slice(0, SIDE) if narrow else slice(SIDE, QKV)
        value = tn(nrm_v[m % 2].reshape(tokens, span), gq_v[:, :, at].reshape(tokens, at.stop - at.start))
        terms = da_v if narrow else dc_v
        terms[pl.ds(turn_of(i) * PLANE, PLANE)] = value.astype(BF16).reshape((PLANE,) + terms.shape[1:])
        if m + 2 < 2 * planes:
            nrm_copy(m + 2).start()
    for way in (True, False):
        sum_c.start((way,))
        sum_a.start((way,))
    scatter.turn()
    sum_b.total(sb_v.at[pl.ds(FIRST, PLANE - FIRST)], sb_v.at[pl.ds(FIRST, PLANE - FIRST)])
    b_cps = group_copies(0, lambda sl: sb_v.at[sl], out_b, (FIRST, PLANE))

    for cp in send_s:
        cp.wait_recv()
    for cp in send_s:
        cp.wait_send()
    small_v[...] = small_v[...] + sum(small_in[d] for d in range(planes - 1))
    small_cps = group_copies(2, lambda sl: small_v, out_small)

    sum_o.combine(lambda t: do_v.at[pl.ds(t, 1)])
    sum_c.combine(lambda t: dc_v.at[pl.ds(t * PLANE, PLANE)])

    sum_a.combine(lambda t: da_v.at[pl.ds(t * PLANE, PLANE)])

    layer.arrive()

    def result(at):
        cp = pltpu.make_async_copy(resid.at[at], strip_v, loc.at[0])
        cp.start()
        cp.wait()
        strip_v[...] = strip_v[...] + layer.total(at)
        cp = pltpu.make_async_copy(strip_v, layer_out.at[at], loc.at[0])
        cp.start()
        cp.wait()

    strips(length, result)

    scatter.arrive()

    def middle(at):
        g_normed = scatter.total(at)
        tok32 = tok_v[at].astype(F32)
        s = lax.rsqrt(jnp.mean(tok32 * tok32, axis=-1, keepdims=True) + 1e-6)
        line_v[0:1] = line_v[0:1] + jnp.sum(g_normed * tok32 * s, axis=0, keepdims=True)
        pulled = g_normed * gains[0:1]
        back = g_res[at] + s * pulled
        g_tokens[at] = back - tok32 * (s * s * s * jnp.mean(pulled * tok32, axis=-1, keepdims=True))

    line_v[...] = jnp.zeros(line_v.shape, F32)
    strips(length, middle)
    line = line_v[0:1]
    last_v[...] = jnp.zeros(last_v.shape, F32)
    for j in range(width // 128):
        last_v[j : j + 1] = line[:, j * 128 : (j + 1) * 128]
    for cp in send_l:
        cp.start()

    sum_o.total(so_v, do_v.at[pl.ds(me.g, 1)])
    o_to = me.pair * per_pair + lax.div(me.g, 2)
    o_half = lax.rem(me.g, 2)

    def o_copy(y):
        return remote(so_v.at[0], out_o.at[o_half], t_send.at[4, y], t_recv.at[4, o_half], (y, o_to))

    o_here = pltpu.make_async_copy(so_v.at[0], out_o.at[o_half], t_send.at[4, 2])

    def o_each(act, act_here):
        for y in range(2):
            mine = (y == me.y) & (o_to == me.f)

            @pl.when(jnp.logical_not(mine))
            def _():
                act(o_copy(y))

            @pl.when(mine)
            def _():
                act_here(o_here)

    o_each(lambda cp: cp.start(), lambda cp: cp.start())
    sum_c.total(sc_v, dc_v.at[pl.ds(me.g * PLANE, PLANE)])
    c_cps = group_copies(5, lambda sl: sc_v.at[sl], out_c)

    sum_a.total(sa_v, da_v.at[pl.ds(me.g * PLANE, PLANE)])
    a_cps = group_copies(1, lambda sl: sa_v.at[sl], out_a)

    for cp in send_l:
        cp.wait_recv()
    for cp in send_l:
        cp.wait_send()
    last_v[...] = last_v[...] + sum(last_in[d] for d in range(planes - 1))
    line_cps = group_copies(6, lambda sl: last_v, out_line)

    group_wait(2, small_cps, out_small)
    d_cp.wait_send()
    remote(out_d.at[1 - me.y], out_d.at[1 - me.y], t_send.at[3, 0], t_recv.at[3, 0], me.yn).wait_recv()
    d_here.wait()
    group_wait(0, b_cps, out_b)
    src_y = jnp.where((me.g == 1) | (me.g == 2), 1, 0)
    src_s = me.x * 2 + jnp.where(me.g >= 2, 1, 0)
    for h in range(2):
        src_f = (2 * lax.rem(me.f, per_pair) + h) * PLANE + src_s

        @pl.when(jnp.logical_not((src_y == me.y) & (src_f == me.f)))
        def _():
            remote(out_o.at[h], out_o.at[h], t_send.at[4, 0], t_recv.at[4, h], me.sib).wait_recv()

    o_each(lambda cp: cp.wait_send(), lambda cp: cp.wait())
    group_wait(5, c_cps, out_c)
    group_wait(1, a_cps, out_a)
    group_wait(6, line_cps, out_line)
    for group in (sum_b, sum_a, sum_c, sum_o):
        group.finish()
    scatter.finish_cores()
    scatter.finish_chips()
    layer.finish_chips()


def backward_call(cfg, *args):
    branch_all, o_all, a_all, tok = args[0], args[1], args[2], args[10]
    length, width = tok.shape
    planes, ff = cfg["planes"], cfg["ff"]
    n, r = a_all.shape[:2]
    chunk = ff // planes
    taps = cfg["kq"] * length
    pad_rows = -(-SIDE // o_all.shape[1])
    piece = 2 * cfg["dh"] // planes
    small = (3, 16, 128)
    hbm, vmem, smem = pl.BlockSpec(memory_space=pl.ANY), pl.BlockSpec(memory_space=pltpu.VMEM), pl.BlockSpec(memory_space=pltpu.SMEM)
    sds = jax.ShapeDtypeStruct
    dma = pltpu.SemaphoreType.DMA
    rows = (GROUP, length)
    others = planes - 1
    v16 = lambda *shape: pltpu.VMEM(shape, BF16)
    v32 = lambda *shape: pltpu.VMEM(shape, F32)
    b_block, o_block = (PLANE - FIRST, r, 2 * ff), (1, piece, width)
    a_block, c_block = (PLANE, r, SIDE), (PLANE, r, QKV - SIDE)
    return pl.pallas_call(
        functools.partial(backward_kernel, cfg),
        out_shape=(
            sds((length, width), F32), sds((length, width), F32), sds((GROUP, r, SIDE), BF16), sds((GROUP, r, QKV - SIDE), BF16),
            sds((GROUP, r, 2 * ff), BF16),
            sds((2, chunk, width), BF16), sds((2, piece, width), BF16), sds((GROUP,) + small, F32), sds((GROUP, 16, 128), F32),
        ),
        in_specs=[hbm] * 14 + [vmem] * 2,
        out_specs=(vmem,) + (hbm,) * 8,
        scratch_shapes=[
            v32(8, width), v32(*args[12].shape), v32(*args[13].shape), v16(*rows, width), v16(pad_rows, *o_all.shape[1:]), v16(n, r, QKV), v16(2, *rows, PLANE * r), v16(SLOTS, length, 3 * SIDE),
            v16(SLOTS, 2, 2, length, length), v16(SLOTS, 2, length, length),
            v16(2, taps, length), v16(length, taps), v32(length + 8, length), v32(2, length, taps), v16(*rows, QKV),
            v16(n, r, SIDE), v16(n, r, QKV - SIDE), v16(planes, piece, width), v16(length, width), v32(8, SIDE), v32(8, width), v32(16, 128),
            v16(others, *b_block), v16(others, *a_block), v16(others, *c_block), v16(others, *o_block),
            v16(*b_block), v16(*a_block), v16(*c_block), v16(*o_block),
            v16(PLANE, r, 2 * ff), v16(*a_block), v16(*c_block), v16(*o_block), v16(*b_block), v32(64, width), v16(chunk, width),
            v32(*small), v32(others, *small), v32(16, 128), v32(others, 16, 128),
            *Scatter.scratch(length, width), *Scatter.scratch(length, width, cores=False),
            dma((4, planes)), dma((4, planes)), dma((others,)), dma((others,)), dma((others,)), dma((others,)), dma((7, GROUP)), dma((7, GROUP)),
            dma((12,)), dma((4, GROUP)),
        ],
        compiler_params=pltpu.CompilerParams(collective_id=3, has_side_effects=True, vmem_limit_bytes=54 * 2**20),
        name="attention_backward",
    )(*args)


def results_kernel(cfg, a_ref, c_ref, b_ref, d_ref, o_ref, small_ref, line_ref, g_tok, layer, qkv_ref, gate_ref, up_ref, down_ref, out_ref,
                   taps_ref, mix_ref, in_ref, mid_ref, heads_ref, tok_ref, layer_ref, vec_v):
    planes, ff = cfg["planes"], cfg["ff"]
    rows, width = out_ref.shape
    chunk = ff // planes
    low = lanes(rows, 128) < 64

    def slot(pair):
        home, x = pair // 2, pair % 2
        y, c = (0, 1, 1, 0)[home], (0, 0, 1, 1)[home]
        return y * PLANE + x * 2 + c

    def joined(even, odd, low):
        o0, o1 = pltpu.roll(odd[0], 64, 1), pltpu.roll(odd[1], 64, 1)
        return even[0], jnp.where(low, even[1], o0), jnp.where(low, o0, o1)

    def tiles(pair, j):
        def t(i):
            ref, i = (a_ref, i) if i < 2 else (c_ref, i - 2)
            return ref[slot(pair), :, i * 128 : (i + 1) * 128].astype(F32)

        if j == 2:
            return t(4), pltpu.roll(t(1), 64, 1)
        return t(2 * j), t(2 * j + 1)

    for j in range(3):
        for two in range(GROUP // 2):
            for i, t in enumerate(joined(tiles(2 * two, j), tiles(2 * two + 1, j), low)):
                at = j * width + two * 384 + i * 128
                qkv_ref[:, at : at + 128] = t
    for z in range(planes):
        for s in range(PLANE):
            for y in range(2):
                at = ((z * PLANE + s) * 2 + y) * chunk
                src = b_ref.at[y * PLANE + s]
                gate_ref[:, at : at + chunk] = src[:, z * chunk : (z + 1) * chunk].astype(F32)
                up_ref[:, at : at + chunk] = src[:, ff + z * chunk : ff + (z + 1) * chunk].astype(F32)
    down_ref[...] = d_ref[0].astype(F32)
    out_ref[...] = o_ref[0].astype(F32)

    tok_ref[...] = g_tok[...]
    layer_ref[...] = layer[...]

    @pl.when(pl.program_id(0) == 0)
    def _():
        base = 1
        heads = 2 * GROUP
        taps = small_ref[0, 0]
        for s in range(1, GROUP):
            taps = taps + small_ref[s, 0]
        for k in range(cfg["kk"]):
            for q in range(cfg["kq"]):
                taps_ref[k, q : q + 1] = taps[k : k + 1, q * heads : (q + 1) * heads]
        mixed = [jnp.sum(small_ref[slot(pair), base], axis=-1, keepdims=True) for pair in range(GROUP)]
        for g in range(2):
            line = jnp.zeros((1, heads), F32)
            for pair in range(GROUP):
                for o in range(2):
                    k = 2 * o + g
                    line = jnp.where(lanes(1, heads) == 2 * pair + o, mixed[pair][k : k + 1], line)
            mix_ref[g : g + 1] = line
        vec_v[...] = jnp.zeros(vec_v.shape, F32)
        for k, part in enumerate((lambda s: line_ref[s], lambda s: small_ref[s, base + 1])):
            total = part(0)
            for s in range(1, GROUP):
                total = total + part(s)
            for j in range(width // 128):
                vec_v[k : k + 1, j * 128 : (j + 1) * 128] = total[j : j + 1]
        line = lambda pair: tuple(small_ref[slot(pair), base, 4 + j : 5 + j] for j in range(2))
        for two in range(GROUP // 2):
            for i, t in enumerate(joined(line(2 * two), line(2 * two + 1), lanes(1, 128) < 64)):
                vec_v[2:3, two * 384 + i * 128 : two * 384 + (i + 1) * 128] = t
        own = in_ref.shape[1]
        mine = pltpu.roll(vec_v[...], lax.rem(width - lax.axis_index("fsdp") * own, width), 1)
        for k, ref in enumerate((in_ref, mid_ref, heads_ref)):
            ref[...] = mine[k : k + 1, 0:own]


def results_call(cfg, out_a, out_c, out_b, out_d, out_o, small, line, g_tokens, layer_out):
    r = out_a.shape[1]
    _, chunk, width = out_d.shape
    half = r // 2
    sds = jax.ShapeDtypeStruct
    whole = lambda shape: pl.BlockSpec(shape, lambda i: (0,) * len(shape))
    rows = lambda n, w: pl.BlockSpec((n, w), lambda i: (i, 0))
    moved = 6 * (out_a.size + out_c.size + out_b.size + out_d.size + out_o.size) + 16 * g_tokens.size
    return pl.pallas_call(
        functools.partial(results_kernel, cfg),
        grid=(2,),
        out_shape=(
            sds((r, 3 * width), F32), sds((r, n_cols(cfg)), F32), sds((r, n_cols(cfg)), F32), sds((2 * chunk, width), F32),
            sds((r, width), F32), sds((cfg["kk"], cfg["kq"], 2 * GROUP), F32), sds((2, 2 * GROUP), F32),
            sds((1, r), F32), sds((1, r), F32), sds((1, r), F32), sds(g_tokens.shape, F32), sds(g_tokens.shape, F32),
        ),
        in_specs=[
            pl.BlockSpec((GROUP, half, out_a.shape[2]), lambda i: (0, i, 0)),
            pl.BlockSpec((GROUP, half, out_c.shape[2]), lambda i: (0, i, 0)),
            pl.BlockSpec((GROUP, half, out_b.shape[2]), lambda i: (0, i, 0)),
            pl.BlockSpec((1, chunk, width), lambda i: (i, 0, 0)),
            pl.BlockSpec((1, half, width), lambda i: (i, 0, 0)),
            whole(small.shape),
            whole(line.shape),
            rows(g_tokens.shape[0] // 2, width),
            rows(g_tokens.shape[0] // 2, width),
        ],
        scratch_shapes=[pltpu.VMEM((8, width), F32)],
        out_specs=(
            rows(half, 3 * width), rows(half, n_cols(cfg)), rows(half, n_cols(cfg)), rows(chunk, width), rows(half, width),
            whole((cfg["kk"], cfg["kq"], 2 * GROUP)), whole((2, 2 * GROUP)),
            whole((1, r)), whole((1, r)), whole((1, r)), rows(g_tokens.shape[0] // 2, width), rows(g_tokens.shape[0] // 2, width),
        ),
        compiler_params=pltpu.CompilerParams(vmem_limit_bytes=60 * 2**20),
        cost_estimate=pl.CostEstimate(flops=0, bytes_accessed=moved, transcendentals=0),
        name="results",
    )(out_a, out_c, out_b, out_d, out_o, small, line, g_tokens, layer_out)


def n_cols(cfg):
    return cfg["ff"] * GROUP


def fits(mesh, tokens, kernel, w_gate):
    n = mesh.shape["fsdp"]
    width, length, heads, ff = tokens.shape[2], tokens.shape[1], kernel.shape[0], w_gate.shape[1]
    return (
        mesh.shape["rep"] == 2
        and n == 4 * PLANE
        and heads == 2 * GROUP
        and width == heads * 96
        and (width // n) % 32 == 0
        and ff % (2 * n * 128) == 0
        and length == SIDE
    )


def per_device_group(
    planes,
    tokens,
    doc_lengths,
    pad_counts,
    norm_in,
    w_qkv,
    kernel,
    mixing,
    norm_heads,
    w_out,
    norm_mid,
    w_gate,
    w_up,
    w_down,
    cotangent,
):
    length, width = tokens.shape[1:]
    heads, kq, kk = kernel.shape
    dh = width // heads
    n = planes * PLANE
    r = width // n
    chunk = w_down.shape[0] // 2
    ff = planes * chunk
    cfg = dict(planes=planes, dh=dh, kq=kq, kk=kk, ff=ff)

    gain_rows = jnp.pad(jnp.stack([norm_in, norm_mid, norm_heads]).astype(F32), ((0, 5), (0, 128 - r)))
    tok, ct = tokens[0], cotangent[0]
    kern, mix = kernel.transpose(2, 1, 0), mixing.T

    (_, ct_all, a_all, b_all, d_all, o_all, nrm_all, qkv_all, p_all, m_all, gated_all, mid_all, resid, ends) = (
        forward_call(
            cfg, tok, ct, w_qkv, w_gate, w_up, w_down, w_out, kern, mix, gain_rows, doc_lengths, pad_counts
        )
    )
    g_res, branch_all, dw_b, out_red = feed_call(cfg, mid_all, ct_all, b_all, d_all, resid)
    g_tokens, layer_out, out_a, out_c, out_b, out_d, out_o, small, line = backward_call(
        cfg, branch_all, o_all, a_all, nrm_all, qkv_all, p_all, m_all, gated_all, dw_b.reshape(n, r, 2 * ff), out_red,
        tok, resid, kern, mix, g_res, ends,
    )

    g_qkv, g_gate, g_up, g_down, g_out, g_kernel, g_mixing, g_in, g_mid, g_heads, g_tokens, layer_out = results_call(
        cfg, out_a, out_c, out_b, out_d, out_o, small, line, g_tokens, layer_out
    )
    return (
        layer_out[None],
        g_tokens[None],
        g_in[0],
        g_qkv,
        g_kernel.transpose(2, 1, 0),
        g_mixing.T,
        g_heads[0],
        g_out,
        g_mid[0],
        g_gate,
        g_up,
        g_down,
    )


def solution(mesh):
    in_specs = (
        P(("rep", "fsdp"), None, None),
        P(("rep", "fsdp"), None),
        P(("rep", "fsdp")),
        P("fsdp"),
        P("fsdp", None),
        P(),
        P(),
        P("fsdp"),
        P("fsdp", None),
        P("fsdp"),
        P("fsdp", None),
        P("fsdp", None),
        P("fsdp", None),
        P(("rep", "fsdp"), None, None),
    )
    out_specs = (
        P(("rep", "fsdp"), None, None),
        P(("rep", "fsdp"), None, None),
        P("fsdp"),
        P("fsdp", None),
        P(),
        P(),
        P("fsdp"),
        P("fsdp", None),
        P("fsdp"),
        P("fsdp", None),
        P("fsdp", None),
        P("fsdp", None),
    )

    def layer(*args):
        body = per_device
        if fits(mesh, args[0], args[5], args[10]):
            body = functools.partial(per_device_group, mesh.shape["fsdp"] // PLANE)
        return jax.shard_map(body, mesh=mesh, in_specs=in_specs, out_specs=out_specs, check_vma=False)(*args)

    return layer
```

```python
import functools

import jax
import jax.numpy as jnp
from jax import lax
from jax.experimental import pallas as pl
from jax.experimental.pallas import tpu as pltpu
from jax.sharding import PartitionSpec as P

F32 = jnp.float32
BF16 = jnp.bfloat16
NEG_FILL = -1e30
MESH = pl.DeviceIdType.MESH
PLANE = 4
GROUP = 8
SIDE = 256
FIRST = 1
SLOTS = 2
QKV = 640


class Place:
    def __init__(self, planes):
        self.planes = planes
        self.y = lax.axis_index("rep")
        self.f = lax.axis_index("fsdp")
        self.g = lax.div(self.f, PLANE)
        self.s = lax.rem(self.f, PLANE)
        self.x = lax.div(self.s, 2)
        self.c = lax.rem(self.s, 2)
        self.slot = self.y * PLANE + self.s
        self.home = self.y + self.c * (planes - 1 - 2 * self.y)
        self.pair = 2 * self.home + self.x
        self.sib = self.dev(self.y, self.x, 1 - self.c)
        self.xn = self.dev(self.y, 1 - self.x, self.c)
        self.yn = self.dev(1 - self.y, self.x, self.c)

    def dev(self, y, x, c):
        return (y, self.g * PLANE + x * 2 + c)

    def plane_dev(self, g):
        return (self.y, g * PLANE + self.s)

    def row(self, dy, dx, dc):
        y = self.y + dy - 2 * dy * self.y
        x = self.x + dx - 2 * dx * self.x
        c = self.c + dc - 2 * dc * self.c
        return y * 4 + x * 2 + c

    def hail(self):
        sem = pltpu.get_barrier_semaphore()
        n = self.planes * PLANE
        for d in range(1, n):
            pl.semaphore_signal(sem, inc=1, device_id=(self.y, lax.rem(self.f + d, n)), device_id_type=MESH)
        for s in range(PLANE):
            pl.semaphore_signal(sem, inc=1, device_id=(1 - self.y, self.g * PLANE + s), device_id_type=MESH)

    def await_all(self):
        pl.semaphore_wait(pltpu.get_barrier_semaphore(), self.planes * PLANE - 1 + PLANE)


def meet(me, sem):
    pl.semaphore_signal(sem, inc=1, device_id=me.sib, device_id_type=MESH)
    pl.semaphore_wait(sem, 1)


def remote(src, dst, send, recv, dev):
    return pltpu.make_async_remote_copy(
        src_ref=src, dst_ref=dst, send_sem=send, recv_sem=recv, device_id=dev, device_id_type=MESH
    )


class Gather:
    SENDS = 14
    RECVS = 14

    def __init__(self, me, own, buf, send, recv, local):
        self.me, self.own, self.buf = me, own, buf
        self.send, self.recv, self.local = send, recv, local
        self.half = own.shape[0] // 2
        self.sent = []

    def _own(self, h):
        return self.own.at[pl.ds(h * self.half, self.half)]

    def _blk(self, row, h):
        return self.buf.at[row, pl.ds(h * self.half, self.half)]

    def _copy(self, i):
        own, row, h, kind, dev = self.sent[i]
        src = self._own(h) if own else self._blk(row, h)
        return remote(src, self._blk(row, h), self.send.at[i], self.recv.at[kind * 2 + h], dev)

    def _go(self, own, row, h, kind, dev):
        self.sent.append((own, row, h, kind, dev))
        self._copy(len(self.sent) - 1).start()

    def _await(self, row, h, kind):
        b = self._blk(row, h)
        remote(b, b, self.send.at[0], self.recv.at[kind * 2 + h], self.me.sib).wait_recv()

    def start(self):
        me = self.me
        self.rows = [me.row(0, 0, 1), me.row(0, 1, 0), me.row(1, 0, 0), me.row(1, 1, 0), me.row(0, 1, 1), me.row(1, 0, 1), me.row(1, 1, 1)]
        self.here = pltpu.make_async_copy(self.own, self.buf.at[me.slot], self.local)
        self.here.start()
        self._go(True, me.slot, 0, 1, me.xn)
        self._go(True, me.slot, 1, 2, me.yn)
        self._go(True, me.slot, 0, 0, me.sib)
        self._go(True, me.slot, 1, 0, me.sib)
        self._go(True, me.slot, 1, 1, me.xn)
        self._go(True, me.slot, 0, 2, me.yn)

    def relay(self):
        me, rows = self.me, self.rows
        self._await(rows[1], 0, 1)
        self._go(False, rows[1], 0, 3, me.yn)
        self._go(False, rows[1], 0, 4, me.sib)
        self._await(rows[2], 1, 2)
        self._go(False, rows[2], 1, 3, me.xn)
        self._go(False, rows[2], 1, 5, me.sib)

    def share(self):
        me, rows = self.me, self.rows
        self._await(rows[1], 1, 1)
        self._go(False, rows[1], 1, 4, me.sib)
        self._await(rows[2], 0, 2)
        self._go(False, rows[2], 0, 5, me.sib)

    def last(self):
        me, rows = self.me, self.rows
        for h in (0, 1):
            self._await(rows[3], h, 3)
            self._go(False, rows[3], h, 6, me.sib)

    def finish(self):
        for kind in (0, 4, 5, 6):
            for h in (0, 1):
                self._await(self.rows[kind], h, kind)
        for i in range(len(self.sent)):
            self._copy(i).wait_send()
        self.here.wait()


class Scatter:
    SENDS = 10
    RECVS = 10

    @staticmethod
    def scratch(rows, width, cores=True, chips=True):
        bufs = []
        if cores:
            bufs.append(pltpu.VMEM((2, rows, width), BF16))
        bufs.append(pltpu.VMEM((4, rows, width), BF16))
        if chips:
            bufs += [pltpu.VMEM((2, rows // 2, width), BF16), pltpu.VMEM((2, rows, width), BF16)]
        return bufs + [pltpu.SemaphoreType.DMA((Scatter.SENDS,)), pltpu.SemaphoreType.DMA((Scatter.RECVS,))]

    def __init__(self, me, out, red, diag, near, send, recv):
        self.me, self.out, self.red, self.diag, self.near = me, out, red, diag, near
        self.send, self.recv = send, recv
        self.half = red.shape[1] // 2

    def _sib(self, k):
        return remote(self.out.at[lax.rem(k, 2)], self.red.at[k], self.send.at[k], self.recv.at[k], self.me.sib)

    def put_sib(self, k, value):
        @pl.when(k >= 2)
        def _():
            self._sib(k - 2).wait_send()

        self.out[lax.rem(k, 2)] = value.astype(BF16)
        self._sib(k).start()

    def put_self(self, k, value):
        self._sib(k).wait_recv()
        self.red[k] = (value + self.red[k].astype(F32)).astype(BF16)

    def _copy(self, name):
        h, me = self.half, self.me
        lo, hi = pl.ds(0, h), pl.ds(h, h)
        src, dst, i, dev = {
            "da": (self.red.at[0, lo], self.diag.at[0], 4, me.xn),
            "db": (self.red.at[0, hi], self.diag.at[1], 5, me.yn),
            "xa": (self.red.at[1, lo], self.near.at[0, lo], 6, me.xn),
            "xb": (self.red.at[1, hi], self.near.at[0, hi], 7, me.xn),
            "ya": (self.red.at[2, lo], self.near.at[1, lo], 8, me.yn),
            "yb": (self.red.at[2, hi], self.near.at[1, hi], 9, me.yn),
        }[name]
        return remote(src, dst, self.send.at[i], self.recv.at[i], dev)

    def push(self, i, turn=True):
        @pl.when(i == 1)
        def _():
            self._copy("da").start()
            self._copy("db").start()

        @pl.when(i == 3)
        def _():
            self._copy("xa").start()

        @pl.when(i == 5)
        def _():
            self._copy("yb").start()
            if turn:
                self.turn()

    def ahead(self):
        self._copy("yb").start()

    def turn(self):
        h = self.half
        self._copy("db").wait_recv()
        self.red[1, h:] = (self.red[1, h:].astype(F32) + self.diag[1].astype(F32)).astype(BF16)
        self._copy("xb").start()
        self._copy("da").wait_recv()
        self.red[2, :h] = (self.red[2, :h].astype(F32) + self.diag[0].astype(F32)).astype(BF16)
        self._copy("ya").start()

    def arrive(self):
        for name in ("xa", "xb", "ya", "yb"):
            self._copy(name).wait_recv()

    def total(self, at):
        return self.red[3, at].astype(F32) + self.near[0, at].astype(F32) + self.near[1, at].astype(F32)

    def finish_cores(self):
        for k in (2, 3):
            self._sib(k).wait_send()

    def finish_chips(self):
        for name in ("da", "db", "xa", "xb", "ya", "yb"):
            self._copy(name).wait_send()


class Spread:
    def __init__(self, me, blocks, send, recv):
        self.me, self.blocks, self.send, self.recv = me, blocks, send, recv

    def _copy(self, b, t, i):
        return remote(self.blocks(b), self.blocks(b), self.send.at[i], self.recv.at[b], self.me.plane_dev(t))

    def _sends(self, b):
        last = self.me.planes - 1
        if b in (0, last):
            return [(b, 1 if b == 0 else last - 1, 0)] + [(b, t, 1) for t in sorted(range(last + 1), key=lambda t: abs(t - b))[2:]]
        other, end = (2, 0) if b == 1 else (1, 3)
        return [(b, b - 1, 0), (b, b + 1, 0), (other, end, 1)]

    def _each(self, act, steps):
        for g in range(self.me.planes):

            @pl.when(self.me.g == g)
            def _():
                for i, (b, t, step) in enumerate(self._sends(g)):
                    if step in steps:
                        act(self._copy(b, t, i))

    def near(self):
        self._each(lambda cp: cp.start(), (0,))

    def settle(self):
        inner = (self.me.g == 0) | (self.me.g == 2)

        @pl.when(inner)
        def _():
            self._copy(1, 0, 0).wait_recv()

        @pl.when(jnp.logical_not(inner))
        def _():
            self._copy(2, 0, 0).wait_recv()

    def rest(self):
        self._each(lambda cp: cp.start(), (1,))

    def arrive(self):
        for g in range(self.me.planes):

            @pl.when(self.me.g == g)
            def _():
                for b in range(self.me.planes):
                    if b not in (g, 1 if g in (0, 2) else 2):
                        self._copy(b, b, 0).wait_recv()

    def finish(self):
        self._each(lambda cp: cp.wait_send(), (0, 1))


class Collect:
    def __init__(self, me, blocks, landing, via, send, recv):
        self.me, self.blocks, self.landing, self.via, self.send, self.recv = me, blocks, landing, via, send, recv
        self.by = {(0, 3): 1, (3, 0): 2} if me.planes == 4 else {}

    def _copy(self, b, t, src, i):
        at = (b - t) % self.me.planes - 1
        return remote(src, self.landing.at[at], self.send.at[i], self.recv.at[at], self.me.plane_dev(t))

    def _plan(self, b):
        combined = [t for (s, t), by in self.by.items() if by == b]
        direct = [t for t in range(self.me.planes) if t != b and t not in combined]
        direct.sort(key=lambda t: -abs(t - b))
        return [(t, (b, t) in self.by, i) for i, t in enumerate(direct)]

    def _each(self, b, act, ways=(True, False)):
        @pl.when(self.me.g == b)
        def _():
            for t, through, i in self._plan(b):
                if through not in ways:
                    continue
                if through:
                    z = self.me.planes
                    by = self.by[(b, t)]
                    act(remote(self.blocks(t), self.via, self.send.at[i], self.recv.at[z - 1], self.me.plane_dev(by)))
                else:
                    act(self._copy(b, t, self.blocks(t), i))

    def start(self, ways=(True, False)):
        for b in range(self.me.planes):
            self._each(b, lambda cp: cp.start(), ways)

    def _combined(self, b, t):
        return self._copy(b, t, self.via, self.me.planes - 2)

    def combine(self, own):
        for (s, t), by in self.by.items():

            @pl.when(self.me.g == by)
            def _():
                z = self.me.planes
                remote(self.via, self.via, self.send.at[0], self.recv.at[z - 1], self.me.plane_dev(by)).wait_recv()
                for q in range(self.via.shape[0]):
                    self.via[q] = (self.via[q].astype(F32) + own(t)[q].astype(F32)).astype(BF16)
                self._combined(by, t).start()

    def clear(self):
        for s, t in self.by:

            @pl.when(self.me.g == t)
            def _():
                at = (s - t) % self.me.planes - 1
                self.landing[at] = jnp.zeros(self.landing.shape[1:], BF16)

    def total(self, out, own):
        z = self.me.planes
        for t in range(z):

            @pl.when(self.me.g == t)
            def _():
                for b in range(z):
                    if b != t and (b, t) not in self.by:
                        at = (b - t) % z - 1
                        self._copy(b, t, self.landing.at[at], 0).wait_recv()

        for q in range(out.shape[0]):
            value = own[q].astype(F32)
            for at in range(z - 1):
                value = value + self.landing[at, q].astype(F32)
            out[q] = value.astype(BF16)

    def finish(self):
        for b in range(self.me.planes):
            self._each(b, lambda cp: cp.wait_send())
        for (s, t), by in self.by.items():

            @pl.when(self.me.g == by)
            def _():
                self._combined(by, t).wait_send()


def order(me, i):
    k = lax.div(i, 2)
    dx = 1 - lax.div(k, 2)
    dy = 1 - lax.rem(k, 2)
    dc = 1 - lax.rem(i, 2)
    return me.row(dy, dx, dc), k


def strips(length, body, strip=64):
    def one(i, carry):
        body(pl.ds(pl.multiple_of(i * strip, strip), strip))
        return carry

    lax.fori_loop(0, length // strip, one, 0)


def lanes(rows, width):
    return lax.broadcasted_iota(jnp.int32, (rows, width), 1)


def nt(a, b):
    return lax.dot_general(a, b, (((1,), (1,)), ((), ())), preferred_element_type=F32)


def tn(a, b):
    return lax.dot_general(a, b, (((0,), (0,)), ((), ())), preferred_element_type=F32)


def nn(a, b):
    return jnp.dot(a, b, preferred_element_type=F32)


def head_lanes(rows, dh):
    at = lanes(rows, SIDE)
    return at < dh, (at >= dh) & (at < 2 * dh)


def allowed_mask(length, ends):
    i = lax.broadcasted_iota(jnp.int32, (length, length), 0)
    j = lax.broadcasted_iota(jnp.int32, (length, length), 1)
    return (i >= j) & (i.astype(F32) < ends)


def of_head(value, head):
    at = lax.broadcasted_iota(jnp.int32, value.shape, value.ndim - 1)
    return jnp.sum(jnp.where(at == head, value, 0.0), axis=-1, keepdims=True)


def pair_mixing(mix_ref, pair):
    return [[of_head(mix_ref[g : g + 1], 2 * pair + o) for g in range(2)] for o in range(2)]


def mix_lanes(mixing, g, dh):
    at = lanes(1, SIDE)
    return jnp.where(at < dh, mixing[0][g], jnp.where(at < 2 * dh, mixing[1][g], 0.0))


def head_stats(value, dh, h0, h1):
    m0 = jnp.sum(jnp.where(h0, value, 0.0), axis=-1, keepdims=True) / dh
    m1 = jnp.sum(jnp.where(h1, value, 0.0), axis=-1, keepdims=True) / dh
    return jnp.where(h0, m0, jnp.where(h1, m1, 0.0))


def bands(kern_ref, head, length, flip):
    taps_k, taps_q, _ = kern_ref.shape
    r = lax.broadcasted_iota(jnp.int32, (length, length), 0)
    c = lax.broadcasted_iota(jnp.int32, (length, length), 1)
    diff = (c - r) if flip else (r - c)
    taps = [of_head(kern_ref[b], head) for b in range(taps_k)]
    for a in range(taps_q):
        acc = jnp.zeros((length, length), F32)
        for b in range(taps_k):
            acc = jnp.where(diff == b - taps_k // 2, taps[b][a : a + 1], acc)
        yield a, acc


def rms_norm(values_in, scaling):
    return (
        values_in
        * lax.rsqrt(jnp.mean(values_in * values_in, axis=-1, keepdims=True) + 1e-06)
        * scaling
    )


def group_norm(values_in, scaling):
    centred = values_in - jnp.mean(values_in, axis=-1, keepdims=True)
    scaled = centred * lax.rsqrt(jnp.mean(centred * centred, axis=-1, keepdims=True) + 1e-05)
    return scaled.reshape(values_in.shape[0], -1) * scaling


def convolve(scores, kernel):
    length = scores.shape[1]
    taps_query = kernel.shape[1]
    taps_key = kernel.shape[2]
    half_width = taps_key // 2
    padded = jnp.pad(scores, ((0, 0), (taps_query - 1, 0), (half_width, half_width)))
    summed = jnp.zeros_like(scores)
    for shift_q in range(taps_query):
        for shift_k in range(taps_key):
            start_q = taps_query - 1 - shift_q
            window = padded[:, start_q : start_q + length, shift_k : shift_k + length]
            summed = summed + kernel[:, shift_q, shift_k][:, None, None] * window
    return summed


def convolve_back(grad_conv, masked, kernel):
    length = masked.shape[1]
    taps_query = kernel.shape[1]
    taps_key = kernel.shape[2]
    half_width = taps_key // 2
    padded = jnp.pad(masked, ((0, 0), (taps_query - 1, 0), (half_width, half_width)))
    grad_padded = jnp.pad(grad_conv, ((0, 0), (0, taps_query - 1), (half_width, half_width)))
    grad_masked = jnp.zeros_like(masked)
    grad_taps = []
    for shift_q in range(taps_query):
        for shift_k in range(taps_key):
            start_q = taps_query - 1 - shift_q
            window = padded[:, start_q : start_q + length, shift_k : shift_k + length]
            grad_taps.append(jnp.sum(grad_conv * window, axis=(1, 2)))
            start_k = taps_key - 1 - shift_k
            back_window = grad_padded[:, shift_q : shift_q + length, start_k : start_k + length]
            grad_masked = grad_masked + kernel[:, shift_q, shift_k][:, None, None] * back_window
    grad_kern = jnp.stack(grad_taps, axis=1).reshape(kernel.shape)
    return (grad_masked, grad_kern)


def build_mask(doc_lengths, pad_count, length):
    places = jnp.arange(length, dtype=jnp.int32)
    doc_ends = jnp.cumsum(doc_lengths)
    segment = jnp.sum((places[:, None] >= doc_ends[None, :]).astype(jnp.int32), axis=1)
    live_end = length - pad_count
    same_doc = segment[:, None] == segment[None, :]
    causal = places[None, :] <= places[:, None]
    usable = (places[None, :] < live_end) | (places[None, :] == places[:, None])
    return same_doc & causal & usable


def outer_sum(left_rows, right_rows):
    return lax.dot_general(
        left_rows, right_rows, (((0,), (0,)), ((), ())), preferred_element_type=jnp.float32
    )


def back_product(grad_rows, weight_full):
    return lax.dot_general(
        grad_rows, weight_full, (((1,), (1,)), ((), ())), preferred_element_type=jnp.float32
    )


def attention_weights(norm_in, w_qkv, norm_heads, w_out):
    return (
        lax.all_gather(norm_in, "fsdp", axis=0, tiled=True),
        lax.all_gather(w_qkv, "fsdp", axis=0, tiled=True),
        lax.all_gather(norm_heads, "fsdp", axis=0, tiled=True),
        lax.all_gather(w_out, "fsdp", axis=0, tiled=True),
    )


def feed_weights(norm_mid, w_gate, w_up, w_down):
    return (
        lax.all_gather(norm_mid, "fsdp", axis=0, tiled=True),
        lax.all_gather(w_gate, "fsdp", axis=0, tiled=True),
        lax.all_gather(w_up, "fsdp", axis=0, tiled=True),
        lax.all_gather(w_down, "fsdp", axis=0, tiled=True),
    )


def per_device(
    tokens,
    doc_lengths,
    pad_counts,
    norm_in,
    w_qkv,
    kernel,
    mixing,
    norm_heads,
    w_out,
    norm_mid,
    w_gate,
    w_up,
    w_down,
    cotangent,
):
    inputs = tokens[0].astype(jnp.float32)
    length = inputs.shape[0]
    model_width = inputs.shape[1]
    head_count = kernel.shape[0]
    head_size = model_width // head_count
    pair_count = head_count // 2
    score_scale = head_size ** (-0.5)
    allowed = build_mask(doc_lengths[0], pad_counts[0], length)[None]
    kern_pairs = kernel.reshape(pair_count, 2, kernel.shape[1], kernel.shape[2])
    mix_pairs = mixing.reshape(pair_count, 2, 2)
    attn_set = attention_weights(norm_in, w_qkv, norm_heads, w_out)
    normed = rms_norm(inputs, attn_set[0].astype(jnp.float32)).astype(jnp.bfloat16)
    projected = jnp.dot(normed, attn_set[1], preferred_element_type=jnp.float32).astype(
        jnp.bfloat16
    )
    split_qkv = projected.reshape(length, 3, pair_count, 2, head_size).transpose(1, 2, 3, 0, 4)

    def pair_scores(queries, key_rows, kern_pair):
        raw_scores = (
            jnp.einsum("gie,gje->gij", queries, key_rows, preferred_element_type=jnp.float32)
            * score_scale
        )
        masked = jnp.where(allowed, raw_scores, 0.0)
        logits = jnp.where(allowed, convolve(masked, kern_pair), NEG_FILL)
        return (masked, logits)

    def pair_forward(pieces):
        queries, key_rows, value_rows, kern_pair, mix_pair = pieces
        masked, logits = pair_scores(queries, key_rows, kern_pair)
        row_peak = jnp.max(logits, axis=-1, keepdims=True)
        log_total = row_peak + jnp.log(jnp.sum(jnp.exp(logits - row_peak), axis=-1, keepdims=True))
        attn_probs = jnp.exp(logits - log_total)
        mixed_probs = jnp.einsum("og,gij->oij", mix_pair, attn_probs, precision=lax.Precision.HIGHEST)
        output = jnp.einsum(
            "oij,oje->oie", mixed_probs, value_rows.astype(jnp.float32), precision=lax.Precision.HIGHEST
        )
        return (output, log_total)

    attended_pairs, log_totals = lax.map(
        pair_forward, (split_qkv[0], split_qkv[1], split_qkv[2], kern_pairs, mix_pairs)
    )
    attended = attended_pairs.transpose(2, 0, 1, 3).reshape(length, head_count, head_size)
    gated_out = group_norm(attended, attn_set[2].astype(jnp.float32)).astype(jnp.bfloat16)
    residual = inputs + jnp.dot(gated_out, attn_set[3], preferred_element_type=jnp.float32)
    ffn_set = feed_weights(norm_mid, w_gate, w_up, w_down)
    normed_mid = rms_norm(residual, ffn_set[0].astype(jnp.float32)).astype(jnp.bfloat16)
    gate_pre = jnp.dot(normed_mid, ffn_set[1], preferred_element_type=jnp.float32)
    up_pre = jnp.dot(normed_mid, ffn_set[2], preferred_element_type=jnp.float32)
    sigmoid_gate = jax.nn.sigmoid(gate_pre)
    silu_gate = gate_pre * sigmoid_gate
    hidden = (silu_gate * up_pre).astype(jnp.bfloat16)
    layer_out = (residual + jnp.dot(hidden, ffn_set[3], preferred_element_type=jnp.float32))[None]
    ffn_again = feed_weights(norm_mid, w_gate, w_up, w_down)
    grad_y = cotangent[0]
    grad_w_down = outer_sum(hidden, grad_y)
    grad_hidden = back_product(grad_y, ffn_again[3])
    grad_gate = (
        grad_hidden * up_pre * sigmoid_gate * (1.0 + gate_pre * (1.0 - sigmoid_gate))
    ).astype(jnp.bfloat16)
    grad_up = (grad_hidden * silu_gate).astype(jnp.bfloat16)
    grad_w_gate = outer_sum(normed_mid, grad_gate)
    grad_w_up = outer_sum(normed_mid, grad_up)
    grad_mid = back_product(grad_gate, ffn_again[1]) + back_product(grad_up, ffn_again[2])
    mid_pull = jax.vjp(rms_norm, residual, ffn_again[0].astype(jnp.float32))[1]
    grad_residual_norm, grad_norm_mid = mid_pull(grad_mid)
    grad_residual = grad_y.astype(jnp.float32) + grad_residual_norm
    ffn_shards = (
        lax.psum_scatter(grad_norm_mid, "fsdp", scatter_dimension=0, tiled=True),
        lax.psum_scatter(grad_w_gate, "fsdp", scatter_dimension=0, tiled=True),
        lax.psum_scatter(grad_w_up, "fsdp", scatter_dimension=0, tiled=True),
        lax.psum_scatter(grad_w_down, "fsdp", scatter_dimension=0, tiled=True),
    )
    attn_again = attention_weights(norm_in, w_qkv, norm_heads, w_out)
    grad_branch = grad_residual.astype(jnp.bfloat16)
    grad_w_out = outer_sum(gated_out, grad_branch)
    grad_gated = back_product(grad_branch, attn_again[3])
    head_pull = jax.vjp(group_norm, attended, attn_again[2].astype(jnp.float32))[1]
    grad_attended, grad_norm_heads = head_pull(grad_gated)
    grad_att_pairs = (
        grad_attended.astype(jnp.bfloat16)
        .reshape(length, pair_count, 2, head_size)
        .transpose(1, 2, 0, 3)
    )

    def pair_backward(pieces):
        queries, key_rows, value_rows, kern_pair, mix_pair, log_total, grad_output = pieces
        masked, logits = pair_scores(queries, key_rows, kern_pair)
        attn_probs = jnp.exp(logits - log_total)
        mixed_probs = jnp.einsum("og,gij->oij", mix_pair, attn_probs, precision=lax.Precision.HIGHEST)
        grad_wide = grad_output.astype(jnp.float32)
        grad_mixed = jnp.einsum(
            "oie,oje->oij", grad_wide, value_rows.astype(jnp.float32), precision=lax.Precision.HIGHEST
        )
        grad_values = jnp.einsum("oij,oie->oje", mixed_probs, grad_wide, precision=lax.Precision.HIGHEST)
        grad_mix = jnp.einsum("oij,gij->og", grad_mixed, attn_probs, precision=lax.Precision.HIGHEST)
        grad_probs = jnp.einsum("og,oij->gij", mix_pair, grad_mixed, precision=lax.Precision.HIGHEST)
        grad_logits = attn_probs * (
            grad_probs - jnp.sum(attn_probs * grad_probs, axis=-1, keepdims=True)
        )
        grad_conv = jnp.where(allowed, grad_logits, 0.0)
        grad_masked, grad_kern = convolve_back(grad_conv, masked, kern_pair)
        grad_raw = jnp.where(allowed, grad_masked, 0.0)
        grad_query = (
            jnp.einsum("gij,gje->gie", grad_raw, key_rows.astype(jnp.float32), precision=lax.Precision.HIGHEST)
            * score_scale
        )
        grad_key = (
            jnp.einsum("gij,gie->gje", grad_raw, queries.astype(jnp.float32), precision=lax.Precision.HIGHEST)
            * score_scale
        )
        return (
            grad_query.astype(jnp.bfloat16),
            grad_key.astype(jnp.bfloat16),
            grad_values.astype(jnp.bfloat16),
            grad_kern,
            grad_mix,
        )

    grads_query, grads_key, grads_value, grad_kern_pairs, grad_mix_pairs = lax.map(
        pair_backward,
        (
            split_qkv[0],
            split_qkv[1],
            split_qkv[2],
            kern_pairs,
            mix_pairs,
            log_totals,
            grad_att_pairs,
        ),
    )
    grad_qkv = (
        jnp.stack([grads_query, grads_key, grads_value])
        .transpose(3, 0, 1, 2, 4)
        .reshape(length, 3 * model_width)
    )
    grad_w_qkv = outer_sum(normed, grad_qkv)
    grad_normed = back_product(grad_qkv, attn_again[1])
    in_pull = jax.vjp(rms_norm, inputs, attn_again[0].astype(jnp.float32))[1]
    grad_inputs_norm, grad_norm_in = in_pull(grad_normed)
    grad_tokens = (grad_residual + grad_inputs_norm)[None]
    small_sums = lax.psum(
        (grad_kern_pairs.reshape(kernel.shape), grad_mix_pairs.reshape(mixing.shape)),
        ("rep", "fsdp"),
    )
    attn_shards = (
        lax.psum_scatter(grad_norm_in, "fsdp", scatter_dimension=0, tiled=True),
        lax.psum_scatter(grad_w_qkv, "fsdp", scatter_dimension=0, tiled=True),
        lax.psum_scatter(grad_norm_heads, "fsdp", scatter_dimension=0, tiled=True),
        lax.psum_scatter(grad_w_out, "fsdp", scatter_dimension=0, tiled=True),
    )
    summed = (
        lax.psum(ffn_shards[0].astype(jnp.bfloat16), "rep").astype(jnp.float32),
        lax.psum(ffn_shards[1].astype(jnp.bfloat16), "rep").astype(jnp.float32),
        lax.psum(ffn_shards[2].astype(jnp.bfloat16), "rep").astype(jnp.float32),
        lax.psum(ffn_shards[3].astype(jnp.bfloat16), "rep").astype(jnp.float32),
        lax.psum(attn_shards[0].astype(jnp.bfloat16), "rep").astype(jnp.float32),
        lax.psum(attn_shards[1].astype(jnp.bfloat16), "rep").astype(jnp.float32),
        lax.psum(attn_shards[2].astype(jnp.bfloat16), "rep").astype(jnp.float32),
        lax.psum(attn_shards[3].astype(jnp.bfloat16), "rep").astype(jnp.float32),
    )
    return (
        layer_out,
        grad_tokens,
        summed[4],
        summed[5],
        small_sums[0],
        small_sums[1],
        summed[6],
        summed[7],
        summed[0],
        summed[1],
        summed[2],
        summed[3],
    )


def forward_kernel(cfg, *refs):
    (tok, ct, w_qkv, w_gate, w_up, w_down, w_o, kern_in, mix_in, gain_rows, docs, pads,
     tok_all, ct_all, a_all, b_all, d_all, o_all, nrm_all, qkv_all, p_all, m_all, gated_all, mid_all, resid, ends,
     gains, kern, mix, wq_v, w_a, w_b, meta, gain_v, ct_v, down_v, own_o,
     x_v, wa_v, wo_v, t_v, cat_v, shift_v, qkv_v, p_v, m_v, gated_v, meta_v, mid_v, tok_v,
     out_v, red, diag, near, rs_send, rs_recv,
     g_send, g_recv, g_loc, a_send, a_recv, ch_send, ch_recv, o_send, o_recv, meta_send, meta_recv, gain_send, gain_recv, meet_sems, loc, pack, row_in, row_out) = refs
    planes, dh, taps_q, taps_k = cfg["planes"], cfg["dh"], cfg["kq"], cfg["kk"]
    length, width = tok.shape
    per_pair = o_all.shape[0]
    scale = dh ** (-0.5)
    ff, chunk = cfg["ff"], cfg["ff"] // planes
    me = Place(planes)

    me.hail()

    wq_in = pltpu.make_async_copy(w_qkv, wq_v, loc.at[1])
    wq_in.start()
    tok_in = pltpu.make_async_copy(tok, tok_v, loc.at[0])
    tok_in.start()
    taps_in = [pltpu.make_async_copy(kern_in, kern, loc.at[6]), pltpu.make_async_copy(mix_in, mix, loc.at[7])]
    for cp in taps_in:
        cp.start()
    o_in = pltpu.make_async_copy(w_o, own_o, loc.at[4])
    o_in.start()
    down_in = pltpu.make_async_copy(w_down.at[pl.ds(me.y * chunk, chunk)], down_v, loc.at[3])
    down_in.start()
    ct_in = pltpu.make_async_copy(ct, ct_v, loc.at[5])
    ct_in.start()

    def columns(j, s, z):
        at = pl.multiple_of(z * (2 * PLANE * chunk) + s * (2 * chunk) + me.y * chunk, 128)
        src = (w_gate, w_up)[j].at[:, pl.ds(at, chunk)]
        return pltpu.make_async_copy(src, w_b.at[s, :, pl.ds(j * ff + z * chunk, chunk)], pack.at[j, s, z])

    for j in range(2):
        for s in range(PLANE):
            for z in range(planes):
                columns(j, s, z).start()

    places = lanes(8, length).astype(F32)
    last = length * 1.0
    reach = [docs[0, 0]]
    for k in range(1, docs.shape[1]):
        reach.append(reach[-1] + docs[0, k])
    own_end = jnp.full((8, length), last, F32)
    for end in reversed(reach):
        own_end = jnp.where(places < end.astype(F32), end.astype(F32), own_end)
    meta[...] = jnp.where(places < last - pads[0].astype(F32), own_end, places + 1.0)

    wq_in.wait()
    low = lanes(w_qkv.shape[0], 128) < 64
    for s in range(PLANE):
        base = (me.y if s % 2 == 0 else planes - 1 - me.y) * (4 * dh)

        def part(j):
            blk = wq_v[:, pl.ds(pl.multiple_of(j * width + base, 128), 4 * dh)].astype(F32)
            t0, t1, t2 = blk[:, 0:128], blk[:, 128:256], blk[:, 256:384]
            if s // 2 == 0:
                return t0, t1
            t1, t2 = pltpu.roll(t1, 64, 1), pltpu.roll(t2, 64, 1)
            return jnp.where(low, t1, t2), t2

        (q0, q1), (k0, k1), (v0, v1) = part(0), part(1), part(2)
        tiles = (
            q0,
            jnp.where(low, q1, pltpu.roll(v1, 64, 1)),
            k0,
            jnp.where(low, k1, 0.0),
            v0,
        )
        for i, t in enumerate(tiles):
            w_a[s, :, i * 128 : (i + 1) * 128] = t.astype(BF16)

    down_in.wait()
    down_out = pltpu.make_async_copy(down_v, d_all.at[me.g], loc.at[3])
    down_out.start()
    o_in.wait()
    tok_in.wait()
    for cp in taps_in:
        cp.wait()
    me.await_all()

    def first(src, dst_all, base):
        cps = []
        for d in range(1, PLANE):
            s = lax.rem(me.s + d, PLANE)
            cp = remote(src.at[s], dst_all.at[me.f], a_send.at[base + d], a_recv.at[base + d], (me.y, me.g * PLANE + s))
            cp.start()
            cps.append(cp)
        own = pltpu.make_async_copy(src.at[me.s], dst_all.at[me.f], a_send.at[base])
        own.start()
        return cps, own

    def first_wait(src, dst_all, base, own):
        for d in range(1, PLANE):
            s = lax.rem(me.s - d + PLANE, PLANE)
            blk = dst_all.at[me.g * PLANE + s]
            remote(blk, blk, a_send.at[base + d], a_recv.at[base + d], me.sib).wait_recv()
        own.wait()

    meta_sent = []
    for d in range(1, GROUP):
        to = lax.rem(me.slot + d, GROUP)
        cp = remote(
            meta, meta_v.at[me.slot], meta_send.at[d], meta_recv.at[d],
            (lax.div(to, PLANE), me.g * PLANE + lax.rem(to, PLANE)),
        )
        cp.start()
        meta_sent.append(cp)
    meta_here = pltpu.make_async_copy(meta, meta_v.at[me.slot], meta_send.at[0])
    meta_here.start()
    gain_here = pltpu.make_async_copy(gain_rows, gain_v.at[me.f], gain_send.at[0])
    gain_here.start()
    gain_sent = []
    for d in range(1, PLANE):
        to = lax.rem(me.s + d, PLANE)
        gain_sent.append(remote(gain_rows, gain_v.at[me.f], gain_send.at[d], gain_recv.at[d], (me.y, me.g * PLANE + to)))
        gain_sent[-1].start()
    sent_a, own_a = first(w_a, a_all, 0)
    tokens = Gather(me, tok_v, tok_all, g_send.at[0], g_recv.at[0], g_loc.at[0])
    tokens.start()

    o_y = jnp.where((me.g == 1) | (me.g == 2), 1, 0)
    o_c = jnp.where(me.g >= 2, 1, 0)
    o_here = pltpu.make_async_copy(own_o, o_all.at[me.c], o_send.at[0])
    o_sib = remote(own_o, o_all.at[me.c], o_send.at[0], o_recv.at[0], me.sib)

    @pl.when((o_y == me.y) & (o_c == me.c))
    def _():
        o_here.start()

    @pl.when((o_y == me.y) & (o_c != me.c))
    def _():
        o_sib.start()

    def o_copy(t, i):
        return remote(o_all, o_all, o_send.at[i], o_recv.at[1], me.plane_dev(t))

    o_way = ((2, 1), (2, 0), (1, 3), (1, 2))

    def o_each(act):
        for home, (first_to, then_to) in enumerate(o_way):

            @pl.when((me.g == home) & (me.home == home))
            def _():
                act(o_copy(first_to, 1))
                act(o_copy(then_to, 2))

    o_relays = ((me.home < 2) & (me.g == 2)) | ((me.home >= 2) & (me.g == 1))

    def o_from_home():
        o_here.wait()
        remote(o_all.at[1 - me.c], o_all.at[1 - me.c], o_send.at[0], o_recv.at[0], me.sib).wait_recv()

    def o_relay():
        o_copy(0, 1).wait_recv()
        o_copy(jnp.where(me.home < 2, planes - 1, 0), 1).start()

    blocks4 = lambda ref: (lambda b: ref.at[pl.ds(b * PLANE, PLANE)])
    spread_a = Spread(me, blocks4(a_all), ch_send.at[0], ch_recv.at[0])
    spread_b = Spread(me, blocks4(b_all), ch_send.at[1], ch_recv.at[1])
    spread_d = Spread(me, lambda b: d_all.at[b], ch_send.at[2], ch_recv.at[2])

    for g in range(2):
        for a, t in bands(kern, 2 * me.pair + g, length, False):
            high = t.astype(BF16)
            at = slice(a * length, (a + 1) * length)
            t_v[g, 0:length, at] = high
            t_v[g, length : 2 * length, at] = high
            t_v[g, 2 * length :, at] = (t - high.astype(F32)).astype(BF16)
    shift_v[0:8] = jnp.zeros((8, taps_q * length), F32)
    wo_v[...] = jnp.zeros(wo_v.shape, BF16)

    pl.when(me.g == me.home)(o_from_home)
    o_each(lambda cp: cp.start())
    gain_here.wait()
    for d in range(1, PLANE):
        fr = me.g * PLANE + lax.rem(me.s - d + PLANE, PLANE)
        remote(gain_rows, gain_v.at[fr], gain_send.at[d], gain_recv.at[d], me.sib).wait_recv()
    for d in range(1, planes):
        to = lax.rem(me.g + d, planes)
        part = gain_v.at[pl.ds(me.g * PLANE, PLANE)]
        gain_sent.append(remote(part, part, gain_send.at[PLANE + d], gain_recv.at[PLANE + d], me.plane_dev(to)))
        gain_sent[-1].start()
    first_wait(w_a, a_all, 0, own_a)
    spread_a.near()
    pl.when(o_relays)(o_relay)

    tokens.relay()
    for j in range(2):
        for s in range(PLANE):
            for z in range(planes):
                columns(j, s, z).wait()
    sent_b, own_b = first(w_b, b_all, PLANE)
    cots = Gather(me, ct_v, ct_all, g_send.at[1], g_recv.at[1], g_loc.at[1])
    ct_in.wait()
    cots.start()
    spread_a.settle()
    meet(me, meet_sems.at[0])
    spread_a.rest()

    down_out.wait()

    tokens.share()
    tokens.last()
    tokens.finish()
    for row in range(GROUP):
        pltpu.make_async_copy(tok_all.at[row], x_v.at[row], row_in.at[row]).start()
    first_wait(w_b, b_all, PLANE, own_b)
    for d in range(1, GROUP):
        fr = lax.rem(me.slot - d + GROUP, GROUP)
        remote(meta, meta_v.at[fr], meta_send.at[d], meta_recv.at[d], me.sib).wait_recv()
    meta_here.wait()
    ends[...] = meta_v[...]
    for d in range(1, planes):
        part = gain_v.at[pl.ds(lax.rem(me.g - d + planes, planes) * PLANE, PLANE)]
        remote(part, part, gain_send.at[PLANE + d], gain_recv.at[PLANE + d], me.sib).wait_recv()
    gains[...] = jnp.zeros(gains.shape, F32)
    lane = lanes(8, 128)
    for k in range(planes):
        v0, v1, v2, v3 = (gain_v[k * PLANE + j] for j in range(PLANE))
        v1, v2, v3 = pltpu.roll(v1, 96, 1), pltpu.roll(v2, 64, 1), pltpu.roll(v3, 32, 1)
        for j, t in enumerate((jnp.where(lane < 96, v0, v1), jnp.where(lane < 64, v1, v2), jnp.where(lane < 32, v2, v3))):
            at = k * PLANE * w_o.shape[0] + j * 128
            gains[0:2, at : at + 128] = t[0:2]
    v0, v1 = gain_v[2 * me.pair], pltpu.roll(gain_v[2 * me.pair + 1], 96, 1)
    gains[2:3, 0:128] = jnp.where(lane < 96, v0, v1)[2:3]
    gains[2:3, 128:256] = jnp.where(lane < 64, v1, 0.0)[2:3]

    resid[length:] = gains[...]

    def norms(i, carry):
        row, _ = order(me, i)
        pltpu.make_async_copy(tok_all.at[row], x_v.at[row], row_in.at[row]).wait()

        def norm(at):
            x = x_v[row, at].astype(F32)
            s = lax.rsqrt(jnp.mean(x * x, axis=-1, keepdims=True) + 1e-6)
            x_v[row, at] = (x * s * gains[0:1]).astype(BF16)

        strips(length, norm)
        pltpu.make_async_copy(x_v.at[row], nrm_all.at[row], row_out.at[0, row]).start()
        return carry

    lax.fori_loop(0, GROUP, norms, 0)
    spread_a.arrive()
    wa_in = pltpu.make_async_copy(a_all, wa_v, loc.at[1])
    wa_in.start()
    @pl.when((me.g != me.home) & jnp.logical_not(o_relays))
    def _():
        o_copy(0, 1).wait_recv()

    wo_in = pltpu.make_async_copy(o_all, wo_v.at[pl.ds(0, per_pair)], loc.at[2])
    wo_in.start()
    spread_d.near()
    spread_b.near()
    wa_in.wait()
    wo_in.wait()
    h0, h1 = head_lanes(length, dh)
    scatter = Scatter(me, out_v, red, diag, near, rs_send, rs_recv)

    mixing = pair_mixing(mix, me.pair)

    def attention(i):
        row, k = order(me, i)
        acc = nn(x_v[row], wa_v[...].reshape(width, QKV))
        at = lanes(length, 128)
        q = jnp.where(h0 | h1, acc[:, 0:SIDE], 0.0)
        kk = jnp.where(h0 | h1, acc[:, SIDE : 2 * SIDE], 0.0)
        tail = jnp.where(at < 64, pltpu.roll(acc[:, 128:256], 64, 1), 0.0)
        v = jnp.concatenate([acc[:, 2 * SIDE : QKV], tail], axis=1)
        q, kk, v = q.astype(BF16), kk.astype(BF16), v.astype(BF16)
        qkv_v[row, :, 0:SIDE] = q
        qkv_v[row, :, SIDE : 2 * SIDE] = kk
        qkv_v[row, :, 2 * SIDE : 3 * SIDE] = v
        pltpu.make_async_copy(qkv_v.at[row], qkv_all.at[row], row_out.at[1, row]).start()
        ok = allowed_mask(length, meta_v[row, 0:1, :])
        attended = jnp.zeros((length, SIDE), F32)
        for g in range(2):
            kg = jnp.where(h0 if g == 0 else h1, kk.astype(F32), 0.0).astype(BF16)
            raw = nt(q, kg) * scale
            masked = jnp.where(ok, raw, 0.0)
            m_v[row, g] = masked.astype(BF16)
            high = masked.astype(BF16)
            cat_v[:, 0:length] = high
            cat_v[:, length : 2 * length] = (masked - high.astype(F32)).astype(BF16)
            cat_v[:, 2 * length :] = high
            shift_v[8 : 8 + length] = nn(cat_v[...], t_v[g])
            conv = shift_v[8 : 8 + length, 0:length]
            for a in range(1, taps_q):
                conv = conv + shift_v[8 - a : 8 - a + length, a * length : (a + 1) * length]
            logits = jnp.where(ok, conv, NEG_FILL)
            e = jnp.exp(logits - jnp.max(logits, axis=-1, keepdims=True))
            probs = e / jnp.sum(e, axis=-1, keepdims=True)
            high = probs.astype(BF16)
            low = (probs - high.astype(F32)).astype(BF16)
            p_v[row, g, 0] = high
            p_v[row, g, 1] = low
            attended = attended + (nn(high, v) + nn(low, v)) * mix_lanes(mixing, g, dh)
        pltpu.make_async_copy(m_v.at[row], m_all.at[row], row_out.at[2, row]).start()
        pltpu.make_async_copy(p_v.at[row], p_all.at[row], row_out.at[3, row]).start()
        centred = attended - head_stats(attended, dh, h0, h1)
        centred = jnp.where(h0 | h1, centred, 0.0)
        scaled = centred * lax.rsqrt(head_stats(centred * centred, dh, h0, h1) + 1e-5)
        gated = (scaled * gains[2:3, 0:SIDE]).astype(BF16)
        gated_v[row] = gated
        pltpu.make_async_copy(gated_v.at[row], gated_all.at[row], row_out.at[4, row]).start()
        wo = wo_v[...].reshape(wo_v.shape[0] * wo_v.shape[1], width)

    def project(i):
        row, k = order(me, i)
        wo = wo_v[...].reshape(wo_v.shape[0] * wo_v.shape[1], width)
        part = nn(gated_v[row], wo[0:SIDE])

        @pl.when(lax.rem(i, 2) == 0)
        def _():
            scatter.put_sib(k, part)

        @pl.when(lax.rem(i, 2) == 1)
        def _():
            scatter.put_self(k, part)

        scatter.push(i)

    def one(i, carry):
        attention(i)

        project(i)

        @pl.when(i == 1)
        def _():
            cots.relay()

        @pl.when(i == 5)
        def _():
            spread_d.settle()
            spread_b.settle()
            meet(me, meet_sems.at[1])
            spread_d.rest()
            spread_b.rest()

        return carry

    lax.fori_loop(0, GROUP, one, 0)
    scatter.arrive()

    def middle(at):
        res = tok_v[at].astype(F32) + scatter.total(at)
        resid[at] = res
        s = lax.rsqrt(jnp.mean(res * res, axis=-1, keepdims=True) + 1e-6)
        mid_v[at] = (res * s * gains[1:2]).astype(BF16)

    strips(length, middle)
    mids = Gather(me, mid_v, mid_all, g_send.at[2], g_recv.at[2], g_loc.at[2])
    mids.start()
    mids.relay()
    cots.share()
    cots.last()
    mids.share()
    mids.last()
    mids.finish()
    cots.finish()
    spread_d.arrive()
    spread_b.arrive()
    scatter.finish_cores()
    scatter.finish_chips()
    for sp in (spread_a, spread_b, spread_d):
        sp.finish()
    o_each(lambda cp: cp.wait_send())

    @pl.when(o_relays)
    def _():
        o_copy(0, 1).wait_send()

    @pl.when((o_y == me.y) & (o_c != me.c))
    def _():
        o_sib.wait_send()

    for cp in meta_sent + gain_sent + sent_a + sent_b:
        cp.wait_send()
    for r in range(GROUP):
        pltpu.make_async_copy(x_v.at[r], nrm_all.at[r], row_out.at[0, r]).wait()
        pltpu.make_async_copy(qkv_v.at[r], qkv_all.at[r], row_out.at[1, r]).wait()
        pltpu.make_async_copy(m_v.at[r], m_all.at[r], row_out.at[2, r]).wait()
        pltpu.make_async_copy(p_v.at[r], p_all.at[r], row_out.at[3, r]).wait()
        pltpu.make_async_copy(gated_v.at[r], gated_all.at[r], row_out.at[4, r]).wait()


def forward_call(cfg, tok, ct, w_qkv, w_gate, w_up, w_down, w_o, kern, mix, gain_rows, docs, pads):
    length, width = tok.shape
    planes, ff, r = cfg["planes"], cfg["ff"], w_qkv.shape[0]
    n = planes * PLANE
    chunk = ff // planes
    per_pair = n // GROUP
    taps = cfg["kq"] * length
    pad_rows = -(-SIDE // w_o.shape[0])
    hbm, vmem, smem = pl.BlockSpec(memory_space=pl.ANY), pl.BlockSpec(memory_space=pltpu.VMEM), pl.BlockSpec(memory_space=pltpu.SMEM)
    sds = jax.ShapeDtypeStruct
    rows = (GROUP, length)
    dma = pltpu.SemaphoreType.DMA
    v16 = lambda *shape: pltpu.VMEM(shape, BF16)
    v32 = lambda *shape: pltpu.VMEM(shape, F32)
    return pl.pallas_call(
        functools.partial(forward_kernel, cfg),
        out_shape=(
            sds(rows + (width,), BF16), sds(rows + (width,), BF16),
            sds((n, r, QKV), BF16), sds((n, r, 2 * ff), BF16), sds((planes, chunk, width), BF16),
            sds((per_pair,) + w_o.shape, BF16), sds(rows + (width,), BF16), sds(rows + (3 * SIDE,), BF16),
            sds((GROUP, 2, 2, length, length), BF16), sds((GROUP, 2, length, length), BF16), sds(rows + (SIDE,), BF16),
            sds(rows + (width,), BF16), sds((length + 8, width), F32), sds((GROUP, 8, length), F32),
        ),
        in_specs=[hbm] * 9 + [vmem] + [smem] * 2,
        out_specs=(hbm,) * 12 + (vmem,) * 2,
        scratch_shapes=[
            v32(8, width), v32(*kern.shape), v32(*mix.shape), v16(*w_qkv.shape), v16(PLANE, r, QKV), v16(PLANE, r, 2 * ff), v32(8, length), v32(n, 8, 128), v16(length, width), v16(chunk, width), v16(*w_o.shape),
            v16(*rows, width), v16(n, r, QKV), v16(pad_rows, *w_o.shape),
            v16(2, 3 * length, taps), v16(length, 3 * length), v32(length + 8, taps),
            v16(*rows, 3 * SIDE), v16(GROUP, 2, 2, length, length), v16(GROUP, 2, length, length), v16(*rows, SIDE),
            v32(GROUP, 8, length), v16(length, width), v16(length, width),
            *Scatter.scratch(length, width),
            dma((3, Gather.SENDS)), dma((3, Gather.RECVS)), dma((3,)), dma((2 * PLANE,)), dma((2 * PLANE,)),
            dma((3, planes)), dma((3, planes)), dma((3,)), dma((2,)), dma((GROUP,)), dma((GROUP,)), dma((PLANE + planes,)), dma((PLANE + planes,)), pltpu.SemaphoreType.REGULAR((2,)),
            dma((8,)), dma((2, PLANE, planes)), dma((GROUP,)), dma((5, GROUP)),
        ],
        compiler_params=pltpu.CompilerParams(collective_id=1, has_side_effects=True, vmem_limit_bytes=60 * 2**20),
        name="attention_forward",
    )(tok, ct, w_qkv, w_gate, w_up, w_down, w_o, kern, mix, gain_rows, docs, pads)


def feed_kernel(cfg, *refs):
    (mid_all, ct_all, w_b, w_d, resid,
     g_res, branch_all, dw_b, out_red,
     mid_v, ct_v, wb_v, wd_v, hid_v, gu_v, tile_v, dd_v, zd_v, via_v, sd_v, first_v, zf_v, via_f, sf_v, flat_v,
     o_out, o_red, o_send, o_recv,
     m_out, m_red, m_diag, m_near, m_send, m_recv,
     g_send, g_recv, g_loc, z_send, z_recv, loc, row_in, out_sem) = refs
    length, width = ct_all.shape[1:]
    ff = cfg["ff"]
    gain = slice(length + 1, length + 2)
    me = Place(cfg["planes"])
    me.hail()
    wb_in = pltpu.make_async_copy(w_b, wb_v, loc.at[0])
    wb_in.start()
    wd_in = pltpu.make_async_copy(w_d, wd_v, loc.at[1])
    wd_in.start()

    def row_copies(row):
        return (
            pltpu.make_async_copy(mid_all.at[row], mid_v.at[row], row_in.at[0, row]),
            pltpu.make_async_copy(ct_all.at[row], ct_v.at[row], row_in.at[1, row]),
        )

    for i in range(2):
        for cp in row_copies(order(me, i)[0]):
            cp.start()
    me.await_all()
    sum_out = Scatter(me, o_out, o_red, None, None, o_send, o_recv)
    down_sum = Collect(me, lambda b: dd_v.at[pl.ds(b, 1)], zd_v, via_v, z_send.at[0], z_recv.at[0])
    down_sum.clear()
    first_sum = Collect(me, lambda b: first_v.at[b], zf_v, via_f, z_send.at[1], z_recv.at[1])
    first_sum.clear()
    sum_mid = Scatter(me, m_out, m_red, m_diag, m_near, m_send, m_recv)
    wb_in.wait()
    wd_in.wait()
    for i in range(2, GROUP):
        for cp in row_copies(order(me, i)[0]):
            cp.start()

    def one(i, carry):
        row, k = order(me, i)
        for cp in row_copies(row):
            cp.wait()
        wb = wb_v[...].reshape(width, 2 * ff)
        wd = wd_v[...].reshape(ff, width)
        pre = nn(mid_v[row], wb)
        gate, up = pre[:, :ff], pre[:, ff:]
        g_hidden = nt(ct_v[row], wd)
        sig = jax.nn.sigmoid(gate)
        silu = gate * sig
        hid_v[row] = (silu * up).astype(BF16)
        gu_v[row, :, :ff] = (g_hidden * up * sig * (1.0 + gate * (1.0 - sig))).astype(BF16)
        gu_v[row, :, ff:] = (g_hidden * silu).astype(BF16)
        mid_part = nt(gu_v[row], wb)

        @pl.when(lax.rem(i, 2) == 0)
        def _():
            sum_mid.put_sib(k, mid_part)

        @pl.when(lax.rem(i, 2) == 1)
        def _():
            sum_mid.put_self(k, mid_part)

        sum_mid.push(i)
        return carry

    def output(i, carry):
        row, k = order(me, i)
        out_part = nn(hid_v[row], wd_v[...].reshape(ff, width))

        @pl.when(lax.rem(i, 2) == 0)
        def _():
            sum_out.put_sib(k, out_part)

        @pl.when(lax.rem(i, 2) == 1)
        def _():
            sum_out.put_self(k, out_part)

        return carry

    lax.fori_loop(0, GROUP, one, 0)

    tokens = GROUP * length
    tile = SIDE

    def down(i, carry):
        at = pl.ds(pl.multiple_of(i * tile, tile), tile)
        value = tn(hid_v[:, :, at].reshape(tokens, tile), ct_v[...].reshape(tokens, width)).astype(BF16)
        per = tile // dd_v.shape[1]
        dd_v[pl.ds(i * per, per)] = value.reshape((per,) + dd_v.shape[1:])
        return carry

    lax.fori_loop(0, ff // tile, down, 0)
    down_sum.start()

    steps = width // tile

    def tile_out(i):
        slot = lax.rem(i, 2)
        at = pl.ds(pl.multiple_of(i * tile, tile), tile)
        return pltpu.make_async_copy(tile_v.at[slot], dw_b.at[at], out_sem.at[slot])

    def gate_up(i, carry):
        @pl.when(i >= 2)
        def _():
            tile_out(i - 2).wait()

        at = pl.ds(pl.multiple_of(i * tile, tile), tile)
        value = tn(mid_v[:, :, at].reshape(tokens, tile), gu_v[...].reshape(tokens, 2 * ff)).astype(BF16)
        tile_v[lax.rem(i, 2)] = value
        tile_out(i).start()
        r = first_v.shape[2]
        for z in range(first_v.shape[0]):
            for q in range(FIRST):
                lo = (z * PLANE + q) * r
                for tile_at in range(lo // tile, (lo + r - 1) // tile + 1):
                    begin, end = max(lo, tile_at * tile), min(lo + r, (tile_at + 1) * tile)

                    @pl.when(i == tile_at)
                    def _():
                        first_v[z, q, begin - lo : end - lo] = value[begin - tile_at * tile : end - tile_at * tile]

        return carry

    lax.fori_loop(0, steps, gate_up, 0)
    first_sum.start()
    g_res[length:] = jnp.zeros((8, width), F32)
    sum_mid.arrive()

    def middle(at):
        g_mid = sum_mid.total(at)
        res = resid[at]
        s = lax.rsqrt(jnp.mean(res * res, axis=-1, keepdims=True) + 1e-6)
        g_res[length : length + 1] = g_res[length : length + 1] + jnp.sum(g_mid * res * s, axis=0, keepdims=True)
        pulled = g_mid * resid[gain]
        back = ct_v[me.slot, at].astype(F32) + s * pulled
        back = back - res * (s * s * s * jnp.mean(pulled * res, axis=-1, keepdims=True))
        g_res[at] = back
        ct_v[me.slot, at] = back.astype(BF16)

    strips(length, middle)
    branch = Gather(me, ct_v.at[me.slot], branch_all, g_send, g_recv, g_loc.at[0])
    branch.start()

    down_sum.combine(lambda t: dd_v.at[pl.ds(t, 1)])
    lax.fori_loop(0, GROUP // 2, output, 0)
    branch.relay()
    lax.fori_loop(GROUP // 2, GROUP, output, 0)
    red_out = pltpu.make_async_copy(o_red, out_red.at[pl.ds(0, 4)], out_sem.at[2])
    red_out.start()
    first_sum.combine(lambda t: first_v.at[t])
    branch.share()
    branch.last()
    down_sum.total(sd_v, dd_v.at[pl.ds(me.g, 1)])
    sd_out = pltpu.make_async_copy(sd_v.at[0], out_red.at[4, pl.ds(0, sd_v.shape[1])], out_sem.at[3])
    sd_out.start()
    first_sum.total(sf_v, first_v.at[me.g])
    flat_v[...] = sf_v[...].reshape(flat_v.shape)
    r = sf_v.shape[1]
    own_rows = pl.ds(pl.multiple_of(me.g * (PLANE * r), 16), FIRST * r)
    tile_out(steps - 2).wait()
    tile_out(steps - 1).wait()
    sf_out = pltpu.make_async_copy(flat_v, dw_b.at[own_rows], out_sem.at[4])
    sf_out.start()
    branch.finish()
    sum_mid.finish_cores()
    sum_mid.finish_chips()
    sum_out.finish_cores()
    down_sum.finish()
    first_sum.finish()
    red_out.wait()
    sd_out.wait()
    sf_out.wait()


def feed_call(cfg, mid_all, ct_all, w_b, w_d, resid):
    length, width = ct_all.shape[1:]
    ff = cfg["ff"]
    hbm, vmem = pl.BlockSpec(memory_space=pl.ANY), pl.BlockSpec(memory_space=pltpu.VMEM)
    sds = jax.ShapeDtypeStruct
    dma = pltpu.SemaphoreType.DMA
    rows = (GROUP, length)
    chunk = ff // cfg["planes"]
    others = cfg["planes"] - 1
    r = w_b.shape[1]
    v16 = lambda *shape: pltpu.VMEM(shape, BF16)
    return pl.pallas_call(
        functools.partial(feed_kernel, cfg),
        out_shape=(
            sds((length + 8, width), F32), sds(rows + (width,), BF16),
            sds((width, 2 * ff), BF16), sds((5, length, width), BF16),
        ),
        in_specs=[hbm] * 4 + [vmem],
        out_specs=(vmem, hbm, hbm, hbm),
        scratch_shapes=[
            v16(*rows, width), v16(*rows, width), v16(*w_b.shape), v16(*w_d.shape), v16(*rows, ff), v16(*rows, 2 * ff),
            v16(2, SIDE, 2 * ff), v16(others + 1, chunk, width), v16(others, 1, chunk, width), v16(1, chunk, width), v16(1, chunk, width),
            v16(others + 1, FIRST, r, 2 * ff), v16(others, FIRST, r, 2 * ff), v16(FIRST, r, 2 * ff), v16(FIRST, r, 2 * ff), v16(FIRST * r, 2 * ff),
            *Scatter.scratch(length, width, chips=False), *Scatter.scratch(length, width),
            dma((Gather.SENDS,)), dma((Gather.RECVS,)), dma((1,)), dma((2, others + 1)), dma((2, others + 1)),
            dma((2,)), dma((2, GROUP)), dma((5,)),
        ],
        compiler_params=pltpu.CompilerParams(collective_id=2, has_side_effects=True, vmem_limit_bytes=63 * 2**20),
        name="feed_forward",
    )(mid_all, ct_all, w_b, w_d, resid)


def backward_kernel(cfg, *refs):
    (branch_all, o_all, a_all, nrm_all, qkv_all, p_all, m_all, gated_all, dw_b, out_red, tok,
     resid, kern_in, mix_in, g_res, ends,
     g_tokens, layer_out, out_a, out_c, out_b, out_d, out_o, out_small, out_line,
     gains, kern, mix, gb_v, wo_v, wa_v, nrm_v, qkv_v, p_v, m_v, t_v, cat_v, shift_v, corr_v, gq_v, da_v, dc_v, do_v, tok_v, rows_v, line_v, taps_v,
     zb_v, za_v, zc_v, zo_v, via_b, via_a, via_c, via_o, sb_v, sa_v, sc_v, so_v, far_b, strip_v, sd_v, small_v, small_in, last_v, last_in,
     s_out, s_red, s_diag, s_near, rs_send, rs_recv,
     l_red, l_diag, l_near, l_send, l_recv,
     z_send, z_recv, small_send, small_recv, line_send, line_recv, t_send, t_recv, loc, row_in) = refs
    planes, dh, taps_q, taps_k = cfg["planes"], cfg["dh"], cfg["kq"], cfg["kk"]
    length, width = tok.shape
    scale = dh ** (-0.5)
    me = Place(planes)
    per_pair = o_all.shape[0]
    r = a_all.shape[1]
    far = jnp.where(me.g == 1, planes - 1, 0)
    loads = [
        pltpu.make_async_copy(src, dst, loc.at[i])
        for i, (src, dst) in enumerate(
            [(a_all, wa_v), (o_all, wo_v.at[pl.ds(0, per_pair)]), (tok, tok_v)]
            + [(dw_b.at[pl.ds(me.g * PLANE, PLANE)], sb_v), (resid.at[pl.ds(length, 8)], gains)]
            + [(dw_b.at[pl.ds(far * PLANE + FIRST, PLANE - FIRST)], far_b), (out_red.at[pl.ds(0, 4)], l_red), (out_red.at[4, pl.ds(0, sd_v.shape[0])], sd_v)]
        )
    ]

    span = PLANE * r

    turns = ((3, 2, 1, 0), (0, 2, 3, 1), (3, 1, 0, 2), (0, 1, 2, 3))

    def turn_of(i):
        return sum(jnp.where(me.g == b, turns[b][i], 0) for b in range(planes))

    def nrm_copy(m):
        at = pl.ds(pl.multiple_of(turn_of(m % planes) * span, 128), span)
        return pltpu.make_async_copy(nrm_all.at[:, :, at], nrm_v.at[m % 2], loc.at[8 + m % 2])

    def row_copies(i):
        row = order(me, i)[0]
        at = lax.rem(i, SLOTS)
        cps = [pltpu.make_async_copy(branch_all.at[row], gb_v.at[row], row_in.at[0, i])]
        for j, (src, dst) in enumerate(((qkv_all, qkv_v), (p_all, p_v), (m_all, m_v))):
            cps.append(pltpu.make_async_copy(src.at[row], dst.at[at], row_in.at[j + 1, i]))
        return cps

    me.hail()
    taps_in = [pltpu.make_async_copy(kern_in, kern, loc.at[10]), pltpu.make_async_copy(mix_in, mix, loc.at[11])]
    for cp in taps_in:
        cp.start()
    wo_v[...] = jnp.zeros(wo_v.shape, BF16)
    loads[1].start()
    loads[0].start()
    for i in range(SLOTS):
        for cp in row_copies(i):
            cp.start()
    for cp in loads[2:]:
        cp.start()
    for j in range(2):
        nrm_copy(j).start()
    for cp in taps_in:
        cp.wait()
    for g in range(2):
        for a, t in bands(kern, 2 * me.pair + g, length, True):
            t_v[g, a * length : (a + 1) * length] = t.astype(BF16)
    shift_v[length:] = jnp.zeros((8, length), F32)
    corr_v[...] = jnp.zeros(corr_v.shape, F32)
    rows_v[...] = jnp.zeros(rows_v.shape, F32)
    small_v[...] = jnp.zeros(small_v.shape, F32)
    me.await_all()

    blocks4 = lambda ref: (lambda b: ref.at[pl.ds(b * PLANE, PLANE)])
    sum_b = Collect(me, lambda b: dw_b.at[pl.ds(b * PLANE + FIRST, PLANE - FIRST)], zb_v, via_b, z_send.at[0], z_recv.at[0])
    sum_a = Collect(me, blocks4(da_v), za_v, via_a, z_send.at[1], z_recv.at[1])
    sum_c = Collect(me, blocks4(dc_v), zc_v, via_c, z_send.at[3], z_recv.at[3])
    sum_o = Collect(me, lambda b: do_v.at[pl.ds(b, 1)], zo_v, via_o, z_send.at[2], z_recv.at[2])
    send_s = []
    for d in range(1, planes):
        to = lax.rem(me.g + d, planes)
        send_s.append(remote(small_v, small_in.at[d - 1], small_send.at[d - 1], small_recv.at[d - 1], me.plane_dev(to)))
    send_l = []
    for d in range(1, planes):
        to = lax.rem(me.g + d, planes)
        send_l.append(remote(last_v, last_in.at[d - 1], line_send.at[d - 1], line_recv.at[d - 1], me.plane_dev(to)))
    sum_b.start()
    for group in (sum_b, sum_a, sum_c, sum_o):
        group.clear()
    h0, h1 = head_lanes(length, dh)
    scatter = Scatter(me, s_out, s_red, s_diag, s_near, rs_send, rs_recv)
    layer = Scatter(me, None, l_red, l_diag, l_near, l_send, l_recv)
    def to_slot(d):
        to = lax.rem(me.slot + d, GROUP)
        return lax.div(to, PLANE), lax.rem(to, PLANE)

    def group_copies(kind, src_of, landing, places=None):
        def one_of(d):
            y, sl = to_slot(d)
            return remote(src_of(sl), landing.at[me.slot], t_send.at[kind, d], t_recv.at[kind, d], (y, me.g * PLANE + sl))

        own = pltpu.make_async_copy(src_of(me.s), landing.at[me.slot], t_send.at[kind, 0])
        cps = [one_of(d) for d in range(1, GROUP)] + [own]
        for d, cp in enumerate(cps, 1):
            if places is None:
                cp.start()
            else:
                sl = to_slot(d % GROUP)[1]
                pl.when((sl >= places[0]) & (sl < places[1]))(cp.start)
        return cps

    def group_wait(kind, cps, landing):
        for d in range(1, GROUP):
            fr = lax.rem(me.slot - d + GROUP, GROUP)
            remote(landing.at[fr], landing.at[fr], t_send.at[kind, d], t_recv.at[kind, d], me.sib).wait_recv()
        for cp in cps[:-1]:
            cp.wait_send()
        cps[-1].wait()

    loads[0].wait()
    loads[1].wait()
    loads[5].wait()
    loads[6].wait()
    layer.push(1)
    layer.push(3)
    layer.ahead()
    loads[3].wait()
    loads[4].wait()
    group_copies(0, lambda sl: sb_v.at[sl], out_b, (0, FIRST))
    loads[7].wait()
    d_cp = remote(sd_v, out_d.at[me.y], t_send.at[3, 0], t_recv.at[3, 0], me.yn)
    d_cp.start()
    d_here = pltpu.make_async_copy(sd_v, out_d.at[me.y], t_send.at[3, 1])
    d_here.start()

    mixing = pair_mixing(mix, me.pair)

    def one(i, carry):
        row, k = order(me, i)
        at = lax.rem(i, SLOTS)
        for cp in row_copies(i):
            cp.wait()
        wo = wo_v[...].reshape(wo_v.shape[0] * wo_v.shape[1], width)[0:SIDE]
        q, kk, v = qkv_v[at, :, 0:SIDE], qkv_v[at, :, SIDE : 2 * SIDE], qkv_v[at, :, 2 * SIDE : 3 * SIDE]
        parts = [nn(p_v[at, g, 0], v) + nn(p_v[at, g, 1], v) for g in range(2)]
        probs = [p_v[at, g, 0].astype(F32) + p_v[at, g, 1].astype(F32) for g in range(2)]
        lane_mix = [mix_lanes(mixing, g, dh) for g in range(2)]
        attended = parts[0] * lane_mix[0] + parts[1] * lane_mix[1]
        centred = jnp.where(h0 | h1, attended - head_stats(attended, dh, h0, h1), 0.0)
        inv = lax.rsqrt(head_stats(centred * centred, dh, h0, h1) + 1e-5)
        normal = centred * inv
        g_gated = nt(gb_v[row], wo)
        rows_v[0:1] = rows_v[0:1] + jnp.sum(g_gated * normal, axis=0, keepdims=True)
        u = g_gated * gains[2:3, 0:SIDE]
        g_att = inv * (u - head_stats(u, dh, h0, h1) - normal * head_stats(u * normal, dh, h0, h1))
        g_exact = jnp.where(h0 | h1, g_att, 0.0)
        g_att = g_exact.astype(BF16).astype(F32)
        ok = allowed_mask(length, ends[row, 0:1, :])
        g_q = jnp.zeros((length, SIDE), F32)
        g_k = jnp.zeros((length, SIDE), F32)
        g_v = jnp.zeros((length, SIDE), F32)
        for o in range(2):
            mixed = mixing[o][0] * probs[0] + mixing[o][1] * probs[1]
            g_v = g_v + tn(mixed.astype(BF16), jnp.where(h0 if o == 0 else h1, g_att, 0.0).astype(BF16))
        for g in range(2):
            mine = h0 if g == 0 else h1
            rows_v[1 + g : 2 + g] = rows_v[1 + g : 2 + g] + jnp.sum(g_exact * parts[g], axis=0, keepdims=True)
            g_out = (g_att * lane_mix[g]).astype(BF16)
            g_probs = nt(g_out, v)
            g_conv = probs[g] * (g_probs - jnp.sum(probs[g] * g_probs, axis=-1, keepdims=True))
            shift_v[0:length] = g_conv
            for a in range(taps_q):
                cat_v[:, a * length : (a + 1) * length] = shift_v[a : a + length].astype(BF16)
            corr_v[g] = corr_v[g] + tn(m_v[at, g], cat_v[...])
            g_raw = jnp.where(ok, nn(cat_v[...], t_v[g]), 0.0).astype(BF16)
            g_q = g_q + nn(g_raw, jnp.where(mine, kk.astype(F32), 0.0).astype(BF16))
            g_k = g_k + tn(g_raw, jnp.where(mine, q.astype(F32), 0.0).astype(BF16))
        g_q, g_k = g_q * scale, g_k * scale
        mid_tile = g_q[:, 128:256] + pltpu.roll(g_v[:, 128:256], 64, 1)
        packed = jnp.concatenate([g_q[:, 0:128], mid_tile, g_k, g_v[:, 0:128]], axis=1).astype(BF16)
        gq_v[row] = packed
        part = nt(packed, wa_v[...].reshape(width, QKV))

        @pl.when(lax.rem(i, 2) == 0)
        def _():
            scatter.put_sib(k, part)

        @pl.when(lax.rem(i, 2) == 1)
        def _():
            scatter.put_self(k, part)

        scatter.push(i, turn=False)

        @pl.when(i + SLOTS < GROUP)
        def _():
            for cp in row_copies(i + SLOTS):
                cp.start()

        @pl.when(i == 4)
        def _():
            layer.turn()

        @pl.when(i == 5)
        def _():
            sum_b.combine(lambda t: far_b)

        return carry

    lax.fori_loop(0, GROUP, one, 0)
    loads[2].wait()
    gated_in = [
        pltpu.make_async_copy(gated_all.at[i], p_v.at[i // 4, i // 2 % 2, i % 2], row_in.at[0, i]) for i in range(GROUP)
    ]
    for cp in gated_in:
        cp.start()

    tokens = GROUP * length
    for cp in gated_in:
        cp.wait()
    value = tn(p_v[...].reshape(tokens, SIDE), gb_v[...].reshape(tokens, width))
    do_v[...] = value[0 : 2 * dh].astype(BF16).reshape(do_v.shape)

    sum_o.start()
    def taps(at, carry):
        g, a = lax.div(at, taps_q), lax.rem(at, taps_q)
        lanes_at = pl.ds(pl.multiple_of(a * length, length), length)
        e = corr_v[g, :, lanes_at]
        diff = lax.broadcasted_iota(jnp.int32, (length, length), 0) - lax.broadcasted_iota(jnp.int32, (length, length), 1)
        for b in range(taps_k):
            line = jnp.sum(jnp.where(diff == b - taps_k // 2, e, 0.0), axis=0, keepdims=True)
            taps_v[b : b + 1] = line[:, 0:128] + line[:, 128:256]
        each = jnp.sum(taps_v[...], axis=-1, keepdims=True)
        small_v[0] = jnp.where(lanes(16, 128) == a * 2 * GROUP + 2 * me.pair + g, each, small_v[0])
        return carry

    taps_v[...] = jnp.zeros(taps_v.shape, F32)
    lax.fori_loop(0, 2 * taps_q, taps, 0)
    base = 1
    at = lanes(1, SIDE)
    for o in range(2):
        for g in range(2):
            line = jnp.where((at >= o * dh) & (at < (o + 1) * dh), rows_v[1 + g : 2 + g], 0.0)
            small_v[base, 2 * o + g : 2 * o + g + 1] = line[:, 0:128] + line[:, 128:256]
    for j in range(2):
        small_v[base, 4 + j : 5 + j] = rows_v[0:1, j * 128 : (j + 1) * 128]

    for j in range(width // 128):
        small_v[2, j : j + 1] = g_res[length : length + 1, j * 128 : (j + 1) * 128]
    for cp in send_s:
        cp.start()

    for m in range(2 * planes):
        i, narrow = m % planes, m >= planes
        nrm_copy(m).wait()
        at = slice(0, SIDE) if narrow else slice(SIDE, QKV)
        value = tn(nrm_v[m % 2].reshape(tokens, span), gq_v[:, :, at].reshape(tokens, at.stop - at.start))
        terms = da_v if narrow else dc_v
        terms[pl.ds(turn_of(i) * PLANE, PLANE)] = value.astype(BF16).reshape((PLANE,) + terms.shape[1:])
        if m + 2 < 2 * planes:
            nrm_copy(m + 2).start()
    for way in (True, False):
        sum_c.start((way,))
        sum_a.start((way,))
    scatter.turn()
    sum_b.total(sb_v.at[pl.ds(FIRST, PLANE - FIRST)], sb_v.at[pl.ds(FIRST, PLANE - FIRST)])
    b_cps = group_copies(0, lambda sl: sb_v.at[sl], out_b, (FIRST, PLANE))

    for cp in send_s:
        cp.wait_recv()
    for cp in send_s:
        cp.wait_send()
    small_v[...] = small_v[...] + sum(small_in[d] for d in range(planes - 1))
    small_cps = group_copies(2, lambda sl: small_v, out_small)

    sum_o.combine(lambda t: do_v.at[pl.ds(t, 1)])
    sum_c.combine(lambda t: dc_v.at[pl.ds(t * PLANE, PLANE)])

    sum_a.combine(lambda t: da_v.at[pl.ds(t * PLANE, PLANE)])

    layer.arrive()

    def result(at):
        cp = pltpu.make_async_copy(resid.at[at], strip_v, loc.at[0])
        cp.start()
        cp.wait()
        strip_v[...] = strip_v[...] + layer.total(at)
        cp = pltpu.make_async_copy(strip_v, layer_out.at[at], loc.at[0])
        cp.start()
        cp.wait()

    strips(length, result)

    scatter.arrive()

    def middle(at):
        g_normed = scatter.total(at)
        tok32 = tok_v[at].astype(F32)
        s = lax.rsqrt(jnp.mean(tok32 * tok32, axis=-1, keepdims=True) + 1e-6)
        line_v[0:1] = line_v[0:1] + jnp.sum(g_normed * tok32 * s, axis=0, keepdims=True)
        pulled = g_normed * gains[0:1]
        back = g_res[at] + s * pulled
        g_tokens[at] = back - tok32 * (s * s * s * jnp.mean(pulled * tok32, axis=-1, keepdims=True))

    line_v[...] = jnp.zeros(line_v.shape, F32)
    strips(length, middle)
    line = line_v[0:1]
    last_v[...] = jnp.zeros(last_v.shape, F32)
    for j in range(width // 128):
        last_v[j : j + 1] = line[:, j * 128 : (j + 1) * 128]
    for cp in send_l:
        cp.start()

    sum_o.total(so_v, do_v.at[pl.ds(me.g, 1)])
    o_to = me.pair * per_pair + lax.div(me.g, 2)
    o_half = lax.rem(me.g, 2)

    def o_copy(y):
        return remote(so_v.at[0], out_o.at[o_half], t_send.at[4, y], t_recv.at[4, o_half], (y, o_to))

    o_here = pltpu.make_async_copy(so_v.at[0], out_o.at[o_half], t_send.at[4, 2])

    def o_each(act, act_here):
        for y in range(2):
            mine = (y == me.y) & (o_to == me.f)

            @pl.when(jnp.logical_not(mine))
            def _():
                act(o_copy(y))

            @pl.when(mine)
            def _():
                act_here(o_here)

    o_each(lambda cp: cp.start(), lambda cp: cp.start())
    sum_c.total(sc_v, dc_v.at[pl.ds(me.g * PLANE, PLANE)])
    c_cps = group_copies(5, lambda sl: sc_v.at[sl], out_c)

    sum_a.total(sa_v, da_v.at[pl.ds(me.g * PLANE, PLANE)])
    a_cps = group_copies(1, lambda sl: sa_v.at[sl], out_a)

    for cp in send_l:
        cp.wait_recv()
    for cp in send_l:
        cp.wait_send()
    last_v[...] = last_v[...] + sum(last_in[d] for d in range(planes - 1))
    line_cps = group_copies(6, lambda sl: last_v, out_line)

    group_wait(2, small_cps, out_small)
    d_cp.wait_send()
    remote(out_d.at[1 - me.y], out_d.at[1 - me.y], t_send.at[3, 0], t_recv.at[3, 0], me.yn).wait_recv()
    d_here.wait()
    group_wait(0, b_cps, out_b)
    src_y = jnp.where((me.g == 1) | (me.g == 2), 1, 0)
    src_s = me.x * 2 + jnp.where(me.g >= 2, 1, 0)
    for h in range(2):
        src_f = (2 * lax.rem(me.f, per_pair) + h) * PLANE + src_s

        @pl.when(jnp.logical_not((src_y == me.y) & (src_f == me.f)))
        def _():
            remote(out_o.at[h], out_o.at[h], t_send.at[4, 0], t_recv.at[4, h], me.sib).wait_recv()

    o_each(lambda cp: cp.wait_send(), lambda cp: cp.wait())
    group_wait(5, c_cps, out_c)
    group_wait(1, a_cps, out_a)
    group_wait(6, line_cps, out_line)
    for group in (sum_b, sum_a, sum_c, sum_o):
        group.finish()
    scatter.finish_cores()
    scatter.finish_chips()
    layer.finish_chips()


def backward_call(cfg, *args):
    branch_all, o_all, a_all, tok = args[0], args[1], args[2], args[10]
    length, width = tok.shape
    planes, ff = cfg["planes"], cfg["ff"]
    n, r = a_all.shape[:2]
    chunk = ff // planes
    taps = cfg["kq"] * length
    pad_rows = -(-SIDE // o_all.shape[1])
    piece = 2 * cfg["dh"] // planes
    small = (3, 16, 128)
    hbm, vmem, smem = pl.BlockSpec(memory_space=pl.ANY), pl.BlockSpec(memory_space=pltpu.VMEM), pl.BlockSpec(memory_space=pltpu.SMEM)
    sds = jax.ShapeDtypeStruct
    dma = pltpu.SemaphoreType.DMA
    rows = (GROUP, length)
    others = planes - 1
    v16 = lambda *shape: pltpu.VMEM(shape, BF16)
    v32 = lambda *shape: pltpu.VMEM(shape, F32)
    b_block, o_block = (PLANE - FIRST, r, 2 * ff), (1, piece, width)
    a_block, c_block = (PLANE, r, SIDE), (PLANE, r, QKV - SIDE)
    return pl.pallas_call(
        functools.partial(backward_kernel, cfg),
        out_shape=(
            sds((length, width), F32), sds((length, width), F32), sds((GROUP, r, SIDE), BF16), sds((GROUP, r, QKV - SIDE), BF16),
            sds((GROUP, r, 2 * ff), BF16),
            sds((2, chunk, width), BF16), sds((2, piece, width), BF16), sds((GROUP,) + small, F32), sds((GROUP, 16, 128), F32),
        ),
        in_specs=[hbm] * 14 + [vmem] * 2,
        out_specs=(vmem,) + (hbm,) * 8,
        scratch_shapes=[
            v32(8, width), v32(*args[12].shape), v32(*args[13].shape), v16(*rows, width), v16(pad_rows, *o_all.shape[1:]), v16(n, r, QKV), v16(2, *rows, PLANE * r), v16(SLOTS, length, 3 * SIDE),
            v16(SLOTS, 2, 2, length, length), v16(SLOTS, 2, length, length),
            v16(2, taps, length), v16(length, taps), v32(length + 8, length), v32(2, length, taps), v16(*rows, QKV),
            v16(n, r, SIDE), v16(n, r, QKV - SIDE), v16(planes, piece, width), v16(length, width), v32(8, SIDE), v32(8, width), v32(16, 128),
            v16(others, *b_block), v16(others, *a_block), v16(others, *c_block), v16(others, *o_block),
            v16(*b_block), v16(*a_block), v16(*c_block), v16(*o_block),
            v16(PLANE, r, 2 * ff), v16(*a_block), v16(*c_block), v16(*o_block), v16(*b_block), v32(64, width), v16(chunk, width),
            v32(*small), v32(others, *small), v32(16, 128), v32(others, 16, 128),
            *Scatter.scratch(length, width), *Scatter.scratch(length, width, cores=False),
            dma((4, planes)), dma((4, planes)), dma((others,)), dma((others,)), dma((others,)), dma((others,)), dma((7, GROUP)), dma((7, GROUP)),
            dma((12,)), dma((4, GROUP)),
        ],
        compiler_params=pltpu.CompilerParams(collective_id=3, has_side_effects=True, vmem_limit_bytes=54 * 2**20),
        name="attention_backward",
    )(*args)


def results_kernel(cfg, a_ref, c_ref, b_ref, d_ref, o_ref, small_ref, line_ref, g_tok, layer, qkv_ref, gate_ref, up_ref, down_ref, out_ref,
                   taps_ref, mix_ref, in_ref, mid_ref, heads_ref, tok_ref, layer_ref, vec_v):
    planes, ff = cfg["planes"], cfg["ff"]
    rows, width = out_ref.shape
    chunk = ff // planes
    low = lanes(rows, 128) < 64

    def slot(pair):
        home, x = pair // 2, pair % 2
        y, c = (0, 1, 1, 0)[home], (0, 0, 1, 1)[home]
        return y * PLANE + x * 2 + c

    def joined(even, odd, low):
        o0, o1 = pltpu.roll(odd[0], 64, 1), pltpu.roll(odd[1], 64, 1)
        return even[0], jnp.where(low, even[1], o0), jnp.where(low, o0, o1)

    def tiles(pair, j):
        def t(i):
            ref, i = (a_ref, i) if i < 2 else (c_ref, i - 2)
            return ref[slot(pair), :, i * 128 : (i + 1) * 128].astype(F32)

        if j == 2:
            return t(4), pltpu.roll(t(1), 64, 1)
        return t(2 * j), t(2 * j + 1)

    for j in range(3):
        for two in range(GROUP // 2):
            for i, t in enumerate(joined(tiles(2 * two, j), tiles(2 * two + 1, j), low)):
                at = j * width + two * 384 + i * 128
                qkv_ref[:, at : at + 128] = t
    for z in range(planes):
        for s in range(PLANE):
            for y in range(2):
                at = ((z * PLANE + s) * 2 + y) * chunk
                src = b_ref.at[y * PLANE + s]
                gate_ref[:, at : at + chunk] = src[:, z * chunk : (z + 1) * chunk].astype(F32)
                up_ref[:, at : at + chunk] = src[:, ff + z * chunk : ff + (z + 1) * chunk].astype(F32)
    down_ref[...] = d_ref[0].astype(F32)
    out_ref[...] = o_ref[0].astype(F32)

    tok_ref[...] = g_tok[...]
    layer_ref[...] = layer[...]

    @pl.when(pl.program_id(0) == 0)
    def _():
        base = 1
        heads = 2 * GROUP
        taps = small_ref[0, 0]
        for s in range(1, GROUP):
            taps = taps + small_ref[s, 0]
        for k in range(cfg["kk"]):
            for q in range(cfg["kq"]):
                taps_ref[k, q : q + 1] = taps[k : k + 1, q * heads : (q + 1) * heads]
        mixed = [jnp.sum(small_ref[slot(pair), base], axis=-1, keepdims=True) for pair in range(GROUP)]
        for g in range(2):
            line = jnp.zeros((1, heads), F32)
            for pair in range(GROUP):
                for o in range(2):
                    k = 2 * o + g
                    line = jnp.where(lanes(1, heads) == 2 * pair + o, mixed[pair][k : k + 1], line)
            mix_ref[g : g + 1] = line
        vec_v[...] = jnp.zeros(vec_v.shape, F32)
        for k, part in enumerate((lambda s: line_ref[s], lambda s: small_ref[s, base + 1])):
            total = part(0)
            for s in range(1, GROUP):
                total = total + part(s)
            for j in range(width // 128):
                vec_v[k : k + 1, j * 128 : (j + 1) * 128] = total[j : j + 1]
        line = lambda pair: tuple(small_ref[slot(pair), base, 4 + j : 5 + j] for j in range(2))
        for two in range(GROUP // 2):
            for i, t in enumerate(joined(line(2 * two), line(2 * two + 1), lanes(1, 128) < 64)):
                vec_v[2:3, two * 384 + i * 128 : two * 384 + (i + 1) * 128] = t
        own = in_ref.shape[1]
        mine = pltpu.roll(vec_v[...], lax.rem(width - lax.axis_index("fsdp") * own, width), 1)
        for k, ref in enumerate((in_ref, mid_ref, heads_ref)):
            ref[...] = mine[k : k + 1, 0:own]


def results_call(cfg, out_a, out_c, out_b, out_d, out_o, small, line, g_tokens, layer_out):
    r = out_a.shape[1]
    _, chunk, width = out_d.shape
    half = r // 2
    sds = jax.ShapeDtypeStruct
    whole = lambda shape: pl.BlockSpec(shape, lambda i: (0,) * len(shape))
    rows = lambda n, w: pl.BlockSpec((n, w), lambda i: (i, 0))
    moved = 6 * (out_a.size + out_c.size + out_b.size + out_d.size + out_o.size) + 16 * g_tokens.size
    return pl.pallas_call(
        functools.partial(results_kernel, cfg),
        grid=(2,),
        out_shape=(
            sds((r, 3 * width), F32), sds((r, n_cols(cfg)), F32), sds((r, n_cols(cfg)), F32), sds((2 * chunk, width), F32),
            sds((r, width), F32), sds((cfg["kk"], cfg["kq"], 2 * GROUP), F32), sds((2, 2 * GROUP), F32),
            sds((1, r), F32), sds((1, r), F32), sds((1, r), F32), sds(g_tokens.shape, F32), sds(g_tokens.shape, F32),
        ),
        in_specs=[
            pl.BlockSpec((GROUP, half, out_a.shape[2]), lambda i: (0, i, 0)),
            pl.BlockSpec((GROUP, half, out_c.shape[2]), lambda i: (0, i, 0)),
            pl.BlockSpec((GROUP, half, out_b.shape[2]), lambda i: (0, i, 0)),
            pl.BlockSpec((1, chunk, width), lambda i: (i, 0, 0)),
            pl.BlockSpec((1, half, width), lambda i: (i, 0, 0)),
            whole(small.shape),
            whole(line.shape),
            rows(g_tokens.shape[0] // 2, width),
            rows(g_tokens.shape[0] // 2, width),
        ],
        scratch_shapes=[pltpu.VMEM((8, width), F32)],
        out_specs=(
            rows(half, 3 * width), rows(half, n_cols(cfg)), rows(half, n_cols(cfg)), rows(chunk, width), rows(half, width),
            whole((cfg["kk"], cfg["kq"], 2 * GROUP)), whole((2, 2 * GROUP)),
            whole((1, r)), whole((1, r)), whole((1, r)), rows(g_tokens.shape[0] // 2, width), rows(g_tokens.shape[0] // 2, width),
        ),
        compiler_params=pltpu.CompilerParams(vmem_limit_bytes=60 * 2**20),
        cost_estimate=pl.CostEstimate(flops=0, bytes_accessed=moved, transcendentals=0),
        name="results",
    )(out_a, out_c, out_b, out_d, out_o, small, line, g_tokens, layer_out)


def n_cols(cfg):
    return cfg["ff"] * GROUP


def fits(mesh, tokens, kernel, w_gate):
    n = mesh.shape["fsdp"]
    width, length, heads, ff = tokens.shape[2], tokens.shape[1], kernel.shape[0], w_gate.shape[1]
    return (
        mesh.shape["rep"] == 2
        and n == 4 * PLANE
        and heads == 2 * GROUP
        and width == heads * 96
        and (width // n) % 32 == 0
        and ff % (2 * n * 128) == 0
        and length == SIDE
    )


def per_device_group(
    planes,
    tokens,
    doc_lengths,
    pad_counts,
    norm_in,
    w_qkv,
    kernel,
    mixing,
    norm_heads,
    w_out,
    norm_mid,
    w_gate,
    w_up,
    w_down,
    cotangent,
):
    length, width = tokens.shape[1:]
    heads, kq, kk = kernel.shape
    dh = width // heads
    n = planes * PLANE
    r = width // n
    chunk = w_down.shape[0] // 2
    ff = planes * chunk
    cfg = dict(planes=planes, dh=dh, kq=kq, kk=kk, ff=ff)

    gain_rows = jnp.pad(jnp.stack([norm_in, norm_mid, norm_heads]).astype(F32), ((0, 5), (0, 128 - r)))
    tok, ct = tokens[0], cotangent[0]
    kern, mix = kernel.transpose(2, 1, 0), mixing.T

    (_, ct_all, a_all, b_all, d_all, o_all, nrm_all, qkv_all, p_all, m_all, gated_all, mid_all, resid, ends) = (
        forward_call(
            cfg, tok, ct, w_qkv, w_gate, w_up, w_down, w_out, kern, mix, gain_rows, doc_lengths, pad_counts
        )
    )
    g_res, branch_all, dw_b, out_red = feed_call(cfg, mid_all, ct_all, b_all, d_all, resid)
    g_tokens, layer_out, out_a, out_c, out_b, out_d, out_o, small, line = backward_call(
        cfg, branch_all, o_all, a_all, nrm_all, qkv_all, p_all, m_all, gated_all, dw_b.reshape(n, r, 2 * ff), out_red,
        tok, resid, kern, mix, g_res, ends,
    )

    g_qkv, g_gate, g_up, g_down, g_out, g_kernel, g_mixing, g_in, g_mid, g_heads, g_tokens, layer_out = results_call(
        cfg, out_a, out_c, out_b, out_d, out_o, small, line, g_tokens, layer_out
    )
    return (
        layer_out[None],
        g_tokens[None],
        g_in[0],
        g_qkv,
        g_kernel.transpose(2, 1, 0),
        g_mixing.T,
        g_heads[0],
        g_out,
        g_mid[0],
        g_gate,
        g_up,
        g_down,
    )


def solution(mesh):
    in_specs = (
        P(("rep", "fsdp"), None, None),
        P(("rep", "fsdp"), None),
        P(("rep", "fsdp")),
        P("fsdp"),
        P("fsdp", None),
        P(),
        P(),
        P("fsdp"),
        P("fsdp", None),
        P("fsdp"),
        P("fsdp", None),
        P("fsdp", None),
        P("fsdp", None),
        P(("rep", "fsdp"), None, None),
    )
    out_specs = (
        P(("rep", "fsdp"), None, None),
        P(("rep", "fsdp"), None, None),
        P("fsdp"),
        P("fsdp", None),
        P(),
        P(),
        P("fsdp"),
        P("fsdp", None),
        P("fsdp"),
        P("fsdp", None),
        P("fsdp", None),
        P("fsdp", None),
    )

    def layer(*args):
        body = per_device
        if fits(mesh, args[0], args[5], args[10]):
            body = functools.partial(per_device_group, mesh.shape["fsdp"] // PLANE)
        return jax.shard_map(body, mesh=mesh, in_specs=in_specs, out_specs=out_specs, check_vma=False)(*args)

    return layer
```
